32 devices in a mesh: grp: 4 (over y, x), seq: 8 (over z, core).
Axes of the slice: x: 2, y: 2, z: 4, core: 2. Of those that a mesh axis runs over, the one named last changes fastest.
Arguments:
- tokens: bfloat16 [12288, 1024], P(('grp', 'seq')), may hold values from -6 to 6
- valid: int32 [12288], P(('grp', 'seq')), may hold values from 0 to 1, as said below
- prompt_of: int32 [32], P(('grp', 'seq')), may hold values from 0 to 1, as said below
- teacher: bfloat16 [12288, 1024], P(('grp', 'seq')), may hold values from -8 to 8
- cotangent: bfloat16 [12288, 1024], P(('grp', 'seq')), may hold values from -6 to 6
- ln1_gain: bfloat16 [1024], P(('grp', 'seq')), may hold values from 0.25 to 1.75
- ln1_bias: bfloat16 [1024], P(('grp', 'seq')), may hold values from -1.75 to 1.75
- ln2_gain: bfloat16 [1024], P(('grp', 'seq')), may hold values from 0.25 to 1.75
- ln2_bias: bfloat16 [1024], P(('grp', 'seq')), may hold values from -1.75 to 1.75
- qkv_weight: bfloat16 [1024, 3072], P(('grp', 'seq')), may hold values from -0.25 to 0.25
- qkv_bias: bfloat16 [3072], P(('grp', 'seq')), may hold values from -1.75 to 1.75
- out_weight: bfloat16 [1024, 1024], P(('grp', 'seq')), may hold values from -1 to 1
- out_bias: bfloat16 [1024], P(('grp', 'seq')), may hold values from -1.75 to 1.75
- up_weight: bfloat16 [1024, 4096], P(('grp', 'seq')), may hold values from -0.1875 to 0.1875
- up_bias: bfloat16 [4096], P(('grp', 'seq')), may hold values from -1.75 to 1.75
- down_weight: bfloat16 [4096, 1024], P(('grp', 'seq')), may hold values from -0.1875 to 0.1875
- down_bias: bfloat16 [1024], P(('grp', 'seq')), may hold values from -1.75 to 1.75
Outputs:
- output: bfloat16 [12288, 1024], P(('grp', 'seq'))
- loss_value: float32 [], replicated
- input_grad: float32 [12288, 1024], P(('grp', 'seq'))
- ln1_gain_grad: float32 [1024], P(('grp', 'seq'))
- ln1_bias_grad: float32 [1024], P(('grp', 'seq'))
- ln2_gain_grad: float32 [1024], P(('grp', 'seq'))
- ln2_bias_grad: float32 [1024], P(('grp', 'seq'))
- qkv_weight_grad: float32 [1024, 3072], P(('grp', 'seq'))
- qkv_bias_grad: float32 [3072], P(('grp', 'seq'))
- out_weight_grad: float32 [1024, 1024], P(('grp', 'seq'))
- out_bias_grad: float32 [1024], P(('grp', 'seq'))
- up_weight_grad: float32 [1024, 4096], P(('grp', 'seq'))
- up_bias_grad: float32 [4096], P(('grp', 'seq'))
- down_weight_grad: float32 [4096, 1024], P(('grp', 'seq'))
- down_bias_grad: float32 [1024], P(('grp', 'seq'))
The draws below stay inside these ranges and needn't reach their ends.
Inputs may be any that keep to these rules, and one draw needn't show every extreme that they name: Prompt tokens are all valid; the valid tokens of a continuation are a prefix of 1 to 512 tokens, and in each group one continuation is valid throughout. `prompt_of`: entries 2 * i and 2 * i + 1 of each group's 8 entries are equal; each group uses both prompts.
All inputs are finite; a program needn't handle non-finite values.
Results may differ from the reference program's by a relative error of at most 0.012.
The reference program's roundings to bfloat16 on the way count: a program that leaves them out, or rounds other values in their place, can miss the bound.
Values may be sent and summed in bfloat16 or wider, within the bound.
A program may use at most 320 MiB of HBM per device.

```python
import jax
import jax.numpy as jnp
from jax import lax

D = 1024
H = 16
HD = 64
ROT = 16
FF = 4096
PSH = 64
CONT = 512
PLEN = 512
TOK_DEV = 384
TOKENS = 12288
N_GRP = 4
N_SEQ = 8
DEVICES = 32


def draw_valid(key, part):
    key = jax.random.fold_in(key, 11)
    length_key, whole_key = jax.random.split(key)
    cont_count = N_SEQ // 2
    lengths = jax.random.randint(length_key, (N_GRP, cont_count), 1, CONT + 1)
    whole_one = jax.random.randint(whole_key, (N_GRP, 1), 0, cont_count)
    lengths = jnp.where(jnp.arange(cont_count)[None, :] == whole_one, CONT, lengths)
    seat_ids = jnp.arange(N_SEQ)
    length_seat = lengths[:, seat_ids // 2]
    steps_here = (seat_ids % 2)[None, :, None] * (CONT // 2) + jnp.arange(CONT // 2)[None, None, :]
    cont_flags = (steps_here < length_seat[:, :, None]).astype(jnp.int32)
    prompt_flags = jnp.ones((N_GRP, N_SEQ, 2 * PSH), jnp.int32)
    return jnp.concatenate([prompt_flags, cont_flags], axis=2).reshape(-1)


def draw_prompt_of(key, part):
    key = jax.random.fold_in(key, 7)
    pick_key, anchor_key = jax.random.split(key)
    cont_count = N_SEQ // 2
    prompt_pick = jax.random.randint(pick_key, (N_GRP, cont_count), 0, 2)
    anchor = jax.random.randint(anchor_key, (N_GRP, 1), 0, cont_count)
    position = jnp.arange(cont_count)[None, :]
    prompt_pick = jnp.where(position == anchor, 0, prompt_pick)
    prompt_pick = jnp.where(position == (anchor + 1) % cont_count, 1, prompt_pick)
    return jnp.repeat(prompt_pick, 2, axis=1).reshape(-1).astype(jnp.int32)


def teacher_field(key, base, ratio, noise):
    device_ids = jnp.arange(TOKENS, dtype=jnp.float32) // TOK_DEV
    fraction = device_ids / max(DEVICES - 1, 1)
    scales = base * ratio ** fraction
    return scales[:, None] * noise


def draw_teacher(key, part):
    key = jax.random.fold_in(key, 23)
    noise = jnp.clip(jax.random.normal(key, (TOKENS, D), jnp.float32), -4.5, 4.5)
    return teacher_field(key, 0.5, 3.0, noise).astype(jnp.bfloat16)


def shard_levels(key, extent, cuts, least, top_value):
    loudness, own = 1.0, jax.random.fold_in(key, 6)
    for dim, blocks in cuts:
        steps = jnp.exp(jax.random.uniform(jax.random.fold_in(own, dim), (blocks,), jnp.float32, least / len(cuts), top_value / len(cuts)))
        loudness = loudness * jnp.repeat(steps, extent[dim] // blocks).reshape([-1 if axis == dim else 1 for axis in range(len(extent))])
    return loudness


def bell_draw(key, dims, deviation, reach, shards=(), held_as=jnp.bfloat16):
    values = deviation * jax.random.normal(key, dims, jnp.float32)
    if shards:
        values = values * shard_levels(key, dims, shards, -0.22, 0.18)
    return jnp.clip(values, -reach, reach).astype(held_as)


def setup_inputs(seed: int = 0) -> dict:
    key_list = jax.random.split(jax.random.key(seed), 18)
    return {
        "tokens": bell_draw(key_list[0], (TOKENS, D), 1.0, 6.0, ((0, 32),)),
        "valid": draw_valid(jax.random.fold_in(key_list[17], 71), 0),
        "prompt_of": draw_prompt_of(jax.random.fold_in(key_list[17], 71), 0),
        "teacher": draw_teacher(jax.random.fold_in(key_list[17], 71), 0),
        "cotangent": bell_draw(key_list[4], (TOKENS, D), 1.0, 6.0, ((0, 32),)),
        "ln1_gain": jnp.clip(1.0 + 0.15 * jax.random.normal(key_list[5], (D,), jnp.float32), 0.25, 1.75).astype(jnp.bfloat16),
        "ln1_bias": bell_draw(key_list[6], (D,), 0.3, 1.75, ((0, 32),)),
        "ln2_gain": jnp.clip(1.0 + 0.15 * jax.random.normal(key_list[7], (D,), jnp.float32), 0.25, 1.75).astype(jnp.bfloat16),
        "ln2_bias": bell_draw(key_list[8], (D,), 0.3, 1.75, ((0, 32),)),
        "qkv_weight": bell_draw(key_list[9], (D, 3 * D), (D // 2) ** -0.5, 0.25, ((0, 32),)),
        "qkv_bias": bell_draw(key_list[10], (3 * D,), 0.3, 1.75, ((0, 32),)),
        "out_weight": bell_draw(key_list[11], (D, D), (D // 32) ** -0.5, 1.0, ((0, 32),)),
        "out_bias": bell_draw(key_list[12], (D,), 0.3, 1.75, ((0, 32),)),
        "up_weight": bell_draw(key_list[13], (D, FF), D ** -0.5, 0.1875, ((0, 32),)),
        "up_bias": bell_draw(key_list[14], (FF,), 0.3, 1.75, ((0, 32),)),
        "down_weight": bell_draw(key_list[15], (FF, D), (FF // 4) ** -0.5, 0.1875, ((0, 32),)),
        "down_bias": bell_draw(key_list[16], (D,), 0.3, 1.75, ((0, 32),)),
    }


HIGHEST = lax.Precision.HIGHEST
EPSILON = 1e-05
NEGATIVE = -1e+30
SCALE = 0.125

@jax.custom_vjp
def low(v):
    return lax.optimization_barrier(v.astype(jnp.bfloat16)).astype(jnp.float32)

@jax.custom_vjp
def low_back(v):
    return v

def low_keep(v):
    return (low(v), None)

def low_pass(kept, grad):
    return (grad,)

def back_keep(v):
    return (v, None)

def back_low(kept, grad):
    return (low(grad),)
low.defvjp(low_keep, low_pass)
low_back.defvjp(back_keep, back_low)

def layer_norm(values, scales, offset):
    center = values - lax.optimization_barrier(jnp.mean(values, axis=-1, keepdims=True))
    variance = lax.optimization_barrier(jnp.mean(center * center, axis=-1, keepdims=True))
    return center * lax.rsqrt(variance + EPSILON) * scales + offset

def rotate_heads(values, places, direction):
    halfrot = ROT // 2
    inverse = 10000.0 ** (-jnp.arange(halfrot, dtype=jnp.float32) / halfrot)
    angles = places.astype(jnp.float32)[..., None] * inverse
    cosine = jnp.cos(angles)[..., None, :]
    sine_part = direction * jnp.sin(angles)[..., None, :]
    leading = values[..., :halfrot]
    trailing = values[..., halfrot:ROT]
    return jnp.concatenate([leading * cosine - trailing * sine_part, trailing * cosine + leading * sine_part, values[..., ROT:]], axis=-1)

def token_places():
    seat_ids = jnp.arange(N_SEQ, dtype=jnp.int32)[:, None]
    row_ids = jnp.arange(TOK_DEV, dtype=jnp.int32)[None, :]
    prompt_place = seat_ids * PSH + row_ids % PSH
    cont_place = PSH * N_SEQ + seat_ids % 2 * (CONT // 2) + row_ids - 2 * PSH
    return jnp.where(row_ids < 2 * PSH, prompt_place, cont_place)

def prompt_rows(array_in):
    trailing_dims = array_in.shape[2:]
    blocked = array_in[:, :2 * PSH].reshape((N_SEQ, 2, PSH) + trailing_dims)
    return jnp.swapaxes(blocked, 0, 1).reshape((2, N_SEQ * PSH) + trailing_dims)

def cont_rows(array_in):
    trailing_dims = array_in.shape[2:]
    return array_in[:, 2 * PSH:].reshape((N_SEQ // 2, CONT) + trailing_dims)

def masked_softmax(scores, allowed):
    scores = jnp.where(allowed, scores, NEGATIVE)
    largest = lax.optimization_barrier(jnp.max(scores, axis=-1, keepdims=True))
    weights = jnp.exp(scores - largest)
    return weights / lax.optimization_barrier(jnp.sum(weights, axis=-1, keepdims=True))

def head_attention(query_head, key_head, value_head, cont_valid, prompt_ids):
    prompt_query = prompt_rows(query_head)
    prompt_key = prompt_rows(key_head)
    prompt_value = prompt_rows(value_head)
    causal = jnp.arange(PLEN)[None, :] <= jnp.arange(PLEN)[:, None]
    prompt_scores = low_back(jnp.einsum('pqd,pkd->pqk', prompt_query, prompt_key, precision=HIGHEST) * SCALE)
    prompt_weights = low(masked_softmax(prompt_scores, causal[None]))
    prompt_out = jnp.einsum('pqk,pkd->pqd', prompt_weights, prompt_value, precision=HIGHEST)
    cont_query = cont_rows(query_head)
    cont_key = cont_rows(key_head)
    cont_value = cont_rows(value_head)
    chosen_key = prompt_key[prompt_ids]
    chosen_value = prompt_value[prompt_ids]
    far_scores = jnp.einsum('cqd,ckd->cqk', cont_query, chosen_key, precision=HIGHEST)
    near_scores = jnp.einsum('cqd,ckd->cqk', cont_query, cont_key, precision=HIGHEST)
    joint_scores = low_back(jnp.concatenate([far_scores, near_scores], axis=-1) * SCALE)
    steps_seen = jnp.arange(CONT)[None, :] <= jnp.arange(CONT)[:, None]
    allowed = jnp.concatenate([jnp.ones((N_SEQ // 2, CONT, PLEN), dtype=bool), steps_seen[None] & cont_valid[:, None, :]], axis=-1)
    joint_weights = low(masked_softmax(joint_scores, allowed))
    cont_out = jnp.einsum('cqk,ckd->cqd', joint_weights[..., :PLEN], chosen_value, precision=HIGHEST)
    cont_out = cont_out + jnp.einsum('cqk,ckd->cqd', joint_weights[..., PLEN:], cont_value, precision=HIGHEST)
    prompt_back = jnp.swapaxes(prompt_out.reshape(2, N_SEQ, PSH, HD), 0, 1).reshape(N_SEQ, 2 * PSH, HD)
    return jnp.concatenate([prompt_back, cont_out.reshape(N_SEQ, CONT // 2, HD)], axis=1)

def group_layer(inputs, cont_valid, prompt_ids, params):
    ln1_scale, ln1_offset, ln2_scale, ln2_offset, qkv_matrix, qkv_offset, out_matrix, out_offset, up_matrix, up_offset, down_matrix, down_offset = params
    first_in = low(layer_norm(inputs, ln1_scale, ln1_offset))
    second_in = low(layer_norm(inputs, ln2_scale, ln2_offset))
    projected = low_back(jnp.dot(first_in, qkv_matrix, precision=HIGHEST) + qkv_offset)
    projected = projected.reshape(N_SEQ, TOK_DEV, 3, H, HD)
    places = token_places()
    queries = low(rotate_heads(projected[:, :, 0], places, 1.0))
    keys_all = low(rotate_heads(projected[:, :, 1], places, 1.0))
    values_all = low(projected[:, :, 2])

    def one_head(operands):
        return head_attention(operands[0], operands[1], operands[2], cont_valid, prompt_ids)
    mixed_heads = lax.map(jax.checkpoint(one_head), (jnp.moveaxis(queries, 2, 0), jnp.moveaxis(keys_all, 2, 0), jnp.moveaxis(values_all, 2, 0)))
    joined = jnp.moveaxis(mixed_heads, 0, 2).reshape(N_SEQ * TOK_DEV, D)
    attended = low_back(low(joined))
    attn_branch = low_back(jnp.dot(attended, out_matrix, precision=HIGHEST) + out_offset)
    hidden_pre = low_back(jnp.dot(second_in, up_matrix, precision=HIGHEST) + up_offset)
    activated = low(jax.nn.gelu(hidden_pre, approximate=False))
    mlp_branch = low_back(jnp.dot(activated, down_matrix, precision=HIGHEST) + down_offset)
    return inputs + attn_branch + mlp_branch

def reference(tokens, valid, prompt_of, teacher, cotangent, ln1_gain, ln1_bias, ln2_gain, ln2_bias, qkv_weight, qkv_bias, out_weight, out_bias, up_weight, up_bias, down_weight, down_bias):
    params = tuple((array_in.astype(jnp.float32) for array_in in (ln1_gain, ln1_bias, ln2_gain, ln2_bias, qkv_weight, qkv_bias, out_weight, out_bias, up_weight, up_bias, down_weight, down_bias)))
    inputs = tokens.astype(jnp.float32)
    targets = teacher.astype(jnp.float32).reshape(N_GRP, N_SEQ * TOK_DEV, D)
    live_rows = valid.astype(jnp.float32).reshape(N_GRP, N_SEQ * TOK_DEV, 1)
    cont_live = (valid.reshape(N_GRP, N_SEQ, TOK_DEV)[:, :, 2 * PSH:] > 0).reshape(N_GRP, N_SEQ // 2, CONT)
    group_ids = prompt_of.reshape(N_GRP, N_SEQ)[:, ::2]
    total_count = jnp.sum(live_rows)

    def forward(inputs, params):
        grouped = inputs.reshape(N_GRP, N_SEQ * TOK_DEV, D)

        def per_group(running, operands):
            group_in, group_live, group_pick, group_target, group_mask = operands
            result = group_layer(group_in, group_live, group_pick, params)
            squared = jnp.sum(group_mask * (result - group_target) ** 2)
            return (running + squared, result)
        summed, results = lax.scan(jax.checkpoint(per_group), jnp.zeros((), jnp.float32), (grouped, cont_live, group_ids, targets, live_rows))
        return (results.reshape(TOKENS, D), summed / (total_count * D))
    (output, loss_value), pullback = jax.vjp(forward, inputs, params)
    input_grad, param_grads = pullback((cotangent.astype(jnp.float32), jnp.ones_like(loss_value)))
    return (output.astype(jnp.bfloat16), loss_value, input_grad, param_grads[0], param_grads[1], param_grads[2], param_grads[3], param_grads[4], param_grads[5], param_grads[6], param_grads[7], param_grads[8], param_grads[9], param_grads[10], param_grads[11])
```

```python
import functools

import jax
import jax.numpy as jnp
import numpy as np
from jax import lax
from jax.experimental import pallas as pl
from jax.experimental.pallas import tpu as pltpu
from jax.sharding import Mesh
from jax.sharding import PartitionSpec as P

D = 1024
H = 16
HD = 64
ROT = 16
FF = 4096
PSH = 64
CONT = 512
HALF = CONT // 2
HC = H // 2 * HD
EPSILON = 1e-05
NEGATIVE = -1e30
SCALE = 0.125
BF = jnp.bfloat16
F32 = jnp.float32
ALL = ("grp", "chip", "core")
CHIPS = ("grp", "chip")


def swap_cores(x):
    return lax.ppermute(x, "core", [(0, 1), (1, 0)])


def pair_rows(own):
    both = lax.all_gather(own, "core", axis=0)
    prompts = both[:, : 2 * PSH].reshape((2, 2, PSH) + own.shape[1:])
    prompts = prompts.swapaxes(0, 1).reshape((4 * PSH,) + own.shape[1:])
    return jnp.concatenate([prompts, both[:, 2 * PSH :].reshape((CONT,) + own.shape[1:])], axis=0)


def split_rows(rows):
    prompts = rows[: 4 * PSH].reshape((2, 2, PSH) + rows.shape[1:]).swapaxes(0, 1)
    prompts = prompts.reshape((2, 2 * PSH) + rows.shape[1:])
    return jnp.concatenate([prompts, rows[4 * PSH :].reshape((2, HALF) + rows.shape[1:])], axis=1)


def normalize(values):
    center = values - jnp.mean(values, axis=-1, keepdims=True)
    inverse_dev = lax.rsqrt(jnp.mean(center * center, axis=-1, keepdims=True) + EPSILON)
    return (center * inverse_dev, inverse_dev)


def rotate_heads(values, places, direction):
    halfrot = ROT // 2
    inverse = 10000.0 ** (-jnp.arange(halfrot, dtype=F32) / halfrot)
    angles = places.astype(F32)[..., None] * inverse
    cosine = jnp.cos(angles)[..., None, :]
    sine_part = direction * jnp.sin(angles)[..., None, :]
    leading = values[..., :halfrot]
    trailing = values[..., halfrot:ROT]
    return jnp.concatenate(
        [
            leading * cosine - trailing * sine_part,
            trailing * cosine + leading * sine_part,
            values[..., ROT:],
        ],
        axis=-1,
    )


def gelu_slope(values):
    return (
        0.5 * (1.0 + lax.erf(values * 0.7071067811865476))
        + values * jnp.exp(-0.5 * values * values) * 0.3989422804014327
    )


def dot(a, b, contract):
    return lax.dot_general(a, b, ((contract[:1], contract[1:]), ((), ())), preferred_element_type=F32)


def g_weights(c, qkv_weight, out_weight, up_weight, down_weight):
    r = qkv_weight.shape[0]
    mine = functools.partial(lax.dynamic_index_in_dim, index=c, keepdims=False)
    both = lambda w: lax.all_gather(w, "core", axis=0, tiled=True)
    qkv = mine(both(qkv_weight).reshape(2 * r, 3, 2, HC), axis=2).reshape(2 * r, 3 * HC)
    qkv = lax.all_gather(qkv, CHIPS, axis=0, tiled=True)
    rd = down_weight.shape[0]
    up = mine(both(up_weight).reshape(2 * r, FF // (2 * rd), 2, rd), axis=2).reshape(2 * r, FF // 2)
    up = lax.all_gather(up, CHIPS, axis=0, tiled=True)
    down = lax.all_gather(down_weight, CHIPS, axis=0, tiled=True)
    out = lax.all_gather(out_weight, ALL, axis=0, tiled=True)
    out = mine(out.reshape(2, HC, D), axis=0)
    return qkv, out, up, down


def g_small(c, rd, ln1_gain, ln1_bias, ln2_gain, ln2_bias, qkv_bias, out_bias, up_bias, down_bias):
    sizes = [v.shape[0] for v in (ln1_gain, ln1_bias, ln2_gain, ln2_bias, out_bias, down_bias, qkv_bias, up_bias)]
    packed = jnp.concatenate([ln1_gain, ln1_bias, ln2_gain, ln2_bias, out_bias, down_bias, qkv_bias, up_bias])
    rows = lax.all_gather(packed, ALL, axis=0)
    parts, at = [], 0
    for size in sizes:
        parts.append(rows[:, at : at + size].reshape(-1).astype(F32))
        at += size
    qb = lax.dynamic_index_in_dim(parts[6].reshape(3, 2, HC), c, axis=1, keepdims=False).reshape(-1)
    ub = lax.dynamic_index_in_dim(parts[7].reshape(-1, 2, rd), c, axis=1, keepdims=False).reshape(-1)
    return parts[:6] + [qb, ub]


def places_of(z, chips):
    prompt = z * 2 * PSH + jnp.arange(2 * PSH)
    return jnp.concatenate([prompt, prompt, chips * 2 * PSH + jnp.arange(CONT)])


def masks_of(z, chips, cont_valid):
    length = chips * 2 * PSH
    prompt = jnp.arange(length)[None, :] <= z * 2 * PSH + jnp.arange(2 * PSH)[:, None]
    own = jnp.arange(CONT)[None, :] <= jnp.arange(CONT)[:, None]
    own = own & (cont_valid > 0)[None, :]
    return prompt, jnp.concatenate([jnp.ones((CONT, length), bool), own], axis=1)


def g_attention(q, prompt_kv, kv, chosen, masks):
    nh = HC // HD
    chips = prompt_kv.shape[0]
    pk = prompt_kv.reshape(chips, 2, 2 * PSH, 2, nh, HD).transpose(3, 4, 1, 0, 2, 5)
    pk = pk.reshape(2, nh, 2, chips * 2 * PSH, HD)
    qh = q.reshape(-1, nh, HD).swapaxes(0, 1)
    pq = qh[:, : 4 * PSH].reshape(nh, 2, 2 * PSH, HD)
    scores = jnp.einsum("hpqd,hpkd->hpqk", pq, pk[0], preferred_element_type=F32) * SCALE
    scores = jnp.where(masks[0], scores, NEGATIVE)
    top = jnp.max(scores, axis=-1, keepdims=True)
    weights = jnp.exp(scores - top)
    total = jnp.sum(weights, axis=-1, keepdims=True)
    p_out = jnp.einsum("hpqk,hpkd->hpqd", (weights / total).astype(BF), pk[1], preferred_element_type=F32)
    p_lse = (top + jnp.log(total))[..., 0].reshape(nh, 4 * PSH)
    far = lax.dynamic_index_in_dim(pk, chosen, axis=2, keepdims=False)
    near = kv[4 * PSH :].reshape(CONT, 2, nh, HD).transpose(1, 2, 0, 3)
    ck = jnp.concatenate([far, near], axis=2)
    cq = qh[:, 4 * PSH :]
    scores = jnp.einsum("hqd,hkd->hqk", cq, ck[0], preferred_element_type=F32) * SCALE
    scores = jnp.where(masks[1], scores, NEGATIVE)
    top = jnp.max(scores, axis=-1, keepdims=True)
    weights = jnp.exp(scores - top)
    total = jnp.sum(weights, axis=-1, keepdims=True)
    c_out = jnp.einsum("hqk,hkd->hqd", (weights / total).astype(BF), ck[1], preferred_element_type=F32)
    c_lse = (top + jnp.log(total))[..., 0]
    att = jnp.concatenate([p_out.reshape(nh, 4 * PSH, HD), c_out], axis=1)
    return att.swapaxes(0, 1).reshape(-1, HC).astype(BF), jnp.concatenate([p_lse, c_lse], axis=1)


def g_attention_back(q, prompt_kv, kv, att_grad, lse, chosen, masks):
    nh = HC // HD
    chips = prompt_kv.shape[0]
    pk = prompt_kv.reshape(chips, 2, 2 * PSH, 2, nh, HD).transpose(3, 4, 1, 0, 2, 5)
    pk = pk.reshape(2, nh, 2, chips * 2 * PSH, HD)
    qh = q.reshape(-1, nh, HD).swapaxes(0, 1)
    gh = att_grad.reshape(-1, nh, HD).swapaxes(0, 1)
    pq = qh[:, : 4 * PSH].reshape(nh, 2, 2 * PSH, HD)
    pg = gh[:, : 4 * PSH].reshape(nh, 2, 2 * PSH, HD)
    ein = functools.partial(jnp.einsum, preferred_element_type=F32)

    def back(eq, ek, query, key, value, grad, mask, lse_rows):
        scores = jnp.where(mask, ein(f"{eq},{ek}->{eq[:-1]}k", query, key) * SCALE, NEGATIVE)
        probs = jnp.exp(scores - lse_rows[..., None])
        prob_grad = ein(f"{eq},{ek}->{eq[:-1]}k", grad, value)
        inner = jnp.sum(probs * prob_grad, axis=-1, keepdims=True)
        score_grad = (probs * (prob_grad - inner)).astype(BF)
        es = eq[:-1] + "k"
        dq = ein(f"{es},{ek}->{eq}", score_grad, key) * SCALE
        dk = ein(f"{es},{eq}->{ek}", score_grad, query) * SCALE
        dv = ein(f"{es},{eq}->{ek}", probs.astype(BF), grad)
        return dq, dk, dv

    dq_p, dk_p, dv_p = back("hpqd", "hpkd", pq, pk[0], pk[1], pg, masks[0], lse[:, : 4 * PSH].reshape(nh, 2, 2 * PSH))
    far = lax.dynamic_index_in_dim(pk, chosen, axis=2, keepdims=False)
    near = kv[4 * PSH :].reshape(CONT, 2, nh, HD).transpose(1, 2, 0, 3)
    ck = jnp.concatenate([far, near], axis=2)
    dq_c, dk_c, dv_c = back("hqd", "hkd", qh[:, 4 * PSH :], ck[0], ck[1], gh[:, 4 * PSH :], masks[1], lse[:, 4 * PSH :])
    length = chips * 2 * PSH
    pick = (jnp.arange(2) == chosen).astype(F32)[None, :, None, None]
    dk_p = dk_p + pick * dk_c[:, None, :length]
    dv_p = dv_p + pick * dv_c[:, None, :length]
    dq = jnp.concatenate([dq_p.reshape(nh, 4 * PSH, HD), dq_c], axis=1).swapaxes(0, 1).reshape(-1, HC)
    pair = jnp.stack([dk_p, dv_p])
    pair = pair.reshape(2, nh, 2, chips, 2 * PSH, HD).transpose(3, 2, 4, 0, 1, 5).reshape(chips * 4 * PSH, 2 * HC)
    near_grad = jnp.stack([dk_c[:, length:], dv_c[:, length:]]).transpose(2, 0, 1, 3).reshape(CONT, 2 * HC)
    return dq, pair, near_grad


def generic_body(
    tokens, valid, prompt_of, teacher, cotangent,
    ln1_gain, ln1_bias, ln2_gain, ln2_bias, qkv_weight, qkv_bias, out_weight, out_bias,
    up_weight, up_bias, down_weight, down_bias, stop=None,
):
    c = lax.axis_index("core")
    z = lax.axis_index("chip")
    chips = lax.axis_size("chip")
    nh = HC // HD
    rd = down_weight.shape[0]
    device = lax.axis_index(ALL)
    w_qkv, w_out, w_up, w_down = g_weights(c, qkv_weight, out_weight, up_weight, down_weight)
    gain1, bias1, gain2, bias2, b_out, b_down, b_qkv, b_up = g_small(
        c, rd, ln1_gain, ln1_bias, ln2_gain, ln2_bias, qkv_bias, out_bias, up_bias, down_bias
    )
    x = pair_rows(tokens).astype(F32)
    normed, rstd = normalize(x)
    first_in = (normed * gain1 + bias1).astype(BF)
    second_in = (normed * gain2 + bias2).astype(BF)
    projected = dot(first_in, w_qkv, (1, 0)) + b_qkv
    places = places_of(z, chips)
    turn = lambda v, d: rotate_heads(v.reshape(-1, nh, HD), places, d).reshape(-1, HC)
    q = turn(projected[:, :HC], 1.0).astype(BF)
    k = turn(projected[:, HC : 2 * HC], 1.0).astype(BF)
    kv = jnp.concatenate([k, projected[:, 2 * HC :].astype(BF)], axis=1)
    prompt_kv = lax.all_gather(kv[: 4 * PSH].reshape(2, 2 * PSH, 2 * HC), "chip", axis=0)
    cont_valid = lax.all_gather(valid[2 * PSH :], "core", axis=0, tiled=True)
    masks = masks_of(z, chips, cont_valid)
    chosen = prompt_of[0]
    attended, lse = g_attention(q, prompt_kv, kv, chosen, masks)
    hidden_pre = dot(second_in, w_up, (1, 0)) + b_up
    activated = jax.nn.gelu(hidden_pre, approximate=False).astype(BF)
    partial = dot(attended, w_out, (1, 0)) + dot(activated, w_down, (1, 0))
    halves = split_rows(partial)
    take = lambda a: lax.dynamic_index_in_dim(a, c, axis=0, keepdims=False)
    give = lambda a: lax.dynamic_index_in_dim(a, 1 - c, axis=0, keepdims=False)
    output = tokens.astype(F32) + take(halves) + swap_cores(give(halves)) + b_out + b_down
    live = (valid > 0).astype(F32)[:, None]
    missed = output - teacher.astype(F32)
    count_all, squared_all = lax.psum((jnp.sum(live), jnp.sum(live * missed * missed)), ALL)
    loss_value = squared_all / (count_all * D)
    out_grad = cotangent.astype(F32) + 2.0 / (count_all * D) * live * missed
    out_low = pair_rows(out_grad.astype(BF))
    if stop == "fwd":
        return output, out_grad, out_low, attended, lse, activated, q, kv, first_in, second_in
    out_bias_grad = jnp.sum(out_grad.astype(BF).astype(F32), axis=0)
    dw_out = dot(attended, out_low, (0, 0))
    dw_down = dot(activated, out_low, (0, 0))
    att_grad = dot(out_low, w_out, (1, 1)).astype(BF)
    hidden_grad = (dot(out_low, w_down, (1, 1)) * gelu_slope(hidden_pre)).astype(BF)
    dw_up = dot(second_in, hidden_grad, (0, 0))
    db_up = jnp.sum(hidden_grad.astype(F32), axis=0)
    second_grad = dot(hidden_grad, w_up, (1, 1))
    dq, pair, near = g_attention_back(q, prompt_kv, kv, att_grad, lse, chosen, masks)
    own_pair = lax.psum_scatter(pair.astype(BF), "chip", scatter_dimension=0, tiled=True).astype(F32)
    pair = jnp.concatenate([own_pair, near], axis=0)
    projected_grad = jnp.concatenate([turn(dq, -1.0), turn(pair[:, :HC], -1.0), pair[:, HC:]], axis=1).astype(BF)
    dw_qkv = dot(first_in, projected_grad, (0, 0))
    db_qkv = jnp.sum(projected_grad.astype(F32), axis=0)
    first_grad = dot(projected_grad, w_qkv, (1, 1))
    if stop == "bwd":
        return dw_out, dw_down, dw_up, dw_qkv, second_grad, first_grad, projected_grad, hidden_grad, att_grad
    joint = first_grad * gain1 + second_grad * gain2
    halves = split_rows(joint)
    joint = take(halves) + swap_cores(give(halves))
    own_normed = take(split_rows(normed))
    own_rstd = take(split_rows(rstd))
    input_grad = out_grad + own_rstd * (
        joint
        - jnp.mean(joint, axis=-1, keepdims=True)
        - own_normed * jnp.mean(joint * own_normed, axis=-1, keepdims=True)
    )
    wide = lambda v, n: jnp.zeros((v.shape[0], 2, v.shape[1]), F32).at[:, c].set(v).reshape(-1)
    small = jnp.concatenate(
        [
            jnp.sum(first_grad * normed, axis=0),
            jnp.sum(first_grad, axis=0),
            jnp.sum(second_grad * normed, axis=0),
            jnp.sum(second_grad, axis=0),
            out_bias_grad,
            wide(db_qkv.reshape(3, HC), 3),
            wide(db_up.reshape(-1, rd), 16),
        ]
    )
    small = lax.psum(small, ALL)
    shares, at = [], 0
    for size in (D, D, D, D, D, 3 * D, FF):
        own = size // lax.axis_size(ALL)
        shares.append(lax.dynamic_slice_in_dim(small, at + device * own, own))
        at += size
    rs = lambda v: lax.psum_scatter(v.astype(BF), CHIPS, scatter_dimension=0, tiled=True).astype(F32)
    r = qkv_weight.shape[0]
    s_qkv = rs(dw_qkv).reshape(2, r, 3, HC)
    s_up = rs(dw_up).reshape(2, r, FF // (2 * rd), rd)
    s_down = rs(dw_down)
    pairs = lambda own, other, axis: jnp.where(c == 0, jnp.stack([own, other], axis), jnp.stack([other, own], axis))
    s_qkv = pairs(take(s_qkv), swap_cores(give(s_qkv)), 2).reshape(r, 3 * D)
    s_up = pairs(take(s_up), swap_cores(give(s_up)), 2).reshape(r, FF)
    o = dw_out.reshape(H // 2, -1, 2, r, D)
    o_own = lax.dynamic_index_in_dim(o, c, axis=2, keepdims=False)
    o_other = swap_cores(lax.dynamic_index_in_dim(o, 1 - c, axis=2, keepdims=False))
    s_out = rs(pairs(o_own, o_other, 0).reshape(-1, D))
    return (
        output.astype(BF), loss_value, input_grad, shares[0], shares[1], shares[2], shares[3],
        s_qkv, shares[5], s_out, shares[4], s_up, shares[6], s_down, shares[4],
    )


def solution(mesh):
    groups, seats = mesh.shape["grp"], mesh.shape["seq"]
    fine = Mesh(mesh.devices.reshape(groups, seats // 2, 2), ALL)
    rows, row = P(ALL, None), P(ALL)
    in_specs = (rows, row, row, rows, rows) + (row,) * 4 + (rows, row) * 4
    out_specs = (rows, P(), rows) + (row,) * 4 + (rows, row) * 4
    return jax.shard_map(generic_body, mesh=fine, in_specs=in_specs, out_specs=out_specs, check_vma=False)
```

```python
import functools

import jax
import jax.numpy as jnp
import numpy as np
from jax import lax
from jax.experimental import pallas as pl
from jax.experimental.pallas import tpu as pltpu
from jax.sharding import Mesh
from jax.sharding import PartitionSpec as P

D = 1024
H = 16
HD = 64
ROT = 16
FF = 4096
PSH = 64
CONT = 512
HALF = CONT // 2
HC = H // 2 * HD
EPSILON = 1e-05
NEGATIVE = -1e30
SCALE = 0.125
BF = jnp.bfloat16
F32 = jnp.float32
ALL = ("grp", "chip", "core")
CHIPS = ("grp", "chip")


def swap_cores(x):
    return lax.ppermute(x, "core", [(0, 1), (1, 0)])


def pair_rows(own):
    both = lax.all_gather(own, "core", axis=0)
    prompts = both[:, : 2 * PSH].reshape((2, 2, PSH) + own.shape[1:])
    prompts = prompts.swapaxes(0, 1).reshape((4 * PSH,) + own.shape[1:])
    return jnp.concatenate([prompts, both[:, 2 * PSH :].reshape((CONT,) + own.shape[1:])], axis=0)


def split_rows(rows):
    prompts = rows[: 4 * PSH].reshape((2, 2, PSH) + rows.shape[1:]).swapaxes(0, 1)
    prompts = prompts.reshape((2, 2 * PSH) + rows.shape[1:])
    return jnp.concatenate([prompts, rows[4 * PSH :].reshape((2, HALF) + rows.shape[1:])], axis=1)


def normalize(values):
    center = values - jnp.mean(values, axis=-1, keepdims=True)
    inverse_dev = lax.rsqrt(jnp.mean(center * center, axis=-1, keepdims=True) + EPSILON)
    return (center * inverse_dev, inverse_dev)


def rotate_heads(values, places, direction):
    halfrot = ROT // 2
    inverse = 10000.0 ** (-jnp.arange(halfrot, dtype=F32) / halfrot)
    angles = places.astype(F32)[..., None] * inverse
    cosine = jnp.cos(angles)[..., None, :]
    sine_part = direction * jnp.sin(angles)[..., None, :]
    leading = values[..., :halfrot]
    trailing = values[..., halfrot:ROT]
    return jnp.concatenate(
        [
            leading * cosine - trailing * sine_part,
            trailing * cosine + leading * sine_part,
            values[..., ROT:],
        ],
        axis=-1,
    )


def gelu_slope(values):
    return (
        0.5 * (1.0 + lax.erf(values * 0.7071067811865476))
        + values * jnp.exp(-0.5 * values * values) * 0.3989422804014327
    )


def dot(a, b, contract):
    return lax.dot_general(a, b, ((contract[:1], contract[1:]), ((), ())), preferred_element_type=F32)


def g_weights(c, qkv_weight, out_weight, up_weight, down_weight):
    r = qkv_weight.shape[0]
    mine = functools.partial(lax.dynamic_index_in_dim, index=c, keepdims=False)
    both = lambda w: lax.all_gather(w, "core", axis=0, tiled=True)
    qkv = mine(both(qkv_weight).reshape(2 * r, 3, 2, HC), axis=2).reshape(2 * r, 3 * HC)
    qkv = lax.all_gather(qkv, CHIPS, axis=0, tiled=True)
    rd = down_weight.shape[0]
    up = mine(both(up_weight).reshape(2 * r, FF // (2 * rd), 2, rd), axis=2).reshape(2 * r, FF // 2)
    up = lax.all_gather(up, CHIPS, axis=0, tiled=True)
    down = lax.all_gather(down_weight, CHIPS, axis=0, tiled=True)
    out = lax.all_gather(out_weight, ALL, axis=0, tiled=True)
    out = mine(out.reshape(2, HC, D), axis=0)
    return qkv, out, up, down


def g_small(c, rd, ln1_gain, ln1_bias, ln2_gain, ln2_bias, qkv_bias, out_bias, up_bias, down_bias):
    sizes = [v.shape[0] for v in (ln1_gain, ln1_bias, ln2_gain, ln2_bias, out_bias, down_bias, qkv_bias, up_bias)]
    packed = jnp.concatenate([ln1_gain, ln1_bias, ln2_gain, ln2_bias, out_bias, down_bias, qkv_bias, up_bias])
    rows = lax.all_gather(packed, ALL, axis=0)
    parts, at = [], 0
    for size in sizes:
        parts.append(rows[:, at : at + size].reshape(-1).astype(F32))
        at += size
    qb = lax.dynamic_index_in_dim(parts[6].reshape(3, 2, HC), c, axis=1, keepdims=False).reshape(-1)
    ub = lax.dynamic_index_in_dim(parts[7].reshape(-1, 2, rd), c, axis=1, keepdims=False).reshape(-1)
    return parts[:6] + [qb, ub]


def places_of(z, chips):
    prompt = z * 2 * PSH + jnp.arange(2 * PSH)
    return jnp.concatenate([prompt, prompt, chips * 2 * PSH + jnp.arange(CONT)])


def masks_of(z, chips, cont_valid):
    length = chips * 2 * PSH
    prompt = jnp.arange(length)[None, :] <= z * 2 * PSH + jnp.arange(2 * PSH)[:, None]
    own = jnp.arange(CONT)[None, :] <= jnp.arange(CONT)[:, None]
    own = own & (cont_valid > 0)[None, :]
    return prompt, jnp.concatenate([jnp.ones((CONT, length), bool), own], axis=1)


def g_attention(q, prompt_kv, kv, chosen, masks):
    nh = HC // HD
    chips = prompt_kv.shape[0]
    pk = prompt_kv.reshape(chips, 2, 2 * PSH, 2, nh, HD).transpose(3, 4, 1, 0, 2, 5)
    pk = pk.reshape(2, nh, 2, chips * 2 * PSH, HD)
    qh = q.reshape(-1, nh, HD).swapaxes(0, 1)
    pq = qh[:, : 4 * PSH].reshape(nh, 2, 2 * PSH, HD)
    scores = jnp.einsum("hpqd,hpkd->hpqk", pq, pk[0], preferred_element_type=F32) * SCALE
    scores = jnp.where(masks[0], scores, NEGATIVE)
    top = jnp.max(scores, axis=-1, keepdims=True)
    weights = jnp.exp(scores - top)
    total = jnp.sum(weights, axis=-1, keepdims=True)
    p_out = jnp.einsum("hpqk,hpkd->hpqd", (weights / total).astype(BF), pk[1], preferred_element_type=F32)
    p_lse = (top + jnp.log(total))[..., 0].reshape(nh, 4 * PSH)
    far = lax.dynamic_index_in_dim(pk, chosen, axis=2, keepdims=False)
    near = kv[4 * PSH :].reshape(CONT, 2, nh, HD).transpose(1, 2, 0, 3)
    ck = jnp.concatenate([far, near], axis=2)
    cq = qh[:, 4 * PSH :]
    scores = jnp.einsum("hqd,hkd->hqk", cq, ck[0], preferred_element_type=F32) * SCALE
    scores = jnp.where(masks[1], scores, NEGATIVE)
    top = jnp.max(scores, axis=-1, keepdims=True)
    weights = jnp.exp(scores - top)
    total = jnp.sum(weights, axis=-1, keepdims=True)
    c_out = jnp.einsum("hqk,hkd->hqd", (weights / total).astype(BF), ck[1], preferred_element_type=F32)
    c_lse = (top + jnp.log(total))[..., 0]
    att = jnp.concatenate([p_out.reshape(nh, 4 * PSH, HD), c_out], axis=1)
    return att.swapaxes(0, 1).reshape(-1, HC).astype(BF), jnp.concatenate([p_lse, c_lse], axis=1)


def g_attention_back(q, prompt_kv, kv, att_grad, lse, chosen, masks):
    nh = HC // HD
    chips = prompt_kv.shape[0]
    pk = prompt_kv.reshape(chips, 2, 2 * PSH, 2, nh, HD).transpose(3, 4, 1, 0, 2, 5)
    pk = pk.reshape(2, nh, 2, chips * 2 * PSH, HD)
    qh = q.reshape(-1, nh, HD).swapaxes(0, 1)
    gh = att_grad.reshape(-1, nh, HD).swapaxes(0, 1)
    pq = qh[:, : 4 * PSH].reshape(nh, 2, 2 * PSH, HD)
    pg = gh[:, : 4 * PSH].reshape(nh, 2, 2 * PSH, HD)
    ein = functools.partial(jnp.einsum, preferred_element_type=F32)

    def back(eq, ek, query, key, value, grad, mask, lse_rows):
        scores = jnp.where(mask, ein(f"{eq},{ek}->{eq[:-1]}k", query, key) * SCALE, NEGATIVE)
        probs = jnp.exp(scores - lse_rows[..., None])
        prob_grad = ein(f"{eq},{ek}->{eq[:-1]}k", grad, value)
        inner = jnp.sum(probs * prob_grad, axis=-1, keepdims=True)
        score_grad = (probs * (prob_grad - inner)).astype(BF)
        es = eq[:-1] + "k"
        dq = ein(f"{es},{ek}->{eq}", score_grad, key) * SCALE
        dk = ein(f"{es},{eq}->{ek}", score_grad, query) * SCALE
        dv = ein(f"{es},{eq}->{ek}", probs.astype(BF), grad)
        return dq, dk, dv

    dq_p, dk_p, dv_p = back("hpqd", "hpkd", pq, pk[0], pk[1], pg, masks[0], lse[:, : 4 * PSH].reshape(nh, 2, 2 * PSH))
    far = lax.dynamic_index_in_dim(pk, chosen, axis=2, keepdims=False)
    near = kv[4 * PSH :].reshape(CONT, 2, nh, HD).transpose(1, 2, 0, 3)
    ck = jnp.concatenate([far, near], axis=2)
    dq_c, dk_c, dv_c = back("hqd", "hkd", qh[:, 4 * PSH :], ck[0], ck[1], gh[:, 4 * PSH :], masks[1], lse[:, 4 * PSH :])
    length = chips * 2 * PSH
    pick = (jnp.arange(2) == chosen).astype(F32)[None, :, None, None]
    dk_p = dk_p + pick * dk_c[:, None, :length]
    dv_p = dv_p + pick * dv_c[:, None, :length]
    dq = jnp.concatenate([dq_p.reshape(nh, 4 * PSH, HD), dq_c], axis=1).swapaxes(0, 1).reshape(-1, HC)
    pair = jnp.stack([dk_p, dv_p])
    pair = pair.reshape(2, nh, 2, chips, 2 * PSH, HD).transpose(3, 2, 4, 0, 1, 5).reshape(chips * 4 * PSH, 2 * HC)
    near_grad = jnp.stack([dk_c[:, length:], dv_c[:, length:]]).transpose(2, 0, 1, 3).reshape(CONT, 2 * HC)
    return dq, pair, near_grad


def generic_body(
    tokens, valid, prompt_of, teacher, cotangent,
    ln1_gain, ln1_bias, ln2_gain, ln2_bias, qkv_weight, qkv_bias, out_weight, out_bias,
    up_weight, up_bias, down_weight, down_bias, stop=None,
):
    c = lax.axis_index("core")
    z = lax.axis_index("chip")
    chips = lax.axis_size("chip")
    nh = HC // HD
    rd = down_weight.shape[0]
    device = lax.axis_index(ALL)
    w_qkv, w_out, w_up, w_down = g_weights(c, qkv_weight, out_weight, up_weight, down_weight)
    gain1, bias1, gain2, bias2, b_out, b_down, b_qkv, b_up = g_small(
        c, rd, ln1_gain, ln1_bias, ln2_gain, ln2_bias, qkv_bias, out_bias, up_bias, down_bias
    )
    x = pair_rows(tokens).astype(F32)
    normed, rstd = normalize(x)
    first_in = (normed * gain1 + bias1).astype(BF)
    second_in = (normed * gain2 + bias2).astype(BF)
    projected = dot(first_in, w_qkv, (1, 0)) + b_qkv
    places = places_of(z, chips)
    turn = lambda v, d: rotate_heads(v.reshape(-1, nh, HD), places, d).reshape(-1, HC)
    q = turn(projected[:, :HC], 1.0).astype(BF)
    k = turn(projected[:, HC : 2 * HC], 1.0).astype(BF)
    kv = jnp.concatenate([k, projected[:, 2 * HC :].astype(BF)], axis=1)
    prompt_kv = lax.all_gather(kv[: 4 * PSH].reshape(2, 2 * PSH, 2 * HC), "chip", axis=0)
    cont_valid = lax.all_gather(valid[2 * PSH :], "core", axis=0, tiled=True)
    masks = masks_of(z, chips, cont_valid)
    chosen = prompt_of[0]
    attended, lse = g_attention(q, prompt_kv, kv, chosen, masks)
    hidden_pre = dot(second_in, w_up, (1, 0)) + b_up
    activated = jax.nn.gelu(hidden_pre, approximate=False).astype(BF)
    partial = dot(attended, w_out, (1, 0)) + dot(activated, w_down, (1, 0))
    halves = split_rows(partial)
    take = lambda a: lax.dynamic_index_in_dim(a, c, axis=0, keepdims=False)
    give = lambda a: lax.dynamic_index_in_dim(a, 1 - c, axis=0, keepdims=False)
    output = tokens.astype(F32) + take(halves) + swap_cores(give(halves)) + b_out + b_down
    live = (valid > 0).astype(F32)[:, None]
    missed = output - teacher.astype(F32)
    count_all, squared_all = lax.psum((jnp.sum(live), jnp.sum(live * missed * missed)), ALL)
    loss_value = squared_all / (count_all * D)
    out_grad = cotangent.astype(F32) + 2.0 / (count_all * D) * live * missed
    out_low = pair_rows(out_grad.astype(BF))
    if stop == "fwd":
        return output, out_grad, out_low, attended, lse, activated, q, kv, first_in, second_in
    out_bias_grad = jnp.sum(out_grad.astype(BF).astype(F32), axis=0)
    dw_out = dot(attended, out_low, (0, 0))
    dw_down = dot(activated, out_low, (0, 0))
    att_grad = dot(out_low, w_out, (1, 1)).astype(BF)
    hidden_grad = (dot(out_low, w_down, (1, 1)) * gelu_slope(hidden_pre)).astype(BF)
    dw_up = dot(second_in, hidden_grad, (0, 0))
    db_up = jnp.sum(hidden_grad.astype(F32), axis=0)
    second_grad = dot(hidden_grad, w_up, (1, 1))
    dq, pair, near = g_attention_back(q, prompt_kv, kv, att_grad, lse, chosen, masks)
    own_pair = lax.psum_scatter(pair.astype(BF), "chip", scatter_dimension=0, tiled=True).astype(F32)
    pair = jnp.concatenate([own_pair, near], axis=0)
    projected_grad = jnp.concatenate([turn(dq, -1.0), turn(pair[:, :HC], -1.0), pair[:, HC:]], axis=1).astype(BF)
    dw_qkv = dot(first_in, projected_grad, (0, 0))
    db_qkv = jnp.sum(projected_grad.astype(F32), axis=0)
    first_grad = dot(projected_grad, w_qkv, (1, 1))
    if stop == "bwd":
        return dw_out, dw_down, dw_up, dw_qkv, second_grad, first_grad, projected_grad, hidden_grad, att_grad
    joint = first_grad * gain1 + second_grad * gain2
    halves = split_rows(joint)
    joint = take(halves) + swap_cores(give(halves))
    own_normed = take(split_rows(normed))
    own_rstd = take(split_rows(rstd))
    input_grad = out_grad + own_rstd * (
        joint
        - jnp.mean(joint, axis=-1, keepdims=True)
        - own_normed * jnp.mean(joint * own_normed, axis=-1, keepdims=True)
    )
    wide = lambda v, n: jnp.zeros((v.shape[0], 2, v.shape[1]), F32).at[:, c].set(v).reshape(-1)
    small = jnp.concatenate(
        [
            jnp.sum(first_grad * normed, axis=0),
            jnp.sum(first_grad, axis=0),
            jnp.sum(second_grad * normed, axis=0),
            jnp.sum(second_grad, axis=0),
            out_bias_grad,
            wide(db_qkv.reshape(3, HC), 3),
            wide(db_up.reshape(-1, rd), 16),
        ]
    )
    small = lax.psum(small, ALL)
    shares, at = [], 0
    for size in (D, D, D, D, D, 3 * D, FF):
        own = size // lax.axis_size(ALL)
        shares.append(lax.dynamic_slice_in_dim(small, at + device * own, own))
        at += size
    rs = lambda v: lax.psum_scatter(v.astype(BF), CHIPS, scatter_dimension=0, tiled=True).astype(F32)
    r = qkv_weight.shape[0]
    s_qkv = rs(dw_qkv).reshape(2, r, 3, HC)
    s_up = rs(dw_up).reshape(2, r, FF // (2 * rd), rd)
    s_down = rs(dw_down)
    pairs = lambda own, other, axis: jnp.where(c == 0, jnp.stack([own, other], axis), jnp.stack([other, own], axis))
    s_qkv = pairs(take(s_qkv), swap_cores(give(s_qkv)), 2).reshape(r, 3 * D)
    s_up = pairs(take(s_up), swap_cores(give(s_up)), 2).reshape(r, FF)
    o = dw_out.reshape(H // 2, -1, 2, r, D)
    o_own = lax.dynamic_index_in_dim(o, c, axis=2, keepdims=False)
    o_other = swap_cores(lax.dynamic_index_in_dim(o, 1 - c, axis=2, keepdims=False))
    s_out = rs(pairs(o_own, o_other, 0).reshape(-1, D))
    return (
        output.astype(BF), loss_value, input_grad, shares[0], shares[1], shares[2], shares[3],
        s_qkv, shares[5], s_out, shares[4], s_up, shares[6], s_down, shares[4],
    )


MESH_ID = pl.DeviceIdType.MESH
RANKS = 4


class Net:
    def __init__(self, send, recv):
        self.g, self.z, self.c = (lax.axis_index(a) for a in ALL)
        self.y, self.x = self.g // 2, self.g % 2
        self.send, self.recv, self.used = send, recv, 0
        self.chip = self.g * RANKS + self.z
        self.core = {"grp": self.g, "chip": self.z, "core": 1 - self.c}
        self.right = {"grp": self.y * 2 + 1 - self.x, "chip": self.z, "core": self.c}
        self.up = {"grp": (1 - self.y) * 2 + self.x, "chip": self.z, "core": self.c}
        self.line = [{"grp": self.g, "chip": (self.z + j) % RANKS, "core": self.c} for j in (1, 2, 3)]
        self.sent = []

    def enter(self):
        barrier = pltpu.get_barrier_semaphore()
        for peer in [self.core, self.right, self.up] + self.line:
            pl.semaphore_signal(barrier, inc=1, device_id=peer, device_id_type=MESH_ID)
        pl.semaphore_wait(barrier, 6)

    def copy(self, src, dst, peer):
        i = self.used
        self.used += 1
        made = pltpu.make_async_remote_copy(
            src_ref=src, dst_ref=dst, send_sem=self.send.at[i], recv_sem=self.recv.at[i],
            device_id=peer, device_id_type=MESH_ID,
        )
        made.start()
        self.sent.append(made)
        return made

    def same(self, view, peer):
        return self.copy(view, view, peer)

    def settle(self, made):
        made.wait_recv()
        made.wait_send()
        self.sent = [m for m in self.sent if m is not made]

    def leave(self):
        for made in self.sent:
            made.wait_send()
        self.sent = []


def gather_steps(net, dst, rb, col, width, before):
    a, b, both = pl.ds(col, width // 2), pl.ds(col + width // 2, width // 2), pl.ds(col, width)
    quad = 4 * rb
    held = {}

    def line():
        for made in before:
            made.wait_recv()
        view = dst.at[pl.ds(net.chip * rb, rb), both]
        held[0] = [net.same(view, peer) for peer in net.line]

    def first():
        for made in held[0]:
            made.wait_recv()
        rows = pl.ds(net.g * quad, quad)
        held[1] = [net.same(dst.at[rows, a], net.right), net.same(dst.at[rows, b], net.up)]

    def second():
        for made in held[1]:
            made.wait_recv()
        held[2] = [net.same(dst.at[pl.ds(net.y * 2 * quad, 2 * quad), a], net.up)]
        for y in range(2):
            held[2].append(net.same(dst.at[pl.ds((y * 2 + net.x) * quad, quad), b], net.right))

    def last():
        for made in held[2]:
            made.wait_recv()

    return [line, first, second, last]


def small_steps(net, rows):
    held = {}

    def pair():
        held[0] = [net.same(rows.at[net.chip * 2 + net.c], net.core)]

    def line():
        held[0][0].wait_recv()
        held[1] = [net.same(rows.at[pl.ds(net.chip * 2, 2)], peer) for peer in net.line]

    def first():
        for made in held[1]:
            made.wait_recv()
        held[2] = [net.same(rows.at[pl.ds(net.g * 8, 8)], net.right)]

    def second():
        held[2][0].wait_recv()
        held[3] = [net.same(rows.at[pl.ds(net.y * 16, 16)], net.up)]

    def last():
        held[3][0].wait_recv()

    return [pair, line, first, second, last]


def run_diagonal(tasks):
    longest = max(len(steps) + t for t, steps in enumerate(tasks))
    for time in range(longest):
        for t, steps in enumerate(tasks):
            if 0 <= time - t < len(steps):
                steps[time - t]()


def add_rows(dst, dst_rows, cols, src, src_rows, count, tile=64):
    @pl.loop(0, count // tile)
    def _(i):
        to = pl.ds(pl.multiple_of(dst_rows + i * tile, tile), tile)
        total = dst[to, cols].astype(F32) + src[pl.ds(pl.multiple_of(src_rows + i * tile, tile), tile), :].astype(F32)
        dst[to, cols] = total.astype(dst.dtype)


def scatter_steps(net, src, rb, got_a, got_b, got_z, total):
    cols = src.shape[1]
    a, b = pl.ds(0, cols // 2), pl.ds(cols // 2, cols // 2)
    tile = min(64, rb)
    quad = 4 * rb
    at = lambda y, x: pl.ds((y * 2 + x) * quad, quad)
    held = {}

    def first():
        rows = pl.ds((1 - net.y) * 2 * quad, 2 * quad)
        held[0] = [net.copy(src.at[rows, a], got_a.at[pl.ds(0, 2 * quad)], net.up)]
        for y in range(2):
            held[0].append(net.copy(src.at[at(y, 1 - net.x), b], got_b.at[pl.ds(y * quad, quad)], net.right))

    def second():
        for made in held[0]:
            made.wait_recv()
        add_rows(src, (net.y * 2 + 1 - net.x) * quad, a, got_a, (1 - net.x) * quad, quad, tile)
        add_rows(src, ((1 - net.y) * 2 + net.x) * quad, b, got_b, (1 - net.y) * quad, quad, tile)
        held[1] = [
            net.copy(src.at[at(net.y, 1 - net.x), a], got_a.at[pl.ds(2 * quad, quad)], net.right),
            net.copy(src.at[at(1 - net.y, net.x), b], got_b.at[pl.ds(2 * quad, quad)], net.up),
        ]
        add_rows(src, (net.y * 2 + net.x) * quad, a, got_a, net.x * quad, quad, tile)
        add_rows(src, (net.y * 2 + net.x) * quad, b, got_b, net.y * quad, quad, tile)

    def third():
        for made in held[1]:
            made.wait_recv()
        line = (net.y * 2 + net.x) * quad
        add_rows(src, line, a, got_a, 2 * quad, quad, tile)
        add_rows(src, line, b, got_b, 2 * quad, quad, tile)
        held[2] = [
            net.copy(src.at[pl.ds(line + (net.z + j) % 4 * rb, rb)], got_z.at[j - 1], net.line[j - 1])
            for j in (1, 2, 3)
        ]

    def last():
        for made in held[2]:
            made.wait_recv()
        line = (net.y * 2 + net.x) * quad + net.z * rb

        @pl.loop(0, rb // tile)
        def _(i):
            rows = pl.ds(pl.multiple_of(i * tile, tile), tile)
            value = src[pl.ds(pl.multiple_of(line + i * tile, tile), tile), :].astype(F32)
            for j in range(3):
                value = value + got_z[j, rows, :].astype(F32)
            total[rows, :] = value

    return [first, second, third, last]


def sum_steps(net, value, got):
    held = {}
    peers = [net.core, net.right, net.up]

    def make(i):
        def step():
            if i > 0:
                held[i - 1].wait_recv()
                held[i - 1].wait_send()
                net.sent = [m for m in net.sent if m is not held[i - 1]]
                value[...] = value[...] + got[i - 1]
            if i < 3:
                held[i] = net.copy(value, got.at[i], peers[i])
            else:
                held[3] = [net.copy(value, got.at[3 + net.z], peer) for peer in net.line]
                got[3 + net.z] = value[...]

        return step

    def last():
        for made in held[3]:
            made.wait_recv()
            made.wait_send()
            net.sent = [m for m in net.sent if m is not made]
        value[...] = (got[3] + got[4]) + (got[5] + got[6])

    return [make(i) for i in range(4)] + [last]


VM = pl.BlockSpec(memory_space=pltpu.VMEM)
PROMPT = RANKS * 2 * PSH
KEYS = 2 * PROMPT + CONT
ROWS = 4 * PSH + CONT


def nt(a, b):
    return lax.dot_general(a, b, (((1,), (1,)), ((), ())), preferred_element_type=F32)


def nn(a, b):
    return lax.dot_general(a, b, (((1,), (0,)), ((), ())), preferred_element_type=F32)


def tn(a, b):
    return lax.dot_general(a, b, (((0,), (0,)), ((), ())), preferred_element_type=F32)


def tile_at(i, size):
    return pl.ds(pl.multiple_of(i * size, size), size)


def move_rows(dst, to, src, at, count, tile=32):
    @pl.loop(0, count // tile)
    def _(i):
        step = pl.multiple_of(i * tile, tile)
        dst[pl.ds(pl.multiple_of(to + step, tile), tile), :] = src[pl.ds(pl.multiple_of(at + step, tile), tile), :]


def spread_row(rows, field, index, owner, lane, size):
    table = rows[:, field, :].astype(BF)
    lanes = lax.broadcasted_iota(jnp.int32, (128, size), 0)
    pick = (lanes == index[lane : lane + 1, :size]).astype(F32).astype(BF)
    wide = nn(table, pick)
    owners = lax.broadcasted_iota(jnp.int32, (rows.shape[0], size), 0)
    return jnp.sum(jnp.where(owners == index[owner : owner + 1, :size], wide, 0.0), axis=0, keepdims=True)


def norm_rows(x):
    x = x.astype(F32)
    center = x - jnp.mean(x, axis=-1, keepdims=True)
    return center * lax.rsqrt(jnp.mean(center * center, axis=-1, keepdims=True) + EPSILON)


def turn(value, table, sign):
    cos, low_sin, high_sin = (table[:, 128 * i : 128 * i + 128] for i in range(3))
    out = []
    for j in range(value.shape[1] // 128):
        v = value[:, 128 * j : 128 * j + 128]
        other = pltpu.roll(v, 120, 1) * low_sin + pltpu.roll(v, 8, 1) * high_sin
        out.append(v * cos + sign * other)
    return out[0] if len(out) == 1 else jnp.concatenate(out, axis=1)


def rotary_table(length):
    half = ROT // 2
    inverse = (10000.0 ** (-np.arange(half, dtype=np.float32) / half)).astype(np.float32)
    angles = (np.arange(length, dtype=np.float32)[:, None] * inverse).astype(np.float64)
    cos, sin = np.cos(angles), np.sin(angles)
    table = np.zeros((length, 3, 2, HD), np.float32)
    table[:, 0] = 1.0
    for head in range(2):
        table[:, 0, head, :half] = cos
        table[:, 0, head, half:ROT] = cos
        table[:, 1, head, :half] = -sin
        table[:, 2, head, half:ROT] = sin
    return table.reshape(length, 384)


def index_table(rd):
    n = np.arange(2048)
    table = np.zeros((2, 16, 2048), np.int32)
    for c in range(2):
        col = np.minimum(n // HC, 2) * D + c * HC + n % HC
        table[c, 0], table[c, 1] = col // 96, col % 96
        unit = n // rd * (2 * rd) + c * rd + n % rd
        table[c, 2], table[c, 3] = unit // rd, unit % rd
        table[c, 4] = n // 32 % 32
        for i in range(4):
            table[c, 8 + i] = n % 32 + 32 * i
    return table


def seen(keys_at, queries_at, shape, length=None):
    keys = lax.broadcasted_iota(jnp.int32, shape, 0) + keys_at
    queries = lax.broadcasted_iota(jnp.int32, shape, 1) + queries_at
    mask = keys <= queries
    return mask if length is None else mask & (keys < length)


def head_lanes(rows):
    return lax.broadcasted_iota(jnp.int32, (rows, 128), 1) < HD


def attend(query, keys, values, masks, head):
    lanes = head_lanes(query.shape[0])
    own = jnp.where(lanes if head == 0 else ~lanes, query.astype(F32) * SCALE, 0.0).astype(BF)
    scores = [nt(k, own) for k in keys]
    scores = [s if m is None else jnp.where(m, s, NEGATIVE) for s, m in zip(scores, masks)]
    top = functools.reduce(jnp.maximum, [jnp.max(s, axis=0, keepdims=True) for s in scores])
    weights = [jnp.exp(s - top) for s in scores]
    total = sum(jnp.sum(w, axis=0, keepdims=True) for w in weights)
    share = 1.0 / total
    out = sum(tn(v, (w * share).astype(BF)) for v, w in zip(values, weights))
    return out[head * HD : head * HD + HD], top + jnp.log(total)


def forward_kernel(
    tokens, small, qkv, out, up, down, rotary, index,
    rows, w_qkv, w_out, w_up, w_down, x_all, first_in, second_in, q, kv, attended, lse, activated, slope,
    spread, swapped, send, recv,
):
    net = Net(send, recv)
    c, z, chip = net.c, net.z, net.chip
    net.enter()
    for p in range(2):
        move_rows(x_all, p * PROMPT + z * 2 * PSH + c * PSH, tokens, p * PSH, PSH)
    move_rows(x_all, 2 * PROMPT + c * HALF, tokens, 2 * PSH, HALF)
    rows[chip * 2 + c] = small[...]
    pieces = [pl.ds(p * PROMPT + z * 2 * PSH + c * PSH, PSH) for p in range(2)]
    smalls = small_steps(net, rows)
    smalls[0]()
    own_tokens = [net.same(x_all.at[piece], peer) for peer in net.line for piece in pieces]
    mates = [net.same(x_all.at[piece], net.core) for piece in pieces + [pl.ds(2 * PROMPT + c * HALF, HALF)]]
    half_rows = pl.ds(pl.multiple_of(chip * 64 + c * 32, 32), 32)
    given = pl.ds(0, 32)
    w_qkv[half_rows, :] = qkv[c]
    swapped[given, : 3 * HC] = qkv[1 - c]
    from_core = {}
    from_core["qkv"] = net.copy(swapped.at[given, pl.ds(0, 3 * HC)], w_qkv.at[half_rows], net.core)
    w_up[half_rows, :] = up[c]
    given = pl.ds(32, 32)
    swapped[given, : FF // 2] = up[1 - c]
    from_core["up"] = net.copy(swapped.at[given, pl.ds(0, FF // 2)], w_up.at[half_rows], net.core)
    w_down[pl.ds(pl.multiple_of(chip * 128, 128), 128), :] = down[...]
    spread[pl.ds(pl.multiple_of(chip * 32, 32), 32), :] = out[...]
    none = []
    tasks = [
        gather_steps(net, w_qkv, 64, 0, 768, [from_core["qkv"]]),
        gather_steps(net, w_qkv, 64, 768, 768, none),
        gather_steps(net, w_up, 64, 0, 1024, [from_core["up"]]),
        gather_steps(net, w_up, 64, 1024, 1024, none),
        gather_steps(net, spread, 32, 0, 1024, none),
        gather_steps(net, w_down, 128, 0, 512, none),
        gather_steps(net, w_down, 128, 512, 512, none),
    ]
    clock = [0]

    def advance(until):
        while clock[0] < until:
            for t, steps in enumerate(tasks):
                if (clock[0] - t) % 2 == 0 and 0 <= (clock[0] - t) // 2 < len(steps):
                    steps[(clock[0] - t) // 2]()
            clock[0] += 1

    advance(1)
    smalls[1]()
    for made in own_tokens:
        made.wait_recv()
    relays = []
    for j in (1, 2, 3):
        for p in range(2):
            piece = pl.ds(p * PROMPT + (z + j) % RANKS * 2 * PSH + c * PSH, PSH)
            relays.append(net.same(x_all.at[piece], net.core))
    advance(2)
    smalls[2]()
    smalls[3]()
    smalls[4]()
    advance(3)
    for made in mates + relays:
        made.wait_recv()
    places = index.at[c]
    gain1, bias1, gain2, bias2 = (spread_row(rows, 0, places, 4, 8 + i, D) for i in range(4))

    @pl.loop(0, KEYS // 64)
    def _(i):
        at = tile_at(i, 64)
        first_in[at, :] = (norm_rows(x_all[at, :]) * gain1 + bias1).astype(BF)

    advance(4)

    def own_at(i):
        prompt = (i // 2) * PROMPT + z * 2 * PSH + (i % 2) * 64
        return pl.multiple_of(jnp.where(i < 4, prompt, 2 * PROMPT + (i - 4) * 64), 64)

    @pl.loop(0, ROWS // 64)
    def _(i):
        second_in[tile_at(i, 64), :] = (norm_rows(x_all[pl.ds(own_at(i), 64), :]) * gain2 + bias2).astype(BF)

    b_qkv = spread_row(rows, 2, places, 0, 1, 3 * HC)
    b_up = spread_row(rows, 3, places, 2, 3, FF // 2)
    advance(8)

    @pl.loop(0, KEYS // 256)
    def _(i):
        at = tile_at(i, 256)
        here = first_in[at, :]
        place = pl.multiple_of(jnp.where(i < 4, (i % 2) * 256, PROMPT + (i - 4) * 256), 256)
        table = rotary[pl.ds(place, 256), :]
        for j in range(4):
            cols = slice(HC + 256 * j, HC + 256 * j + 256)
            value = nn(here, w_qkv[:, cols]) + b_qkv[:, cols]
            kv[at, 256 * j : 256 * j + 256] = (turn(value, table, 1.0) if j < 2 else value).astype(BF)

    @pl.loop(0, ROWS // 128)
    def _(i):
        prompt = i * PROMPT + z * 2 * PSH
        source = pl.multiple_of(jnp.where(i < 2, prompt, 2 * PROMPT + (i - 2) * 128), 128)
        place = pl.multiple_of(jnp.where(i < 2, z * 2 * PSH, PROMPT + (i - 2) * 128), 128)
        here = first_in[pl.ds(source, 128), :]
        table = rotary[pl.ds(place, 128), :]
        for j in range(2):
            cols = slice(256 * j, 256 * j + 256)
            q[tile_at(i, 128), cols] = turn(nn(here, w_qkv[:, cols]) + b_qkv[:, cols], table, 1.0).astype(BF)

    advance(9)
    length = jnp.sum(jnp.sum(rows[pl.ds(chip * 2, 2), 5:7, :], axis=0), keepdims=True).astype(jnp.int32)
    second = jnp.broadcast_to(small[7:8, :], (PROMPT, 128)) > 0.5

    def attend_pair(pair):
        k_at, v_at = pl.ds(128 * pair, 128), pl.ds(HC + 128 * pair, 128)
        prompts = [(kv[p * PROMPT : (p + 1) * PROMPT, k_at], kv[p * PROMPT : (p + 1) * PROMPT, v_at]) for p in range(2)]

        def put(row, size, key_list, value_list, masks):
            outs = []
            for head in range(2):
                o, stat = attend(q[row : row + size, k_at], key_list, value_list, masks, head)
                outs.append(o)
                lse[2 * pair + head, :, row : row + size] = stat
            attended[row : row + size, k_at] = jnp.concatenate(outs, axis=0).T.astype(BF)

        for p in range(2):
            put(p * 128, 128, [prompts[p][0]], [prompts[p][1]], [seen(0, z * 2 * PSH, (PROMPT, 128))])
        chosen = [jnp.where(second, b.astype(F32), a.astype(F32)).astype(BF) for a, b in zip(*prompts)]
        for i in range(CONT // 128):
            near = 128 * i + 128
            put(
                256 + 128 * i, 128,
                [chosen[0], kv[2 * PROMPT : 2 * PROMPT + near, k_at]],
                [chosen[1], kv[2 * PROMPT : 2 * PROMPT + near, v_at]],
                [None, seen(0, 128 * i, (near, 128), length)],
            )

    def hidden(j):
        cols = slice(256 * j, 256 * j + 256)

        @pl.loop(0, ROWS // 128)
        def _(i):
            at = tile_at(i, 128)
            pre = nn(second_in[at, :], w_up[:, cols]) + b_up[:, cols]
            gate = 0.5 * (1.0 + lax.erf(pre * 0.7071067811865476))
            activated[at, cols] = (pre * gate).astype(BF)
            slope[at, cols] = (gate + pre * jnp.exp(-0.5 * pre * pre) * 0.3989422804014327).astype(slope.dtype)

    attend_pair(0)
    attend_pair(1)
    advance(10)
    for j in range(4):
        hidden(j)
    advance(11)
    attend_pair(2)
    attend_pair(3)
    advance(12)
    for j in range(4, 8):
        hidden(j)
    advance(13)
    given = pl.ds(pl.multiple_of((1 - c) * 256, 256), 256)
    swap = net.copy(spread.at[given], swapped.at[pl.ds(64, 256), pl.ds(0, D)], net.core)
    advance(20)
    swap.wait_recv()
    for h in range(8):
        w_out[pl.ds(pl.multiple_of(h * 64 + c * 32, 32), 32), :] = spread[pl.ds(pl.multiple_of(c * 256 + h * 32, 32), 32), :]
        w_out[pl.ds(pl.multiple_of(h * 64 + (1 - c) * 32, 32), 32), :] = swapped[64 + h * 32 : 96 + h * 32, :D]
    net.leave()


def forward(tokens, small, qkv, out, up, down):
    shape = jax.ShapeDtypeStruct
    return pl.pallas_call(
        forward_kernel,
        out_shape=(
            shape((32, 8, 128), F32), shape((D, 3 * HC), BF), shape((HC, D), BF), shape((D, FF // 2), BF), shape((FF // 2, D), BF),
            shape((KEYS, D), BF), shape((KEYS, D), BF), shape((ROWS, D), BF), shape((ROWS, HC), BF), shape((KEYS, 2 * HC), BF),
            shape((ROWS, HC), BF), shape((8, 1, ROWS), F32), shape((ROWS, FF // 2), BF), shape((ROWS, FF // 2), F32),
        ),
        in_specs=[VM] * 8,
        out_specs=(VM,) * 14,
        scratch_shapes=[
            pltpu.VMEM((HC, D), BF), pltpu.VMEM((320, FF // 2), BF),
            pltpu.SemaphoreType.DMA((96,)), pltpu.SemaphoreType.DMA((96,)),
        ],
        compiler_params=pltpu.CompilerParams(collective_id=0, has_side_effects=True, vmem_limit_bytes=60 << 20),
    )(tokens, small, qkv, out, up, down, jnp.asarray(rotary_table(PROMPT + CONT)), jnp.asarray(index_table(128)))


HBM = pl.BlockSpec(memory_space=pl.ANY)


def scatter_line_kernel(given, total, pair, got, send, recv):
    net = Net(send, recv)
    for j in range(4):
        move_rows(pair.at[j], 0, given.at[j], 0, given.shape[1])
    net.enter()
    made = [net.copy(pair.at[(net.z + j) % 4], got.at[j - 1], net.line[j - 1]) for j in (1, 2, 3)]
    for m in made:
        m.wait_recv()
    n = pair.shape[1]

    @pl.loop(0, n // 64)
    def _(i):
        rows = pl.ds(pl.multiple_of(i * 64, 64), 64)
        value = pair[net.z, rows, :].astype(F32)
        for j in range(3):
            value = value + got[j, rows, :].astype(F32)
        total[rows, :] = value

    net.leave()


def scatter_line(pair):
    _, n, w = pair.shape
    return pl.pallas_call(
        scatter_line_kernel,
        out_shape=jax.ShapeDtypeStruct((n, w), F32),
        in_specs=[VM],
        out_specs=VM,
        scratch_shapes=[pltpu.VMEM((4, n, w), pair.dtype), pltpu.VMEM((3, n, w), pair.dtype), pltpu.SemaphoreType.DMA((4,)), pltpu.SemaphoreType.DMA((4,))],
        compiler_params=pltpu.CompilerParams(collective_id=2, has_side_effects=True, vmem_limit_bytes=32 << 20),
    )(pair)


def scatter_kernel(value, qkv, out, up, down, o_sum, o_qkv, o_out, o_up, o_down, got_s, *scratch):
    bufs, (send, recv) = scratch[:-2], scratch[-2:]
    net = Net(send, recv)
    net.enter()
    o_sum[...] = value[...]
    tasks = [sum_steps(net, o_sum, got_s)]
    plan = ((down, 128, o_down), (up, 64, o_up), (out, 32, o_out), (qkv, 64, o_qkv))
    for i, (src, rb, total) in enumerate(plan):
        held = bufs[4 * i]
        move_rows(held, 0, src, 0, src.shape[0])
        tasks.append(scatter_steps(net, held, rb, *bufs[4 * i + 1 : 4 * i + 4], total))
    run_diagonal(tasks)
    net.leave()


def scatter_all(value, qkv, out, up, down):
    shape = jax.ShapeDtypeStruct
    n = value.shape[0]
    bufs = []
    for src in (down, up, out, qkv):
        rb, cols = src.shape[0] // 16, src.shape[1]
        bufs += [pltpu.VMEM(src.shape, BF), pltpu.VMEM((12 * rb, cols // 2), BF), pltpu.VMEM((12 * rb, cols // 2), BF), pltpu.VMEM((3, rb, cols), BF)]
    return pl.pallas_call(
        scatter_kernel,
        out_shape=(
            shape((n, 128), F32), shape((64, 3 * HC), F32), shape((32, D), F32), shape((64, FF // 2), F32), shape((128, D), F32),
        ),
        in_specs=[VM] * 5,
        out_specs=(VM,) * 5,
        scratch_shapes=[pltpu.VMEM((7, n, 128), F32)] + bufs
        + [pltpu.SemaphoreType.DMA((64,)), pltpu.SemaphoreType.DMA((64,))],
        compiler_params=pltpu.CompilerParams(collective_id=3, has_side_effects=True, vmem_limit_bytes=56 << 20),
    )(value, qkv, out, up, down)


def fast_body(
    tokens, valid, prompt_of, teacher, cotangent,
    ln1_gain, ln1_bias, ln2_gain, ln2_bias, qkv_weight, qkv_bias, out_weight, out_bias,
    up_weight, up_bias, down_weight, down_bias, stop=None,
):
    c = lax.axis_index("core")
    z = lax.axis_index("chip")
    chips = lax.axis_size("chip")
    nh = HC // HD
    rd = down_weight.shape[0]
    device = lax.axis_index(ALL)
    pad = lambda v: jnp.pad(v.astype(F32), (0, 128 - v.shape[0]))[None]
    live_own = (valid > 0).astype(F32)
    small = jnp.concatenate(
        [
            jnp.concatenate([ln1_gain, ln1_bias, ln2_gain, ln2_bias]).astype(F32)[None],
            pad(jnp.concatenate([out_bias, down_bias])),
            pad(qkv_bias),
            pad(up_bias),
            live_own.reshape(3, 128),
            jnp.broadcast_to(prompt_of.astype(F32)[:, None], (1, 128)),
        ]
    )
    rows, w_qkv, w_out, w_up, w_down, x_all, first_all, second_in, q, kv, attended, lse, activated, slope = forward(
        tokens,
        small,
        qkv_weight.reshape(32, 3, 2, HC).transpose(2, 0, 1, 3).reshape(2, 32, 3 * HC),
        out_weight,
        up_weight.reshape(32, 16, 2, 128).transpose(2, 0, 1, 3).reshape(2, 32, FF // 2),
        down_weight,
    )
    def own_of(a):
        prompts = lax.dynamic_slice_in_dim(a[: 2 * PROMPT].reshape(2, PROMPT, -1), z * 2 * PSH, 2 * PSH, axis=1)
        return jnp.concatenate([prompts.reshape(4 * PSH, -1), a[2 * PROMPT :]])
    x = own_of(x_all).astype(F32)
    first_in = own_of(first_all)
    prompt_kv = kv[: 2 * PROMPT].reshape(2, 4, 2 * PSH, 2 * HC).swapaxes(0, 1)
    kv = own_of(kv)
    lse = lse[:, 0]
    normed, rstd = normalize(x)
    gain1, bias1, gain2, bias2 = (rows[:, 0, 32 * i : 32 * i + 32].reshape(-1) for i in range(4))
    b_out, b_down = (rows[:, 1, 32 * i : 32 * i + 32].reshape(-1) for i in range(2))
    count_all = jnp.sum(rows[:, 4:7])
    places = places_of(z, chips)
    turn_own = lambda v, d: rotate_heads(v.reshape(-1, nh, HD), places, d).reshape(-1, HC)
    cont_valid = lax.dynamic_slice_in_dim(rows, (device // 2) * 2, 2)[:, 5:7].reshape(-1)
    masks = masks_of(z, chips, cont_valid)
    chosen = prompt_of[0]
    partial = dot(attended, w_out, (1, 0)) + dot(activated, w_down, (1, 0))
    halves = split_rows(partial)
    take = lambda a: lax.dynamic_index_in_dim(a, c, axis=0, keepdims=False)
    give = lambda a: lax.dynamic_index_in_dim(a, 1 - c, axis=0, keepdims=False)
    output = tokens.astype(F32) + take(halves) + swap_cores(give(halves)) + b_out + b_down
    live = (valid > 0).astype(F32)[:, None]
    missed = output - teacher.astype(F32)
    squared = jnp.sum(live * missed * missed)
    out_grad = cotangent.astype(F32) + 2.0 / (count_all * D) * live * missed
    out_low = pair_rows(out_grad.astype(BF))
    if stop == "fwd":
        return output
    out_bias_grad = jnp.sum(out_grad.astype(BF).astype(F32), axis=0)
    dw_out = dot(attended, out_low, (0, 0))
    dw_down = dot(activated, out_low, (0, 0))
    att_grad = dot(out_low, w_out, (1, 1)).astype(BF)
    hidden_grad = (dot(out_low, w_down, (1, 1)) * slope).astype(BF)
    dw_up = dot(second_in, hidden_grad, (0, 0))
    db_up = jnp.sum(hidden_grad.astype(F32), axis=0)
    second_grad = dot(hidden_grad, w_up, (1, 1))
    dq, pair, near = g_attention_back(q, prompt_kv, kv, att_grad, lse, chosen, masks)
    own_pair = scatter_line(pair.astype(BF).reshape(4, 4 * PSH, 2 * HC))
    pair = jnp.concatenate([own_pair, near], axis=0)
    projected_grad = jnp.concatenate([turn_own(dq, -1.0), turn_own(pair[:, :HC], -1.0), pair[:, HC:]], axis=1).astype(BF)
    dw_qkv = dot(first_in, projected_grad, (0, 0))
    db_qkv = jnp.sum(projected_grad.astype(F32), axis=0)
    first_grad = dot(projected_grad, w_qkv, (1, 1))
    if stop == "bwd":
        return dw_out, dw_down, dw_up, dw_qkv, second_grad, first_grad, projected_grad, hidden_grad, att_grad
    joint = first_grad * gain1 + second_grad * gain2
    halves = split_rows(joint)
    joint = take(halves) + swap_cores(give(halves))
    own_normed = take(split_rows(normed))
    own_rstd = take(split_rows(rstd))
    input_grad = out_grad + own_rstd * (
        joint
        - jnp.mean(joint, axis=-1, keepdims=True)
        - own_normed * jnp.mean(joint * own_normed, axis=-1, keepdims=True)
    )
    wide = lambda v, n: jnp.zeros((v.shape[0], 2, v.shape[1]), F32).at[:, c].set(v).reshape(-1)
    small = jnp.concatenate(
        [
            jnp.sum(first_grad * normed, axis=0),
            jnp.sum(first_grad, axis=0),
            jnp.sum(second_grad * normed, axis=0),
            jnp.sum(second_grad, axis=0),
            out_bias_grad,
            wide(db_qkv.reshape(3, HC), 3),
            wide(db_up.reshape(-1, rd), 16),
        ]
    )
    small = jnp.concatenate([small, jnp.full((128,), squared), jnp.zeros((7 * 128,), F32)]).reshape(-1, 128)
    pairs = lambda own, other, axis: jnp.where(c == 0, jnp.stack([own, other], axis), jnp.stack([other, own], axis))
    o = dw_out.astype(BF).reshape(H // 2, 2, 32, D)
    o_own = lax.dynamic_index_in_dim(o, c, axis=1, keepdims=False)
    o_other = swap_cores(lax.dynamic_index_in_dim(o, 1 - c, axis=1, keepdims=False))
    small, s_qkv, s_out, s_up, s_down = scatter_all(
        small, dw_qkv.astype(BF), pairs(o_own, o_other, 0).reshape(-1, D), dw_up.astype(BF), dw_down.astype(BF)
    )
    s_qkv = s_qkv.reshape(2, 32, 3, HC)
    s_up = s_up.reshape(2, 32, 16, 128)
    s_qkv = pairs(take(s_qkv), swap_cores(give(s_qkv)), 2).reshape(32, 3 * D)
    s_up = pairs(take(s_up), swap_cores(give(s_up)), 2).reshape(32, FF)
    small = small.reshape(-1)
    shares, at = [], 0
    for size in (D, D, D, D, D, 3 * D, FF):
        own = size // lax.axis_size(ALL)
        shares.append(lax.dynamic_slice_in_dim(small, at + device * own, own))
        at += size
    loss_value = small[at] / (count_all * D)
    return (
        output.astype(BF), loss_value, input_grad, shares[0], shares[1], shares[2], shares[3],
        s_qkv, shares[5], s_out, shares[4], s_up, shares[6], s_down, shares[4],
    )


def solution(mesh):
    groups, seats = mesh.shape["grp"], mesh.shape["seq"]
    fine = Mesh(mesh.devices.reshape(groups, seats // 2, 2), ALL)
    rows, row = P(ALL, None), P(ALL)
    in_specs = (rows, row, row, rows, rows) + (row,) * 4 + (rows, row) * 4
    out_specs = (rows, P(), rows) + (row,) * 4 + (rows, row) * 4
    return jax.shard_map(fast_body if (groups, seats) == (4, 8) else generic_body, mesh=fine, in_specs=in_specs, out_specs=out_specs, check_vma=False)
```

```python
import functools

import jax
import jax.numpy as jnp
import numpy as np
from jax import lax
from jax.experimental import pallas as pl
from jax.experimental.pallas import tpu as pltpu
from jax.sharding import Mesh
from jax.sharding import PartitionSpec as P

D = 1024
H = 16
HD = 64
ROT = 16
FF = 4096
PSH = 64
CONT = 512
HALF = CONT // 2
HC = H // 2 * HD
EPSILON = 1e-05
NEGATIVE = -1e30
SCALE = 0.125
BF = jnp.bfloat16
F32 = jnp.float32
ALL = ("grp", "chip", "core")
CHIPS = ("grp", "chip")


def swap_cores(x):
    return lax.ppermute(x, "core", [(0, 1), (1, 0)])


def pair_rows(own):
    both = lax.all_gather(own, "core", axis=0)
    prompts = both[:, : 2 * PSH].reshape((2, 2, PSH) + own.shape[1:])
    prompts = prompts.swapaxes(0, 1).reshape((4 * PSH,) + own.shape[1:])
    return jnp.concatenate([prompts, both[:, 2 * PSH :].reshape((CONT,) + own.shape[1:])], axis=0)


def split_rows(rows):
    prompts = rows[: 4 * PSH].reshape((2, 2, PSH) + rows.shape[1:]).swapaxes(0, 1)
    prompts = prompts.reshape((2, 2 * PSH) + rows.shape[1:])
    return jnp.concatenate([prompts, rows[4 * PSH :].reshape((2, HALF) + rows.shape[1:])], axis=1)


def normalize(values):
    center = values - jnp.mean(values, axis=-1, keepdims=True)
    inverse_dev = lax.rsqrt(jnp.mean(center * center, axis=-1, keepdims=True) + EPSILON)
    return (center * inverse_dev, inverse_dev)


def rotate_heads(values, places, direction):
    halfrot = ROT // 2
    inverse = 10000.0 ** (-jnp.arange(halfrot, dtype=F32) / halfrot)
    angles = places.astype(F32)[..., None] * inverse
    cosine = jnp.cos(angles)[..., None, :]
    sine_part = direction * jnp.sin(angles)[..., None, :]
    leading = values[..., :halfrot]
    trailing = values[..., halfrot:ROT]
    return jnp.concatenate(
        [
            leading * cosine - trailing * sine_part,
            trailing * cosine + leading * sine_part,
            values[..., ROT:],
        ],
        axis=-1,
    )


def gelu_slope(values):
    return (
        0.5 * (1.0 + lax.erf(values * 0.7071067811865476))
        + values * jnp.exp(-0.5 * values * values) * 0.3989422804014327
    )


def dot(a, b, contract):
    return lax.dot_general(a, b, ((contract[:1], contract[1:]), ((), ())), preferred_element_type=F32)


def g_weights(c, qkv_weight, out_weight, up_weight, down_weight):
    r = qkv_weight.shape[0]
    mine = functools.partial(lax.dynamic_index_in_dim, index=c, keepdims=False)
    both = lambda w: lax.all_gather(w, "core", axis=0, tiled=True)
    qkv = mine(both(qkv_weight).reshape(2 * r, 3, 2, HC), axis=2).reshape(2 * r, 3 * HC)
    qkv = lax.all_gather(qkv, CHIPS, axis=0, tiled=True)
    rd = down_weight.shape[0]
    up = mine(both(up_weight).reshape(2 * r, FF // (2 * rd), 2, rd), axis=2).reshape(2 * r, FF // 2)
    up = lax.all_gather(up, CHIPS, axis=0, tiled=True)
    down = lax.all_gather(down_weight, CHIPS, axis=0, tiled=True)
    out = lax.all_gather(out_weight, ALL, axis=0, tiled=True)
    out = mine(out.reshape(2, HC, D), axis=0)
    return qkv, out, up, down


def g_small(c, rd, ln1_gain, ln1_bias, ln2_gain, ln2_bias, qkv_bias, out_bias, up_bias, down_bias):
    sizes = [v.shape[0] for v in (ln1_gain, ln1_bias, ln2_gain, ln2_bias, out_bias, down_bias, qkv_bias, up_bias)]
    packed = jnp.concatenate([ln1_gain, ln1_bias, ln2_gain, ln2_bias, out_bias, down_bias, qkv_bias, up_bias])
    rows = lax.all_gather(packed, ALL, axis=0)
    parts, at = [], 0
    for size in sizes:
        parts.append(rows[:, at : at + size].reshape(-1).astype(F32))
        at += size
    qb = lax.dynamic_index_in_dim(parts[6].reshape(3, 2, HC), c, axis=1, keepdims=False).reshape(-1)
    ub = lax.dynamic_index_in_dim(parts[7].reshape(-1, 2, rd), c, axis=1, keepdims=False).reshape(-1)
    return parts[:6] + [qb, ub]


def places_of(z, chips):
    prompt = z * 2 * PSH + jnp.arange(2 * PSH)
    return jnp.concatenate([prompt, prompt, chips * 2 * PSH + jnp.arange(CONT)])


def masks_of(z, chips, cont_valid):
    length = chips * 2 * PSH
    prompt = jnp.arange(length)[None, :] <= z * 2 * PSH + jnp.arange(2 * PSH)[:, None]
    own = jnp.arange(CONT)[None, :] <= jnp.arange(CONT)[:, None]
    own = own & (cont_valid > 0)[None, :]
    return prompt, jnp.concatenate([jnp.ones((CONT, length), bool), own], axis=1)


def g_attention(q, prompt_kv, kv, chosen, masks):
    nh = HC // HD
    chips = prompt_kv.shape[0]
    pk = prompt_kv.reshape(chips, 2, 2 * PSH, 2, nh, HD).transpose(3, 4, 1, 0, 2, 5)
    pk = pk.reshape(2, nh, 2, chips * 2 * PSH, HD)
    qh = q.reshape(-1, nh, HD).swapaxes(0, 1)
    pq = qh[:, : 4 * PSH].reshape(nh, 2, 2 * PSH, HD)
    scores = jnp.einsum("hpqd,hpkd->hpqk", pq, pk[0], preferred_element_type=F32) * SCALE
    scores = jnp.where(masks[0], scores, NEGATIVE)
    top = jnp.max(scores, axis=-1, keepdims=True)
    weights = jnp.exp(scores - top)
    total = jnp.sum(weights, axis=-1, keepdims=True)
    p_out = jnp.einsum("hpqk,hpkd->hpqd", (weights / total).astype(BF), pk[1], preferred_element_type=F32)
    p_lse = (top + jnp.log(total))[..., 0].reshape(nh, 4 * PSH)
    far = lax.dynamic_index_in_dim(pk, chosen, axis=2, keepdims=False)
    near = kv[4 * PSH :].reshape(CONT, 2, nh, HD).transpose(1, 2, 0, 3)
    ck = jnp.concatenate([far, near], axis=2)
    cq = qh[:, 4 * PSH :]
    scores = jnp.einsum("hqd,hkd->hqk", cq, ck[0], preferred_element_type=F32) * SCALE
    scores = jnp.where(masks[1], scores, NEGATIVE)
    top = jnp.max(scores, axis=-1, keepdims=True)
    weights = jnp.exp(scores - top)
    total = jnp.sum(weights, axis=-1, keepdims=True)
    c_out = jnp.einsum("hqk,hkd->hqd", (weights / total).astype(BF), ck[1], preferred_element_type=F32)
    c_lse = (top + jnp.log(total))[..., 0]
    att = jnp.concatenate([p_out.reshape(nh, 4 * PSH, HD), c_out], axis=1)
    return att.swapaxes(0, 1).reshape(-1, HC).astype(BF), jnp.concatenate([p_lse, c_lse], axis=1)


def g_attention_back(q, prompt_kv, kv, att_grad, lse, chosen, masks):
    nh = HC // HD
    chips = prompt_kv.shape[0]
    pk = prompt_kv.reshape(chips, 2, 2 * PSH, 2, nh, HD).transpose(3, 4, 1, 0, 2, 5)
    pk = pk.reshape(2, nh, 2, chips * 2 * PSH, HD)
    qh = q.reshape(-1, nh, HD).swapaxes(0, 1)
    gh = att_grad.reshape(-1, nh, HD).swapaxes(0, 1)
    pq = qh[:, : 4 * PSH].reshape(nh, 2, 2 * PSH, HD)
    pg = gh[:, : 4 * PSH].reshape(nh, 2, 2 * PSH, HD)
    ein = functools.partial(jnp.einsum, preferred_element_type=F32)

    def back(eq, ek, query, key, value, grad, mask, lse_rows):
        scores = jnp.where(mask, ein(f"{eq},{ek}->{eq[:-1]}k", query, key) * SCALE, NEGATIVE)
        probs = jnp.exp(scores - lse_rows[..., None])
        prob_grad = ein(f"{eq},{ek}->{eq[:-1]}k", grad, value)
        inner = jnp.sum(probs * prob_grad, axis=-1, keepdims=True)
        score_grad = (probs * (prob_grad - inner)).astype(BF)
        es = eq[:-1] + "k"
        dq = ein(f"{es},{ek}->{eq}", score_grad, key) * SCALE
        dk = ein(f"{es},{eq}->{ek}", score_grad, query) * SCALE
        dv = ein(f"{es},{eq}->{ek}", probs.astype(BF), grad)
        return dq, dk, dv

    dq_p, dk_p, dv_p = back("hpqd", "hpkd", pq, pk[0], pk[1], pg, masks[0], lse[:, : 4 * PSH].reshape(nh, 2, 2 * PSH))
    far = lax.dynamic_index_in_dim(pk, chosen, axis=2, keepdims=False)
    near = kv[4 * PSH :].reshape(CONT, 2, nh, HD).transpose(1, 2, 0, 3)
    ck = jnp.concatenate([far, near], axis=2)
    dq_c, dk_c, dv_c = back("hqd", "hkd", qh[:, 4 * PSH :], ck[0], ck[1], gh[:, 4 * PSH :], masks[1], lse[:, 4 * PSH :])
    length = chips * 2 * PSH
    pick = (jnp.arange(2) == chosen).astype(F32)[None, :, None, None]
    dk_p = dk_p + pick * dk_c[:, None, :length]
    dv_p = dv_p + pick * dv_c[:, None, :length]
    dq = jnp.concatenate([dq_p.reshape(nh, 4 * PSH, HD), dq_c], axis=1).swapaxes(0, 1).reshape(-1, HC)
    pair = jnp.stack([dk_p, dv_p])
    pair = pair.reshape(2, nh, 2, chips, 2 * PSH, HD).transpose(3, 2, 4, 0, 1, 5).reshape(chips * 4 * PSH, 2 * HC)
    near_grad = jnp.stack([dk_c[:, length:], dv_c[:, length:]]).transpose(2, 0, 1, 3).reshape(CONT, 2 * HC)
    return dq, pair, near_grad


def generic_body(
    tokens, valid, prompt_of, teacher, cotangent,
    ln1_gain, ln1_bias, ln2_gain, ln2_bias, qkv_weight, qkv_bias, out_weight, out_bias,
    up_weight, up_bias, down_weight, down_bias, stop=None,
):
    c = lax.axis_index("core")
    z = lax.axis_index("chip")
    chips = lax.axis_size("chip")
    nh = HC // HD
    rd = down_weight.shape[0]
    device = lax.axis_index(ALL)
    w_qkv, w_out, w_up, w_down = g_weights(c, qkv_weight, out_weight, up_weight, down_weight)
    gain1, bias1, gain2, bias2, b_out, b_down, b_qkv, b_up = g_small(
        c, rd, ln1_gain, ln1_bias, ln2_gain, ln2_bias, qkv_bias, out_bias, up_bias, down_bias
    )
    x = pair_rows(tokens).astype(F32)
    normed, rstd = normalize(x)
    first_in = (normed * gain1 + bias1).astype(BF)
    second_in = (normed * gain2 + bias2).astype(BF)
    projected = dot(first_in, w_qkv, (1, 0)) + b_qkv
    places = places_of(z, chips)
    turn = lambda v, d: rotate_heads(v.reshape(-1, nh, HD), places, d).reshape(-1, HC)
    q = turn(projected[:, :HC], 1.0).astype(BF)
    k = turn(projected[:, HC : 2 * HC], 1.0).astype(BF)
    kv = jnp.concatenate([k, projected[:, 2 * HC :].astype(BF)], axis=1)
    prompt_kv = lax.all_gather(kv[: 4 * PSH].reshape(2, 2 * PSH, 2 * HC), "chip", axis=0)
    cont_valid = lax.all_gather(valid[2 * PSH :], "core", axis=0, tiled=True)
    masks = masks_of(z, chips, cont_valid)
    chosen = prompt_of[0]
    attended, lse = g_attention(q, prompt_kv, kv, chosen, masks)
    hidden_pre = dot(second_in, w_up, (1, 0)) + b_up
    activated = jax.nn.gelu(hidden_pre, approximate=False).astype(BF)
    partial = dot(attended, w_out, (1, 0)) + dot(activated, w_down, (1, 0))
    halves = split_rows(partial)
    take = lambda a: lax.dynamic_index_in_dim(a, c, axis=0, keepdims=False)
    give = lambda a: lax.dynamic_index_in_dim(a, 1 - c, axis=0, keepdims=False)
    output = tokens.astype(F32) + take(halves) + swap_cores(give(halves)) + b_out + b_down
    live = (valid > 0).astype(F32)[:, None]
    missed = output - teacher.astype(F32)
    count_all, squared_all = lax.psum((jnp.sum(live), jnp.sum(live * missed * missed)), ALL)
    loss_value = squared_all / (count_all * D)
    out_grad = cotangent.astype(F32) + 2.0 / (count_all * D) * live * missed
    out_low = pair_rows(out_grad.astype(BF))
    if stop == "fwd":
        return output, out_grad, out_low, attended, lse, activated, q, kv, first_in, second_in
    out_bias_grad = jnp.sum(out_grad.astype(BF).astype(F32), axis=0)
    dw_out = dot(attended, out_low, (0, 0))
    dw_down = dot(activated, out_low, (0, 0))
    att_grad = dot(out_low, w_out, (1, 1)).astype(BF)
    hidden_grad = (dot(out_low, w_down, (1, 1)) * gelu_slope(hidden_pre)).astype(BF)
    dw_up = dot(second_in, hidden_grad, (0, 0))
    db_up = jnp.sum(hidden_grad.astype(F32), axis=0)
    second_grad = dot(hidden_grad, w_up, (1, 1))
    dq, pair, near = g_attention_back(q, prompt_kv, kv, att_grad, lse, chosen, masks)
    own_pair = lax.psum_scatter(pair.astype(BF), "chip", scatter_dimension=0, tiled=True).astype(F32)
    pair = jnp.concatenate([own_pair, near], axis=0)
    projected_grad = jnp.concatenate([turn(dq, -1.0), turn(pair[:, :HC], -1.0), pair[:, HC:]], axis=1).astype(BF)
    dw_qkv = dot(first_in, projected_grad, (0, 0))
    db_qkv = jnp.sum(projected_grad.astype(F32), axis=0)
    first_grad = dot(projected_grad, w_qkv, (1, 1))
    if stop == "bwd":
        return dw_out, dw_down, dw_up, dw_qkv, second_grad, first_grad, projected_grad, hidden_grad, att_grad
    joint = first_grad * gain1 + second_grad * gain2
    halves = split_rows(joint)
    joint = take(halves) + swap_cores(give(halves))
    own_normed = take(split_rows(normed))
    own_rstd = take(split_rows(rstd))
    input_grad = out_grad + own_rstd * (
        joint
        - jnp.mean(joint, axis=-1, keepdims=True)
        - own_normed * jnp.mean(joint * own_normed, axis=-1, keepdims=True)
    )
    wide = lambda v, n: jnp.zeros((v.shape[0], 2, v.shape[1]), F32).at[:, c].set(v).reshape(-1)
    small = jnp.concatenate(
        [
            jnp.sum(first_grad * normed, axis=0),
            jnp.sum(first_grad, axis=0),
            jnp.sum(second_grad * normed, axis=0),
            jnp.sum(second_grad, axis=0),
            out_bias_grad,
            wide(db_qkv.reshape(3, HC), 3),
            wide(db_up.reshape(-1, rd), 16),
        ]
    )
    small = lax.psum(small, ALL)
    shares, at = [], 0
    for size in (D, D, D, D, D, 3 * D, FF):
        own = size // lax.axis_size(ALL)
        shares.append(lax.dynamic_slice_in_dim(small, at + device * own, own))
        at += size
    rs = lambda v: lax.psum_scatter(v.astype(BF), CHIPS, scatter_dimension=0, tiled=True).astype(F32)
    r = qkv_weight.shape[0]
    s_qkv = rs(dw_qkv).reshape(2, r, 3, HC)
    s_up = rs(dw_up).reshape(2, r, FF // (2 * rd), rd)
    s_down = rs(dw_down)
    pairs = lambda own, other, axis: jnp.where(c == 0, jnp.stack([own, other], axis), jnp.stack([other, own], axis))
    s_qkv = pairs(take(s_qkv), swap_cores(give(s_qkv)), 2).reshape(r, 3 * D)
    s_up = pairs(take(s_up), swap_cores(give(s_up)), 2).reshape(r, FF)
    o = dw_out.reshape(H // 2, -1, 2, r, D)
    o_own = lax.dynamic_index_in_dim(o, c, axis=2, keepdims=False)
    o_other = swap_cores(lax.dynamic_index_in_dim(o, 1 - c, axis=2, keepdims=False))
    s_out = rs(pairs(o_own, o_other, 0).reshape(-1, D))
    return (
        output.astype(BF), loss_value, input_grad, shares[0], shares[1], shares[2], shares[3],
        s_qkv, shares[5], s_out, shares[4], s_up, shares[6], s_down, shares[4],
    )


MESH_ID = pl.DeviceIdType.MESH
RANKS = 4


class Net:
    def __init__(self, send, recv):
        self.g, self.z, self.c = (lax.axis_index(a) for a in ALL)
        self.y, self.x = self.g // 2, self.g % 2
        self.send, self.recv, self.used = send, recv, 0
        self.chip = self.g * RANKS + self.z
        self.core = {"grp": self.g, "chip": self.z, "core": 1 - self.c}
        self.right = {"grp": self.y * 2 + 1 - self.x, "chip": self.z, "core": self.c}
        self.up = {"grp": (1 - self.y) * 2 + self.x, "chip": self.z, "core": self.c}
        self.line = [{"grp": self.g, "chip": (self.z + j) % RANKS, "core": self.c} for j in (1, 2, 3)]
        self.sent = []

    def enter(self):
        barrier = pltpu.get_barrier_semaphore()
        for peer in [self.core, self.right, self.up] + self.line:
            pl.semaphore_signal(barrier, inc=1, device_id=peer, device_id_type=MESH_ID)
        pl.semaphore_wait(barrier, 6)

    def copy(self, src, dst, peer):
        i = self.used
        self.used += 1
        made = pltpu.make_async_remote_copy(
            src_ref=src, dst_ref=dst, send_sem=self.send.at[i], recv_sem=self.recv.at[i],
            device_id=peer, device_id_type=MESH_ID,
        )
        made.start()
        self.sent.append(made)
        return made

    def same(self, view, peer):
        return self.copy(view, view, peer)

    def settle(self, made):
        made.wait_recv()
        made.wait_send()
        self.sent = [m for m in self.sent if m is not made]

    def leave(self):
        for made in self.sent:
            made.wait_send()
        self.sent = []


def gather_steps(net, dst, rb, col, width, before):
    a, b, both = pl.ds(col, width // 2), pl.ds(col + width // 2, width // 2), pl.ds(col, width)
    quad = 4 * rb
    held = {}

    def line():
        for made in before:
            made.wait_recv()
        view = dst.at[pl.ds(net.chip * rb, rb), both]
        held[0] = [net.same(view, peer) for peer in net.line]

    def first():
        for made in held[0]:
            made.wait_recv()
        rows = pl.ds(net.g * quad, quad)
        held[1] = [net.same(dst.at[rows, a], net.right), net.same(dst.at[rows, b], net.up)]

    def second():
        for made in held[1]:
            made.wait_recv()
        held[2] = [net.same(dst.at[pl.ds(net.y * 2 * quad, 2 * quad), a], net.up)]
        for y in range(2):
            held[2].append(net.same(dst.at[pl.ds((y * 2 + net.x) * quad, quad), b], net.right))

    def last():
        for made in held[2]:
            made.wait_recv()

    return [line, first, second, last]


def small_steps(net, rows):
    held = {}

    def pair():
        held[0] = [net.same(rows.at[net.chip * 2 + net.c], net.core)]

    def line():
        held[0][0].wait_recv()
        held[1] = [net.same(rows.at[pl.ds(net.chip * 2, 2)], peer) for peer in net.line]

    def first():
        for made in held[1]:
            made.wait_recv()
        held[2] = [net.same(rows.at[pl.ds(net.g * 8, 8)], net.right)]

    def second():
        held[2][0].wait_recv()
        held[3] = [net.same(rows.at[pl.ds(net.y * 16, 16)], net.up)]

    def last():
        held[3][0].wait_recv()

    return [pair, line, first, second, last]


VM = pl.BlockSpec(memory_space=pltpu.VMEM)
PROMPT = RANKS * 2 * PSH
KEYS = 2 * PROMPT + CONT
ROWS = 4 * PSH + CONT


def nt(a, b):
    return lax.dot_general(a, b, (((1,), (1,)), ((), ())), preferred_element_type=F32)


def nn(a, b):
    return lax.dot_general(a, b, (((1,), (0,)), ((), ())), preferred_element_type=F32)


def tn(a, b):
    return lax.dot_general(a, b, (((0,), (0,)), ((), ())), preferred_element_type=F32)


def tile_at(i, size):
    return pl.ds(pl.multiple_of(i * size, size), size)


def move_rows(dst, to, src, at, count, tile=32):
    @pl.loop(0, count // tile)
    def _(i):
        step = pl.multiple_of(i * tile, tile)
        dst[pl.ds(pl.multiple_of(to + step, tile), tile), :] = src[pl.ds(pl.multiple_of(at + step, tile), tile), :]


def spread_row(rows, field, index, owner, lane, size):
    table = rows[:, field, :].astype(BF)
    lanes = lax.broadcasted_iota(jnp.int32, (128, size), 0)
    pick = (lanes == index[lane : lane + 1, :size]).astype(F32).astype(BF)
    wide = nn(table, pick)
    owners = lax.broadcasted_iota(jnp.int32, (rows.shape[0], size), 0)
    return jnp.sum(jnp.where(owners == index[owner : owner + 1, :size], wide, 0.0), axis=0, keepdims=True)


def norm_rows(x):
    x = x.astype(F32)
    center = x - jnp.mean(x, axis=-1, keepdims=True)
    return center * lax.rsqrt(jnp.mean(center * center, axis=-1, keepdims=True) + EPSILON)


def turn(value, table, sign):
    cos, low_sin, high_sin = (table[:, 128 * i : 128 * i + 128] for i in range(3))
    out = []
    for j in range(value.shape[1] // 128):
        v = value[:, 128 * j : 128 * j + 128]
        other = pltpu.roll(v, 120, 1) * low_sin + pltpu.roll(v, 8, 1) * high_sin
        out.append(v * cos + sign * other)
    return out[0] if len(out) == 1 else jnp.concatenate(out, axis=1)


def rotary_table(length):
    half = ROT // 2
    inverse = (10000.0 ** (-np.arange(half, dtype=np.float32) / half)).astype(np.float32)
    angles = (np.arange(length, dtype=np.float32)[:, None] * inverse).astype(np.float64)
    cos, sin = np.cos(angles), np.sin(angles)
    table = np.zeros((length, 3, 2, HD), np.float32)
    table[:, 0] = 1.0
    for head in range(2):
        table[:, 0, head, :half] = cos
        table[:, 0, head, half:ROT] = cos
        table[:, 1, head, :half] = -sin
        table[:, 2, head, half:ROT] = sin
    return table.reshape(length, 384)


def index_table(rd):
    n = np.arange(2048)
    table = np.zeros((2, 16, 2048), np.int32)
    for c in range(2):
        col = np.minimum(n // HC, 2) * D + c * HC + n % HC
        table[c, 0], table[c, 1] = col // 96, col % 96
        unit = n // rd * (2 * rd) + c * rd + n % rd
        table[c, 2], table[c, 3] = unit // rd, unit % rd
        table[c, 4] = n // 32 % 32
        for i in range(4):
            table[c, 8 + i] = n % 32 + 32 * i
    return table


def seen(keys_at, queries_at, shape, length=None):
    keys = lax.broadcasted_iota(jnp.int32, shape, 0) + keys_at
    queries = lax.broadcasted_iota(jnp.int32, shape, 1) + queries_at
    mask = keys <= queries
    return mask if length is None else mask & (keys < length)


def head_lanes(rows):
    return lax.broadcasted_iota(jnp.int32, (rows, 128), 1) < HD


def attend(query, keys, values, masks, head):
    lanes = head_lanes(query.shape[0])
    own = jnp.where(lanes if head == 0 else ~lanes, query.astype(F32) * SCALE, 0.0).astype(BF)
    scores = [nt(k, own) for k in keys]
    scores = [s if m is None else jnp.where(m, s, NEGATIVE) for s, m in zip(scores, masks)]
    top = functools.reduce(jnp.maximum, [jnp.max(s, axis=0, keepdims=True) for s in scores])
    weights = [jnp.exp(s - top) for s in scores]
    total = sum(jnp.sum(w, axis=0, keepdims=True) for w in weights)
    share = 1.0 / total
    out = sum(tn(v, (w * share).astype(BF)) for v, w in zip(values, weights))
    return out[head * HD : head * HD + HD], top + jnp.log(total)


def forward_kernel(
    tokens, small, qkv, out, up, down, rotary, index,
    rows, w_qkv, w_out, w_up, w_down, x_own, first_own, second_in, q, kv, attended, lse, activated, slope,
    x_all, first_in, spread, swapped, send, recv,
):
    net = Net(send, recv)
    c, z, chip = net.c, net.z, net.chip
    net.enter()
    for p in range(2):
        move_rows(x_all, p * PROMPT + z * 2 * PSH + c * PSH, tokens, p * PSH, PSH)
    move_rows(x_all, 2 * PROMPT + c * HALF, tokens, 2 * PSH, HALF)
    rows[chip * 2 + c] = small[...]
    pieces = [pl.ds(p * PROMPT + z * 2 * PSH + c * PSH, PSH) for p in range(2)]
    smalls = small_steps(net, rows)
    smalls[0]()
    mates = [net.same(x_all.at[piece], net.core) for piece in pieces + [pl.ds(2 * PROMPT + c * HALF, HALF)]]
    half_rows = pl.ds(pl.multiple_of(chip * 64 + c * 32, 32), 32)
    given = pl.ds(0, 32)
    w_qkv[half_rows, :] = qkv[c]
    swapped[given, : 3 * HC] = qkv[1 - c]
    from_core = {}
    from_core["qkv"] = net.copy(swapped.at[given, pl.ds(0, 3 * HC)], w_qkv.at[half_rows], net.core)
    w_up[half_rows, :] = up[c]
    given = pl.ds(32, 32)
    swapped[given, : FF // 2] = up[1 - c]
    from_core["up"] = net.copy(swapped.at[given, pl.ds(0, FF // 2)], w_up.at[half_rows], net.core)
    w_down[pl.ds(pl.multiple_of(chip * 128, 128), 128), :] = down[...]
    spread[pl.ds(pl.multiple_of(chip * 32, 32), 32), :] = out[...]
    none = []
    tasks = [gather_steps(net, w_up, 64, 512 * i, 512, [] if i else [from_core["up"]]) for i in range(4)]
    tasks += [gather_steps(net, w_qkv, 64, 512 * i, 512, [] if i else [from_core["qkv"]]) for i in range(3)]
    tasks += [gather_steps(net, spread, 32, 0, 1024, [])]
    tasks += [gather_steps(net, w_down, 128, 256 * i, 256, []) for i in range(4)]
    clock = [0]

    def advance(until):
        while clock[0] < until:
            for t, steps in enumerate(tasks):
                if (clock[0] - t) % 2 == 0 and 0 <= (clock[0] - t) // 2 < len(steps):
                    steps[(clock[0] - t) // 2]()
            clock[0] += 1

    advance(1)
    smalls[1]()
    advance(2)
    smalls[2]()
    advance(3)
    smalls[3]()
    smalls[4]()
    advance(4)
    own_tokens = [net.same(x_all.at[piece], peer) for peer in net.line for piece in pieces]
    places = index.at[c]
    gain1, bias1, gain2, bias2 = (spread_row(rows, 0, places, 4, 8 + i, D) for i in range(4))
    b_qkv = spread_row(rows, 2, places, 0, 1, 3 * HC)
    b_up = spread_row(rows, 3, places, 2, 3, FF // 2)
    for made in mates:
        made.wait_recv()

    @pl.loop(0, ROWS // 64)
    def _(i):
        prompt = (i // 2) * PROMPT + z * 2 * PSH + (i % 2) * 64
        here = pl.ds(pl.multiple_of(jnp.where(i < 4, prompt, 2 * PROMPT + (i - 4) * 64), 64), 64)
        at = tile_at(i, 64)
        normed = norm_rows(x_all[here, :])
        x_own[at, :] = x_all[here, :]
        low = (normed * gain1 + bias1).astype(BF)
        first_in[here, :] = low
        first_own[at, :] = low
        second_in[at, :] = (normed * gain2 + bias2).astype(BF)

    advance(7)
    for made in own_tokens:
        made.wait_recv()
    relays = []
    for j in (1, 2, 3):
        for p in range(2):
            piece = pl.ds(p * PROMPT + (z + j) % RANKS * 2 * PSH + c * PSH, PSH)
            relays.append(net.same(x_all.at[piece], net.core))
    advance(8)
    for made in relays:
        made.wait_recv()

    @pl.loop(0, 12)
    def _(i):
        row = (i // 2 % 2) * PROMPT + (z + 1 + i // 4) % RANKS * 2 * PSH + (i % 2) * 64
        here = pl.ds(pl.multiple_of(row, 64), 64)
        first_in[here, :] = (norm_rows(x_all[here, :]) * gain1 + bias1).astype(BF)

    def hidden(j):
        cols = slice(256 * j, 256 * j + 256)

        @pl.loop(0, ROWS // 128)
        def _(i):
            at = tile_at(i, 128)
            pre = nn(second_in[at, :], w_up[:, cols]) + b_up[:, cols]
            gate = 0.5 * (1.0 + lax.erf(pre * 0.7071067811865476))
            activated[at, cols] = (pre * gate).astype(BF)
            slope[at, cols] = (gate + pre * jnp.exp(-0.5 * pre * pre) * 0.3989422804014327).astype(slope.dtype)

    advance(9)
    for j in range(0, 4):
        hidden(j)
    advance(10)
    for j in range(4, 6):
        hidden(j)
    advance(11)
    for j in range(6, 8):
        hidden(j)
    advance(12)
    advance(13)

    @pl.loop(0, KEYS // 256)
    def _(i):
        at = tile_at(i, 256)
        here = first_in[at, :]
        place = pl.multiple_of(jnp.where(i < 4, (i % 2) * 256, PROMPT + (i - 4) * 256), 256)
        table = rotary[pl.ds(place, 256), :]
        for j in range(4):
            cols = slice(HC + 256 * j, HC + 256 * j + 256)
            value = nn(here, w_qkv[:, cols]) + b_qkv[:, cols]
            kv[at, 256 * j : 256 * j + 256] = (turn(value, table, 1.0) if j < 2 else value).astype(BF)

    @pl.loop(0, ROWS // 128)
    def _(i):
        prompt = i * PROMPT + z * 2 * PSH
        source = pl.multiple_of(jnp.where(i < 2, prompt, 2 * PROMPT + (i - 2) * 128), 128)
        place = pl.multiple_of(jnp.where(i < 2, z * 2 * PSH, PROMPT + (i - 2) * 128), 128)
        here = first_in[pl.ds(source, 128), :]
        table = rotary[pl.ds(place, 128), :]
        for j in range(2):
            cols = slice(256 * j, 256 * j + 256)
            q[tile_at(i, 128), cols] = turn(nn(here, w_qkv[:, cols]) + b_qkv[:, cols], table, 1.0).astype(BF)

    advance(14)
    length = jnp.sum(jnp.sum(rows[pl.ds(chip * 2, 2), 5:7, :], axis=0), keepdims=True).astype(jnp.int32)
    second = jnp.broadcast_to(small[7:8, :], (PROMPT, 128)) > 0.5

    def attend_pair(pair):
        k_at, v_at = pl.ds(128 * pair, 128), pl.ds(HC + 128 * pair, 128)
        prompts = [(kv[p * PROMPT : (p + 1) * PROMPT, k_at], kv[p * PROMPT : (p + 1) * PROMPT, v_at]) for p in range(2)]

        def put(row, size, key_list, value_list, masks):
            outs = []
            for head in range(2):
                o, stat = attend(q[row : row + size, k_at], key_list, value_list, masks, head)
                outs.append(o)
                lse[2 * pair + head, :, row : row + size] = stat
            attended[row : row + size, k_at] = jnp.concatenate(outs, axis=0).T.astype(BF)

        for p in range(2):
            put(p * 128, 128, [prompts[p][0]], [prompts[p][1]], [seen(0, z * 2 * PSH, (PROMPT, 128))])
        chosen = [jnp.where(second, b.astype(F32), a.astype(F32)).astype(BF) for a, b in zip(*prompts)]
        for i in range(CONT // 128):
            near = 128 * i + 128
            put(
                256 + 128 * i, 128,
                [chosen[0], kv[2 * PROMPT : 2 * PROMPT + near, k_at]],
                [chosen[1], kv[2 * PROMPT : 2 * PROMPT + near, v_at]],
                [None, seen(0, 128 * i, (near, 128), length)],
            )

    attend_pair(0)
    advance(15)
    attend_pair(1)
    advance(16)
    attend_pair(2)
    advance(17)
    attend_pair(3)
    given = pl.ds(pl.multiple_of((1 - c) * 256, 256), 256)
    swap = net.copy(spread.at[given], swapped.at[pl.ds(64, 256), pl.ds(0, D)], net.core)
    advance(20)
    swap.wait_recv()
    for h in range(8):
        w_out[pl.ds(pl.multiple_of(h * 64 + c * 32, 32), 32), :] = spread[pl.ds(pl.multiple_of(c * 256 + h * 32, 32), 32), :]
        w_out[pl.ds(pl.multiple_of(h * 64 + (1 - c) * 32, 32), 32), :] = swapped[64 + h * 32 : 96 + h * 32, :D]
    net.leave()


def forward(tokens, small, qkv, out, up, down):
    shape = jax.ShapeDtypeStruct
    return pl.pallas_call(
        forward_kernel,
        out_shape=(
            shape((32, 8, 128), F32), shape((D, 3 * HC), BF), shape((HC, D), BF), shape((D, FF // 2), BF), shape((FF // 2, D), BF),
            shape((ROWS, D), BF), shape((ROWS, D), BF), shape((ROWS, D), BF), shape((ROWS, HC), BF), shape((KEYS, 2 * HC), BF),
            shape((ROWS, HC), BF), shape((8, 1, ROWS), F32), shape((ROWS, FF // 2), BF), shape((ROWS, FF // 2), F32),
        ),
        in_specs=[VM] * 8,
        out_specs=(VM,) * 14,
        scratch_shapes=[
            pltpu.VMEM((KEYS, D), BF), pltpu.VMEM((KEYS, D), BF), pltpu.VMEM((HC, D), BF), pltpu.VMEM((320, FF // 2), BF),
            pltpu.SemaphoreType.DMA((140,)), pltpu.SemaphoreType.DMA((140,)),
        ],
        compiler_params=pltpu.CompilerParams(collective_id=0, has_side_effects=True, vmem_limit_bytes=60 << 20),
    )(tokens, small, qkv, out, up, down, jnp.asarray(rotary_table(PROMPT + CONT)), jnp.asarray(index_table(128)))


def add_rows(dst, dst_rows, src, src_rows, count, cols, tile):
    @pl.loop(0, count // tile)
    def _(i):
        to = pl.ds(pl.multiple_of(dst_rows + i * tile, tile), tile)
        more = src[pl.ds(pl.multiple_of(src_rows + i * tile, tile), tile), cols].astype(F32)
        dst[to, :] = (dst[to, :].astype(F32) + more).astype(dst.dtype)


def scatter_steps(net, src, rb, col, width, before, got_a, got_b, got_z, put):
    half = width // 2
    a, b, both = pl.ds(col, half), pl.ds(col + half, half), pl.ds(col, width)
    quad = 4 * rb
    tile = min(64, rb)
    at = lambda y, x: pl.ds((y * 2 + x) * quad, quad)
    held = {}

    def first():
        for made in before:
            made.wait()
        rows = pl.ds((1 - net.y) * 2 * quad, 2 * quad)
        held[0] = [net.copy(src.at[rows, a], got_a.at[pl.ds(0, 2 * quad)], net.up)]
        for y in range(2):
            held[0].append(net.copy(src.at[at(y, 1 - net.x), b], got_b.at[pl.ds(y * quad, quad)], net.right))

    def second():
        for made in held[0]:
            made.wait_recv()
        add_rows(got_a, (1 - net.x) * quad, src, (net.y * 2 + 1 - net.x) * quad, quad, a, tile)
        add_rows(got_b, (1 - net.y) * quad, src, ((1 - net.y) * 2 + net.x) * quad, quad, b, tile)
        held[1] = [
            net.copy(got_a.at[pl.ds((1 - net.x) * quad, quad)], got_a.at[pl.ds(2 * quad, quad)], net.right),
            net.copy(got_b.at[pl.ds((1 - net.y) * quad, quad)], got_b.at[pl.ds(2 * quad, quad)], net.up),
        ]
        add_rows(got_a, net.x * quad, src, (net.y * 2 + net.x) * quad, quad, a, tile)
        add_rows(got_b, net.y * quad, src, (net.y * 2 + net.x) * quad, quad, b, tile)

    def third():
        for made in held[1]:
            made.wait_recv()
        add_rows(got_a, net.x * quad, got_a, 2 * quad, quad, slice(None), tile)
        add_rows(got_b, net.y * quad, got_b, 2 * quad, quad, slice(None), tile)
        held[2] = []
        for j in (1, 2, 3):
            there = (net.z + j) % RANKS * rb
            peer = net.line[j - 1]
            held[2].append(net.copy(got_a.at[pl.ds(net.x * quad + there, rb)], got_z.at[j - 1, :, pl.ds(0, half)], peer))
            held[2].append(net.copy(got_b.at[pl.ds(net.y * quad + there, rb)], got_z.at[j - 1, :, pl.ds(half, half)], peer))

    def last():
        for made in held[2]:
            made.wait_recv()
        for k, (got, way) in enumerate(((got_a, net.x), (got_b, net.y))):
            cols = slice(k * half, k * half + half)

            @pl.loop(0, rb // tile)
            def _(i):
                rows = pl.ds(pl.multiple_of(way * quad + net.z * rb + i * tile, tile), tile)
                value = got[rows, :].astype(F32)
                for j in range(3):
                    value = value + got_z[j, tile_at(i, tile), cols].astype(F32)
                put(tile_at(i, tile), slice(col + k * half, col + k * half + half), value)

    return [first, second, third, last]


def sum_steps(net, value, got):
    held = {}
    peers = [net.core, net.right, net.up]

    def make(i):
        def step():
            if i > 0:
                net.settle(held[i - 1])
                value[...] = value[...] + got[i - 1]
            if i < 3:
                held[i] = net.copy(value, got.at[i], peers[i])
            else:
                held[3] = [net.copy(value, got.at[3 + net.z], peer) for peer in net.line]
                got[3 + net.z] = value[...]

        return step

    def last():
        for made in held[3]:
            net.settle(made)
        value[...] = (got[3] + got[4]) + (got[5] + got[6])

    return [make(i) for i in range(4)] + [last]


def attend_back(query, grad, keys, values, masks, stat, head):
    lanes = head_lanes(query.shape[0])
    lanes = lanes if head == 0 else ~lanes
    own = jnp.where(lanes, query.astype(F32) * SCALE, 0.0).astype(BF)
    own_grad = jnp.where(lanes, grad.astype(F32), 0.0).astype(BF)
    inner, kept = 0.0, []
    for k, v, m in zip(keys, values, masks):
        scores = nt(k, own)
        probs = jnp.exp((scores if m is None else jnp.where(m, scores, NEGATIVE)) - stat)
        prob_grad = nt(v, own_grad)
        inner = inner + jnp.sum(probs * prob_grad, axis=0, keepdims=True)
        kept.append((probs, prob_grad))
    dq, dks, dvs = 0.0, [], []
    for k, (probs, prob_grad) in zip(keys, kept):
        score_grad = (probs * (prob_grad - inner)).astype(BF)
        dq = dq + tn(k, score_grad)
        dks.append(nn(score_grad, own))
        dvs.append(nn(probs.astype(BF), own_grad))
    return dq[head * HD : head * HD + HD] * SCALE, dks, dvs


def backward_kernel(
    rows, small, value_in, gain, rotary, q, kv, att_grad, lse, first, x, w_qkv, joint_in, dw_out_in, dw_down_in, dw_up_in,
    value, o_qkv, o_out, o_up, o_down, joint_own,
    dw_qkv, dw_out, dw_down, dw_up, spread, pairs, got_pairs, far_k, far_v, projected, joint, peer_joint,
    got_s, s_qkv, s_up, peer_qkv, peer_up, *rest,
):
    bufs, (send, recv, local) = rest[:-3], rest[-3:]
    net = Net(send, recv)
    c, z, chip = net.c, net.z, net.chip
    loads = [pltpu.make_async_copy(src, dst, local.at[i]) for i, (src, dst) in enumerate(
        ((dw_down_in, dw_down), (dw_up_in, dw_up), (dw_out_in, dw_out)))]
    for load in loads:
        load.start()
    value[...] = value_in[...]
    net.enter()
    bufs = list(bufs)
    take3 = lambda: [bufs.pop(0) for _ in range(3)]

    def put_into(ref):
        def put(at, cols, total):
            ref[at, cols] = total

        return put

    clock, tasks = [0], []

    def advance(until):
        while clock[0] < until:
            for t, steps in tasks:
                if (clock[0] - t) % 2 == 0 and 0 <= (clock[0] - t) // 2 < len(steps):
                    steps[(clock[0] - t) // 2]()
            clock[0] += 1

    loads[0].wait()
    tasks.append((0, scatter_steps(net, dw_down, 128, 0, 512, [], *take3(), put_into(o_down))))
    tasks.append((1, scatter_steps(net, dw_down, 128, 512, 512, [], *take3(), put_into(o_down))))
    tasks.append((2, scatter_steps(net, dw_up, 64, 0, 1024, [loads[1]], *take3(), put_into(s_up))))
    tasks.append((3, scatter_steps(net, dw_up, 64, 1024, 1024, [], *take3(), put_into(s_up))))
    advance(2)
    loads[2].wait()
    swaps = []
    for h in range(8):
        theirs = dw_out.at[pl.ds(h * 64 + (1 - c) * 32, 32)]
        swaps.append(net.copy(theirs, spread.at[pl.ds((8 * c + h) * 32, 32)], net.core))
        spread[pl.ds(pl.multiple_of((8 * c + h) * 32, 32), 32), :] = dw_out[pl.ds(pl.multiple_of(h * 64 + c * 32, 32), 32), :]
    tasks.append((4, scatter_steps(net, spread, 32, 0, 1024, [], *take3(), put_into(o_out))))

    length = jnp.sum(jnp.sum(rows[pl.ds(chip * 2, 2), 5:7, :], axis=0), keepdims=True).astype(jnp.int32)
    second = jnp.broadcast_to(small[7:8, :], (PROMPT, 128)) > 0.5
    weight = small[7:8, :]
    pair_sends = []

    def back_pair(pair):
        k_at, v_at = pl.ds(128 * pair, 128), pl.ds(HC + 128 * pair, 128)
        prompts = [(kv[p * PROMPT : (p + 1) * PROMPT, k_at], kv[p * PROMPT : (p + 1) * PROMPT, v_at]) for p in range(2)]
        chosen = [jnp.where(second, b.astype(F32), a.astype(F32)).astype(BF) for a, b in zip(*prompts)]

        def both_heads(row, size, keys, values, masks, place):
            dq, dks, dvs = [], None, None
            for head in range(2):
                stat = lse[2 * pair + head, :, row : row + size]
                d, k_parts, v_parts = attend_back(
                    q[row : row + size, k_at], att_grad[row : row + size, k_at], keys, values, masks, stat, head
                )
                dq.append(d)
                dks = k_parts if dks is None else [a + b for a, b in zip(dks, k_parts)]
                dvs = v_parts if dvs is None else [a + b for a, b in zip(dvs, v_parts)]
            dq = jnp.concatenate(dq, axis=0).T
            projected[row : row + size, k_at] = turn(dq, rotary[pl.ds(place, size), :], -1.0).astype(BF)
            return dks, dvs

        near_k, near_v = None, None
        for i in range(2):
            near = 256 * i + 256
            masks = [None, seen(0, 256 * i, (near, 256), length)]
            near_keys = kv[2 * PROMPT : 2 * PROMPT + near, k_at], kv[2 * PROMPT : 2 * PROMPT + near, v_at]
            dks, dvs = both_heads(
                256 + 256 * i, 256, [chosen[0], near_keys[0]], [chosen[1], near_keys[1]], masks, PROMPT + 256 * i
            )
            if i == 0:
                far_k[...], far_v[...] = dks[0], dvs[0]
                near_k, near_v = dks[1], dvs[1]
            else:
                far_k[...] = far_k[...] + dks[0]
                far_v[...] = far_v[...] + dvs[0]
                near_k = [near_k + dks[1][:256], dks[1][256:]]
                near_v = [near_v + dvs[1][:256], dvs[1][256:]]
        for i in range(2):
            at = slice(256 + 256 * i, 512 + 256 * i)
            table = rotary[PROMPT + 256 * i : PROMPT + 256 * i + 256, :]
            projected[at, HC + 128 * pair : HC + 128 * pair + 128] = turn(near_k[i], table, -1.0).astype(BF)
            projected[at, 2 * HC + 128 * pair : 2 * HC + 128 * pair + 128] = near_v[i].astype(BF)
        for p in range(2):
            place = pl.multiple_of(z * 2 * PSH, 128)
            dks, dvs = both_heads(
                128 * p, 128, [prompts[p][0]], [prompts[p][1]], [seen(0, z * 2 * PSH, (PROMPT, 128))], place
            )
            share = weight if p == 1 else 1.0 - weight
            at = slice(p * PROMPT, p * PROMPT + PROMPT)
            pairs[pair, at, :128] = (dks[0] + share * far_k[...]).astype(BF)
            pairs[pair, at, 128:] = (dvs[0] + share * far_v[...]).astype(BF)
        for j in (1, 2, 3):
            for p in range(2):
                there = pl.ds(p * PROMPT + (z + j) % RANKS * 2 * PSH, 2 * PSH)
                pair_sends.append(
                    net.copy(pairs.at[pair, there], got_pairs.at[j - 1, pair, pl.ds(p * 2 * PSH, 2 * PSH)], net.line[j - 1])
                )

    back_pair(0)
    advance(3)
    back_pair(1)
    advance(4)
    for made in swaps:
        made.wait_recv()
    back_pair(2)
    advance(5)
    back_pair(3)
    advance(6)
    for made in pair_sends:
        made.wait_recv()
    table = rotary[pl.ds(pl.multiple_of(z * 2 * PSH, 128), 128), :]
    for pair in range(4):
        for p in range(2):
            at = slice(p * 128, p * 128 + 128)
            total = pairs[pair, pl.ds(pl.multiple_of(p * PROMPT + z * 2 * PSH, 128), 128), :].astype(F32)
            for j in range(3):
                total = total + got_pairs[j, pair, at, :].astype(F32)
            projected[at, HC + 128 * pair : HC + 128 * pair + 128] = turn(total[:, :128], table, -1.0).astype(BF)
            projected[at, 2 * HC + 128 * pair : 2 * HC + 128 * pair + 128] = total[:, 128:].astype(BF)

    def weight_columns(col, width):
        @pl.loop(0, D // 256)
        def _(i):
            part = tn(first[:, tile_at(i, 256)], projected[:, col : col + width])
            dw_qkv[tile_at(i, 256), col : col + width] = part.astype(BF)

    weight_columns(0, 768)
    tasks.append((6, scatter_steps(net, dw_qkv, 64, 0, 768, [], *take3(), put_into(s_qkv))))
    advance(7)
    weight_columns(768, 768)
    tasks.append((7, scatter_steps(net, dw_qkv, 64, 768, 768, [], *take3(), put_into(s_qkv))))
    advance(8)
    fg_sum, fg_normed = jnp.zeros((1, D), F32), jnp.zeros((1, D), F32)
    bias = jnp.zeros((1, 3 * HC), F32)

    def first_rows(i, sums):
        at = tile_at(i, 128)
        here = projected[at, :]
        grad = nt(here, w_qkv[...])
        normed = norm_rows(x[at, :])
        joint[at, :] = grad * gain[...] + joint_in[at, :]
        return (
            sums[0] + jnp.sum(grad, axis=0, keepdims=True),
            sums[1] + jnp.sum(grad * normed, axis=0, keepdims=True),
            sums[2] + jnp.sum(here.astype(F32), axis=0, keepdims=True),
        )

    fg_sum, fg_normed, bias = lax.fori_loop(0, ROWS // 128, first_rows, (fg_sum, fg_normed, bias))
    ranges = ((0, PSH, lambda o: o * PSH), (PSH, PSH, lambda o: 2 * PSH + o * PSH), (2 * PSH, HALF, lambda o: 4 * PSH + o * HALF))
    joints = [
        net.copy(joint.at[pl.ds(there(1 - c), size)], peer_joint.at[pl.ds(at, size)], net.core) for at, size, there in ranges
    ]
    for i in range(8):
        cols = slice(128 * i, 128 * i + 128)
        value[i : i + 1, :] = value[i : i + 1, :] + fg_normed[:, cols]
        value[8 + i : 9 + i, :] = value[8 + i : 9 + i, :] + fg_sum[:, cols]
    for i in range(12):
        row = pl.ds(40 + i // 4 * 8 + c * 4 + i % 4, 1)
        value[row, :] = value[row, :] + bias[:, 128 * i : 128 * i + 128]
    sums = sum_steps(net, value, got_s)
    sums[0]()
    advance(9)
    for made in joints:
        made.wait_recv()
    for at, size, there in ranges:
        mine = pl.ds(pl.multiple_of(there(c), 64), size)
        joint_own[at : at + size, :] = joint[mine, :] + peer_joint[at : at + size, :]
    sums[1]()
    advance(10)
    sums[2]()
    ups = []

    def give(total, peer_ref):
        return net.copy(total.at[pl.ds((1 - c) * 32, 32)], peer_ref, net.core)

    advance(11)
    ups.append(give(s_up, peer_up))
    sums[3]()
    advance(12)
    sums[4]()
    advance(16)
    ups.append(give(s_qkv, peer_qkv))
    own_rows = pl.ds(pl.multiple_of(c * 32, 32), 32)
    ups[0].wait_recv()
    for i in range(16):
        for who, part in ((c, s_up[own_rows, 128 * i : 128 * i + 128]), (1 - c, peer_up[:, 128 * i : 128 * i + 128])):
            o_up[:, pl.ds(pl.multiple_of((2 * i + who) * 128, 128), 128)] = part
    ups[1].wait_recv()
    for i in range(3):
        for who, part in ((c, s_qkv[own_rows, HC * i : HC * i + HC]), (1 - c, peer_qkv[:, HC * i : HC * i + HC])):
            o_qkv[:, pl.ds(pl.multiple_of(i * D + who * HC, 128), HC)] = part
    net.leave()


def backward(*args):
    shape = jax.ShapeDtypeStruct
    bufs = []
    for rb, width, count in ((128, 512, 2), (64, 1024, 2), (32, 1024, 1), (64, 768, 2)):
        for _ in range(count):
            bufs += [pltpu.VMEM((12 * rb, width // 2), BF), pltpu.VMEM((12 * rb, width // 2), BF), pltpu.VMEM((3, rb, width), BF)]
    return pl.pallas_call(
        backward_kernel,
        out_shape=(
            shape((104, 128), F32), shape((32, 3 * D), F32), shape((32, D), F32), shape((32, FF), F32), shape((128, D), F32),
            shape((384, D), F32),
        ),
        in_specs=[VM] * 13 + [pl.BlockSpec(memory_space=pl.ANY)] * 3,
        out_specs=(VM,) * 6,
        scratch_shapes=[
            pltpu.VMEM((D, 3 * HC), BF), pltpu.VMEM((HC, D), BF), pltpu.VMEM((FF // 2, D), BF), pltpu.VMEM((D, FF // 2), BF),
            pltpu.VMEM((HC, D), BF), pltpu.VMEM((4, 2 * PROMPT, 256), BF), pltpu.VMEM((3, 4, 4 * PSH, 256), BF),
            pltpu.VMEM((PROMPT, 128), F32), pltpu.VMEM((PROMPT, 128), F32), pltpu.VMEM((ROWS, 3 * HC), BF),
            pltpu.VMEM((ROWS, D), F32), pltpu.VMEM((384, D), F32), pltpu.VMEM((7, 104, 128), F32),
            pltpu.VMEM((64, 3 * HC), F32), pltpu.VMEM((64, FF // 2), F32), pltpu.VMEM((32, 3 * HC), F32), pltpu.VMEM((32, FF // 2), F32),
        ] + bufs
        + [pltpu.SemaphoreType.DMA((140,)), pltpu.SemaphoreType.DMA((140,)), pltpu.SemaphoreType.DMA((4,))],
        compiler_params=pltpu.CompilerParams(collective_id=1, has_side_effects=True, vmem_limit_bytes=63 << 20),
    )(*args)


def fast_body(
    tokens, valid, prompt_of, teacher, cotangent,
    ln1_gain, ln1_bias, ln2_gain, ln2_bias, qkv_weight, qkv_bias, out_weight, out_bias,
    up_weight, up_bias, down_weight, down_bias,
):
    c = lax.axis_index("core")
    z = lax.axis_index("chip")
    chips = lax.axis_size("chip")
    nh = HC // HD
    rd = down_weight.shape[0]
    device = lax.axis_index(ALL)
    pad = lambda v: jnp.pad(v.astype(F32), (0, 128 - v.shape[0]))[None]
    live_own = (valid > 0).astype(F32)
    small = jnp.concatenate(
        [
            jnp.concatenate([ln1_gain, ln1_bias, ln2_gain, ln2_bias]).astype(F32)[None],
            pad(jnp.concatenate([out_bias, down_bias])),
            pad(qkv_bias),
            pad(up_bias),
            live_own.reshape(3, 128),
            jnp.broadcast_to(prompt_of.astype(F32)[:, None], (1, 128)),
        ]
    )
    rows, w_qkv, w_out, w_up, w_down, x_own, first_own, second_in, q, kv, attended, lse, activated, slope = forward(
        tokens,
        small,
        qkv_weight.reshape(32, 3, 2, HC).transpose(2, 0, 1, 3).reshape(2, 32, 3 * HC),
        out_weight,
        up_weight.reshape(32, 16, 2, 128).transpose(2, 0, 1, 3).reshape(2, 32, FF // 2),
        down_weight,
    )
    normed, _ = normalize(x_own.astype(F32))
    gain1, bias1, gain2, bias2 = (rows[:, 0, 32 * i : 32 * i + 32].reshape(-1) for i in range(4))
    b_out, b_down = (rows[:, 1, 32 * i : 32 * i + 32].reshape(-1) for i in range(2))
    count_all = jnp.sum(rows[:, 4:7])
    partial = dot(attended, w_out, (1, 0)) + dot(activated, w_down, (1, 0))
    halves = split_rows(partial)
    take = lambda a: lax.dynamic_index_in_dim(a, c, axis=0, keepdims=False)
    give = lambda a: lax.dynamic_index_in_dim(a, 1 - c, axis=0, keepdims=False)
    output = tokens.astype(F32) + take(halves) + swap_cores(give(halves)) + b_out + b_down
    live = (valid > 0).astype(F32)[:, None]
    missed = output - teacher.astype(F32)
    squared = jnp.sum(live * missed * missed)
    out_grad = cotangent.astype(F32) + 2.0 / (count_all * D) * live * missed
    out_low = pair_rows(out_grad.astype(BF))
    out_bias_grad = jnp.sum(out_grad.astype(BF).astype(F32), axis=0)
    dw_out = dot(attended, out_low, (0, 0))
    dw_down = dot(activated, out_low, (0, 0))
    att_grad = dot(out_low, w_out, (1, 1)).astype(BF)
    hidden_grad = (dot(out_low, w_down, (1, 1)) * slope).astype(BF)
    dw_up = dot(second_in, hidden_grad, (0, 0))
    db_up = jnp.sum(hidden_grad.astype(F32), axis=0)
    second_grad = dot(hidden_grad, w_up, (1, 1))
    wide = lambda v: jnp.zeros((v.shape[0], 2, v.shape[1]), F32).at[:, c].set(v).reshape(-1)
    value = jnp.concatenate(
        [
            jnp.zeros((2 * D,), F32),
            jnp.sum(second_grad * normed, axis=0),
            jnp.sum(second_grad, axis=0),
            out_bias_grad,
            jnp.zeros((3 * D,), F32),
            wide(db_up.reshape(-1, rd)),
            jnp.full((128,), squared),
            jnp.zeros((7 * 128,), F32),
        ]
    ).reshape(-1, 128)
    value, s_qkv, s_out, s_up, s_down, joint = backward(
        rows, small, value, gain1[None], jnp.asarray(rotary_table(PROMPT + CONT)), q, kv, att_grad, lse, first_own, x_own,
        w_qkv, second_grad * gain2, dw_out.astype(BF), dw_down.astype(BF), dw_up.astype(BF),
    )
    own_normed, own_rstd = normalize(tokens.astype(F32))
    input_grad = out_grad + own_rstd * (
        joint
        - jnp.mean(joint, axis=-1, keepdims=True)
        - own_normed * jnp.mean(joint * own_normed, axis=-1, keepdims=True)
    )
    value = value.reshape(-1)
    shares, at = [], 0
    for size in (D, D, D, D, D, 3 * D, FF):
        own = size // lax.axis_size(ALL)
        shares.append(lax.dynamic_slice_in_dim(value, at + device * own, own))
        at += size
    loss_value = value[at] / (count_all * D)
    return (
        output.astype(BF), loss_value, input_grad, shares[0], shares[1], shares[2], shares[3],
        s_qkv, shares[5], s_out, shares[4], s_up, shares[6], s_down, shares[4],
    )


def solution(mesh):
    groups, seats = mesh.shape["grp"], mesh.shape["seq"]
    fine = Mesh(mesh.devices.reshape(groups, seats // 2, 2), ALL)
    rows, row = P(ALL, None), P(ALL)
    in_specs = (rows, row, row, rows, rows) + (row,) * 4 + (rows, row) * 4
    out_specs = (rows, P(), rows) + (row,) * 4 + (rows, row) * 4
    return jax.shard_map(fast_body if (groups, seats) == (4, 8) else generic_body, mesh=fine, in_specs=in_specs, out_specs=out_specs, check_vma=False)
```

```python
import functools

import jax
import jax.numpy as jnp
import numpy as np
from jax import lax
from jax.experimental import pallas as pl
from jax.experimental.pallas import tpu as pltpu
from jax.sharding import Mesh
from jax.sharding import PartitionSpec as P

D = 1024
H = 16
HD = 64
ROT = 16
FF = 4096
PSH = 64
CONT = 512
HALF = CONT // 2
HC = H // 2 * HD
EPSILON = 1e-05
NEGATIVE = -1e30
SCALE = 0.125
BF = jnp.bfloat16
F32 = jnp.float32
ALL = ("grp", "chip", "core")
CHIPS = ("grp", "chip")


def swap_cores(x):
    return lax.ppermute(x, "core", [(0, 1), (1, 0)])


def pair_rows(own):
    both = lax.all_gather(own, "core", axis=0)
    prompts = both[:, : 2 * PSH].reshape((2, 2, PSH) + own.shape[1:])
    prompts = prompts.swapaxes(0, 1).reshape((4 * PSH,) + own.shape[1:])
    return jnp.concatenate([prompts, both[:, 2 * PSH :].reshape((CONT,) + own.shape[1:])], axis=0)


def split_rows(rows):
    prompts = rows[: 4 * PSH].reshape((2, 2, PSH) + rows.shape[1:]).swapaxes(0, 1)
    prompts = prompts.reshape((2, 2 * PSH) + rows.shape[1:])
    return jnp.concatenate([prompts, rows[4 * PSH :].reshape((2, HALF) + rows.shape[1:])], axis=1)


def normalize(values):
    center = values - jnp.mean(values, axis=-1, keepdims=True)
    inverse_dev = lax.rsqrt(jnp.mean(center * center, axis=-1, keepdims=True) + EPSILON)
    return (center * inverse_dev, inverse_dev)


def rotate_heads(values, places, direction):
    halfrot = ROT // 2
    inverse = 10000.0 ** (-jnp.arange(halfrot, dtype=F32) / halfrot)
    angles = places.astype(F32)[..., None] * inverse
    cosine = jnp.cos(angles)[..., None, :]
    sine_part = direction * jnp.sin(angles)[..., None, :]
    leading = values[..., :halfrot]
    trailing = values[..., halfrot:ROT]
    return jnp.concatenate(
        [
            leading * cosine - trailing * sine_part,
            trailing * cosine + leading * sine_part,
            values[..., ROT:],
        ],
        axis=-1,
    )


def gelu_slope(values):
    return (
        0.5 * (1.0 + lax.erf(values * 0.7071067811865476))
        + values * jnp.exp(-0.5 * values * values) * 0.3989422804014327
    )


def dot(a, b, contract):
    return lax.dot_general(a, b, ((contract[:1], contract[1:]), ((), ())), preferred_element_type=F32)


def g_weights(c, qkv_weight, out_weight, up_weight, down_weight):
    r = qkv_weight.shape[0]
    mine = functools.partial(lax.dynamic_index_in_dim, index=c, keepdims=False)
    both = lambda w: lax.all_gather(w, "core", axis=0, tiled=True)
    qkv = mine(both(qkv_weight).reshape(2 * r, 3, 2, HC), axis=2).reshape(2 * r, 3 * HC)
    qkv = lax.all_gather(qkv, CHIPS, axis=0, tiled=True)
    rd = down_weight.shape[0]
    up = mine(both(up_weight).reshape(2 * r, FF // (2 * rd), 2, rd), axis=2).reshape(2 * r, FF // 2)
    up = lax.all_gather(up, CHIPS, axis=0, tiled=True)
    down = lax.all_gather(down_weight, CHIPS, axis=0, tiled=True)
    out = lax.all_gather(out_weight, ALL, axis=0, tiled=True)
    out = mine(out.reshape(2, HC, D), axis=0)
    return qkv, out, up, down


def g_small(c, rd, ln1_gain, ln1_bias, ln2_gain, ln2_bias, qkv_bias, out_bias, up_bias, down_bias):
    sizes = [v.shape[0] for v in (ln1_gain, ln1_bias, ln2_gain, ln2_bias, out_bias, down_bias, qkv_bias, up_bias)]
    packed = jnp.concatenate([ln1_gain, ln1_bias, ln2_gain, ln2_bias, out_bias, down_bias, qkv_bias, up_bias])
    rows = lax.all_gather(packed, ALL, axis=0)
    parts, at = [], 0
    for size in sizes:
        parts.append(rows[:, at : at + size].reshape(-1).astype(F32))
        at += size
    qb = lax.dynamic_index_in_dim(parts[6].reshape(3, 2, HC), c, axis=1, keepdims=False).reshape(-1)
    ub = lax.dynamic_index_in_dim(parts[7].reshape(-1, 2, rd), c, axis=1, keepdims=False).reshape(-1)
    return parts[:6] + [qb, ub]


def places_of(z, chips):
    prompt = z * 2 * PSH + jnp.arange(2 * PSH)
    return jnp.concatenate([prompt, prompt, chips * 2 * PSH + jnp.arange(CONT)])


def masks_of(z, chips, cont_valid):
    length = chips * 2 * PSH
    prompt = jnp.arange(length)[None, :] <= z * 2 * PSH + jnp.arange(2 * PSH)[:, None]
    own = jnp.arange(CONT)[None, :] <= jnp.arange(CONT)[:, None]
    own = own & (cont_valid > 0)[None, :]
    return prompt, jnp.concatenate([jnp.ones((CONT, length), bool), own], axis=1)


def g_attention(q, prompt_kv, kv, chosen, masks):
    nh = HC // HD
    chips = prompt_kv.shape[0]
    pk = prompt_kv.reshape(chips, 2, 2 * PSH, 2, nh, HD).transpose(3, 4, 1, 0, 2, 5)
    pk = pk.reshape(2, nh, 2, chips * 2 * PSH, HD)
    qh = q.reshape(-1, nh, HD).swapaxes(0, 1)
    pq = qh[:, : 4 * PSH].reshape(nh, 2, 2 * PSH, HD)
    scores = jnp.einsum("hpqd,hpkd->hpqk", pq, pk[0], preferred_element_type=F32) * SCALE
    scores = jnp.where(masks[0], scores, NEGATIVE)
    top = jnp.max(scores, axis=-1, keepdims=True)
    weights = jnp.exp(scores - top)
    total = jnp.sum(weights, axis=-1, keepdims=True)
    p_out = jnp.einsum("hpqk,hpkd->hpqd", (weights / total).astype(BF), pk[1], preferred_element_type=F32)
    p_lse = (top + jnp.log(total))[..., 0].reshape(nh, 4 * PSH)
    far = lax.dynamic_index_in_dim(pk, chosen, axis=2, keepdims=False)
    near = kv[4 * PSH :].reshape(CONT, 2, nh, HD).transpose(1, 2, 0, 3)
    ck = jnp.concatenate([far, near], axis=2)
    cq = qh[:, 4 * PSH :]
    scores = jnp.einsum("hqd,hkd->hqk", cq, ck[0], preferred_element_type=F32) * SCALE
    scores = jnp.where(masks[1], scores, NEGATIVE)
    top = jnp.max(scores, axis=-1, keepdims=True)
    weights = jnp.exp(scores - top)
    total = jnp.sum(weights, axis=-1, keepdims=True)
    c_out = jnp.einsum("hqk,hkd->hqd", (weights / total).astype(BF), ck[1], preferred_element_type=F32)
    c_lse = (top + jnp.log(total))[..., 0]
    att = jnp.concatenate([p_out.reshape(nh, 4 * PSH, HD), c_out], axis=1)
    return att.swapaxes(0, 1).reshape(-1, HC).astype(BF), jnp.concatenate([p_lse, c_lse], axis=1)


def g_attention_back(q, prompt_kv, kv, att_grad, lse, chosen, masks):
    nh = HC // HD
    chips = prompt_kv.shape[0]
    pk = prompt_kv.reshape(chips, 2, 2 * PSH, 2, nh, HD).transpose(3, 4, 1, 0, 2, 5)
    pk = pk.reshape(2, nh, 2, chips * 2 * PSH, HD)
    qh = q.reshape(-1, nh, HD).swapaxes(0, 1)
    gh = att_grad.reshape(-1, nh, HD).swapaxes(0, 1)
    pq = qh[:, : 4 * PSH].reshape(nh, 2, 2 * PSH, HD)
    pg = gh[:, : 4 * PSH].reshape(nh, 2, 2 * PSH, HD)
    ein = functools.partial(jnp.einsum, preferred_element_type=F32)

    def back(eq, ek, query, key, value, grad, mask, lse_rows):
        scores = jnp.where(mask, ein(f"{eq},{ek}->{eq[:-1]}k", query, key) * SCALE, NEGATIVE)
        probs = jnp.exp(scores - lse_rows[..., None])
        prob_grad = ein(f"{eq},{ek}->{eq[:-1]}k", grad, value)
        inner = jnp.sum(probs * prob_grad, axis=-1, keepdims=True)
        score_grad = (probs * (prob_grad - inner)).astype(BF)
        es = eq[:-1] + "k"
        dq = ein(f"{es},{ek}->{eq}", score_grad, key) * SCALE
        dk = ein(f"{es},{eq}->{ek}", score_grad, query) * SCALE
        dv = ein(f"{es},{eq}->{ek}", probs.astype(BF), grad)
        return dq, dk, dv

    dq_p, dk_p, dv_p = back("hpqd", "hpkd", pq, pk[0], pk[1], pg, masks[0], lse[:, : 4 * PSH].reshape(nh, 2, 2 * PSH))
    far = lax.dynamic_index_in_dim(pk, chosen, axis=2, keepdims=False)
    near = kv[4 * PSH :].reshape(CONT, 2, nh, HD).transpose(1, 2, 0, 3)
    ck = jnp.concatenate([far, near], axis=2)
    dq_c, dk_c, dv_c = back("hqd", "hkd", qh[:, 4 * PSH :], ck[0], ck[1], gh[:, 4 * PSH :], masks[1], lse[:, 4 * PSH :])
    length = chips * 2 * PSH
    pick = (jnp.arange(2) == chosen).astype(F32)[None, :, None, None]
    dk_p = dk_p + pick * dk_c[:, None, :length]
    dv_p = dv_p + pick * dv_c[:, None, :length]
    dq = jnp.concatenate([dq_p.reshape(nh, 4 * PSH, HD), dq_c], axis=1).swapaxes(0, 1).reshape(-1, HC)
    pair = jnp.stack([dk_p, dv_p])
    pair = pair.reshape(2, nh, 2, chips, 2 * PSH, HD).transpose(3, 2, 4, 0, 1, 5).reshape(chips * 4 * PSH, 2 * HC)
    near_grad = jnp.stack([dk_c[:, length:], dv_c[:, length:]]).transpose(2, 0, 1, 3).reshape(CONT, 2 * HC)
    return dq, pair, near_grad


def generic_body(
    tokens, valid, prompt_of, teacher, cotangent,
    ln1_gain, ln1_bias, ln2_gain, ln2_bias, qkv_weight, qkv_bias, out_weight, out_bias,
    up_weight, up_bias, down_weight, down_bias, stop=None,
):
    c = lax.axis_index("core")
    z = lax.axis_index("chip")
    chips = lax.axis_size("chip")
    nh = HC // HD
    rd = down_weight.shape[0]
    device = lax.axis_index(ALL)
    w_qkv, w_out, w_up, w_down = g_weights(c, qkv_weight, out_weight, up_weight, down_weight)
    gain1, bias1, gain2, bias2, b_out, b_down, b_qkv, b_up = g_small(
        c, rd, ln1_gain, ln1_bias, ln2_gain, ln2_bias, qkv_bias, out_bias, up_bias, down_bias
    )
    x = pair_rows(tokens).astype(F32)
    normed, rstd = normalize(x)
    first_in = (normed * gain1 + bias1).astype(BF)
    second_in = (normed * gain2 + bias2).astype(BF)
    projected = dot(first_in, w_qkv, (1, 0)) + b_qkv
    places = places_of(z, chips)
    turn = lambda v, d: rotate_heads(v.reshape(-1, nh, HD), places, d).reshape(-1, HC)
    q = turn(projected[:, :HC], 1.0).astype(BF)
    k = turn(projected[:, HC : 2 * HC], 1.0).astype(BF)
    kv = jnp.concatenate([k, projected[:, 2 * HC :].astype(BF)], axis=1)
    prompt_kv = lax.all_gather(kv[: 4 * PSH].reshape(2, 2 * PSH, 2 * HC), "chip", axis=0)
    cont_valid = lax.all_gather(valid[2 * PSH :], "core", axis=0, tiled=True)
    masks = masks_of(z, chips, cont_valid)
    chosen = prompt_of[0]
    attended, lse = g_attention(q, prompt_kv, kv, chosen, masks)
    hidden_pre = dot(second_in, w_up, (1, 0)) + b_up
    activated = jax.nn.gelu(hidden_pre, approximate=False).astype(BF)
    partial = dot(attended, w_out, (1, 0)) + dot(activated, w_down, (1, 0))
    halves = split_rows(partial)
    take = lambda a: lax.dynamic_index_in_dim(a, c, axis=0, keepdims=False)
    give = lambda a: lax.dynamic_index_in_dim(a, 1 - c, axis=0, keepdims=False)
    output = tokens.astype(F32) + take(halves) + swap_cores(give(halves)) + b_out + b_down
    live = (valid > 0).astype(F32)[:, None]
    missed = output - teacher.astype(F32)
    count_all, squared_all = lax.psum((jnp.sum(live), jnp.sum(live * missed * missed)), ALL)
    loss_value = squared_all / (count_all * D)
    out_grad = cotangent.astype(F32) + 2.0 / (count_all * D) * live * missed
    out_low = pair_rows(out_grad.astype(BF))
    if stop == "fwd":
        return output, out_grad, out_low, attended, lse, activated, q, kv, first_in, second_in
    out_bias_grad = jnp.sum(out_grad.astype(BF).astype(F32), axis=0)
    dw_out = dot(attended, out_low, (0, 0))
    dw_down = dot(activated, out_low, (0, 0))
    att_grad = dot(out_low, w_out, (1, 1)).astype(BF)
    hidden_grad = (dot(out_low, w_down, (1, 1)) * gelu_slope(hidden_pre)).astype(BF)
    dw_up = dot(second_in, hidden_grad, (0, 0))
    db_up = jnp.sum(hidden_grad.astype(F32), axis=0)
    second_grad = dot(hidden_grad, w_up, (1, 1))
    dq, pair, near = g_attention_back(q, prompt_kv, kv, att_grad, lse, chosen, masks)
    own_pair = lax.psum_scatter(pair.astype(BF), "chip", scatter_dimension=0, tiled=True).astype(F32)
    pair = jnp.concatenate([own_pair, near], axis=0)
    projected_grad = jnp.concatenate([turn(dq, -1.0), turn(pair[:, :HC], -1.0), pair[:, HC:]], axis=1).astype(BF)
    dw_qkv = dot(first_in, projected_grad, (0, 0))
    db_qkv = jnp.sum(projected_grad.astype(F32), axis=0)
    first_grad = dot(projected_grad, w_qkv, (1, 1))
    if stop == "bwd":
        return dw_out, dw_down, dw_up, dw_qkv, second_grad, first_grad, projected_grad, hidden_grad, att_grad
    joint = first_grad * gain1 + second_grad * gain2
    halves = split_rows(joint)
    joint = take(halves) + swap_cores(give(halves))
    own_normed = take(split_rows(normed))
    own_rstd = take(split_rows(rstd))
    input_grad = out_grad + own_rstd * (
        joint
        - jnp.mean(joint, axis=-1, keepdims=True)
        - own_normed * jnp.mean(joint * own_normed, axis=-1, keepdims=True)
    )
    wide = lambda v, n: jnp.zeros((v.shape[0], 2, v.shape[1]), F32).at[:, c].set(v).reshape(-1)
    small = jnp.concatenate(
        [
            jnp.sum(first_grad * normed, axis=0),
            jnp.sum(first_grad, axis=0),
            jnp.sum(second_grad * normed, axis=0),
            jnp.sum(second_grad, axis=0),
            out_bias_grad,
            wide(db_qkv.reshape(3, HC), 3),
            wide(db_up.reshape(-1, rd), 16),
        ]
    )
    small = lax.psum(small, ALL)
    shares, at = [], 0
    for size in (D, D, D, D, D, 3 * D, FF):
        own = size // lax.axis_size(ALL)
        shares.append(lax.dynamic_slice_in_dim(small, at + device * own, own))
        at += size
    rs = lambda v: lax.psum_scatter(v.astype(BF), CHIPS, scatter_dimension=0, tiled=True).astype(F32)
    r = qkv_weight.shape[0]
    s_qkv = rs(dw_qkv).reshape(2, r, 3, HC)
    s_up = rs(dw_up).reshape(2, r, FF // (2 * rd), rd)
    s_down = rs(dw_down)
    pairs = lambda own, other, axis: jnp.where(c == 0, jnp.stack([own, other], axis), jnp.stack([other, own], axis))
    s_qkv = pairs(take(s_qkv), swap_cores(give(s_qkv)), 2).reshape(r, 3 * D)
    s_up = pairs(take(s_up), swap_cores(give(s_up)), 2).reshape(r, FF)
    o = dw_out.reshape(H // 2, -1, 2, r, D)
    o_own = lax.dynamic_index_in_dim(o, c, axis=2, keepdims=False)
    o_other = swap_cores(lax.dynamic_index_in_dim(o, 1 - c, axis=2, keepdims=False))
    s_out = rs(pairs(o_own, o_other, 0).reshape(-1, D))
    return (
        output.astype(BF), loss_value, input_grad, shares[0], shares[1], shares[2], shares[3],
        s_qkv, shares[5], s_out, shares[4], s_up, shares[6], s_down, shares[4],
    )


MESH_ID = pl.DeviceIdType.MESH
RANKS = 4


class Net:
    def __init__(self, send, recv):
        self.g, self.z, self.c = (lax.axis_index(a) for a in ALL)
        self.y, self.x = self.g // 2, self.g % 2
        self.send, self.recv, self.used = send, recv, 0
        self.chip = self.g * RANKS + self.z
        self.core = {"grp": self.g, "chip": self.z, "core": 1 - self.c}
        self.right = {"grp": self.y * 2 + 1 - self.x, "chip": self.z, "core": self.c}
        self.up = {"grp": (1 - self.y) * 2 + self.x, "chip": self.z, "core": self.c}
        self.line = [{"grp": self.g, "chip": (self.z + j) % RANKS, "core": self.c} for j in (1, 2, 3)]
        self.sent = []

    def enter(self):
        barrier = pltpu.get_barrier_semaphore()
        for peer in [self.core, self.right, self.up] + self.line:
            pl.semaphore_signal(barrier, inc=1, device_id=peer, device_id_type=MESH_ID)
        pl.semaphore_wait(barrier, 6)

    def copy(self, src, dst, peer):
        i = self.used
        self.used += 1
        made = pltpu.make_async_remote_copy(
            src_ref=src, dst_ref=dst, send_sem=self.send.at[i], recv_sem=self.recv.at[i],
            device_id=peer, device_id_type=MESH_ID,
        )
        made.start()
        self.sent.append(made)
        return made

    def same(self, view, peer):
        return self.copy(view, view, peer)

    def settle(self, made):
        made.wait_recv()
        made.wait_send()
        self.sent = [m for m in self.sent if m is not made]

    def leave(self):
        for made in self.sent:
            made.wait_send()
        self.sent = []


def gather_steps(net, dst, rb, col, width, before):
    a, b, both = pl.ds(col, width // 2), pl.ds(col + width // 2, width // 2), pl.ds(col, width)
    quad = 4 * rb
    held = {}

    def line():
        for made in before:
            made.wait_recv()
        view = dst.at[pl.ds(net.chip * rb, rb), both]
        held[0] = [net.same(view, peer) for peer in net.line]

    def first():
        for made in held[0]:
            made.wait_recv()
        rows = pl.ds(net.g * quad, quad)
        held[1] = [net.same(dst.at[rows, a], net.right), net.same(dst.at[rows, b], net.up)]

    def second():
        for made in held[1]:
            made.wait_recv()
        held[2] = [net.same(dst.at[pl.ds(net.y * 2 * quad, 2 * quad), a], net.up)]
        for y in range(2):
            held[2].append(net.same(dst.at[pl.ds((y * 2 + net.x) * quad, quad), b], net.right))

    def last():
        for made in held[2]:
            made.wait_recv()

    return [line, first, second, last]


def small_steps(net, rows):
    held = {}

    def pair():
        held[0] = [net.same(rows.at[net.chip * 2 + net.c], net.core)]

    def line():
        held[0][0].wait_recv()
        held[1] = [net.same(rows.at[pl.ds(net.chip * 2, 2)], peer) for peer in net.line]

    def first():
        for made in held[1]:
            made.wait_recv()
        held[2] = [net.same(rows.at[pl.ds(net.g * 8, 8)], net.right)]

    def second():
        held[2][0].wait_recv()
        held[3] = [net.same(rows.at[pl.ds(net.y * 16, 16)], net.up)]

    def last():
        held[3][0].wait_recv()

    return [pair, line, first, second, last]


VM = pl.BlockSpec(memory_space=pltpu.VMEM)
PROMPT = RANKS * 2 * PSH
KEYS = 2 * PROMPT + CONT
ROWS = 4 * PSH + CONT


def nt(a, b):
    return lax.dot_general(a, b, (((1,), (1,)), ((), ())), preferred_element_type=F32)


def nn(a, b):
    return lax.dot_general(a, b, (((1,), (0,)), ((), ())), preferred_element_type=F32)


def tn(a, b):
    return lax.dot_general(a, b, (((0,), (0,)), ((), ())), preferred_element_type=F32)


def tile_at(i, size):
    return pl.ds(pl.multiple_of(i * size, size), size)


def move_rows(dst, to, src, at, count, tile=32):
    @pl.loop(0, count // tile)
    def _(i):
        step = pl.multiple_of(i * tile, tile)
        dst[pl.ds(pl.multiple_of(to + step, tile), tile), :] = src[pl.ds(pl.multiple_of(at + step, tile), tile), :]


def spread_row(rows, field, index, owner, lane, size):
    table = rows[:, field, :].astype(BF)
    lanes = lax.broadcasted_iota(jnp.int32, (128, size), 0)
    pick = (lanes == index[lane : lane + 1, :size]).astype(F32).astype(BF)
    wide = nn(table, pick)
    owners = lax.broadcasted_iota(jnp.int32, (rows.shape[0], size), 0)
    return jnp.sum(jnp.where(owners == index[owner : owner + 1, :size], wide, 0.0), axis=0, keepdims=True)


def norm_rows(x):
    x = x.astype(F32)
    center = x - jnp.mean(x, axis=-1, keepdims=True)
    return center * lax.rsqrt(jnp.mean(center * center, axis=-1, keepdims=True) + EPSILON)


def turn(value, table, sign):
    cos, low_sin, high_sin = (table[:, 128 * i : 128 * i + 128] for i in range(3))
    out = []
    for j in range(value.shape[1] // 128):
        v = value[:, 128 * j : 128 * j + 128]
        other = pltpu.roll(v, 120, 1) * low_sin + pltpu.roll(v, 8, 1) * high_sin
        out.append(v * cos + sign * other)
    return out[0] if len(out) == 1 else jnp.concatenate(out, axis=1)


def rotary_table(length):
    half = ROT // 2
    inverse = (10000.0 ** (-np.arange(half, dtype=np.float32) / half)).astype(np.float32)
    angles = (np.arange(length, dtype=np.float32)[:, None] * inverse).astype(np.float64)
    cos, sin = np.cos(angles), np.sin(angles)
    table = np.zeros((length, 3, 2, HD), np.float32)
    table[:, 0] = 1.0
    for head in range(2):
        table[:, 0, head, :half] = cos
        table[:, 0, head, half:ROT] = cos
        table[:, 1, head, :half] = -sin
        table[:, 2, head, half:ROT] = sin
    return table.reshape(length, 384)


def index_table(rd):
    n = np.arange(2048)
    table = np.zeros((2, 16, 2048), np.int32)
    for c in range(2):
        col = np.minimum(n // HC, 2) * D + c * HC + n % HC
        table[c, 0], table[c, 1] = col // 96, col % 96
        unit = n // rd * (2 * rd) + c * rd + n % rd
        table[c, 2], table[c, 3] = unit // rd, unit % rd
        table[c, 4] = n // 32 % 32
        for i in range(4):
            table[c, 8 + i] = n % 32 + 32 * i
    return table


def seen(keys_at, queries_at, shape, length=None):
    keys = lax.broadcasted_iota(jnp.int32, shape, 0) + keys_at
    queries = lax.broadcasted_iota(jnp.int32, shape, 1) + queries_at
    mask = keys <= queries
    return mask if length is None else mask & (keys < length)


def head_lanes(rows):
    return lax.broadcasted_iota(jnp.int32, (rows, 128), 1) < HD


def attend(query, keys, values, masks, head):
    lanes = head_lanes(query.shape[0])
    own = jnp.where(lanes if head == 0 else ~lanes, query.astype(F32) * SCALE, 0.0).astype(BF)
    scores = [nt(k, own) for k in keys]
    scores = [s if m is None else jnp.where(m, s, NEGATIVE) for s, m in zip(scores, masks)]
    top = functools.reduce(jnp.maximum, [jnp.max(s, axis=0, keepdims=True) for s in scores])
    weights = [jnp.exp(s - top) for s in scores]
    total = sum(jnp.sum(w, axis=0, keepdims=True) for w in weights)
    share = 1.0 / total
    out = sum(tn(v, (w * share).astype(BF)) for v, w in zip(values, weights))
    return out[head * HD : head * HD + HD], top + jnp.log(total)


def forward_kernel(
    tokens, small, qkv, out, up, down, rotary, index, teacher, cotangent,
    rows, w_qkv, x_own, first_own, q, kv, lse, dw_out, dw_down, dw_up, att_grad, joint, output, out_grad, value,
    w_out, w_up, w_down, second_in, attended, activated, slope, peer, low, x_all, first_in, spread, swapped, send, recv,
):
    net = Net(send, recv)
    c, z, chip = net.c, net.z, net.chip
    net.enter()
    for p in range(2):
        move_rows(x_all, p * PROMPT + z * 2 * PSH + c * PSH, tokens, p * PSH, PSH)
    move_rows(x_all, 2 * PROMPT + c * HALF, tokens, 2 * PSH, HALF)
    rows[chip * 2 + c] = small[...]
    pieces = [pl.ds(p * PROMPT + z * 2 * PSH + c * PSH, PSH) for p in range(2)]
    smalls = small_steps(net, rows)
    smalls[0]()
    mates = [net.same(x_all.at[piece], net.core) for piece in pieces + [pl.ds(2 * PROMPT + c * HALF, HALF)]]
    half_rows = pl.ds(pl.multiple_of(chip * 64 + c * 32, 32), 32)
    given = pl.ds(0, 32)
    w_qkv[half_rows, :] = qkv[c]
    swapped[given, : 3 * HC] = qkv[1 - c]
    from_core = {}
    from_core["qkv"] = net.copy(swapped.at[given, pl.ds(0, 3 * HC)], w_qkv.at[half_rows], net.core)
    w_up[half_rows, :] = up[c]
    given = pl.ds(32, 32)
    swapped[given, : FF // 2] = up[1 - c]
    from_core["up"] = net.copy(swapped.at[given, pl.ds(0, FF // 2)], w_up.at[half_rows], net.core)
    w_down[pl.ds(pl.multiple_of(chip * 128, 128), 128), :] = down[...]
    spread[pl.ds(pl.multiple_of(chip * 32, 32), 32), :] = out[...]
    none = []
    tasks = [gather_steps(net, w_up, 64, 512 * i, 512, [] if i else [from_core["up"]]) for i in range(4)]
    tasks += [gather_steps(net, w_qkv, 64, 512 * i, 512, [] if i else [from_core["qkv"]]) for i in range(3)]
    tasks += [gather_steps(net, spread, 32, 0, 1024, [])]
    tasks += [gather_steps(net, w_down, 128, 256 * i, 256, []) for i in range(4)]
    clock = [0]

    def advance(until):
        while clock[0] < until:
            for t, steps in enumerate(tasks):
                if (clock[0] - t) % 2 == 0 and 0 <= (clock[0] - t) // 2 < len(steps):
                    steps[(clock[0] - t) // 2]()
            clock[0] += 1

    advance(1)
    smalls[1]()
    advance(2)
    smalls[2]()
    advance(3)
    smalls[3]()
    smalls[4]()
    advance(4)
    own_tokens = [net.same(x_all.at[piece], peer) for peer in net.line for piece in pieces]
    places = index.at[c]
    gain1, bias1, gain2, bias2 = (spread_row(rows, 0, places, 4, 8 + i, D) for i in range(4))
    b_qkv = spread_row(rows, 2, places, 0, 1, 3 * HC)
    b_up = spread_row(rows, 3, places, 2, 3, FF // 2)
    for made in mates:
        made.wait_recv()

    @pl.loop(0, ROWS // 64)
    def _(i):
        prompt = (i // 2) * PROMPT + z * 2 * PSH + (i % 2) * 64
        here = pl.ds(pl.multiple_of(jnp.where(i < 4, prompt, 2 * PROMPT + (i - 4) * 64), 64), 64)
        at = tile_at(i, 64)
        normed = norm_rows(x_all[here, :])
        x_own[at, :] = x_all[here, :]
        low = (normed * gain1 + bias1).astype(BF)
        first_in[here, :] = low
        first_own[at, :] = low
        second_in[at, :] = (normed * gain2 + bias2).astype(BF)

    advance(7)
    for made in own_tokens:
        made.wait_recv()
    relays = []
    for j in (1, 2, 3):
        for p in range(2):
            piece = pl.ds(p * PROMPT + (z + j) % RANKS * 2 * PSH + c * PSH, PSH)
            relays.append(net.same(x_all.at[piece], net.core))
    advance(8)
    for made in relays:
        made.wait_recv()

    @pl.loop(0, 12)
    def _(i):
        row = (i // 2 % 2) * PROMPT + (z + 1 + i // 4) % RANKS * 2 * PSH + (i % 2) * 64
        here = pl.ds(pl.multiple_of(row, 64), 64)
        first_in[here, :] = (norm_rows(x_all[here, :]) * gain1 + bias1).astype(BF)

    def hidden(j):
        cols = slice(256 * j, 256 * j + 256)

        @pl.loop(0, ROWS // 128)
        def _(i):
            at = tile_at(i, 128)
            pre = nn(second_in[at, :], w_up[:, cols]) + b_up[:, cols]
            gate = 0.5 * (1.0 + lax.erf(pre * 0.7071067811865476))
            activated[at, cols] = (pre * gate).astype(BF)
            slope[at, cols] = (gate + pre * jnp.exp(-0.5 * pre * pre) * 0.3989422804014327).astype(slope.dtype)

    advance(9)
    for j in range(0, 4):
        hidden(j)
    advance(10)
    for j in range(4, 6):
        hidden(j)
    advance(11)
    for j in range(6, 8):
        hidden(j)
    advance(12)
    advance(13)

    @pl.loop(0, KEYS // 256)
    def _(i):
        at = tile_at(i, 256)
        here = first_in[at, :]
        place = pl.multiple_of(jnp.where(i < 4, (i % 2) * 256, PROMPT + (i - 4) * 256), 256)
        table = rotary[pl.ds(place, 256), :]
        for j in range(4):
            cols = slice(HC + 256 * j, HC + 256 * j + 256)
            value = nn(here, w_qkv[:, cols]) + b_qkv[:, cols]
            kv[at, 256 * j : 256 * j + 256] = (turn(value, table, 1.0) if j < 2 else value).astype(BF)

    @pl.loop(0, ROWS // 128)
    def _(i):
        prompt = i * PROMPT + z * 2 * PSH
        source = pl.multiple_of(jnp.where(i < 2, prompt, 2 * PROMPT + (i - 2) * 128), 128)
        place = pl.multiple_of(jnp.where(i < 2, z * 2 * PSH, PROMPT + (i - 2) * 128), 128)
        here = first_in[pl.ds(source, 128), :]
        table = rotary[pl.ds(place, 128), :]
        for j in range(2):
            cols = slice(256 * j, 256 * j + 256)
            q[tile_at(i, 128), cols] = turn(nn(here, w_qkv[:, cols]) + b_qkv[:, cols], table, 1.0).astype(BF)

    advance(14)
    length = jnp.sum(jnp.sum(rows[pl.ds(chip * 2, 2), 5:7, :], axis=0), keepdims=True).astype(jnp.int32)
    second = jnp.broadcast_to(small[7:8, :], (PROMPT, 128)) > 0.5

    def attend_pair(pair):
        k_at, v_at = pl.ds(128 * pair, 128), pl.ds(HC + 128 * pair, 128)
        prompts = [(kv[p * PROMPT : (p + 1) * PROMPT, k_at], kv[p * PROMPT : (p + 1) * PROMPT, v_at]) for p in range(2)]

        def put(row, size, key_list, value_list, masks):
            outs = []
            for head in range(2):
                o, stat = attend(q[row : row + size, k_at], key_list, value_list, masks, head)
                outs.append(o)
                lse[2 * pair + head, :, row : row + size] = stat
            attended[row : row + size, k_at] = jnp.concatenate(outs, axis=0).T.astype(BF)

        for p in range(2):
            put(p * 128, 128, [prompts[p][0]], [prompts[p][1]], [seen(0, z * 2 * PSH, (PROMPT, 128))])
        chosen = [jnp.where(second, b.astype(F32), a.astype(F32)).astype(BF) for a, b in zip(*prompts)]
        for i in range(CONT // 128):
            near = 128 * i + 128
            put(
                256 + 128 * i, 128,
                [chosen[0], kv[2 * PROMPT : 2 * PROMPT + near, k_at]],
                [chosen[1], kv[2 * PROMPT : 2 * PROMPT + near, v_at]],
                [None, seen(0, 128 * i, (near, 128), length)],
            )

    attend_pair(0)
    advance(15)
    attend_pair(1)
    advance(16)
    attend_pair(2)
    advance(17)
    attend_pair(3)
    given = pl.ds(pl.multiple_of((1 - c) * 256, 256), 256)
    swap = net.copy(spread.at[given], swapped.at[pl.ds(64, 256), pl.ds(0, D)], net.core)
    advance(20)
    swap.wait_recv()
    for h in range(8):
        w_out[pl.ds(pl.multiple_of(h * 64 + c * 32, 32), 32), :] = spread[pl.ds(pl.multiple_of(c * 256 + h * 32, 32), 32), :]
        w_out[pl.ds(pl.multiple_of(h * 64 + (1 - c) * 32, 32), 32), :] = swapped[64 + h * 32 : 96 + h * 32, :D]

    def share(at, size):
        here = pl.ds(pl.multiple_of(at, 128), size)
        joint[here, :] = nn(attended[here, :], w_out[...]) + nn(activated[here, :], w_down[...])

    def chip_range(i, owner):
        return ((owner * PSH, PSH, 0), (2 * PSH + owner * PSH, PSH, PSH), (4 * PSH + owner * HALF, HALF, 2 * PSH))[i]

    def pass_share(i):
        at, size, to = chip_range(i, 1 - c)
        return net.copy(joint.at[pl.ds(pl.multiple_of(at, 64), size)], peer.at[pl.ds(to, size)], net.core)

    share(4 * PSH + (1 - c) * HALF, HALF)
    passed = [pass_share(2)]
    share(0, 256)
    passed += [pass_share(0), pass_share(1)]
    share(4 * PSH + c * HALF, HALF)
    for made in passed:
        net.settle(made)
    count = jnp.sum(jnp.sum(rows[:, 4:7, :], axis=0), keepdims=True)
    pull = 2.0 / (count * D)
    bias = spread_row(rows, 1, places, 4, 8, D) + spread_row(rows, 1, places, 4, 9, D)
    value[...] = jnp.zeros_like(value)
    squared, low_sum = jnp.zeros((1, D), F32), jnp.zeros((1, D), F32)
    lows = []
    for i in range(3):
        at, size, to = chip_range(i, c)

        def rows_out(k, sums, at=at, to=to, i=i):
            here = pl.ds(pl.multiple_of(at + k * 64, 64), 64)
            own = pl.ds(pl.multiple_of(to + k * 64, 64), 64)
            result = tokens[own, :].astype(F32) + joint[here, :] + peer[own, :] + bias
            missed = result - teacher[own, :].astype(F32)
            if i == 2:
                step = lax.broadcasted_iota(jnp.int32, (64, D), 0) + (c * HALF + k * 64)
                missed = jnp.where(step < length, missed, 0.0)
            output[own, :] = result.astype(BF)
            grad = cotangent[own, :].astype(F32) + pull * missed
            out_grad[own, :] = grad
            rounded = grad.astype(BF)
            low[here, :] = rounded
            return (
                sums[0] + jnp.sum(missed * missed, axis=0, keepdims=True),
                sums[1] + jnp.sum(rounded.astype(F32), axis=0, keepdims=True),
            )

        squared, low_sum = lax.fori_loop(0, size // 64, rows_out, (squared, low_sum))
        lows.append(net.same(low.at[pl.ds(pl.multiple_of(at, 64), size)], net.core))
    total = jnp.sum(squared, keepdims=True)
    value[96:97, :] = jnp.broadcast_to(total, (1, 128))

    def put_row(row, vector):
        for k in range(vector.shape[1] // 128):
            value[row + k : row + k + 1, :] = vector[:, 128 * k : 128 * k + 128]

    put_row(32, low_sum)
    for made in lows:
        made.wait_recv()

    @pl.loop(0, 8)
    def _(i):
        at = tile_at(i, 256)
        dw_down[at, :] = tn(activated[:, at], low[...]).astype(BF)

    @pl.loop(0, 2)
    def _(i):
        at = tile_at(i, 256)
        dw_out[at, :] = tn(attended[:, at], low[...]).astype(BF)

    @pl.loop(0, ROWS // 128)
    def _(i):
        at = tile_at(i, 128)
        att_grad[at, :] = nt(low[at, :], w_out[...]).astype(BF)

    for j in range(8):
        cols = slice(256 * j, 256 * j + 256)

        def hidden_rows(i, total, cols=cols):
            at = tile_at(i, 256)
            grad = (nt(low[at, :], w_down[cols, :]) * slope[at, cols].astype(F32)).astype(BF)
            activated[at, cols] = grad
            return total + jnp.sum(grad.astype(F32), axis=0, keepdims=True)

        total = lax.fori_loop(0, ROWS // 256, hidden_rows, jnp.zeros((1, 256), F32))
        for k in range(2):
            value[pl.ds(64 + 4 * j + 2 * k + c, 1), :] = total[:, 128 * k : 128 * k + 128]

    @pl.loop(0, 4)
    def _(i):
        at = tile_at(i, 256)
        for k in range(2):
            cols = slice(1024 * k, 1024 * k + 1024)
            dw_up[at, cols] = tn(second_in[:, at], activated[:, cols]).astype(BF)

    def second_rows(i, sums):
        at = tile_at(i, 128)
        grad = nt(activated[at, :], w_up[...])
        joint[at, :] = grad * gain2
        normed = norm_rows(x_own[at, :])
        return (
            sums[0] + jnp.sum(grad * normed, axis=0, keepdims=True),
            sums[1] + jnp.sum(grad, axis=0, keepdims=True),
        )

    sums = lax.fori_loop(0, ROWS // 128, second_rows, (jnp.zeros((1, D), F32), jnp.zeros((1, D), F32)))
    put_row(16, sums[0])
    put_row(24, sums[1])
    net.leave()


def forward(tokens, small, qkv, out, up, down, teacher, cotangent):
    shape = jax.ShapeDtypeStruct
    return pl.pallas_call(
        forward_kernel,
        out_shape=(
            shape((32, 8, 128), F32), shape((D, 3 * HC), BF), shape((ROWS, D), BF), shape((ROWS, D), BF), shape((ROWS, HC), BF),
            shape((KEYS, 2 * HC), BF), shape((8, 1, ROWS), F32), shape((HC, D), BF), shape((FF // 2, D), BF), shape((D, FF // 2), BF),
            shape((ROWS, HC), BF), shape((ROWS, D), F32), shape((384, D), BF), shape((384, D), F32), shape((104, 128), F32),
        ),
        in_specs=[VM] * 10,
        out_specs=(VM,) * 15,
        scratch_shapes=[
            pltpu.VMEM((HC, D), BF), pltpu.VMEM((D, FF // 2), BF), pltpu.VMEM((FF // 2, D), BF), pltpu.VMEM((ROWS, D), BF),
            pltpu.VMEM((ROWS, HC), BF), pltpu.VMEM((ROWS, FF // 2), BF), pltpu.VMEM((ROWS, FF // 2), BF), pltpu.VMEM((384, D), F32),
            pltpu.VMEM((ROWS, D), BF), pltpu.VMEM((KEYS, D), BF), pltpu.VMEM((KEYS, D), BF), pltpu.VMEM((HC, D), BF),
            pltpu.VMEM((320, FF // 2), BF), pltpu.SemaphoreType.DMA((140,)), pltpu.SemaphoreType.DMA((140,)),
        ],
        compiler_params=pltpu.CompilerParams(collective_id=0, has_side_effects=True, vmem_limit_bytes=63 << 20),
    )(tokens, small, qkv, out, up, down, jnp.asarray(rotary_table(PROMPT + CONT)), jnp.asarray(index_table(128)), teacher, cotangent)


def add_rows(dst, dst_rows, src, src_rows, count, cols, tile):
    @pl.loop(0, count // tile)
    def _(i):
        to = pl.ds(pl.multiple_of(dst_rows + i * tile, tile), tile)
        more = src[pl.ds(pl.multiple_of(src_rows + i * tile, tile), tile), cols].astype(F32)
        dst[to, :] = (dst[to, :].astype(F32) + more).astype(dst.dtype)


def scatter_steps(net, src, rb, col, width, before, got_a, got_b, got_z, put):
    half = width // 2
    a, b, both = pl.ds(col, half), pl.ds(col + half, half), pl.ds(col, width)
    quad = 4 * rb
    tile = min(64, rb)
    at = lambda y, x: pl.ds((y * 2 + x) * quad, quad)
    held = {}

    def first():
        for made in before:
            made.wait()
        rows = pl.ds((1 - net.y) * 2 * quad, 2 * quad)
        held[0] = [net.copy(src.at[rows, a], got_a.at[pl.ds(0, 2 * quad)], net.up)]
        for y in range(2):
            held[0].append(net.copy(src.at[at(y, 1 - net.x), b], got_b.at[pl.ds(y * quad, quad)], net.right))

    def second():
        for made in held[0]:
            made.wait_recv()
        add_rows(got_a, (1 - net.x) * quad, src, (net.y * 2 + 1 - net.x) * quad, quad, a, tile)
        add_rows(got_b, (1 - net.y) * quad, src, ((1 - net.y) * 2 + net.x) * quad, quad, b, tile)
        held[1] = [
            net.copy(got_a.at[pl.ds((1 - net.x) * quad, quad)], got_a.at[pl.ds(2 * quad, quad)], net.right),
            net.copy(got_b.at[pl.ds((1 - net.y) * quad, quad)], got_b.at[pl.ds(2 * quad, quad)], net.up),
        ]
        add_rows(got_a, net.x * quad, src, (net.y * 2 + net.x) * quad, quad, a, tile)
        add_rows(got_b, net.y * quad, src, (net.y * 2 + net.x) * quad, quad, b, tile)

    def third():
        for made in held[1]:
            made.wait_recv()
        add_rows(got_a, net.x * quad, got_a, 2 * quad, quad, slice(None), tile)
        add_rows(got_b, net.y * quad, got_b, 2 * quad, quad, slice(None), tile)
        held[2] = []
        for j in (1, 2, 3):
            there = (net.z + j) % RANKS * rb
            peer = net.line[j - 1]
            held[2].append(net.copy(got_a.at[pl.ds(net.x * quad + there, rb)], got_z.at[j - 1, :, pl.ds(0, half)], peer))
            held[2].append(net.copy(got_b.at[pl.ds(net.y * quad + there, rb)], got_z.at[j - 1, :, pl.ds(half, half)], peer))

    def last():
        for made in held[2]:
            made.wait_recv()
        for k, (got, way) in enumerate(((got_a, net.x), (got_b, net.y))):
            cols = slice(k * half, k * half + half)

            @pl.loop(0, rb // tile)
            def _(i):
                rows = pl.ds(pl.multiple_of(way * quad + net.z * rb + i * tile, tile), tile)
                value = got[rows, :].astype(F32)
                for j in range(3):
                    value = value + got_z[j, tile_at(i, tile), cols].astype(F32)
                put(tile_at(i, tile), slice(col + k * half, col + k * half + half), value)

    return [first, second, third, last]


def sum_steps(net, value, got):
    held = {}
    peers = [net.core, net.right, net.up]

    def make(i):
        def step():
            if i > 0:
                net.settle(held[i - 1])
                value[...] = value[...] + got[i - 1]
            if i < 3:
                held[i] = net.copy(value, got.at[i], peers[i])
            else:
                held[3] = [net.copy(value, got.at[3 + net.z], peer) for peer in net.line]
                got[3 + net.z] = value[...]

        return step

    def last():
        for made in held[3]:
            net.settle(made)
        value[...] = (got[3] + got[4]) + (got[5] + got[6])

    return [make(i) for i in range(4)] + [last]


def attend_back(query, grad, keys, values, masks, stat, head):
    lanes = head_lanes(query.shape[0])
    lanes = lanes if head == 0 else ~lanes
    own = jnp.where(lanes, query.astype(F32) * SCALE, 0.0).astype(BF)
    own_grad = jnp.where(lanes, grad.astype(F32), 0.0).astype(BF)
    inner, kept = 0.0, []
    for k, v, m in zip(keys, values, masks):
        scores = nt(k, own)
        probs = jnp.exp((scores if m is None else jnp.where(m, scores, NEGATIVE)) - stat)
        prob_grad = nt(v, own_grad)
        inner = inner + jnp.sum(probs * prob_grad, axis=0, keepdims=True)
        kept.append((probs, prob_grad))
    dq, dks, dvs = 0.0, [], []
    for k, (probs, prob_grad) in zip(keys, kept):
        score_grad = (probs * (prob_grad - inner)).astype(BF)
        dq = dq + tn(k, score_grad)
        dks.append(nn(score_grad, own))
        dvs.append(nn(probs.astype(BF), own_grad))
    return dq[head * HD : head * HD + HD] * SCALE, dks, dvs


def backward_kernel(
    rows, small, value_in, gain, rotary, q, kv, att_grad, lse, first, x, w_qkv, joint_in, dw_out_in, dw_down_in, dw_up_in,
    value, o_qkv, o_out, o_up, o_down, joint_own,
    dw_qkv, dw_out, dw_down, dw_up, spread, pairs, got_pairs, far_k, far_v, projected, joint, peer_joint,
    got_s, s_qkv, s_up, peer_qkv, peer_up, *rest,
):
    bufs, (send, recv, local) = rest[:-3], rest[-3:]
    net = Net(send, recv)
    c, z, chip = net.c, net.z, net.chip
    loads = [pltpu.make_async_copy(src, dst, local.at[i]) for i, (src, dst) in enumerate(
        ((dw_down_in, dw_down), (dw_up_in, dw_up), (dw_out_in, dw_out)))]
    for load in loads:
        load.start()
    value[...] = value_in[...]
    net.enter()
    bufs = list(bufs)
    take3 = lambda: [bufs.pop(0) for _ in range(3)]

    def put_into(ref):
        def put(at, cols, total):
            ref[at, cols] = total

        return put

    clock, tasks = [0], []

    def advance(until):
        while clock[0] < until:
            for t, steps in tasks:
                if (clock[0] - t) % 2 == 0 and 0 <= (clock[0] - t) // 2 < len(steps):
                    steps[(clock[0] - t) // 2]()
            clock[0] += 1

    loads[0].wait()
    tasks.append((0, scatter_steps(net, dw_down, 128, 0, 512, [], *take3(), put_into(o_down))))
    tasks.append((1, scatter_steps(net, dw_down, 128, 512, 512, [], *take3(), put_into(o_down))))
    tasks.append((2, scatter_steps(net, dw_up, 64, 0, 1024, [loads[1]], *take3(), put_into(s_up))))
    tasks.append((3, scatter_steps(net, dw_up, 64, 1024, 1024, [], *take3(), put_into(s_up))))
    advance(2)
    loads[2].wait()
    swaps = []
    for h in range(8):
        theirs = dw_out.at[pl.ds(h * 64 + (1 - c) * 32, 32)]
        swaps.append(net.copy(theirs, spread.at[pl.ds((8 * c + h) * 32, 32)], net.core))
        spread[pl.ds(pl.multiple_of((8 * c + h) * 32, 32), 32), :] = dw_out[pl.ds(pl.multiple_of(h * 64 + c * 32, 32), 32), :]
    tasks.append((4, scatter_steps(net, spread, 32, 0, 1024, [], *take3(), put_into(o_out))))

    length = jnp.sum(jnp.sum(rows[pl.ds(chip * 2, 2), 5:7, :], axis=0), keepdims=True).astype(jnp.int32)
    second = jnp.broadcast_to(small[7:8, :], (PROMPT, 128)) > 0.5
    weight = small[7:8, :]
    pair_sends = []

    def back_pair(pair):
        k_at, v_at = pl.ds(128 * pair, 128), pl.ds(HC + 128 * pair, 128)
        prompts = [(kv[p * PROMPT : (p + 1) * PROMPT, k_at], kv[p * PROMPT : (p + 1) * PROMPT, v_at]) for p in range(2)]
        chosen = [jnp.where(second, b.astype(F32), a.astype(F32)).astype(BF) for a, b in zip(*prompts)]

        def both_heads(row, size, keys, values, masks, place):
            dq, dks, dvs = [], None, None
            for head in range(2):
                stat = lse[2 * pair + head, :, row : row + size]
                d, k_parts, v_parts = attend_back(
                    q[row : row + size, k_at], att_grad[row : row + size, k_at], keys, values, masks, stat, head
                )
                dq.append(d)
                dks = k_parts if dks is None else [a + b for a, b in zip(dks, k_parts)]
                dvs = v_parts if dvs is None else [a + b for a, b in zip(dvs, v_parts)]
            dq = jnp.concatenate(dq, axis=0).T
            projected[row : row + size, k_at] = turn(dq, rotary[pl.ds(place, size), :], -1.0).astype(BF)
            return dks, dvs

        near_k, near_v = None, None
        for i in range(2):
            near = 256 * i + 256
            masks = [None, seen(0, 256 * i, (near, 256), length)]
            near_keys = kv[2 * PROMPT : 2 * PROMPT + near, k_at], kv[2 * PROMPT : 2 * PROMPT + near, v_at]
            dks, dvs = both_heads(
                256 + 256 * i, 256, [chosen[0], near_keys[0]], [chosen[1], near_keys[1]], masks, PROMPT + 256 * i
            )
            if i == 0:
                far_k[...], far_v[...] = dks[0], dvs[0]
                near_k, near_v = dks[1], dvs[1]
            else:
                far_k[...] = far_k[...] + dks[0]
                far_v[...] = far_v[...] + dvs[0]
                near_k = [near_k + dks[1][:256], dks[1][256:]]
                near_v = [near_v + dvs[1][:256], dvs[1][256:]]
        for i in range(2):
            at = slice(256 + 256 * i, 512 + 256 * i)
            table = rotary[PROMPT + 256 * i : PROMPT + 256 * i + 256, :]
            projected[at, HC + 128 * pair : HC + 128 * pair + 128] = turn(near_k[i], table, -1.0).astype(BF)
            projected[at, 2 * HC + 128 * pair : 2 * HC + 128 * pair + 128] = near_v[i].astype(BF)
        for p in range(2):
            place = pl.multiple_of(z * 2 * PSH, 128)
            dks, dvs = both_heads(
                128 * p, 128, [prompts[p][0]], [prompts[p][1]], [seen(0, z * 2 * PSH, (PROMPT, 128))], place
            )
            share = weight if p == 1 else 1.0 - weight
            at = slice(p * PROMPT, p * PROMPT + PROMPT)
            pairs[pair, at, :128] = (dks[0] + share * far_k[...]).astype(BF)
            pairs[pair, at, 128:] = (dvs[0] + share * far_v[...]).astype(BF)
        for j in (1, 2, 3):
            for p in range(2):
                there = pl.ds(p * PROMPT + (z + j) % RANKS * 2 * PSH, 2 * PSH)
                pair_sends.append(
                    net.copy(pairs.at[pair, there], got_pairs.at[j - 1, pair, pl.ds(p * 2 * PSH, 2 * PSH)], net.line[j - 1])
                )

    back_pair(0)
    advance(3)
    back_pair(1)
    advance(4)
    for made in swaps:
        made.wait_recv()
    back_pair(2)
    advance(5)
    back_pair(3)
    advance(6)
    for made in pair_sends:
        made.wait_recv()
    table = rotary[pl.ds(pl.multiple_of(z * 2 * PSH, 128), 128), :]
    for pair in range(4):
        for p in range(2):
            at = slice(p * 128, p * 128 + 128)
            total = pairs[pair, pl.ds(pl.multiple_of(p * PROMPT + z * 2 * PSH, 128), 128), :].astype(F32)
            for j in range(3):
                total = total + got_pairs[j, pair, at, :].astype(F32)
            projected[at, HC + 128 * pair : HC + 128 * pair + 128] = turn(total[:, :128], table, -1.0).astype(BF)
            projected[at, 2 * HC + 128 * pair : 2 * HC + 128 * pair + 128] = total[:, 128:].astype(BF)

    def weight_columns(col, width):
        @pl.loop(0, D // 256)
        def _(i):
            part = tn(first[:, tile_at(i, 256)], projected[:, col : col + width])
            dw_qkv[tile_at(i, 256), col : col + width] = part.astype(BF)

    weight_columns(0, 768)
    tasks.append((6, scatter_steps(net, dw_qkv, 64, 0, 768, [], *take3(), put_into(s_qkv))))
    advance(7)
    weight_columns(768, 768)
    tasks.append((7, scatter_steps(net, dw_qkv, 64, 768, 768, [], *take3(), put_into(s_qkv))))
    advance(8)
    fg_sum, fg_normed = jnp.zeros((1, D), F32), jnp.zeros((1, D), F32)
    bias = jnp.zeros((1, 3 * HC), F32)

    def first_rows(i, sums):
        at = tile_at(i, 128)
        here = projected[at, :]
        grad = nt(here, w_qkv[...])
        normed = norm_rows(x[at, :])
        joint[at, :] = grad * gain[...] + joint_in[at, :]
        return (
            sums[0] + jnp.sum(grad, axis=0, keepdims=True),
            sums[1] + jnp.sum(grad * normed, axis=0, keepdims=True),
            sums[2] + jnp.sum(here.astype(F32), axis=0, keepdims=True),
        )

    fg_sum, fg_normed, bias = lax.fori_loop(0, ROWS // 128, first_rows, (fg_sum, fg_normed, bias))
    ranges = ((0, PSH, lambda o: o * PSH), (PSH, PSH, lambda o: 2 * PSH + o * PSH), (2 * PSH, HALF, lambda o: 4 * PSH + o * HALF))
    joints = [
        net.copy(joint.at[pl.ds(there(1 - c), size)], peer_joint.at[pl.ds(at, size)], net.core) for at, size, there in ranges
    ]
    for i in range(8):
        cols = slice(128 * i, 128 * i + 128)
        value[i : i + 1, :] = value[i : i + 1, :] + fg_normed[:, cols]
        value[8 + i : 9 + i, :] = value[8 + i : 9 + i, :] + fg_sum[:, cols]
    for i in range(12):
        row = pl.ds(40 + i // 4 * 8 + c * 4 + i % 4, 1)
        value[row, :] = value[row, :] + bias[:, 128 * i : 128 * i + 128]
    sums = sum_steps(net, value, got_s)
    sums[0]()
    advance(9)
    for made in joints:
        made.wait_recv()
    for at, size, there in ranges:
        mine = pl.ds(pl.multiple_of(there(c), 64), size)
        joint_own[at : at + size, :] = joint[mine, :] + peer_joint[at : at + size, :]
    sums[1]()
    advance(10)
    sums[2]()
    ups = []

    def give(total, peer_ref):
        return net.copy(total.at[pl.ds((1 - c) * 32, 32)], peer_ref, net.core)

    advance(11)
    ups.append(give(s_up, peer_up))
    sums[3]()
    advance(12)
    sums[4]()
    advance(16)
    ups.append(give(s_qkv, peer_qkv))
    own_rows = pl.ds(pl.multiple_of(c * 32, 32), 32)
    ups[0].wait_recv()
    for i in range(16):
        for who, part in ((c, s_up[own_rows, 128 * i : 128 * i + 128]), (1 - c, peer_up[:, 128 * i : 128 * i + 128])):
            o_up[:, pl.ds(pl.multiple_of((2 * i + who) * 128, 128), 128)] = part
    ups[1].wait_recv()
    for i in range(3):
        for who, part in ((c, s_qkv[own_rows, HC * i : HC * i + HC]), (1 - c, peer_qkv[:, HC * i : HC * i + HC])):
            o_qkv[:, pl.ds(pl.multiple_of(i * D + who * HC, 128), HC)] = part
    net.leave()


def backward(*args):
    shape = jax.ShapeDtypeStruct
    bufs = []
    for rb, width, count in ((128, 512, 2), (64, 1024, 2), (32, 1024, 1), (64, 768, 2)):
        for _ in range(count):
            bufs += [pltpu.VMEM((12 * rb, width // 2), BF), pltpu.VMEM((12 * rb, width // 2), BF), pltpu.VMEM((3, rb, width), BF)]
    return pl.pallas_call(
        backward_kernel,
        out_shape=(
            shape((104, 128), F32), shape((32, 3 * D), F32), shape((32, D), F32), shape((32, FF), F32), shape((128, D), F32),
            shape((384, D), F32),
        ),
        in_specs=[VM] * 13 + [pl.BlockSpec(memory_space=pl.ANY)] * 3,
        out_specs=(VM,) * 6,
        scratch_shapes=[
            pltpu.VMEM((D, 3 * HC), BF), pltpu.VMEM((HC, D), BF), pltpu.VMEM((FF // 2, D), BF), pltpu.VMEM((D, FF // 2), BF),
            pltpu.VMEM((HC, D), BF), pltpu.VMEM((4, 2 * PROMPT, 256), BF), pltpu.VMEM((3, 4, 4 * PSH, 256), BF),
            pltpu.VMEM((PROMPT, 128), F32), pltpu.VMEM((PROMPT, 128), F32), pltpu.VMEM((ROWS, 3 * HC), BF),
            pltpu.VMEM((ROWS, D), F32), pltpu.VMEM((384, D), F32), pltpu.VMEM((7, 104, 128), F32),
            pltpu.VMEM((64, 3 * HC), F32), pltpu.VMEM((64, FF // 2), F32), pltpu.VMEM((32, 3 * HC), F32), pltpu.VMEM((32, FF // 2), F32),
        ] + bufs
        + [pltpu.SemaphoreType.DMA((140,)), pltpu.SemaphoreType.DMA((140,)), pltpu.SemaphoreType.DMA((4,))],
        compiler_params=pltpu.CompilerParams(collective_id=1, has_side_effects=True, vmem_limit_bytes=63 << 20),
    )(*args)


def fast_body(
    tokens, valid, prompt_of, teacher, cotangent,
    ln1_gain, ln1_bias, ln2_gain, ln2_bias, qkv_weight, qkv_bias, out_weight, out_bias,
    up_weight, up_bias, down_weight, down_bias,
):
    c = lax.axis_index("core")
    z = lax.axis_index("chip")
    chips = lax.axis_size("chip")
    nh = HC // HD
    rd = down_weight.shape[0]
    device = lax.axis_index(ALL)
    pad = lambda v: jnp.pad(v.astype(F32), (0, 128 - v.shape[0]))[None]
    live_own = (valid > 0).astype(F32)
    small = jnp.concatenate(
        [
            jnp.concatenate([ln1_gain, ln1_bias, ln2_gain, ln2_bias]).astype(F32)[None],
            pad(jnp.concatenate([out_bias, down_bias])),
            pad(qkv_bias),
            pad(up_bias),
            live_own.reshape(3, 128),
            jnp.broadcast_to(prompt_of.astype(F32)[:, None], (1, 128)),
        ]
    )
    rows, w_qkv, x_own, first_own, q, kv, lse, dw_out, dw_down, dw_up, att_grad, joint, output, out_grad, value = forward(
        tokens,
        small,
        qkv_weight.reshape(32, 3, 2, HC).transpose(2, 0, 1, 3).reshape(2, 32, 3 * HC),
        out_weight,
        up_weight.reshape(32, 16, 2, 128).transpose(2, 0, 1, 3).reshape(2, 32, FF // 2),
        down_weight,
        teacher,
        cotangent,
    )
    gain1 = rows[:, 0, :32].reshape(-1)
    count_all = jnp.sum(rows[:, 4:7])
    value, s_qkv, s_out, s_up, s_down, joint = backward(
        rows, small, value, gain1[None], jnp.asarray(rotary_table(PROMPT + CONT)), q, kv, att_grad, lse, first_own, x_own,
        w_qkv, joint, dw_out, dw_down, dw_up,
    )
    own_normed, own_rstd = normalize(tokens.astype(F32))
    input_grad = out_grad + own_rstd * (
        joint
        - jnp.mean(joint, axis=-1, keepdims=True)
        - own_normed * jnp.mean(joint * own_normed, axis=-1, keepdims=True)
    )
    value = value.reshape(-1)
    shares, at = [], 0
    for size in (D, D, D, D, D, 3 * D, FF):
        own = size // lax.axis_size(ALL)
        shares.append(lax.dynamic_slice_in_dim(value, at + device * own, own))
        at += size
    loss_value = value[at] / (count_all * D)
    return (
        output, loss_value, input_grad, shares[0], shares[1], shares[2], shares[3],
        s_qkv, shares[5], s_out, shares[4], s_up, shares[6], s_down, shares[4],
    )


def solution(mesh):
    groups, seats = mesh.shape["grp"], mesh.shape["seq"]
    fine = Mesh(mesh.devices.reshape(groups, seats // 2, 2), ALL)
    rows, row = P(ALL, None), P(ALL)
    in_specs = (rows, row, row, rows, rows) + (row,) * 4 + (rows, row) * 4
    out_specs = (rows, P(), rows) + (row,) * 4 + (rows, row) * 4
    return jax.shard_map(fast_body if (groups, seats) == (4, 8) else generic_body, mesh=fine, in_specs=in_specs, out_specs=out_specs, check_vma=False)
```

```python
import functools

import jax
import jax.numpy as jnp
import numpy as np
from jax import lax
from jax.experimental import pallas as pl
from jax.experimental.pallas import tpu as pltpu
from jax.sharding import Mesh
from jax.sharding import PartitionSpec as P

D = 1024
H = 16
HD = 64
ROT = 16
FF = 4096
PSH = 64
CONT = 512
HALF = CONT // 2
HC = H // 2 * HD
EPSILON = 1e-05
NEGATIVE = -1e30
SCALE = 0.125
BF = jnp.bfloat16
F32 = jnp.float32
ALL = ("grp", "chip", "core")
CHIPS = ("grp", "chip")


def swap_cores(x):
    return lax.ppermute(x, "core", [(0, 1), (1, 0)])


def pair_rows(own):
    both = lax.all_gather(own, "core", axis=0)
    prompts = both[:, : 2 * PSH].reshape((2, 2, PSH) + own.shape[1:])
    prompts = prompts.swapaxes(0, 1).reshape((4 * PSH,) + own.shape[1:])
    return jnp.concatenate([prompts, both[:, 2 * PSH :].reshape((CONT,) + own.shape[1:])], axis=0)


def split_rows(rows):
    prompts = rows[: 4 * PSH].reshape((2, 2, PSH) + rows.shape[1:]).swapaxes(0, 1)
    prompts = prompts.reshape((2, 2 * PSH) + rows.shape[1:])
    return jnp.concatenate([prompts, rows[4 * PSH :].reshape((2, HALF) + rows.shape[1:])], axis=1)


def normalize(values):
    center = values - jnp.mean(values, axis=-1, keepdims=True)
    inverse_dev = lax.rsqrt(jnp.mean(center * center, axis=-1, keepdims=True) + EPSILON)
    return (center * inverse_dev, inverse_dev)


def rotate_heads(values, places, direction):
    halfrot = ROT // 2
    inverse = 10000.0 ** (-jnp.arange(halfrot, dtype=F32) / halfrot)
    angles = places.astype(F32)[..., None] * inverse
    cosine = jnp.cos(angles)[..., None, :]
    sine_part = direction * jnp.sin(angles)[..., None, :]
    leading = values[..., :halfrot]
    trailing = values[..., halfrot:ROT]
    return jnp.concatenate(
        [
            leading * cosine - trailing * sine_part,
            trailing * cosine + leading * sine_part,
            values[..., ROT:],
        ],
        axis=-1,
    )


def gelu_slope(values):
    return (
        0.5 * (1.0 + lax.erf(values * 0.7071067811865476))
        + values * jnp.exp(-0.5 * values * values) * 0.3989422804014327
    )


def dot(a, b, contract):
    return lax.dot_general(a, b, ((contract[:1], contract[1:]), ((), ())), preferred_element_type=F32)


def g_weights(c, qkv_weight, out_weight, up_weight, down_weight):
    r = qkv_weight.shape[0]
    mine = functools.partial(lax.dynamic_index_in_dim, index=c, keepdims=False)
    both = lambda w: lax.all_gather(w, "core", axis=0, tiled=True)
    qkv = mine(both(qkv_weight).reshape(2 * r, 3, 2, HC), axis=2).reshape(2 * r, 3 * HC)
    qkv = lax.all_gather(qkv, CHIPS, axis=0, tiled=True)
    rd = down_weight.shape[0]
    up = mine(both(up_weight).reshape(2 * r, FF // (2 * rd), 2, rd), axis=2).reshape(2 * r, FF // 2)
    up = lax.all_gather(up, CHIPS, axis=0, tiled=True)
    down = lax.all_gather(down_weight, CHIPS, axis=0, tiled=True)
    out = lax.all_gather(out_weight, ALL, axis=0, tiled=True)
    out = mine(out.reshape(2, HC, D), axis=0)
    return qkv, out, up, down


def g_small(c, rd, ln1_gain, ln1_bias, ln2_gain, ln2_bias, qkv_bias, out_bias, up_bias, down_bias):
    sizes = [v.shape[0] for v in (ln1_gain, ln1_bias, ln2_gain, ln2_bias, out_bias, down_bias, qkv_bias, up_bias)]
    packed = jnp.concatenate([ln1_gain, ln1_bias, ln2_gain, ln2_bias, out_bias, down_bias, qkv_bias, up_bias])
    rows = lax.all_gather(packed, ALL, axis=0)
    parts, at = [], 0
    for size in sizes:
        parts.append(rows[:, at : at + size].reshape(-1).astype(F32))
        at += size
    qb = lax.dynamic_index_in_dim(parts[6].reshape(3, 2, HC), c, axis=1, keepdims=False).reshape(-1)
    ub = lax.dynamic_index_in_dim(parts[7].reshape(-1, 2, rd), c, axis=1, keepdims=False).reshape(-1)
    return parts[:6] + [qb, ub]


def places_of(z, chips):
    prompt = z * 2 * PSH + jnp.arange(2 * PSH)
    return jnp.concatenate([prompt, prompt, chips * 2 * PSH + jnp.arange(CONT)])


def masks_of(z, chips, cont_valid):
    length = chips * 2 * PSH
    prompt = jnp.arange(length)[None, :] <= z * 2 * PSH + jnp.arange(2 * PSH)[:, None]
    own = jnp.arange(CONT)[None, :] <= jnp.arange(CONT)[:, None]
    own = own & (cont_valid > 0)[None, :]
    return prompt, jnp.concatenate([jnp.ones((CONT, length), bool), own], axis=1)


def g_attention(q, prompt_kv, kv, chosen, masks):
    nh = HC // HD
    chips = prompt_kv.shape[0]
    pk = prompt_kv.reshape(chips, 2, 2 * PSH, 2, nh, HD).transpose(3, 4, 1, 0, 2, 5)
    pk = pk.reshape(2, nh, 2, chips * 2 * PSH, HD)
    qh = q.reshape(-1, nh, HD).swapaxes(0, 1)
    pq = qh[:, : 4 * PSH].reshape(nh, 2, 2 * PSH, HD)
    scores = jnp.einsum("hpqd,hpkd->hpqk", pq, pk[0], preferred_element_type=F32) * SCALE
    scores = jnp.where(masks[0], scores, NEGATIVE)
    top = jnp.max(scores, axis=-1, keepdims=True)
    weights = jnp.exp(scores - top)
    total = jnp.sum(weights, axis=-1, keepdims=True)
    p_out = jnp.einsum("hpqk,hpkd->hpqd", (weights / total).astype(BF), pk[1], preferred_element_type=F32)
    p_lse = (top + jnp.log(total))[..., 0].reshape(nh, 4 * PSH)
    far = lax.dynamic_index_in_dim(pk, chosen, axis=2, keepdims=False)
    near = kv[4 * PSH :].reshape(CONT, 2, nh, HD).transpose(1, 2, 0, 3)
    ck = jnp.concatenate([far, near], axis=2)
    cq = qh[:, 4 * PSH :]
    scores = jnp.einsum("hqd,hkd->hqk", cq, ck[0], preferred_element_type=F32) * SCALE
    scores = jnp.where(masks[1], scores, NEGATIVE)
    top = jnp.max(scores, axis=-1, keepdims=True)
    weights = jnp.exp(scores - top)
    total = jnp.sum(weights, axis=-1, keepdims=True)
    c_out = jnp.einsum("hqk,hkd->hqd", (weights / total).astype(BF), ck[1], preferred_element_type=F32)
    c_lse = (top + jnp.log(total))[..., 0]
    att = jnp.concatenate([p_out.reshape(nh, 4 * PSH, HD), c_out], axis=1)
    return att.swapaxes(0, 1).reshape(-1, HC).astype(BF), jnp.concatenate([p_lse, c_lse], axis=1)


def g_attention_back(q, prompt_kv, kv, att_grad, lse, chosen, masks):
    nh = HC // HD
    chips = prompt_kv.shape[0]
    pk = prompt_kv.reshape(chips, 2, 2 * PSH, 2, nh, HD).transpose(3, 4, 1, 0, 2, 5)
    pk = pk.reshape(2, nh, 2, chips * 2 * PSH, HD)
    qh = q.reshape(-1, nh, HD).swapaxes(0, 1)
    gh = att_grad.reshape(-1, nh, HD).swapaxes(0, 1)
    pq = qh[:, : 4 * PSH].reshape(nh, 2, 2 * PSH, HD)
    pg = gh[:, : 4 * PSH].reshape(nh, 2, 2 * PSH, HD)
    ein = functools.partial(jnp.einsum, preferred_element_type=F32)

    def back(eq, ek, query, key, value, grad, mask, lse_rows):
        scores = jnp.where(mask, ein(f"{eq},{ek}->{eq[:-1]}k", query, key) * SCALE, NEGATIVE)
        probs = jnp.exp(scores - lse_rows[..., None])
        prob_grad = ein(f"{eq},{ek}->{eq[:-1]}k", grad, value)
        inner = jnp.sum(probs * prob_grad, axis=-1, keepdims=True)
        score_grad = (probs * (prob_grad - inner)).astype(BF)
        es = eq[:-1] + "k"
        dq = ein(f"{es},{ek}->{eq}", score_grad, key) * SCALE
        dk = ein(f"{es},{eq}->{ek}", score_grad, query) * SCALE
        dv = ein(f"{es},{eq}->{ek}", probs.astype(BF), grad)
        return dq, dk, dv

    dq_p, dk_p, dv_p = back("hpqd", "hpkd", pq, pk[0], pk[1], pg, masks[0], lse[:, : 4 * PSH].reshape(nh, 2, 2 * PSH))
    far = lax.dynamic_index_in_dim(pk, chosen, axis=2, keepdims=False)
    near = kv[4 * PSH :].reshape(CONT, 2, nh, HD).transpose(1, 2, 0, 3)
    ck = jnp.concatenate([far, near], axis=2)
    dq_c, dk_c, dv_c = back("hqd", "hkd", qh[:, 4 * PSH :], ck[0], ck[1], gh[:, 4 * PSH :], masks[1], lse[:, 4 * PSH :])
    length = chips * 2 * PSH
    pick = (jnp.arange(2) == chosen).astype(F32)[None, :, None, None]
    dk_p = dk_p + pick * dk_c[:, None, :length]
    dv_p = dv_p + pick * dv_c[:, None, :length]
    dq = jnp.concatenate([dq_p.reshape(nh, 4 * PSH, HD), dq_c], axis=1).swapaxes(0, 1).reshape(-1, HC)
    pair = jnp.stack([dk_p, dv_p])
    pair = pair.reshape(2, nh, 2, chips, 2 * PSH, HD).transpose(3, 2, 4, 0, 1, 5).reshape(chips * 4 * PSH, 2 * HC)
    near_grad = jnp.stack([dk_c[:, length:], dv_c[:, length:]]).transpose(2, 0, 1, 3).reshape(CONT, 2 * HC)
    return dq, pair, near_grad


def generic_body(
    tokens, valid, prompt_of, teacher, cotangent,
    ln1_gain, ln1_bias, ln2_gain, ln2_bias, qkv_weight, qkv_bias, out_weight, out_bias,
    up_weight, up_bias, down_weight, down_bias, stop=None,
):
    c = lax.axis_index("core")
    z = lax.axis_index("chip")
    chips = lax.axis_size("chip")
    nh = HC // HD
    rd = down_weight.shape[0]
    device = lax.axis_index(ALL)
    w_qkv, w_out, w_up, w_down = g_weights(c, qkv_weight, out_weight, up_weight, down_weight)
    gain1, bias1, gain2, bias2, b_out, b_down, b_qkv, b_up = g_small(
        c, rd, ln1_gain, ln1_bias, ln2_gain, ln2_bias, qkv_bias, out_bias, up_bias, down_bias
    )
    x = pair_rows(tokens).astype(F32)
    normed, rstd = normalize(x)
    first_in = (normed * gain1 + bias1).astype(BF)
    second_in = (normed * gain2 + bias2).astype(BF)
    projected = dot(first_in, w_qkv, (1, 0)) + b_qkv
    places = places_of(z, chips)
    turn = lambda v, d: rotate_heads(v.reshape(-1, nh, HD), places, d).reshape(-1, HC)
    q = turn(projected[:, :HC], 1.0).astype(BF)
    k = turn(projected[:, HC : 2 * HC], 1.0).astype(BF)
    kv = jnp.concatenate([k, projected[:, 2 * HC :].astype(BF)], axis=1)
    prompt_kv = lax.all_gather(kv[: 4 * PSH].reshape(2, 2 * PSH, 2 * HC), "chip", axis=0)
    cont_valid = lax.all_gather(valid[2 * PSH :], "core", axis=0, tiled=True)
    masks = masks_of(z, chips, cont_valid)
    chosen = prompt_of[0]
    attended, lse = g_attention(q, prompt_kv, kv, chosen, masks)
    hidden_pre = dot(second_in, w_up, (1, 0)) + b_up
    activated = jax.nn.gelu(hidden_pre, approximate=False).astype(BF)
    partial = dot(attended, w_out, (1, 0)) + dot(activated, w_down, (1, 0))
    halves = split_rows(partial)
    take = lambda a: lax.dynamic_index_in_dim(a, c, axis=0, keepdims=False)
    give = lambda a: lax.dynamic_index_in_dim(a, 1 - c, axis=0, keepdims=False)
    output = tokens.astype(F32) + take(halves) + swap_cores(give(halves)) + b_out + b_down
    live = (valid > 0).astype(F32)[:, None]
    missed = output - teacher.astype(F32)
    count_all, squared_all = lax.psum((jnp.sum(live), jnp.sum(live * missed * missed)), ALL)
    loss_value = squared_all / (count_all * D)
    out_grad = cotangent.astype(F32) + 2.0 / (count_all * D) * live * missed
    out_low = pair_rows(out_grad.astype(BF))
    if stop == "fwd":
        return output, out_grad, out_low, attended, lse, activated, q, kv, first_in, second_in
    out_bias_grad = jnp.sum(out_grad.astype(BF).astype(F32), axis=0)
    dw_out = dot(attended, out_low, (0, 0))
    dw_down = dot(activated, out_low, (0, 0))
    att_grad = dot(out_low, w_out, (1, 1)).astype(BF)
    hidden_grad = (dot(out_low, w_down, (1, 1)) * gelu_slope(hidden_pre)).astype(BF)
    dw_up = dot(second_in, hidden_grad, (0, 0))
    db_up = jnp.sum(hidden_grad.astype(F32), axis=0)
    second_grad = dot(hidden_grad, w_up, (1, 1))
    dq, pair, near = g_attention_back(q, prompt_kv, kv, att_grad, lse, chosen, masks)
    own_pair = lax.psum_scatter(pair.astype(BF), "chip", scatter_dimension=0, tiled=True).astype(F32)
    pair = jnp.concatenate([own_pair, near], axis=0)
    projected_grad = jnp.concatenate([turn(dq, -1.0), turn(pair[:, :HC], -1.0), pair[:, HC:]], axis=1).astype(BF)
    dw_qkv = dot(first_in, projected_grad, (0, 0))
    db_qkv = jnp.sum(projected_grad.astype(F32), axis=0)
    first_grad = dot(projected_grad, w_qkv, (1, 1))
    if stop == "bwd":
        return dw_out, dw_down, dw_up, dw_qkv, second_grad, first_grad, projected_grad, hidden_grad, att_grad
    joint = first_grad * gain1 + second_grad * gain2
    halves = split_rows(joint)
    joint = take(halves) + swap_cores(give(halves))
    own_normed = take(split_rows(normed))
    own_rstd = take(split_rows(rstd))
    input_grad = out_grad + own_rstd * (
        joint
        - jnp.mean(joint, axis=-1, keepdims=True)
        - own_normed * jnp.mean(joint * own_normed, axis=-1, keepdims=True)
    )
    wide = lambda v, n: jnp.zeros((v.shape[0], 2, v.shape[1]), F32).at[:, c].set(v).reshape(-1)
    small = jnp.concatenate(
        [
            jnp.sum(first_grad * normed, axis=0),
            jnp.sum(first_grad, axis=0),
            jnp.sum(second_grad * normed, axis=0),
            jnp.sum(second_grad, axis=0),
            out_bias_grad,
            wide(db_qkv.reshape(3, HC), 3),
            wide(db_up.reshape(-1, rd), 16),
        ]
    )
    small = lax.psum(small, ALL)
    shares, at = [], 0
    for size in (D, D, D, D, D, 3 * D, FF):
        own = size // lax.axis_size(ALL)
        shares.append(lax.dynamic_slice_in_dim(small, at + device * own, own))
        at += size
    rs = lambda v: lax.psum_scatter(v.astype(BF), CHIPS, scatter_dimension=0, tiled=True).astype(F32)
    r = qkv_weight.shape[0]
    s_qkv = rs(dw_qkv).reshape(2, r, 3, HC)
    s_up = rs(dw_up).reshape(2, r, FF // (2 * rd), rd)
    s_down = rs(dw_down)
    pairs = lambda own, other, axis: jnp.where(c == 0, jnp.stack([own, other], axis), jnp.stack([other, own], axis))
    s_qkv = pairs(take(s_qkv), swap_cores(give(s_qkv)), 2).reshape(r, 3 * D)
    s_up = pairs(take(s_up), swap_cores(give(s_up)), 2).reshape(r, FF)
    o = dw_out.reshape(H // 2, -1, 2, r, D)
    o_own = lax.dynamic_index_in_dim(o, c, axis=2, keepdims=False)
    o_other = swap_cores(lax.dynamic_index_in_dim(o, 1 - c, axis=2, keepdims=False))
    s_out = rs(pairs(o_own, o_other, 0).reshape(-1, D))
    return (
        output.astype(BF), loss_value, input_grad, shares[0], shares[1], shares[2], shares[3],
        s_qkv, shares[5], s_out, shares[4], s_up, shares[6], s_down, shares[4],
    )


MESH_ID = pl.DeviceIdType.MESH
RANKS = 4


class Net:
    def __init__(self, send, recv):
        self.g, self.z, self.c = (lax.axis_index(a) for a in ALL)
        self.y, self.x = self.g // 2, self.g % 2
        self.send, self.recv, self.used = send, recv, 0
        self.chip = self.g * RANKS + self.z
        self.core = {"grp": self.g, "chip": self.z, "core": 1 - self.c}
        self.right = {"grp": self.y * 2 + 1 - self.x, "chip": self.z, "core": self.c}
        self.up = {"grp": (1 - self.y) * 2 + self.x, "chip": self.z, "core": self.c}
        self.line = [{"grp": self.g, "chip": (self.z + j) % RANKS, "core": self.c} for j in (1, 2, 3)]
        self.sent = []

    def enter(self):
        barrier = pltpu.get_barrier_semaphore()
        for peer in [self.core, self.right, self.up] + self.line:
            pl.semaphore_signal(barrier, inc=1, device_id=peer, device_id_type=MESH_ID)
        pl.semaphore_wait(barrier, 6)

    def copy(self, src, dst, peer):
        i = self.used
        self.used += 1
        made = pltpu.make_async_remote_copy(
            src_ref=src, dst_ref=dst, send_sem=self.send.at[i], recv_sem=self.recv.at[i],
            device_id=peer, device_id_type=MESH_ID,
        )
        made.start()
        self.sent.append(made)
        return made

    def same(self, view, peer):
        return self.copy(view, view, peer)

    def settle(self, made):
        made.wait_recv()
        made.wait_send()
        self.sent = [m for m in self.sent if m is not made]

    def leave(self):
        for made in self.sent:
            made.wait_send()
        self.sent = []


def gather_steps(net, dst, rb, col, width, before):
    a, b, both = pl.ds(col, width // 2), pl.ds(col + width // 2, width // 2), pl.ds(col, width)
    quad = 4 * rb
    held = {}

    def line():
        for made in before:
            made.wait_recv()
        view = dst.at[pl.ds(net.chip * rb, rb), both]
        held[0] = [net.same(view, peer) for peer in net.line]

    def first():
        for made in held[0]:
            made.wait_recv()
        rows = pl.ds(net.g * quad, quad)
        held[1] = [net.same(dst.at[rows, a], net.right), net.same(dst.at[rows, b], net.up)]

    def second():
        for made in held[1]:
            made.wait_recv()
        held[2] = [net.same(dst.at[pl.ds(net.y * 2 * quad, 2 * quad), a], net.up)]
        for y in range(2):
            held[2].append(net.same(dst.at[pl.ds((y * 2 + net.x) * quad, quad), b], net.right))

    def last():
        for made in held[2]:
            made.wait_recv()

    return [line, first, second, last]


def small_steps(net, rows):
    held = {}

    def pair():
        held[0] = [net.same(rows.at[net.chip * 2 + net.c], net.core)]

    def line():
        held[0][0].wait_recv()
        held[1] = [net.same(rows.at[pl.ds(net.chip * 2, 2)], peer) for peer in net.line]

    def first():
        for made in held[1]:
            made.wait_recv()
        held[2] = [net.same(rows.at[pl.ds(net.g * 8, 8)], net.right)]

    def second():
        held[2][0].wait_recv()
        held[3] = [net.same(rows.at[pl.ds(net.y * 16, 16)], net.up)]

    def last():
        held[3][0].wait_recv()

    return [pair, line, first, second, last]


VM = pl.BlockSpec(memory_space=pltpu.VMEM)
HBM = pl.BlockSpec(memory_space=pl.ANY)
PROMPT = RANKS * 2 * PSH
KEYS = 2 * PROMPT + CONT
ROWS = 4 * PSH + CONT


def nt(a, b):
    return lax.dot_general(a, b, (((1,), (1,)), ((), ())), preferred_element_type=F32)


def nn(a, b):
    return lax.dot_general(a, b, (((1,), (0,)), ((), ())), preferred_element_type=F32)


def tn(a, b):
    return lax.dot_general(a, b, (((0,), (0,)), ((), ())), preferred_element_type=F32)


def tile_at(i, size):
    return pl.ds(pl.multiple_of(i * size, size), size)


def move_rows(dst, to, src, at, count, tile=32):
    @pl.loop(0, count // tile)
    def _(i):
        step = pl.multiple_of(i * tile, tile)
        dst[pl.ds(pl.multiple_of(to + step, tile), tile), :] = src[pl.ds(pl.multiple_of(at + step, tile), tile), :]


def spread_row(rows, field, index, owner, lane, size):
    table = rows[:, field, :].astype(BF)
    lanes = lax.broadcasted_iota(jnp.int32, (128, size), 0)
    pick = (lanes == index[lane : lane + 1, :size]).astype(F32).astype(BF)
    wide = nn(table, pick)
    owners = lax.broadcasted_iota(jnp.int32, (rows.shape[0], size), 0)
    return jnp.sum(jnp.where(owners == index[owner : owner + 1, :size], wide, 0.0), axis=0, keepdims=True)


def norm_rows(x):
    x = x.astype(F32)
    center = x - jnp.mean(x, axis=-1, keepdims=True)
    return center * lax.rsqrt(jnp.mean(center * center, axis=-1, keepdims=True) + EPSILON)


def turn(value, table, sign):
    cos, low_sin, high_sin = (table[:, 128 * i : 128 * i + 128] for i in range(3))
    out = []
    for j in range(value.shape[1] // 128):
        v = value[:, 128 * j : 128 * j + 128]
        other = pltpu.roll(v, 120, 1) * low_sin + pltpu.roll(v, 8, 1) * high_sin
        out.append(v * cos + sign * other)
    return out[0] if len(out) == 1 else jnp.concatenate(out, axis=1)


def rotary_table(length):
    half = ROT // 2
    inverse = (10000.0 ** (-np.arange(half, dtype=np.float32) / half)).astype(np.float32)
    angles = (np.arange(length, dtype=np.float32)[:, None] * inverse).astype(np.float64)
    cos, sin = np.cos(angles), np.sin(angles)
    table = np.zeros((length, 3, 2, HD), np.float32)
    table[:, 0] = 1.0
    for head in range(2):
        table[:, 0, head, :half] = cos
        table[:, 0, head, half:ROT] = cos
        table[:, 1, head, :half] = -sin
        table[:, 2, head, half:ROT] = sin
    return table.reshape(length, 384)


def index_table(rd):
    n = np.arange(2048)
    table = np.zeros((2, 16, 2048), np.int32)
    for c in range(2):
        col = np.minimum(n // HC, 2) * D + c * HC + n % HC
        table[c, 0], table[c, 1] = col // 96, col % 96
        unit = n // rd * (2 * rd) + c * rd + n % rd
        table[c, 2], table[c, 3] = unit // rd, unit % rd
        table[c, 4] = n // 32 % 32
        for i in range(4):
            table[c, 8 + i] = n % 32 + 32 * i
    return table


def seen(keys_at, queries_at, shape, length=None):
    keys = lax.broadcasted_iota(jnp.int32, shape, 0) + keys_at
    queries = lax.broadcasted_iota(jnp.int32, shape, 1) + queries_at
    mask = keys <= queries
    return mask if length is None else mask & (keys < length)


def head_lanes(rows):
    return lax.broadcasted_iota(jnp.int32, (rows, 128), 1) < HD


def attend(query, keys, values, masks, head):
    lanes = head_lanes(query.shape[0])
    own = jnp.where(lanes if head == 0 else ~lanes, query.astype(F32) * SCALE, 0.0).astype(BF)
    scores = [nt(k, own) for k in keys]
    scores = [s if m is None else jnp.where(m, s, NEGATIVE) for s, m in zip(scores, masks)]
    top = functools.reduce(jnp.maximum, [jnp.max(s, axis=0, keepdims=True) for s in scores])
    weights = [jnp.exp(s - top) for s in scores]
    total = sum(jnp.sum(w, axis=0, keepdims=True) for w in weights)
    share = 1.0 / total
    out = sum(tn(v, (w * share).astype(BF)) for v, w in zip(values, weights))
    return out[head * HD : head * HD + HD], top + jnp.log(total)


GATHER_ORDER = (
    (0, 0), (0, 1), (6, 0), (6, 0), (1, 0), (0, 2), (0, 3), (1, 1), (6, 0), (2, 0), (6, 0), (6, 0),
    (2, 1), (6, 0), (6, 0), (6, 0), (1, 2), (0, 4), (4, 0), (1, 3), (3, 0), (6, 0), (6, 0), (2, 2),
    (5, 0), (0, 5), (2, 3), (3, 1), (1, 4), (4, 1), (6, 0), (6, 0), (5, 1), (0, 6), (4, 2), (1, 5),
    (2, 4), (3, 2), (6, 0), (6, 0), (3, 3), (5, 2), (0, 7), (2, 5), (6, 0), (1, 6), (4, 3), (6, 0),
    (3, 4), (1, 7), (0, 8), (2, 6), (5, 3), (4, 4), (3, 5), (2, 7), (5, 4), (0, 9), (4, 5), (1, 8),
    (3, 6), (6, 0), (6, 0), (6, 0), (6, 0), (6, 0), (6, 0), (3, 7), (2, 8), (6, 0), (6, 0), (5, 5),
    (0, 10), (6, 0), (1, 9), (0, 11), (6, 0), (6, 0), (6, 0), (6, 0), (6, 0), (3, 8), (2, 9), (6, 0),
    (6, 0), (6, 0), (1, 10), (1, 11), (6, 0), (6, 0), (6, 0), (3, 9), (6, 0), (6, 0), (2, 10), (2, 11),
    (6, 0), (6, 0), (6, 0), (6, 0), (3, 10), (3, 11),
)


def forward_kernel(
    tokens, small, qkv, out, up, down, rotary, index, teacher, cotangent,
    rows, h_w_qkv, h_x, h_first, h_q, h_kv, lse, h_dw_out, h_dw_down, h_dw_up, att_grad, joint, output, out_grad, value,
    w_qkv, x_own, first_own, q, kv, dw_out, dw_down, dw_up, w_out, w_up, w_down, second_in, attended, activated, slope, peer, low, x_all, first_in, spread, swapped, crossed, send, recv, local,
):
    net = Net(send, recv)
    c, z, chip = net.c, net.z, net.chip
    net.enter()
    for p in range(2):
        move_rows(x_all, p * PROMPT + z * 2 * PSH + c * PSH, tokens, p * PSH, PSH)
    move_rows(x_all, 2 * PROMPT + c * HALF, tokens, 2 * PSH, HALF)
    rows[chip * 2 + c] = small[...]
    pieces_at = [pl.ds(p * PROMPT + z * 2 * PSH + c * PSH, PSH) for p in range(2)]
    smalls = small_steps(net, rows)
    smalls[0]()
    mates = [net.same(x_all.at[piece], net.core) for piece in pieces_at + [pl.ds(2 * PROMPT + c * HALF, HALF)]]
    half_rows = pl.ds(pl.multiple_of(chip * 64 + c * 32, 32), 32)
    given = pl.ds(0, 32)
    w_qkv[half_rows, :] = qkv[c]
    swapped[given, : 3 * HC] = qkv[1 - c]
    from_core = {}
    from_core["qkv"] = net.copy(swapped.at[given, pl.ds(0, 3 * HC)], w_qkv.at[half_rows], net.core)
    w_up[half_rows, :] = up[c]
    given = pl.ds(32, 32)
    swapped[given, : FF // 2] = up[1 - c]
    from_core["up"] = net.copy(swapped.at[given, pl.ds(0, FF // 2)], w_up.at[half_rows], net.core)
    w_down[pl.ds(pl.multiple_of(chip * 128, 128), 128), :] = down[...]
    spread[pl.ds(pl.multiple_of(chip * 32, 32), 32), :] = out[...]
    none = []
    tasks = [gather_steps(net, w_up, 64, 512 * i, 512, [] if i else [from_core["up"]]) for i in range(4)]
    tasks += [gather_steps(net, w_qkv, 64, 512 * i, 512, [] if i else [from_core["qkv"]]) for i in range(3)]
    tasks += [gather_steps(net, spread, 32, 0, 1024, [])]
    tasks += [gather_steps(net, w_down, 128, 256 * i, 256, []) for i in range(4)]
    pieces, done = [], set()

    def after(needs, work, *args):
        pieces.append((set(needs), work, args))

    def run_pieces(count):
        while count and pieces and pieces[0][0] <= done:
            needs, work, args = pieces.pop(0)
            work(*args)
            count -= 1

    held = {}

    def learn():
        for made in mates:
            made.wait_recv()
        places = index.at[c]
        held["norm"] = [spread_row(rows, 0, places, 4, 8 + i, D) for i in range(4)]
        held["qkv"] = spread_row(rows, 2, places, 0, 1, 3 * HC)
        held["length"] = jnp.sum(jnp.sum(rows[pl.ds(chip * 2, 2), 5:7, :], axis=0), keepdims=True).astype(jnp.int32)
        held["up"] = spread_row(rows, 3, places, 2, 3, FF // 2)

    def own_norms(first_tile, count):
        gain1, bias1, gain2, bias2 = held["norm"]

        @pl.loop(first_tile, first_tile + count)
        def _(i):
            prompt = (i // 2) * PROMPT + z * 2 * PSH + (i % 2) * 64
            here = pl.ds(pl.multiple_of(jnp.where(i < 4, prompt, 2 * PROMPT + (i - 4) * 64), 64), 64)
            at = tile_at(i, 64)
            normed = norm_rows(x_all[here, :])
            x_own[at, :] = x_all[here, :]
            narrow = (normed * gain1 + bias1).astype(BF)
            first_in[here, :] = narrow
            first_own[at, :] = narrow
            second_in[at, :] = (normed * gain2 + bias2).astype(BF)

    relays = {}
    prompt_pieces = [(j, p) for j in (1, 2, 3) for p in range(2)]

    def send_tokens(k):
        j, p = prompt_pieces[k]
        held[k] = net.same(x_all.at[pieces_at[p]], net.line[j - 1])

    def relay_tokens(k):
        j, p = prompt_pieces[k]
        held[k].wait_recv()
        relays[k] = net.same(x_all.at[pl.ds(p * PROMPT + (z + RANKS - j) % RANKS * 2 * PSH + c * PSH, PSH)], net.core)

    def other_norms(k):
        j, p = prompt_pieces[k]
        relays[k].wait_recv()
        gain1, bias1 = held["norm"][:2]

        @pl.loop(0, 2)
        def _(i):
            here = pl.ds(pl.multiple_of(p * PROMPT + (z + RANKS - j) % RANKS * 2 * PSH + i * 64, 64), 64)
            first_in[here, :] = (norm_rows(x_all[here, :]) * gain1 + bias1).astype(BF)

    def hidden(j):
        cols = slice(256 * j, 256 * j + 256)
        b_up = held["up"]

        @pl.loop(0, ROWS // 128)
        def _(i):
            at = tile_at(i, 128)
            pre = nn(second_in[at, :], w_up[:, cols]) + b_up[:, cols]
            gate = 0.5 * (1.0 + lax.erf(pre * 0.7071067811865476))
            activated[at, cols] = (pre * gate).astype(BF)
            slope[at, cols] = (gate + pre * jnp.exp(-0.5 * pre * pre) * 0.3989422804014327).astype(slope.dtype)

    def key_rows(i):
        at = slice(256 * i, 256 * i + 256)
        here = first_in[at, :]
        place = (i % 2) * 256 if i < 4 else PROMPT + (i - 4) * 256
        table = rotary[place : place + 256, :]
        for j in range(4):
            cols = slice(HC + 256 * j, HC + 256 * j + 256)
            made = nn(here, w_qkv[:, cols]) + held["qkv"][:, cols]
            kv[at, 256 * j : 256 * j + 256] = (turn(made, table, 1.0) if j < 2 else made).astype(BF)

    def query_rows(first_tile, count):
        @pl.loop(first_tile, first_tile + count)
        def _(i):
            place = pl.multiple_of(jnp.where(i < 2, z * 2 * PSH, PROMPT + (i - 2) * 128), 128)
            at = tile_at(i, 128)
            here = first_own[at, :]
            table = rotary[pl.ds(place, 128), :]
            for j in range(2):
                cols = slice(256 * j, 256 * j + 256)
                q[at, cols] = turn(nn(here, w_qkv[:, cols]) + held["qkv"][:, cols], table, 1.0).astype(BF)

    second = jnp.broadcast_to(small[7:8, :], (PROMPT, 128)) > 0.5

    def attend_pair(pair, part):
        k_at, v_at = pl.ds(128 * pair, 128), pl.ds(HC + 128 * pair, 128)
        prompts = [(kv[p * PROMPT : (p + 1) * PROMPT, k_at], kv[p * PROMPT : (p + 1) * PROMPT, v_at]) for p in range(2)]

        def put(row, size, key_list, value_list, masks):
            outs = []
            for head in range(2):
                o, stat = attend(q[row : row + size, k_at], key_list, value_list, masks, head)
                outs.append(o)
                lse[2 * pair + head, :, row : row + size] = stat
            attended[row : row + size, k_at] = jnp.concatenate(outs, axis=0).T.astype(BF)

        for p in range(2) if part == 0 else ():
            put(p * 128, 128, [prompts[p][0]], [prompts[p][1]], [seen(0, z * 2 * PSH, (PROMPT, 128))])
        chosen = [jnp.where(second, b.astype(F32), a.astype(F32)).astype(BF) for a, b in zip(*prompts)]
        for i in ((), (0, 1), (2, 3))[part]:
            near = 128 * i + 128
            put(
                256 + 128 * i, 128,
                [chosen[0], kv[2 * PROMPT : 2 * PROMPT + near, k_at]],
                [chosen[1], kv[2 * PROMPT : 2 * PROMPT + near, v_at]],
                [None, seen(0, 128 * i, (near, 128), held["length"])],
            )

    after([], smalls[1])
    after([(0, 1)], smalls[2])
    after([(1, 0)], smalls[3])
    after([(2, 0)], smalls[4])
    after([(2, 0)], learn)
    for i in range(3):
        after([], own_norms, 4 * i, 4)
    for j in range(8):
        after([(3, j // 2)], hidden, j)
    for i in range(2):
        after([(3, 6)], query_rows, 3 * i, 3)
    for i in range(2):
        after([(3, 6)], key_rows, 4 + i)
    for k in range(6):
        after([(5, k)], other_norms, k)
    for i in range(4):
        after([(5, 5)], key_rows, i)
    for pair in range(4):
        for part in range(3):
            after([], attend_pair, pair, part)
    for event in GATHER_ORDER:
        step, t = event
        if step < 4:
            tasks[t][step]()
        elif step == 4:
            send_tokens(t)
        elif step == 5:
            relay_tokens(t)
        else:
            run_pieces(1)
        done.add(event)
    run_pieces(len(pieces))
    shipped = []

    def ship(src, dst):
        made = pltpu.make_async_copy(src, dst, local.at[len(shipped)])
        made.start()
        shipped.append(made)

    for src, dst in ((w_qkv, h_w_qkv), (x_own, h_x), (first_own, h_first), (q, h_q), (kv, h_kv)):
        ship(src, dst)
    length = held["length"]
    gain2 = held["norm"][2]
    places = index.at[c]
    given = pl.ds(pl.multiple_of((1 - c) * 256, 256), 256)
    swap = net.copy(spread.at[given], crossed, net.core)
    swap.wait_recv()
    for h in range(8):
        w_out[pl.ds(pl.multiple_of(h * 64 + c * 32, 32), 32), :] = spread[pl.ds(pl.multiple_of(c * 256 + h * 32, 32), 32), :]
        w_out[pl.ds(pl.multiple_of(h * 64 + (1 - c) * 32, 32), 32), :] = crossed[h * 32 : h * 32 + 32, :]

    def share(at, size):
        here = pl.ds(pl.multiple_of(at, 128), size)
        joint[here, :] = nn(attended[here, :], w_out[...]) + nn(activated[here, :], w_down[...])

    def chip_range(i, owner):
        return ((owner * PSH, PSH, 0), (2 * PSH + owner * PSH, PSH, PSH), (4 * PSH + owner * HALF, HALF, 2 * PSH))[i]

    def pass_share(i):
        at, size, to = chip_range(i, 1 - c)
        return net.copy(joint.at[pl.ds(pl.multiple_of(at, 64), size)], peer.at[pl.ds(to, size)], net.core)

    share(4 * PSH + (1 - c) * HALF, HALF)
    passed = [pass_share(2)]
    share(0, 256)
    passed += [pass_share(0), pass_share(1)]
    share(4 * PSH + c * HALF, HALF)
    for made in passed:
        net.settle(made)
    count = jnp.sum(jnp.sum(rows[:, 4:7, :], axis=0), keepdims=True)
    pull = 2.0 / (count * D)
    bias = spread_row(rows, 1, places, 4, 8, D) + spread_row(rows, 1, places, 4, 9, D)
    value[...] = jnp.zeros_like(value)
    squared, low_sum = jnp.zeros((1, D), F32), jnp.zeros((1, D), F32)
    lows = []
    for i in range(3):
        at, size, to = chip_range(i, c)

        def rows_out(k, sums, at=at, to=to, i=i):
            here = pl.ds(pl.multiple_of(at + k * 64, 64), 64)
            own = pl.ds(pl.multiple_of(to + k * 64, 64), 64)
            result = tokens[own, :].astype(F32) + joint[here, :] + peer[own, :] + bias
            missed = result - teacher[own, :].astype(F32)
            if i == 2:
                step = lax.broadcasted_iota(jnp.int32, (64, D), 0) + (c * HALF + k * 64)
                missed = jnp.where(step < length, missed, 0.0)
            output[own, :] = result.astype(BF)
            grad = cotangent[own, :].astype(F32) + pull * missed
            out_grad[own, :] = grad
            rounded = grad.astype(BF)
            low[here, :] = rounded
            return (
                sums[0] + jnp.sum(missed * missed, axis=0, keepdims=True),
                sums[1] + jnp.sum(rounded.astype(F32), axis=0, keepdims=True),
            )

        squared, low_sum = lax.fori_loop(0, size // 64, rows_out, (squared, low_sum))
        lows.append(net.same(low.at[pl.ds(pl.multiple_of(at, 64), size)], net.core))
    total = jnp.sum(squared, keepdims=True)
    value[96:97, :] = jnp.broadcast_to(total, (1, 128))

    def put_row(row, vector):
        for k in range(vector.shape[1] // 128):
            value[row + k : row + k + 1, :] = vector[:, 128 * k : 128 * k + 128]

    put_row(32, low_sum)
    for made in lows:
        made.wait_recv()

    @pl.loop(0, 8)
    def _(i):
        at = tile_at(i, 256)
        dw_down[at, :] = tn(activated[:, at], low[...]).astype(BF)

    ship(dw_down, h_dw_down)

    @pl.loop(0, 2)
    def _(i):
        at = tile_at(i, 256)
        dw_out[at, :] = tn(attended[:, at], low[...]).astype(BF)

    ship(dw_out, h_dw_out)

    @pl.loop(0, ROWS // 128)
    def _(i):
        at = tile_at(i, 128)
        att_grad[at, :] = nt(low[at, :], w_out[...]).astype(BF)

    for j in range(8):
        cols = slice(256 * j, 256 * j + 256)

        def hidden_rows(i, total, cols=cols):
            at = tile_at(i, 256)
            grad = (nt(low[at, :], w_down[cols, :]) * slope[at, cols].astype(F32)).astype(BF)
            activated[at, cols] = grad
            return total + jnp.sum(grad.astype(F32), axis=0, keepdims=True)

        total = lax.fori_loop(0, ROWS // 256, hidden_rows, jnp.zeros((1, 256), F32))
        for k in range(2):
            value[pl.ds(64 + 4 * j + 2 * k + c, 1), :] = total[:, 128 * k : 128 * k + 128]

    @pl.loop(0, 4)
    def _(i):
        at = tile_at(i, 256)
        for k in range(2):
            cols = slice(1024 * k, 1024 * k + 1024)
            dw_up[at, cols] = tn(second_in[:, at], activated[:, cols]).astype(BF)

    ship(dw_up, h_dw_up)

    def second_rows(i, sums):
        at = tile_at(i, 128)
        grad = nt(activated[at, :], w_up[...])
        joint[at, :] = grad * gain2
        normed = norm_rows(x_own[at, :])
        return (
            sums[0] + jnp.sum(grad * normed, axis=0, keepdims=True),
            sums[1] + jnp.sum(grad, axis=0, keepdims=True),
        )

    sums = lax.fori_loop(0, ROWS // 128, second_rows, (jnp.zeros((1, D), F32), jnp.zeros((1, D), F32)))
    put_row(16, sums[0])
    put_row(24, sums[1])
    for made in shipped:
        made.wait()
    net.leave()


def forward(tokens, small, qkv, out, up, down, teacher, cotangent):
    shape = jax.ShapeDtypeStruct
    return pl.pallas_call(
        forward_kernel,
        out_shape=(
            shape((32, 8, 128), F32), shape((D, 3 * HC), BF), shape((ROWS, D), BF), shape((ROWS, D), BF), shape((ROWS, HC), BF),
            shape((KEYS, 2 * HC), BF), shape((8, 1, ROWS), F32), shape((HC, D), BF), shape((FF // 2, D), BF), shape((D, FF // 2), BF),
            shape((ROWS, HC), BF), shape((ROWS, D), F32), shape((384, D), BF), shape((384, D), F32), shape((104, 128), F32),
        ),
        in_specs=[VM] * 10,
        out_specs=(VM,) + (HBM,) * 5 + (VM,) + (HBM,) * 3 + (VM,) * 5,
        scratch_shapes=[
            pltpu.VMEM((D, 3 * HC), BF), pltpu.VMEM((ROWS, D), BF), pltpu.VMEM((ROWS, D), BF), pltpu.VMEM((ROWS, HC), BF),
            pltpu.VMEM((KEYS, 2 * HC), BF), pltpu.VMEM((HC, D), BF), pltpu.VMEM((FF // 2, D), BF), pltpu.VMEM((D, FF // 2), BF),
            pltpu.VMEM((HC, D), BF), pltpu.VMEM((D, FF // 2), BF), pltpu.VMEM((FF // 2, D), BF), pltpu.VMEM((ROWS, D), BF),
            pltpu.VMEM((ROWS, HC), BF), pltpu.VMEM((ROWS, FF // 2), BF), pltpu.VMEM((ROWS, FF // 2), BF), pltpu.VMEM((384, D), F32),
            pltpu.VMEM((ROWS, D), BF), pltpu.VMEM((KEYS, D), BF), pltpu.VMEM((KEYS, D), BF), pltpu.VMEM((HC, D), BF),
            pltpu.VMEM((64, FF // 2), BF), pltpu.VMEM((256, D), BF), pltpu.SemaphoreType.DMA((140,)), pltpu.SemaphoreType.DMA((140,)), pltpu.SemaphoreType.DMA((8,)),
        ],
        compiler_params=pltpu.CompilerParams(collective_id=0, has_side_effects=True, vmem_limit_bytes=63 << 20),
    )(tokens, small, qkv, out, up, down, jnp.asarray(rotary_table(PROMPT + CONT)), jnp.asarray(index_table(128)), teacher, cotangent)


def add_rows(dst, dst_rows, src, src_rows, count, cols, tile):
    @pl.loop(0, count // tile)
    def _(i):
        to = pl.ds(pl.multiple_of(dst_rows + i * tile, tile), tile)
        more = src[pl.ds(pl.multiple_of(src_rows + i * tile, tile), tile), cols].astype(F32)
        dst[to, :] = (dst[to, :].astype(F32) + more).astype(dst.dtype)


def scatter_steps(net, src, rb, col, width, before, got_a, got_b, got_z, put):
    half = width // 2
    a, b, both = pl.ds(col, half), pl.ds(col + half, half), pl.ds(col, width)
    quad = 4 * rb
    tile = min(64, rb)
    at = lambda y, x: pl.ds((y * 2 + x) * quad, quad)
    held = {}

    def first():
        for made in before:
            made.wait()
        rows = pl.ds((1 - net.y) * 2 * quad, 2 * quad)
        held[0] = [net.copy(src.at[rows, a], got_a.at[pl.ds(0, 2 * quad)], net.up)]
        for y in range(2):
            held[0].append(net.copy(src.at[at(y, 1 - net.x), b], got_b.at[pl.ds(y * quad, quad)], net.right))

    def second():
        for made in held[0]:
            made.wait_recv()
        add_rows(got_a, (1 - net.x) * quad, src, (net.y * 2 + 1 - net.x) * quad, quad, a, tile)
        add_rows(got_b, (1 - net.y) * quad, src, ((1 - net.y) * 2 + net.x) * quad, quad, b, tile)
        held[1] = [
            net.copy(got_a.at[pl.ds((1 - net.x) * quad, quad)], got_a.at[pl.ds(2 * quad, quad)], net.right),
            net.copy(got_b.at[pl.ds((1 - net.y) * quad, quad)], got_b.at[pl.ds(2 * quad, quad)], net.up),
        ]
        add_rows(got_a, net.x * quad, src, (net.y * 2 + net.x) * quad, quad, a, tile)
        add_rows(got_b, net.y * quad, src, (net.y * 2 + net.x) * quad, quad, b, tile)

    def third():
        for made in held[1]:
            made.wait_recv()
        add_rows(got_a, net.x * quad, got_a, 2 * quad, quad, slice(None), tile)
        add_rows(got_b, net.y * quad, got_b, 2 * quad, quad, slice(None), tile)
        held[2] = []
        for j in (1, 2, 3):
            there = (net.z + j) % RANKS * rb
            peer = net.line[j - 1]
            held[2].append(net.copy(got_a.at[pl.ds(net.x * quad + there, rb)], got_z.at[j - 1, :, pl.ds(0, half)], peer))
            held[2].append(net.copy(got_b.at[pl.ds(net.y * quad + there, rb)], got_z.at[j - 1, :, pl.ds(half, half)], peer))

    def last():
        for made in held[2]:
            made.wait_recv()
        for k, (got, way) in enumerate(((got_a, net.x), (got_b, net.y))):
            cols = slice(k * half, k * half + half)

            @pl.loop(0, rb // tile)
            def _(i):
                rows = pl.ds(pl.multiple_of(way * quad + net.z * rb + i * tile, tile), tile)
                value = got[rows, :].astype(F32)
                for j in range(3):
                    value = value + got_z[j, tile_at(i, tile), cols].astype(F32)
                put(tile_at(i, tile), slice(col + k * half, col + k * half + half), value)

    return [first, second, third, last]


def sum_steps(net, value, got):
    held = {}
    peers = [net.core, net.right, net.up]

    def make(i):
        def step():
            if i > 0:
                net.settle(held[i - 1])
                value[...] = value[...] + got[i - 1]
            if i < 3:
                held[i] = net.copy(value, got.at[i], peers[i])
            else:
                held[3] = [net.copy(value, got.at[3 + net.z], peer) for peer in net.line]
                got[3 + net.z] = value[...]

        return step

    def last():
        for made in held[3]:
            net.settle(made)
        value[...] = (got[3] + got[4]) + (got[5] + got[6])

    return [make(i) for i in range(4)] + [last]


def attend_back(query, grad, keys, values, masks, stat, head):
    lanes = head_lanes(query.shape[0])
    lanes = lanes if head == 0 else ~lanes
    own = jnp.where(lanes, query.astype(F32) * SCALE, 0.0).astype(BF)
    own_grad = jnp.where(lanes, grad.astype(F32), 0.0).astype(BF)
    inner, kept = 0.0, []
    for k, v, m in zip(keys, values, masks):
        scores = nt(k, own)
        probs = jnp.exp((scores if m is None else jnp.where(m, scores, NEGATIVE)) - stat)
        prob_grad = nt(v, own_grad)
        inner = inner + jnp.sum(probs * prob_grad, axis=0, keepdims=True)
        kept.append((probs, prob_grad))
    dq, dks, dvs = 0.0, [], []
    for k, (probs, prob_grad) in zip(keys, kept):
        score_grad = (probs * (prob_grad - inner)).astype(BF)
        dq = dq + tn(k, score_grad)
        dks.append(nn(score_grad, own))
        dvs.append(nn(probs.astype(BF), own_grad))
    return dq[head * HD : head * HD + HD] * SCALE, dks, dvs


def backward_kernel(
    rows, small, value_in, gain, rotary, lse, h_q, h_kv, h_att, h_first, h_x, h_w_qkv, h_joint, dw_out_in, dw_down_in, dw_up_in,
    value, o_qkv, o_out, o_up, o_down, joint_own,
    q, kv, att_grad, first, x, w_qkv, joint_in, dw_qkv, dw_out, dw_down, dw_up, spread, pairs, got_pairs, far_k, far_v, projected, joint, peer_joint,
    got_s, s_qkv, s_up, peer_qkv, peer_up, *rest,
):
    bufs, (send, recv, local) = rest[:-3], rest[-3:]
    net = Net(send, recv)
    c, z, chip = net.c, net.z, net.chip
    loads = [pltpu.make_async_copy(src, dst, local.at[i]) for i, (src, dst) in enumerate(
        ((dw_down_in, dw_down), (dw_up_in, dw_up), (dw_out_in, dw_out), (h_q, q), (h_kv, kv), (h_att, att_grad),
         (h_first, first), (h_w_qkv, w_qkv), (h_x, x), (h_joint, joint_in)))]
    for load in loads:
        load.start()
    value[...] = value_in[...]
    net.enter()
    bufs = list(bufs)
    take3 = lambda: [bufs.pop(0) for _ in range(3)]

    def put_into(ref):
        def put(at, cols, total):
            ref[at, cols] = total

        return put

    clock, tasks = [0], []

    def advance(until):
        while clock[0] < until:
            for t, steps in tasks:
                if (clock[0] - t) % 2 == 0 and 0 <= (clock[0] - t) // 2 < len(steps):
                    steps[(clock[0] - t) // 2]()
            clock[0] += 1

    loads[0].wait()
    tasks.append((0, scatter_steps(net, dw_down, 128, 0, 512, [], *take3(), put_into(o_down))))
    tasks.append((1, scatter_steps(net, dw_down, 128, 512, 512, [], *take3(), put_into(o_down))))
    tasks.append((2, scatter_steps(net, dw_up, 64, 0, 1024, [loads[1]], *take3(), put_into(s_up))))
    tasks.append((3, scatter_steps(net, dw_up, 64, 1024, 1024, [], *take3(), put_into(s_up))))
    advance(2)
    loads[2].wait()
    swaps = []
    for h in range(8):
        theirs = dw_out.at[pl.ds(h * 64 + (1 - c) * 32, 32)]
        swaps.append(net.copy(theirs, spread.at[pl.ds((8 * c + h) * 32, 32)], net.core))
        spread[pl.ds(pl.multiple_of((8 * c + h) * 32, 32), 32), :] = dw_out[pl.ds(pl.multiple_of(h * 64 + c * 32, 32), 32), :]
    tasks.append((4, scatter_steps(net, spread, 32, 0, 1024, [], *take3(), put_into(o_out))))

    length = jnp.sum(jnp.sum(rows[pl.ds(chip * 2, 2), 5:7, :], axis=0), keepdims=True).astype(jnp.int32)
    second = jnp.broadcast_to(small[7:8, :], (PROMPT, 128)) > 0.5
    weight = small[7:8, :]
    pair_sends = []

    def back_pair(pair):
        k_at, v_at = pl.ds(128 * pair, 128), pl.ds(HC + 128 * pair, 128)
        prompts = [(kv[p * PROMPT : (p + 1) * PROMPT, k_at], kv[p * PROMPT : (p + 1) * PROMPT, v_at]) for p in range(2)]
        chosen = [jnp.where(second, b.astype(F32), a.astype(F32)).astype(BF) for a, b in zip(*prompts)]

        def both_heads(row, size, keys, values, masks, place):
            dq, dks, dvs = [], None, None
            for head in range(2):
                stat = lse[2 * pair + head, :, row : row + size]
                d, k_parts, v_parts = attend_back(
                    q[row : row + size, k_at], att_grad[row : row + size, k_at], keys, values, masks, stat, head
                )
                dq.append(d)
                dks = k_parts if dks is None else [a + b for a, b in zip(dks, k_parts)]
                dvs = v_parts if dvs is None else [a + b for a, b in zip(dvs, v_parts)]
            dq = jnp.concatenate(dq, axis=0).T
            projected[row : row + size, k_at] = turn(dq, rotary[pl.ds(place, size), :], -1.0).astype(BF)
            return dks, dvs

        near_k, near_v = None, None
        for i in range(2):
            near = 256 * i + 256
            masks = [None, seen(0, 256 * i, (near, 256), length)]
            near_keys = kv[2 * PROMPT : 2 * PROMPT + near, k_at], kv[2 * PROMPT : 2 * PROMPT + near, v_at]
            dks, dvs = both_heads(
                256 + 256 * i, 256, [chosen[0], near_keys[0]], [chosen[1], near_keys[1]], masks, PROMPT + 256 * i
            )
            if i == 0:
                far_k[...], far_v[...] = dks[0], dvs[0]
                near_k, near_v = dks[1], dvs[1]
            else:
                far_k[...] = far_k[...] + dks[0]
                far_v[...] = far_v[...] + dvs[0]
                near_k = [near_k + dks[1][:256], dks[1][256:]]
                near_v = [near_v + dvs[1][:256], dvs[1][256:]]
        for i in range(2):
            at = slice(256 + 256 * i, 512 + 256 * i)
            table = rotary[PROMPT + 256 * i : PROMPT + 256 * i + 256, :]
            projected[at, HC + 128 * pair : HC + 128 * pair + 128] = turn(near_k[i], table, -1.0).astype(BF)
            projected[at, 2 * HC + 128 * pair : 2 * HC + 128 * pair + 128] = near_v[i].astype(BF)
        for p in range(2):
            place = pl.multiple_of(z * 2 * PSH, 128)
            dks, dvs = both_heads(
                128 * p, 128, [prompts[p][0]], [prompts[p][1]], [seen(0, z * 2 * PSH, (PROMPT, 128))], place
            )
            share = weight if p == 1 else 1.0 - weight
            at = slice(p * PROMPT, p * PROMPT + PROMPT)
            pairs[pair, at, :128] = (dks[0] + share * far_k[...]).astype(BF)
            pairs[pair, at, 128:] = (dvs[0] + share * far_v[...]).astype(BF)
        for j in (1, 2, 3):
            for p in range(2):
                there = pl.ds(p * PROMPT + (z + j) % RANKS * 2 * PSH, 2 * PSH)
                pair_sends.append(
                    net.copy(pairs.at[pair, there], got_pairs.at[j - 1, pair, pl.ds(p * 2 * PSH, 2 * PSH)], net.line[j - 1])
                )

    for load in loads[3:6]:
        load.wait()
    back_pair(0)
    advance(3)
    back_pair(1)
    advance(4)
    for made in swaps:
        made.wait_recv()
    back_pair(2)
    advance(5)
    back_pair(3)
    advance(6)
    for made in pair_sends:
        made.wait_recv()
    table = rotary[pl.ds(pl.multiple_of(z * 2 * PSH, 128), 128), :]
    for pair in range(4):
        for p in range(2):
            at = slice(p * 128, p * 128 + 128)
            total = pairs[pair, pl.ds(pl.multiple_of(p * PROMPT + z * 2 * PSH, 128), 128), :].astype(F32)
            for j in range(3):
                total = total + got_pairs[j, pair, at, :].astype(F32)
            projected[at, HC + 128 * pair : HC + 128 * pair + 128] = turn(total[:, :128], table, -1.0).astype(BF)
            projected[at, 2 * HC + 128 * pair : 2 * HC + 128 * pair + 128] = total[:, 128:].astype(BF)

    def weight_columns(col, width):
        @pl.loop(0, D // 256)
        def _(i):
            part = tn(first[:, tile_at(i, 256)], projected[:, col : col + width])
            dw_qkv[tile_at(i, 256), col : col + width] = part.astype(BF)

    for load in loads[6:]:
        load.wait()
    weight_columns(0, 768)
    tasks.append((6, scatter_steps(net, dw_qkv, 64, 0, 768, [], *take3(), put_into(s_qkv))))
    advance(7)
    weight_columns(768, 768)
    tasks.append((7, scatter_steps(net, dw_qkv, 64, 768, 768, [], *take3(), put_into(s_qkv))))
    advance(8)
    fg_sum, fg_normed = jnp.zeros((1, D), F32), jnp.zeros((1, D), F32)
    bias = jnp.zeros((1, 3 * HC), F32)

    def first_rows(i, sums):
        at = tile_at(i, 128)
        here = projected[at, :]
        grad = nt(here, w_qkv[...])
        normed = norm_rows(x[at, :])
        joint[at, :] = grad * gain[...] + joint_in[at, :]
        return (
            sums[0] + jnp.sum(grad, axis=0, keepdims=True),
            sums[1] + jnp.sum(grad * normed, axis=0, keepdims=True),
            sums[2] + jnp.sum(here.astype(F32), axis=0, keepdims=True),
        )

    fg_sum, fg_normed, bias = lax.fori_loop(0, ROWS // 128, first_rows, (fg_sum, fg_normed, bias))
    ranges = ((0, PSH, lambda o: o * PSH), (PSH, PSH, lambda o: 2 * PSH + o * PSH), (2 * PSH, HALF, lambda o: 4 * PSH + o * HALF))
    joints = [
        net.copy(joint.at[pl.ds(there(1 - c), size)], peer_joint.at[pl.ds(at, size)], net.core) for at, size, there in ranges
    ]
    for i in range(8):
        cols = slice(128 * i, 128 * i + 128)
        value[i : i + 1, :] = value[i : i + 1, :] + fg_normed[:, cols]
        value[8 + i : 9 + i, :] = value[8 + i : 9 + i, :] + fg_sum[:, cols]
    for i in range(12):
        row = pl.ds(40 + i // 4 * 8 + c * 4 + i % 4, 1)
        value[row, :] = value[row, :] + bias[:, 128 * i : 128 * i + 128]
    sums = sum_steps(net, value, got_s)
    sums[0]()
    advance(9)
    for made in joints:
        made.wait_recv()
    for at, size, there in ranges:
        mine = pl.ds(pl.multiple_of(there(c), 64), size)
        joint_own[at : at + size, :] = joint[mine, :] + peer_joint[at : at + size, :]
    sums[1]()
    advance(10)
    sums[2]()
    ups = []

    def give(total, peer_ref):
        return net.copy(total.at[pl.ds((1 - c) * 32, 32)], peer_ref, net.core)

    advance(11)
    ups.append(give(s_up, peer_up))
    sums[3]()
    advance(12)
    sums[4]()
    advance(16)
    ups.append(give(s_qkv, peer_qkv))
    own_rows = pl.ds(pl.multiple_of(c * 32, 32), 32)
    ups[0].wait_recv()
    for i in range(16):
        for who, part in ((c, s_up[own_rows, 128 * i : 128 * i + 128]), (1 - c, peer_up[:, 128 * i : 128 * i + 128])):
            o_up[:, pl.ds(pl.multiple_of((2 * i + who) * 128, 128), 128)] = part
    ups[1].wait_recv()
    for i in range(3):
        for who, part in ((c, s_qkv[own_rows, HC * i : HC * i + HC]), (1 - c, peer_qkv[:, HC * i : HC * i + HC])):
            o_qkv[:, pl.ds(pl.multiple_of(i * D + who * HC, 128), HC)] = part
    net.leave()


def backward(*args):
    shape = jax.ShapeDtypeStruct
    bufs = []
    for rb, width, count in ((128, 512, 2), (64, 1024, 2), (32, 1024, 1), (64, 768, 2)):
        for _ in range(count):
            bufs += [pltpu.VMEM((12 * rb, width // 2), BF), pltpu.VMEM((12 * rb, width // 2), BF), pltpu.VMEM((3, rb, width), BF)]
    return pl.pallas_call(
        backward_kernel,
        out_shape=(
            shape((104, 128), F32), shape((32, 3 * D), F32), shape((32, D), F32), shape((32, FF), F32), shape((128, D), F32),
            shape((384, D), F32),
        ),
        in_specs=[VM] * 6 + [HBM] * 10,
        out_specs=(VM,) * 6,
        scratch_shapes=[
            pltpu.VMEM((ROWS, HC), BF), pltpu.VMEM((KEYS, 2 * HC), BF), pltpu.VMEM((ROWS, HC), BF), pltpu.VMEM((ROWS, D), BF),
            pltpu.VMEM((ROWS, D), BF), pltpu.VMEM((D, 3 * HC), BF), pltpu.VMEM((ROWS, D), F32),
            pltpu.VMEM((D, 3 * HC), BF), pltpu.VMEM((HC, D), BF), pltpu.VMEM((FF // 2, D), BF), pltpu.VMEM((D, FF // 2), BF),
            pltpu.VMEM((HC, D), BF), pltpu.VMEM((4, 2 * PROMPT, 256), BF), pltpu.VMEM((3, 4, 4 * PSH, 256), BF),
            pltpu.VMEM((PROMPT, 128), F32), pltpu.VMEM((PROMPT, 128), F32), pltpu.VMEM((ROWS, 3 * HC), BF),
            pltpu.VMEM((ROWS, D), F32), pltpu.VMEM((384, D), F32), pltpu.VMEM((7, 104, 128), F32),
            pltpu.VMEM((64, 3 * HC), F32), pltpu.VMEM((64, FF // 2), F32), pltpu.VMEM((32, 3 * HC), F32), pltpu.VMEM((32, FF // 2), F32),
        ] + bufs
        + [pltpu.SemaphoreType.DMA((140,)), pltpu.SemaphoreType.DMA((140,)), pltpu.SemaphoreType.DMA((10,))],
        compiler_params=pltpu.CompilerParams(collective_id=1, has_side_effects=True, vmem_limit_bytes=63 << 20),
    )(*args)


def fast_body(
    tokens, valid, prompt_of, teacher, cotangent,
    ln1_gain, ln1_bias, ln2_gain, ln2_bias, qkv_weight, qkv_bias, out_weight, out_bias,
    up_weight, up_bias, down_weight, down_bias,
):
    c = lax.axis_index("core")
    z = lax.axis_index("chip")
    chips = lax.axis_size("chip")
    nh = HC // HD
    rd = down_weight.shape[0]
    device = lax.axis_index(ALL)
    pad = lambda v: jnp.pad(v.astype(F32), (0, 128 - v.shape[0]))[None]
    live_own = (valid > 0).astype(F32)
    small = jnp.concatenate(
        [
            jnp.concatenate([ln1_gain, ln1_bias, ln2_gain, ln2_bias]).astype(F32)[None],
            pad(jnp.concatenate([out_bias, down_bias])),
            pad(qkv_bias),
            pad(up_bias),
            live_own.reshape(3, 128),
            jnp.broadcast_to(prompt_of.astype(F32)[:, None], (1, 128)),
        ]
    )
    rows, w_qkv, x_own, first_own, q, kv, lse, dw_out, dw_down, dw_up, att_grad, joint, output, out_grad, value = forward(
        tokens,
        small,
        qkv_weight.reshape(32, 3, 2, HC).transpose(2, 0, 1, 3).reshape(2, 32, 3 * HC),
        out_weight,
        up_weight.reshape(32, 16, 2, 128).transpose(2, 0, 1, 3).reshape(2, 32, FF // 2),
        down_weight,
        teacher,
        cotangent,
    )
    gain1 = rows[:, 0, :32].reshape(-1)
    count_all = jnp.sum(rows[:, 4:7])
    value, s_qkv, s_out, s_up, s_down, joint = backward(
        rows, small, value, gain1[None], jnp.asarray(rotary_table(PROMPT + CONT)), lse, q, kv, att_grad, first_own, x_own,
        w_qkv, joint, dw_out, dw_down, dw_up,
    )
    own_normed, own_rstd = normalize(tokens.astype(F32))
    input_grad = out_grad + own_rstd * (
        joint
        - jnp.mean(joint, axis=-1, keepdims=True)
        - own_normed * jnp.mean(joint * own_normed, axis=-1, keepdims=True)
    )
    value = value.reshape(-1)
    shares, at = [], 0
    for size in (D, D, D, D, D, 3 * D, FF):
        own = size // lax.axis_size(ALL)
        shares.append(lax.dynamic_slice_in_dim(value, at + device * own, own))
        at += size
    loss_value = value[at] / (count_all * D)
    return (
        output, loss_value, input_grad, shares[0], shares[1], shares[2], shares[3],
        s_qkv, shares[5], s_out, shares[4], s_up, shares[6], s_down, shares[4],
    )


def solution(mesh):
    groups, seats = mesh.shape["grp"], mesh.shape["seq"]
    fine = Mesh(mesh.devices.reshape(groups, seats // 2, 2), ALL)
    rows, row = P(ALL, None), P(ALL)
    in_specs = (rows, row, row, rows, rows) + (row,) * 4 + (rows, row) * 4
    out_specs = (rows, P(), rows) + (row,) * 4 + (rows, row) * 4
    return jax.shard_map(fast_body if (groups, seats) == (4, 8) else generic_body, mesh=fine, in_specs=in_specs, out_specs=out_specs, check_vma=False)
```

```python
import functools

import jax
import jax.numpy as jnp
import numpy as np
from jax import lax
from jax.experimental import pallas as pl
from jax.experimental.pallas import tpu as pltpu
from jax.sharding import Mesh
from jax.sharding import PartitionSpec as P

D = 1024
H = 16
HD = 64
ROT = 16
FF = 4096
PSH = 64
CONT = 512
HALF = CONT // 2
HC = H // 2 * HD
EPSILON = 1e-05
NEGATIVE = -1e30
SCALE = 0.125
BF = jnp.bfloat16
F32 = jnp.float32
ALL = ("grp", "chip", "core")
CHIPS = ("grp", "chip")


def swap_cores(x):
    return lax.ppermute(x, "core", [(0, 1), (1, 0)])


def pair_rows(own):
    both = lax.all_gather(own, "core", axis=0)
    prompts = both[:, : 2 * PSH].reshape((2, 2, PSH) + own.shape[1:])
    prompts = prompts.swapaxes(0, 1).reshape((4 * PSH,) + own.shape[1:])
    return jnp.concatenate([prompts, both[:, 2 * PSH :].reshape((CONT,) + own.shape[1:])], axis=0)


def split_rows(rows):
    prompts = rows[: 4 * PSH].reshape((2, 2, PSH) + rows.shape[1:]).swapaxes(0, 1)
    prompts = prompts.reshape((2, 2 * PSH) + rows.shape[1:])
    return jnp.concatenate([prompts, rows[4 * PSH :].reshape((2, HALF) + rows.shape[1:])], axis=1)


def normalize(values):
    center = values - jnp.mean(values, axis=-1, keepdims=True)
    inverse_dev = lax.rsqrt(jnp.mean(center * center, axis=-1, keepdims=True) + EPSILON)
    return (center * inverse_dev, inverse_dev)


def rotate_heads(values, places, direction):
    halfrot = ROT // 2
    inverse = 10000.0 ** (-jnp.arange(halfrot, dtype=F32) / halfrot)
    angles = places.astype(F32)[..., None] * inverse
    cosine = jnp.cos(angles)[..., None, :]
    sine_part = direction * jnp.sin(angles)[..., None, :]
    leading = values[..., :halfrot]
    trailing = values[..., halfrot:ROT]
    return jnp.concatenate(
        [
            leading * cosine - trailing * sine_part,
            trailing * cosine + leading * sine_part,
            values[..., ROT:],
        ],
        axis=-1,
    )


def gelu_slope(values):
    return (
        0.5 * (1.0 + lax.erf(values * 0.7071067811865476))
        + values * jnp.exp(-0.5 * values * values) * 0.3989422804014327
    )


def dot(a, b, contract):
    return lax.dot_general(a, b, ((contract[:1], contract[1:]), ((), ())), preferred_element_type=F32)


def g_weights(c, qkv_weight, out_weight, up_weight, down_weight):
    r = qkv_weight.shape[0]
    mine = functools.partial(lax.dynamic_index_in_dim, index=c, keepdims=False)
    both = lambda w: lax.all_gather(w, "core", axis=0, tiled=True)
    qkv = mine(both(qkv_weight).reshape(2 * r, 3, 2, HC), axis=2).reshape(2 * r, 3 * HC)
    qkv = lax.all_gather(qkv, CHIPS, axis=0, tiled=True)
    rd = down_weight.shape[0]
    up = mine(both(up_weight).reshape(2 * r, FF // (2 * rd), 2, rd), axis=2).reshape(2 * r, FF // 2)
    up = lax.all_gather(up, CHIPS, axis=0, tiled=True)
    down = lax.all_gather(down_weight, CHIPS, axis=0, tiled=True)
    out = lax.all_gather(out_weight, ALL, axis=0, tiled=True)
    out = mine(out.reshape(2, HC, D), axis=0)
    return qkv, out, up, down


def g_small(c, rd, ln1_gain, ln1_bias, ln2_gain, ln2_bias, qkv_bias, out_bias, up_bias, down_bias):
    sizes = [v.shape[0] for v in (ln1_gain, ln1_bias, ln2_gain, ln2_bias, out_bias, down_bias, qkv_bias, up_bias)]
    packed = jnp.concatenate([ln1_gain, ln1_bias, ln2_gain, ln2_bias, out_bias, down_bias, qkv_bias, up_bias])
    rows = lax.all_gather(packed, ALL, axis=0)
    parts, at = [], 0
    for size in sizes:
        parts.append(rows[:, at : at + size].reshape(-1).astype(F32))
        at += size
    qb = lax.dynamic_index_in_dim(parts[6].reshape(3, 2, HC), c, axis=1, keepdims=False).reshape(-1)
    ub = lax.dynamic_index_in_dim(parts[7].reshape(-1, 2, rd), c, axis=1, keepdims=False).reshape(-1)
    return parts[:6] + [qb, ub]


def places_of(z, chips):
    prompt = z * 2 * PSH + jnp.arange(2 * PSH)
    return jnp.concatenate([prompt, prompt, chips * 2 * PSH + jnp.arange(CONT)])


def masks_of(z, chips, cont_valid):
    length = chips * 2 * PSH
    prompt = jnp.arange(length)[None, :] <= z * 2 * PSH + jnp.arange(2 * PSH)[:, None]
    own = jnp.arange(CONT)[None, :] <= jnp.arange(CONT)[:, None]
    own = own & (cont_valid > 0)[None, :]
    return prompt, jnp.concatenate([jnp.ones((CONT, length), bool), own], axis=1)


def g_attention(q, prompt_kv, kv, chosen, masks):
    nh = HC // HD
    chips = prompt_kv.shape[0]
    pk = prompt_kv.reshape(chips, 2, 2 * PSH, 2, nh, HD).transpose(3, 4, 1, 0, 2, 5)
    pk = pk.reshape(2, nh, 2, chips * 2 * PSH, HD)
    qh = q.reshape(-1, nh, HD).swapaxes(0, 1)
    pq = qh[:, : 4 * PSH].reshape(nh, 2, 2 * PSH, HD)
    scores = jnp.einsum("hpqd,hpkd->hpqk", pq, pk[0], preferred_element_type=F32) * SCALE
    scores = jnp.where(masks[0], scores, NEGATIVE)
    top = jnp.max(scores, axis=-1, keepdims=True)
    weights = jnp.exp(scores - top)
    total = jnp.sum(weights, axis=-1, keepdims=True)
    p_out = jnp.einsum("hpqk,hpkd->hpqd", (weights / total).astype(BF), pk[1], preferred_element_type=F32)
    p_lse = (top + jnp.log(total))[..., 0].reshape(nh, 4 * PSH)
    far = lax.dynamic_index_in_dim(pk, chosen, axis=2, keepdims=False)
    near = kv[4 * PSH :].reshape(CONT, 2, nh, HD).transpose(1, 2, 0, 3)
    ck = jnp.concatenate([far, near], axis=2)
    cq = qh[:, 4 * PSH :]
    scores = jnp.einsum("hqd,hkd->hqk", cq, ck[0], preferred_element_type=F32) * SCALE
    scores = jnp.where(masks[1], scores, NEGATIVE)
    top = jnp.max(scores, axis=-1, keepdims=True)
    weights = jnp.exp(scores - top)
    total = jnp.sum(weights, axis=-1, keepdims=True)
    c_out = jnp.einsum("hqk,hkd->hqd", (weights / total).astype(BF), ck[1], preferred_element_type=F32)
    c_lse = (top + jnp.log(total))[..., 0]
    att = jnp.concatenate([p_out.reshape(nh, 4 * PSH, HD), c_out], axis=1)
    return att.swapaxes(0, 1).reshape(-1, HC).astype(BF), jnp.concatenate([p_lse, c_lse], axis=1)


def g_attention_back(q, prompt_kv, kv, att_grad, lse, chosen, masks):
    nh = HC // HD
    chips = prompt_kv.shape[0]
    pk = prompt_kv.reshape(chips, 2, 2 * PSH, 2, nh, HD).transpose(3, 4, 1, 0, 2, 5)
    pk = pk.reshape(2, nh, 2, chips * 2 * PSH, HD)
    qh = q.reshape(-1, nh, HD).swapaxes(0, 1)
    gh = att_grad.reshape(-1, nh, HD).swapaxes(0, 1)
    pq = qh[:, : 4 * PSH].reshape(nh, 2, 2 * PSH, HD)
    pg = gh[:, : 4 * PSH].reshape(nh, 2, 2 * PSH, HD)
    ein = functools.partial(jnp.einsum, preferred_element_type=F32)

    def back(eq, ek, query, key, value, grad, mask, lse_rows):
        scores = jnp.where(mask, ein(f"{eq},{ek}->{eq[:-1]}k", query, key) * SCALE, NEGATIVE)
        probs = jnp.exp(scores - lse_rows[..., None])
        prob_grad = ein(f"{eq},{ek}->{eq[:-1]}k", grad, value)
        inner = jnp.sum(probs * prob_grad, axis=-1, keepdims=True)
        score_grad = (probs * (prob_grad - inner)).astype(BF)
        es = eq[:-1] + "k"
        dq = ein(f"{es},{ek}->{eq}", score_grad, key) * SCALE
        dk = ein(f"{es},{eq}->{ek}", score_grad, query) * SCALE
        dv = ein(f"{es},{eq}->{ek}", probs.astype(BF), grad)
        return dq, dk, dv

    dq_p, dk_p, dv_p = back("hpqd", "hpkd", pq, pk[0], pk[1], pg, masks[0], lse[:, : 4 * PSH].reshape(nh, 2, 2 * PSH))
    far = lax.dynamic_index_in_dim(pk, chosen, axis=2, keepdims=False)
    near = kv[4 * PSH :].reshape(CONT, 2, nh, HD).transpose(1, 2, 0, 3)
    ck = jnp.concatenate([far, near], axis=2)
    dq_c, dk_c, dv_c = back("hqd", "hkd", qh[:, 4 * PSH :], ck[0], ck[1], gh[:, 4 * PSH :], masks[1], lse[:, 4 * PSH :])
    length = chips * 2 * PSH
    pick = (jnp.arange(2) == chosen).astype(F32)[None, :, None, None]
    dk_p = dk_p + pick * dk_c[:, None, :length]
    dv_p = dv_p + pick * dv_c[:, None, :length]
    dq = jnp.concatenate([dq_p.reshape(nh, 4 * PSH, HD), dq_c], axis=1).swapaxes(0, 1).reshape(-1, HC)
    pair = jnp.stack([dk_p, dv_p])
    pair = pair.reshape(2, nh, 2, chips, 2 * PSH, HD).transpose(3, 2, 4, 0, 1, 5).reshape(chips * 4 * PSH, 2 * HC)
    near_grad = jnp.stack([dk_c[:, length:], dv_c[:, length:]]).transpose(2, 0, 1, 3).reshape(CONT, 2 * HC)
    return dq, pair, near_grad


def generic_body(
    tokens, valid, prompt_of, teacher, cotangent,
    ln1_gain, ln1_bias, ln2_gain, ln2_bias, qkv_weight, qkv_bias, out_weight, out_bias,
    up_weight, up_bias, down_weight, down_bias, stop=None,
):
    c = lax.axis_index("core")
    z = lax.axis_index("chip")
    chips = lax.axis_size("chip")
    nh = HC // HD
    rd = down_weight.shape[0]
    device = lax.axis_index(ALL)
    w_qkv, w_out, w_up, w_down = g_weights(c, qkv_weight, out_weight, up_weight, down_weight)
    gain1, bias1, gain2, bias2, b_out, b_down, b_qkv, b_up = g_small(
        c, rd, ln1_gain, ln1_bias, ln2_gain, ln2_bias, qkv_bias, out_bias, up_bias, down_bias
    )
    x = pair_rows(tokens).astype(F32)
    normed, rstd = normalize(x)
    first_in = (normed * gain1 + bias1).astype(BF)
    second_in = (normed * gain2 + bias2).astype(BF)
    projected = dot(first_in, w_qkv, (1, 0)) + b_qkv
    places = places_of(z, chips)
    turn = lambda v, d: rotate_heads(v.reshape(-1, nh, HD), places, d).reshape(-1, HC)
    q = turn(projected[:, :HC], 1.0).astype(BF)
    k = turn(projected[:, HC : 2 * HC], 1.0).astype(BF)
    kv = jnp.concatenate([k, projected[:, 2 * HC :].astype(BF)], axis=1)
    prompt_kv = lax.all_gather(kv[: 4 * PSH].reshape(2, 2 * PSH, 2 * HC), "chip", axis=0)
    cont_valid = lax.all_gather(valid[2 * PSH :], "core", axis=0, tiled=True)
    masks = masks_of(z, chips, cont_valid)
    chosen = prompt_of[0]
    attended, lse = g_attention(q, prompt_kv, kv, chosen, masks)
    hidden_pre = dot(second_in, w_up, (1, 0)) + b_up
    activated = jax.nn.gelu(hidden_pre, approximate=False).astype(BF)
    partial = dot(attended, w_out, (1, 0)) + dot(activated, w_down, (1, 0))
    halves = split_rows(partial)
    take = lambda a: lax.dynamic_index_in_dim(a, c, axis=0, keepdims=False)
    give = lambda a: lax.dynamic_index_in_dim(a, 1 - c, axis=0, keepdims=False)
    output = tokens.astype(F32) + take(halves) + swap_cores(give(halves)) + b_out + b_down
    live = (valid > 0).astype(F32)[:, None]
    missed = output - teacher.astype(F32)
    count_all, squared_all = lax.psum((jnp.sum(live), jnp.sum(live * missed * missed)), ALL)
    loss_value = squared_all / (count_all * D)
    out_grad = cotangent.astype(F32) + 2.0 / (count_all * D) * live * missed
    out_low = pair_rows(out_grad.astype(BF))
    if stop == "fwd":
        return output, out_grad, out_low, attended, lse, activated, q, kv, first_in, second_in
    out_bias_grad = jnp.sum(out_grad.astype(BF).astype(F32), axis=0)
    dw_out = dot(attended, out_low, (0, 0))
    dw_down = dot(activated, out_low, (0, 0))
    att_grad = dot(out_low, w_out, (1, 1)).astype(BF)
    hidden_grad = (dot(out_low, w_down, (1, 1)) * gelu_slope(hidden_pre)).astype(BF)
    dw_up = dot(second_in, hidden_grad, (0, 0))
    db_up = jnp.sum(hidden_grad.astype(F32), axis=0)
    second_grad = dot(hidden_grad, w_up, (1, 1))
    dq, pair, near = g_attention_back(q, prompt_kv, kv, att_grad, lse, chosen, masks)
    own_pair = lax.psum_scatter(pair.astype(BF), "chip", scatter_dimension=0, tiled=True).astype(F32)
    pair = jnp.concatenate([own_pair, near], axis=0)
    projected_grad = jnp.concatenate([turn(dq, -1.0), turn(pair[:, :HC], -1.0), pair[:, HC:]], axis=1).astype(BF)
    dw_qkv = dot(first_in, projected_grad, (0, 0))
    db_qkv = jnp.sum(projected_grad.astype(F32), axis=0)
    first_grad = dot(projected_grad, w_qkv, (1, 1))
    if stop == "bwd":
        return dw_out, dw_down, dw_up, dw_qkv, second_grad, first_grad, projected_grad, hidden_grad, att_grad
    joint = first_grad * gain1 + second_grad * gain2
    halves = split_rows(joint)
    joint = take(halves) + swap_cores(give(halves))
    own_normed = take(split_rows(normed))
    own_rstd = take(split_rows(rstd))
    input_grad = out_grad + own_rstd * (
        joint
        - jnp.mean(joint, axis=-1, keepdims=True)
        - own_normed * jnp.mean(joint * own_normed, axis=-1, keepdims=True)
    )
    wide = lambda v, n: jnp.zeros((v.shape[0], 2, v.shape[1]), F32).at[:, c].set(v).reshape(-1)
    small = jnp.concatenate(
        [
            jnp.sum(first_grad * normed, axis=0),
            jnp.sum(first_grad, axis=0),
            jnp.sum(second_grad * normed, axis=0),
            jnp.sum(second_grad, axis=0),
            out_bias_grad,
            wide(db_qkv.reshape(3, HC), 3),
            wide(db_up.reshape(-1, rd), 16),
        ]
    )
    small = lax.psum(small, ALL)
    shares, at = [], 0
    for size in (D, D, D, D, D, 3 * D, FF):
        own = size // lax.axis_size(ALL)
        shares.append(lax.dynamic_slice_in_dim(small, at + device * own, own))
        at += size
    rs = lambda v: lax.psum_scatter(v.astype(BF), CHIPS, scatter_dimension=0, tiled=True).astype(F32)
    r = qkv_weight.shape[0]
    s_qkv = rs(dw_qkv).reshape(2, r, 3, HC)
    s_up = rs(dw_up).reshape(2, r, FF // (2 * rd), rd)
    s_down = rs(dw_down)
    pairs = lambda own, other, axis: jnp.where(c == 0, jnp.stack([own, other], axis), jnp.stack([other, own], axis))
    s_qkv = pairs(take(s_qkv), swap_cores(give(s_qkv)), 2).reshape(r, 3 * D)
    s_up = pairs(take(s_up), swap_cores(give(s_up)), 2).reshape(r, FF)
    o = dw_out.reshape(H // 2, -1, 2, r, D)
    o_own = lax.dynamic_index_in_dim(o, c, axis=2, keepdims=False)
    o_other = swap_cores(lax.dynamic_index_in_dim(o, 1 - c, axis=2, keepdims=False))
    s_out = rs(pairs(o_own, o_other, 0).reshape(-1, D))
    return (
        output.astype(BF), loss_value, input_grad, shares[0], shares[1], shares[2], shares[3],
        s_qkv, shares[5], s_out, shares[4], s_up, shares[6], s_down, shares[4],
    )


MESH_ID = pl.DeviceIdType.MESH
RANKS = 4


class Net:
    def __init__(self, send, recv):
        self.g, self.z, self.c = (lax.axis_index(a) for a in ALL)
        self.y, self.x = self.g // 2, self.g % 2
        self.send, self.recv, self.used = send, recv, 0
        self.chip = self.g * RANKS + self.z
        self.core = {"grp": self.g, "chip": self.z, "core": 1 - self.c}
        self.right = {"grp": self.y * 2 + 1 - self.x, "chip": self.z, "core": self.c}
        self.up = {"grp": (1 - self.y) * 2 + self.x, "chip": self.z, "core": self.c}
        self.line = [{"grp": self.g, "chip": (self.z + j) % RANKS, "core": self.c} for j in (1, 2, 3)]
        self.sent = []

    def enter(self):
        barrier = pltpu.get_barrier_semaphore()
        for peer in [self.core, self.right, self.up] + self.line:
            pl.semaphore_signal(barrier, inc=1, device_id=peer, device_id_type=MESH_ID)
        pl.semaphore_wait(barrier, 6)

    def copy(self, src, dst, peer):
        i = self.used
        self.used += 1
        made = pltpu.make_async_remote_copy(
            src_ref=src, dst_ref=dst, send_sem=self.send.at[i], recv_sem=self.recv.at[i],
            device_id=peer, device_id_type=MESH_ID,
        )
        made.start()
        self.sent.append(made)
        return made

    def same(self, view, peer):
        return self.copy(view, view, peer)

    def settle(self, made):
        made.wait_recv()
        made.wait_send()
        self.sent = [m for m in self.sent if m is not made]

    def leave(self):
        for made in self.sent:
            made.wait_send()
        self.sent = []


def gather_steps(net, dst, rb, col, width, before):
    a, b, both = pl.ds(col, width // 2), pl.ds(col + width // 2, width // 2), pl.ds(col, width)
    quad = 4 * rb
    held = {}

    def line():
        for made in before:
            made.wait_recv()
        view = dst.at[pl.ds(net.chip * rb, rb), both]
        held[0] = [net.same(view, peer) for peer in net.line]

    def first():
        for made in held[0]:
            made.wait_recv()
        rows = pl.ds(net.g * quad, quad)
        held[1] = [net.same(dst.at[rows, a], net.right), net.same(dst.at[rows, b], net.up)]

    def second():
        for made in held[1]:
            made.wait_recv()
        held[2] = [net.same(dst.at[pl.ds(net.y * 2 * quad, 2 * quad), a], net.up)]
        for y in range(2):
            held[2].append(net.same(dst.at[pl.ds((y * 2 + net.x) * quad, quad), b], net.right))

    def last():
        for made in held[2]:
            made.wait_recv()

    return [line, first, second, last]


def small_steps(net, rows):
    held = {}

    def pair():
        held[0] = [net.same(rows.at[net.chip * 2 + net.c], net.core)]

    def line():
        held[0][0].wait_recv()
        held[1] = [net.same(rows.at[pl.ds(net.chip * 2, 2)], peer) for peer in net.line]

    def first():
        for made in held[1]:
            made.wait_recv()
        held[2] = [net.same(rows.at[pl.ds(net.g * 8, 8)], net.right)]

    def second():
        held[2][0].wait_recv()
        held[3] = [net.same(rows.at[pl.ds(net.y * 16, 16)], net.up)]

    def last():
        held[3][0].wait_recv()

    return [pair, line, first, second, last]


VM = pl.BlockSpec(memory_space=pltpu.VMEM)
HBM = pl.BlockSpec(memory_space=pl.ANY)
PROMPT = RANKS * 2 * PSH
KEYS = 2 * PROMPT + CONT
ROWS = 4 * PSH + CONT


def nt(a, b):
    return lax.dot_general(a, b, (((1,), (1,)), ((), ())), preferred_element_type=F32)


def nn(a, b):
    return lax.dot_general(a, b, (((1,), (0,)), ((), ())), preferred_element_type=F32)


def tn(a, b):
    return lax.dot_general(a, b, (((0,), (0,)), ((), ())), preferred_element_type=F32)


def tile_at(i, size):
    return pl.ds(pl.multiple_of(i * size, size), size)


def move_rows(dst, to, src, at, count, tile=32):
    @pl.loop(0, count // tile)
    def _(i):
        step = pl.multiple_of(i * tile, tile)
        dst[pl.ds(pl.multiple_of(to + step, tile), tile), :] = src[pl.ds(pl.multiple_of(at + step, tile), tile), :]


def spread_row(rows, field, index, owner, lane, size):
    table = rows[:, field, :].astype(BF)
    lanes = lax.broadcasted_iota(jnp.int32, (128, size), 0)
    pick = (lanes == index[lane : lane + 1, :size]).astype(F32).astype(BF)
    wide = nn(table, pick)
    owners = lax.broadcasted_iota(jnp.int32, (rows.shape[0], size), 0)
    return jnp.sum(jnp.where(owners == index[owner : owner + 1, :size], wide, 0.0), axis=0, keepdims=True)


def norm_rows(x):
    x = x.astype(F32)
    center = x - jnp.mean(x, axis=-1, keepdims=True)
    return center * lax.rsqrt(jnp.mean(center * center, axis=-1, keepdims=True) + EPSILON)


def turn(value, table, sign):
    cos, low_sin, high_sin = (table[:, 128 * i : 128 * i + 128] for i in range(3))
    out = []
    for j in range(value.shape[1] // 128):
        v = value[:, 128 * j : 128 * j + 128]
        other = pltpu.roll(v, 120, 1) * low_sin + pltpu.roll(v, 8, 1) * high_sin
        out.append(v * cos + sign * other)
    return out[0] if len(out) == 1 else jnp.concatenate(out, axis=1)


def rotary_table(length):
    half = ROT // 2
    inverse = (10000.0 ** (-np.arange(half, dtype=np.float32) / half)).astype(np.float32)
    angles = (np.arange(length, dtype=np.float32)[:, None] * inverse).astype(np.float64)
    cos, sin = np.cos(angles), np.sin(angles)
    table = np.zeros((length, 3, 2, HD), np.float32)
    table[:, 0] = 1.0
    for head in range(2):
        table[:, 0, head, :half] = cos
        table[:, 0, head, half:ROT] = cos
        table[:, 1, head, :half] = -sin
        table[:, 2, head, half:ROT] = sin
    return table.reshape(length, 384)


def index_table(rd):
    n = np.arange(2048)
    table = np.zeros((2, 16, 2048), np.int32)
    for c in range(2):
        col = np.minimum(n // HC, 2) * D + c * HC + n % HC
        table[c, 0], table[c, 1] = col // 96, col % 96
        unit = n // rd * (2 * rd) + c * rd + n % rd
        table[c, 2], table[c, 3] = unit // rd, unit % rd
        table[c, 4] = n // 32 % 32
        for i in range(4):
            table[c, 8 + i] = n % 32 + 32 * i
    return table


def seen(keys_at, queries_at, shape, length=None):
    keys = lax.broadcasted_iota(jnp.int32, shape, 0) + keys_at
    queries = lax.broadcasted_iota(jnp.int32, shape, 1) + queries_at
    mask = keys <= queries
    return mask if length is None else mask & (keys < length)


def head_lanes(rows):
    return lax.broadcasted_iota(jnp.int32, (rows, 128), 1) < HD


def attend(query, keys, values, masks, head):
    lanes = head_lanes(query.shape[0])
    own = jnp.where(lanes if head == 0 else ~lanes, query.astype(F32) * SCALE, 0.0).astype(BF)
    scores = [nt(k, own) for k in keys]
    scores = [s if m is None else jnp.where(m, s, NEGATIVE) for s, m in zip(scores, masks)]
    top = functools.reduce(jnp.maximum, [jnp.max(s, axis=0, keepdims=True) for s in scores])
    weights = [jnp.exp(s - top) for s in scores]
    total = sum(jnp.sum(w, axis=0, keepdims=True) for w in weights)
    share = 1.0 / total
    out = sum(tn(v, (w * share).astype(BF)) for v, w in zip(values, weights))
    return out[head * HD : head * HD + HD], top + jnp.log(total)


GATHER_ORDER = (
    (0, 0), (0, 1), (6, 0), (6, 0), (1, 0), (0, 2), (0, 3), (1, 1), (6, 0), (2, 0), (6, 0), (6, 0),
    (2, 1), (6, 0), (6, 0), (6, 0), (1, 2), (0, 4), (4, 0), (1, 3), (3, 0), (6, 0), (6, 0), (2, 2),
    (5, 0), (0, 5), (2, 3), (3, 1), (1, 4), (4, 1), (6, 0), (6, 0), (5, 1), (0, 6), (4, 2), (1, 5),
    (2, 4), (3, 2), (6, 0), (6, 0), (3, 3), (5, 2), (0, 7), (2, 5), (6, 0), (1, 6), (4, 3), (6, 0),
    (3, 4), (1, 7), (0, 8), (2, 6), (5, 3), (4, 4), (3, 5), (2, 7), (5, 4), (0, 9), (4, 5), (1, 8),
    (3, 6), (6, 0), (6, 0), (6, 0), (6, 0), (6, 0), (6, 0), (3, 7), (2, 8), (6, 0), (6, 0), (5, 5),
    (0, 10), (6, 0), (1, 9), (0, 11), (6, 0), (6, 0), (6, 0), (6, 0), (6, 0), (3, 8), (2, 9), (6, 0),
    (6, 0), (6, 0), (1, 10), (1, 11), (6, 0), (6, 0), (6, 0), (3, 9), (6, 0), (6, 0), (2, 10), (2, 11),
    (6, 0), (6, 0), (6, 0), (6, 0), (3, 10), (3, 11),
)


def forward_kernel(
    tokens, small, qkv, out, up, down, rotary, index, teacher, cotangent,
    rows, h_w_qkv, h_x, h_first, h_q, h_kv, lse, h_dw_out, h_dw_down, h_dw_up, att_grad, joint, output, out_grad, value,
    w_qkv, x_own, first_own, q, kv, dw_out, dw_down, dw_up, w_out, w_up, w_down, second_in, attended, activated, slope, peer, low, x_all, first_in, spread, swapped, crossed, send, recv, local,
):
    net = Net(send, recv)
    c, z, chip = net.c, net.z, net.chip
    net.enter()
    for p in range(2):
        move_rows(x_all, p * PROMPT + z * 2 * PSH + c * PSH, tokens, p * PSH, PSH)
    move_rows(x_all, 2 * PROMPT + c * HALF, tokens, 2 * PSH, HALF)
    rows[chip * 2 + c] = small[...]
    pieces_at = [pl.ds(p * PROMPT + z * 2 * PSH + c * PSH, PSH) for p in range(2)]
    smalls = small_steps(net, rows)
    smalls[0]()
    mates = [net.same(x_all.at[piece], net.core) for piece in pieces_at + [pl.ds(2 * PROMPT + c * HALF, HALF)]]
    half_rows = pl.ds(pl.multiple_of(chip * 64 + c * 32, 32), 32)
    given = pl.ds(0, 32)
    for i in range(3):
        cols = slice(HC * i, HC * i + HC)
        w_qkv[half_rows, cols] = qkv[:, pl.ds(pl.multiple_of(i * D + c * HC, 128), HC)]
        swapped[given, cols] = qkv[:, pl.ds(pl.multiple_of(i * D + (1 - c) * HC, 128), HC)]
    from_core = {}
    from_core["qkv"] = net.copy(swapped.at[given, pl.ds(0, 3 * HC)], w_qkv.at[half_rows], net.core)
    given = pl.ds(32, 32)
    for i in range(16):
        cols = slice(128 * i, 128 * i + 128)
        w_up[half_rows, cols] = up[:, pl.ds(pl.multiple_of((2 * i + c) * 128, 128), 128)]
        swapped[given, cols] = up[:, pl.ds(pl.multiple_of((2 * i + 1 - c) * 128, 128), 128)]
    from_core["up"] = net.copy(swapped.at[given, pl.ds(0, FF // 2)], w_up.at[half_rows], net.core)
    w_down[pl.ds(pl.multiple_of(chip * 128, 128), 128), :] = down[...]
    spread[pl.ds(pl.multiple_of(chip * 32, 32), 32), :] = out[...]
    none = []
    tasks = [gather_steps(net, w_up, 64, 512 * i, 512, [] if i else [from_core["up"]]) for i in range(4)]
    tasks += [gather_steps(net, w_qkv, 64, 512 * i, 512, [] if i else [from_core["qkv"]]) for i in range(3)]
    tasks += [gather_steps(net, spread, 32, 0, 1024, [])]
    tasks += [gather_steps(net, w_down, 128, 256 * i, 256, []) for i in range(4)]
    pieces, done = [], set()

    def after(needs, work, *args):
        pieces.append((set(needs), work, args))

    def run_pieces(count):
        while count and pieces and pieces[0][0] <= done:
            needs, work, args = pieces.pop(0)
            work(*args)
            count -= 1

    held = {}

    def learn():
        for made in mates:
            made.wait_recv()
        places = index.at[c]
        held["norm"] = [spread_row(rows, 0, places, 4, 8 + i, D) for i in range(4)]
        held["qkv"] = spread_row(rows, 2, places, 0, 1, 3 * HC)
        held["length"] = jnp.sum(jnp.sum(rows[pl.ds(chip * 2, 2), 5:7, :], axis=0), keepdims=True).astype(jnp.int32)
        held["up"] = spread_row(rows, 3, places, 2, 3, FF // 2)

    def own_norms(first_tile, count):
        gain1, bias1, gain2, bias2 = held["norm"]

        @pl.loop(first_tile, first_tile + count)
        def _(i):
            prompt = (i // 2) * PROMPT + z * 2 * PSH + (i % 2) * 64
            here = pl.ds(pl.multiple_of(jnp.where(i < 4, prompt, 2 * PROMPT + (i - 4) * 64), 64), 64)
            at = tile_at(i, 64)
            normed = norm_rows(x_all[here, :])
            x_own[at, :] = x_all[here, :]
            narrow = (normed * gain1 + bias1).astype(BF)
            first_in[here, :] = narrow
            first_own[at, :] = narrow
            second_in[at, :] = (normed * gain2 + bias2).astype(BF)

    relays = {}
    prompt_pieces = [(j, p) for j in (1, 2, 3) for p in range(2)]

    def send_tokens(k):
        j, p = prompt_pieces[k]
        held[k] = net.same(x_all.at[pieces_at[p]], net.line[j - 1])

    def relay_tokens(k):
        j, p = prompt_pieces[k]
        held[k].wait_recv()
        relays[k] = net.same(x_all.at[pl.ds(p * PROMPT + (z + RANKS - j) % RANKS * 2 * PSH + c * PSH, PSH)], net.core)

    def other_norms(k):
        j, p = prompt_pieces[k]
        relays[k].wait_recv()
        gain1, bias1 = held["norm"][:2]

        @pl.loop(0, 2)
        def _(i):
            here = pl.ds(pl.multiple_of(p * PROMPT + (z + RANKS - j) % RANKS * 2 * PSH + i * 64, 64), 64)
            first_in[here, :] = (norm_rows(x_all[here, :]) * gain1 + bias1).astype(BF)

    def hidden(j):
        cols = slice(256 * j, 256 * j + 256)
        b_up = held["up"]

        @pl.loop(0, ROWS // 128)
        def _(i):
            at = tile_at(i, 128)
            pre = nn(second_in[at, :], w_up[:, cols]) + b_up[:, cols]
            gate = 0.5 * (1.0 + lax.erf(pre * 0.7071067811865476))
            activated[at, cols] = (pre * gate).astype(BF)
            slope[at, cols] = (gate + pre * jnp.exp(-0.5 * pre * pre) * 0.3989422804014327).astype(slope.dtype)

    def key_rows(i):
        at = slice(256 * i, 256 * i + 256)
        here = first_in[at, :]
        place = (i % 2) * 256 if i < 4 else PROMPT + (i - 4) * 256
        table = rotary[place : place + 256, :]
        for j in range(4):
            cols = slice(HC + 256 * j, HC + 256 * j + 256)
            made = nn(here, w_qkv[:, cols]) + held["qkv"][:, cols]
            kv[at, 256 * j : 256 * j + 256] = (turn(made, table, 1.0) if j < 2 else made).astype(BF)

    def query_rows(first_tile, count):
        @pl.loop(first_tile, first_tile + count)
        def _(i):
            place = pl.multiple_of(jnp.where(i < 2, z * 2 * PSH, PROMPT + (i - 2) * 128), 128)
            at = tile_at(i, 128)
            here = first_own[at, :]
            table = rotary[pl.ds(place, 128), :]
            for j in range(2):
                cols = slice(256 * j, 256 * j + 256)
                q[at, cols] = turn(nn(here, w_qkv[:, cols]) + held["qkv"][:, cols], table, 1.0).astype(BF)

    second = jnp.broadcast_to(small[7:8, :], (PROMPT, 128)) > 0.5

    def attend_pair(pair, part):
        k_at, v_at = pl.ds(128 * pair, 128), pl.ds(HC + 128 * pair, 128)
        prompts = [(kv[p * PROMPT : (p + 1) * PROMPT, k_at], kv[p * PROMPT : (p + 1) * PROMPT, v_at]) for p in range(2)]

        def put(row, size, key_list, value_list, masks):
            outs = []
            for head in range(2):
                o, stat = attend(q[row : row + size, k_at], key_list, value_list, masks, head)
                outs.append(o)
                lse[2 * pair + head, :, row : row + size] = stat
            attended[row : row + size, k_at] = jnp.concatenate(outs, axis=0).T.astype(BF)

        for p in range(2) if part == 0 else ():
            put(p * 128, 128, [prompts[p][0]], [prompts[p][1]], [seen(0, z * 2 * PSH, (PROMPT, 128))])
        chosen = [jnp.where(second, b.astype(F32), a.astype(F32)).astype(BF) for a, b in zip(*prompts)]
        for i in ((), (0, 1), (2, 3))[part]:
            near = 128 * i + 128
            put(
                256 + 128 * i, 128,
                [chosen[0], kv[2 * PROMPT : 2 * PROMPT + near, k_at]],
                [chosen[1], kv[2 * PROMPT : 2 * PROMPT + near, v_at]],
                [None, seen(0, 128 * i, (near, 128), held["length"])],
            )

    after([], smalls[1])
    after([(0, 1)], smalls[2])
    after([(1, 0)], smalls[3])
    after([(2, 0)], smalls[4])
    after([(2, 0)], learn)
    for i in range(3):
        after([], own_norms, 4 * i, 4)
    for j in range(8):
        after([(3, j // 2)], hidden, j)
    for i in range(2):
        after([(3, 6)], query_rows, 3 * i, 3)
    for i in range(2):
        after([(3, 6)], key_rows, 4 + i)
    for k in range(6):
        after([(5, k)], other_norms, k)
    for i in range(4):
        after([(5, 5)], key_rows, i)
    for pair in range(4):
        for part in range(3):
            after([], attend_pair, pair, part)
    for event in GATHER_ORDER:
        step, t = event
        if step < 4:
            tasks[t][step]()
        elif step == 4:
            send_tokens(t)
        elif step == 5:
            relay_tokens(t)
        else:
            run_pieces(1)
        done.add(event)
    run_pieces(len(pieces))
    shipped = []

    def ship(src, dst):
        made = pltpu.make_async_copy(src, dst, local.at[len(shipped)])
        made.start()
        shipped.append(made)

    for src, dst in ((w_qkv, h_w_qkv), (x_own, h_x), (first_own, h_first), (q, h_q), (kv, h_kv)):
        ship(src, dst)
    length = held["length"]
    gain2 = held["norm"][2]
    places = index.at[c]
    given = pl.ds(pl.multiple_of((1 - c) * 256, 256), 256)
    swap = net.copy(spread.at[given], crossed, net.core)
    swap.wait_recv()
    for h in range(8):
        w_out[pl.ds(pl.multiple_of(h * 64 + c * 32, 32), 32), :] = spread[pl.ds(pl.multiple_of(c * 256 + h * 32, 32), 32), :]
        w_out[pl.ds(pl.multiple_of(h * 64 + (1 - c) * 32, 32), 32), :] = crossed[h * 32 : h * 32 + 32, :]

    def share(at, size):
        here = pl.ds(pl.multiple_of(at, 128), size)
        joint[here, :] = nn(attended[here, :], w_out[...]) + nn(activated[here, :], w_down[...])

    def chip_range(i, owner):
        return ((owner * PSH, PSH, 0), (2 * PSH + owner * PSH, PSH, PSH), (4 * PSH + owner * HALF, HALF, 2 * PSH))[i]

    def pass_share(i):
        at, size, to = chip_range(i, 1 - c)
        return net.copy(joint.at[pl.ds(pl.multiple_of(at, 64), size)], peer.at[pl.ds(to, size)], net.core)

    share(4 * PSH + (1 - c) * HALF, HALF)
    passed = [pass_share(2)]
    share(0, 256)
    passed += [pass_share(0), pass_share(1)]
    share(4 * PSH + c * HALF, HALF)
    for made in passed:
        net.settle(made)
    count = jnp.sum(jnp.sum(rows[:, 4:7, :], axis=0), keepdims=True)
    pull = 2.0 / (count * D)
    bias = spread_row(rows, 1, places, 4, 8, D) + spread_row(rows, 1, places, 4, 9, D)
    value[...] = jnp.zeros_like(value)
    squared, low_sum = jnp.zeros((1, D), F32), jnp.zeros((1, D), F32)
    lows = []
    for i in range(3):
        at, size, to = chip_range(i, c)

        def rows_out(k, sums, at=at, to=to, i=i):
            here = pl.ds(pl.multiple_of(at + k * 64, 64), 64)
            own = pl.ds(pl.multiple_of(to + k * 64, 64), 64)
            result = tokens[own, :].astype(F32) + joint[here, :] + peer[own, :] + bias
            missed = result - teacher[own, :].astype(F32)
            if i == 2:
                step = lax.broadcasted_iota(jnp.int32, (64, D), 0) + (c * HALF + k * 64)
                missed = jnp.where(step < length, missed, 0.0)
            output[own, :] = result.astype(BF)
            grad = cotangent[own, :].astype(F32) + pull * missed
            out_grad[own, :] = grad
            rounded = grad.astype(BF)
            low[here, :] = rounded
            return (
                sums[0] + jnp.sum(missed * missed, axis=0, keepdims=True),
                sums[1] + jnp.sum(rounded.astype(F32), axis=0, keepdims=True),
            )

        squared, low_sum = lax.fori_loop(0, size // 64, rows_out, (squared, low_sum))
        lows.append(net.same(low.at[pl.ds(pl.multiple_of(at, 64), size)], net.core))
    total = jnp.sum(squared, keepdims=True)
    value[96:97, :] = jnp.broadcast_to(total, (1, 128))

    def put_row(row, vector):
        for k in range(vector.shape[1] // 128):
            value[row + k : row + k + 1, :] = vector[:, 128 * k : 128 * k + 128]

    put_row(32, low_sum)
    for made in lows:
        made.wait_recv()

    @pl.loop(0, 8)
    def _(i):
        at = tile_at(i, 256)
        dw_down[at, :] = tn(activated[:, at], low[...]).astype(BF)

    ship(dw_down, h_dw_down)

    @pl.loop(0, 2)
    def _(i):
        at = tile_at(i, 256)
        dw_out[at, :] = tn(attended[:, at], low[...]).astype(BF)

    ship(dw_out, h_dw_out)

    @pl.loop(0, ROWS // 128)
    def _(i):
        at = tile_at(i, 128)
        att_grad[at, :] = nt(low[at, :], w_out[...]).astype(BF)

    for j in range(8):
        cols = slice(256 * j, 256 * j + 256)

        def hidden_rows(i, total, cols=cols):
            at = tile_at(i, 256)
            grad = (nt(low[at, :], w_down[cols, :]) * slope[at, cols].astype(F32)).astype(BF)
            activated[at, cols] = grad
            return total + jnp.sum(grad.astype(F32), axis=0, keepdims=True)

        total = lax.fori_loop(0, ROWS // 256, hidden_rows, jnp.zeros((1, 256), F32))
        for k in range(2):
            value[pl.ds(64 + 4 * j + 2 * k + c, 1), :] = total[:, 128 * k : 128 * k + 128]

    @pl.loop(0, 4)
    def _(i):
        at = tile_at(i, 256)
        for k in range(2):
            cols = slice(1024 * k, 1024 * k + 1024)
            dw_up[at, cols] = tn(second_in[:, at], activated[:, cols]).astype(BF)

    ship(dw_up, h_dw_up)

    def second_rows(i, sums):
        at = tile_at(i, 128)
        grad = nt(activated[at, :], w_up[...])
        joint[at, :] = grad * gain2
        normed = norm_rows(x_own[at, :])
        return (
            sums[0] + jnp.sum(grad * normed, axis=0, keepdims=True),
            sums[1] + jnp.sum(grad, axis=0, keepdims=True),
        )

    sums = lax.fori_loop(0, ROWS // 128, second_rows, (jnp.zeros((1, D), F32), jnp.zeros((1, D), F32)))
    put_row(16, sums[0])
    put_row(24, sums[1])
    for made in shipped:
        made.wait()
    net.leave()


def forward(tokens, small, qkv, out, up, down, teacher, cotangent):
    shape = jax.ShapeDtypeStruct
    return pl.pallas_call(
        forward_kernel,
        out_shape=(
            shape((32, 8, 128), F32), shape((D, 3 * HC), BF), shape((ROWS, D), BF), shape((ROWS, D), BF), shape((ROWS, HC), BF),
            shape((KEYS, 2 * HC), BF), shape((8, 1, ROWS), F32), shape((HC, D), BF), shape((FF // 2, D), BF), shape((D, FF // 2), BF),
            shape((ROWS, HC), BF), shape((ROWS, D), F32), shape((384, D), BF), shape((384, D), F32), shape((104, 128), F32),
        ),
        in_specs=[VM] * 10,
        out_specs=(VM,) + (HBM,) * 5 + (VM,) + (HBM,) * 3 + (VM,) * 5,
        scratch_shapes=[
            pltpu.VMEM((D, 3 * HC), BF), pltpu.VMEM((ROWS, D), BF), pltpu.VMEM((ROWS, D), BF), pltpu.VMEM((ROWS, HC), BF),
            pltpu.VMEM((KEYS, 2 * HC), BF), pltpu.VMEM((HC, D), BF), pltpu.VMEM((FF // 2, D), BF), pltpu.VMEM((D, FF // 2), BF),
            pltpu.VMEM((HC, D), BF), pltpu.VMEM((D, FF // 2), BF), pltpu.VMEM((FF // 2, D), BF), pltpu.VMEM((ROWS, D), BF),
            pltpu.VMEM((ROWS, HC), BF), pltpu.VMEM((ROWS, FF // 2), BF), pltpu.VMEM((ROWS, FF // 2), BF), pltpu.VMEM((384, D), F32),
            pltpu.VMEM((ROWS, D), BF), pltpu.VMEM((KEYS, D), BF), pltpu.VMEM((KEYS, D), BF), pltpu.VMEM((HC, D), BF),
            pltpu.VMEM((64, FF // 2), BF), pltpu.VMEM((256, D), BF), pltpu.SemaphoreType.DMA((140,)), pltpu.SemaphoreType.DMA((140,)), pltpu.SemaphoreType.DMA((8,)),
        ],
        compiler_params=pltpu.CompilerParams(collective_id=0, has_side_effects=True, vmem_limit_bytes=63 << 20),
    )(tokens, small, qkv, out, up, down, jnp.asarray(rotary_table(PROMPT + CONT)), jnp.asarray(index_table(128)), teacher, cotangent)


def add_rows(dst, dst_rows, src, src_rows, count, cols, tile):
    @pl.loop(0, count // tile)
    def _(i):
        to = pl.ds(pl.multiple_of(dst_rows + i * tile, tile), tile)
        more = src[pl.ds(pl.multiple_of(src_rows + i * tile, tile), tile), cols].astype(F32)
        dst[to, :] = (dst[to, :].astype(F32) + more).astype(dst.dtype)


def scatter_steps(net, src, rb, col, width, before, got_a, got_b, got_z, put):
    half = width // 2
    a, b, both = pl.ds(col, half), pl.ds(col + half, half), pl.ds(col, width)
    quad = 4 * rb
    tile = min(64, rb)
    at = lambda y, x: pl.ds((y * 2 + x) * quad, quad)
    held = {}

    def first():
        for made in before:
            made.wait()
        rows = pl.ds((1 - net.y) * 2 * quad, 2 * quad)
        held[0] = [net.copy(src.at[rows, a], got_a.at[pl.ds(0, 2 * quad)], net.up)]
        for y in range(2):
            held[0].append(net.copy(src.at[at(y, 1 - net.x), b], got_b.at[pl.ds(y * quad, quad)], net.right))

    def second():
        for made in held[0]:
            made.wait_recv()
        add_rows(got_a, (1 - net.x) * quad, src, (net.y * 2 + 1 - net.x) * quad, quad, a, tile)
        add_rows(got_b, (1 - net.y) * quad, src, ((1 - net.y) * 2 + net.x) * quad, quad, b, tile)
        held[1] = [
            net.copy(got_a.at[pl.ds((1 - net.x) * quad, quad)], got_a.at[pl.ds(2 * quad, quad)], net.right),
            net.copy(got_b.at[pl.ds((1 - net.y) * quad, quad)], got_b.at[pl.ds(2 * quad, quad)], net.up),
        ]
        add_rows(got_a, net.x * quad, src, (net.y * 2 + net.x) * quad, quad, a, tile)
        add_rows(got_b, net.y * quad, src, (net.y * 2 + net.x) * quad, quad, b, tile)

    def third():
        for made in held[1]:
            made.wait_recv()
        add_rows(got_a, net.x * quad, got_a, 2 * quad, quad, slice(None), tile)
        add_rows(got_b, net.y * quad, got_b, 2 * quad, quad, slice(None), tile)
        held[2] = []
        for j in (1, 2, 3):
            there = (net.z + j) % RANKS * rb
            peer = net.line[j - 1]
            held[2].append(net.copy(got_a.at[pl.ds(net.x * quad + there, rb)], got_z.at[j - 1, :, pl.ds(0, half)], peer))
            held[2].append(net.copy(got_b.at[pl.ds(net.y * quad + there, rb)], got_z.at[j - 1, :, pl.ds(half, half)], peer))

    def last():
        for made in held[2]:
            made.wait_recv()
        for k, (got, way) in enumerate(((got_a, net.x), (got_b, net.y))):
            cols = slice(k * half, k * half + half)

            @pl.loop(0, rb // tile)
            def _(i):
                rows = pl.ds(pl.multiple_of(way * quad + net.z * rb + i * tile, tile), tile)
                value = got[rows, :].astype(F32)
                for j in range(3):
                    value = value + got_z[j, tile_at(i, tile), cols].astype(F32)
                put(tile_at(i, tile), slice(col + k * half, col + k * half + half), value)

    return [first, second, third, last]


def sum_steps(net, value, got):
    held = {}
    peers = [net.core, net.right, net.up]

    def make(i):
        def step():
            if i > 0:
                net.settle(held[i - 1])
                value[...] = value[...] + got[i - 1]
            if i < 3:
                held[i] = net.copy(value, got.at[i], peers[i])
            else:
                held[3] = [net.copy(value, got.at[3 + net.z], peer) for peer in net.line]
                got[3 + net.z] = value[...]

        return step

    def last():
        for made in held[3]:
            net.settle(made)
        value[...] = (got[3] + got[4]) + (got[5] + got[6])

    return [make(i) for i in range(4)] + [last]


def attend_back(query, grad, keys, values, masks, stat, head):
    lanes = head_lanes(query.shape[0])
    lanes = lanes if head == 0 else ~lanes
    own = jnp.where(lanes, query.astype(F32) * SCALE, 0.0).astype(BF)
    own_grad = jnp.where(lanes, grad.astype(F32), 0.0).astype(BF)
    inner, kept = 0.0, []
    for k, v, m in zip(keys, values, masks):
        scores = nt(k, own)
        probs = jnp.exp((scores if m is None else jnp.where(m, scores, NEGATIVE)) - stat)
        prob_grad = nt(v, own_grad)
        inner = inner + jnp.sum(probs * prob_grad, axis=0, keepdims=True)
        kept.append((probs, prob_grad))
    dq, dks, dvs = 0.0, [], []
    for k, (probs, prob_grad) in zip(keys, kept):
        score_grad = (probs * (prob_grad - inner)).astype(BF)
        dq = dq + tn(k, score_grad)
        dks.append(nn(score_grad, own))
        dvs.append(nn(probs.astype(BF), own_grad))
    return dq[head * HD : head * HD + HD] * SCALE, dks, dvs


def backward_kernel(
    rows, small, value_in, gain, rotary, lse, h_q, h_kv, h_att, h_first, h_x, h_w_qkv, h_joint, dw_out_in, dw_down_in, dw_up_in,
    value, o_qkv, o_out, o_up, o_down, joint_own,
    q, kv, att_grad, first, x, w_qkv, joint_in, dw_qkv, dw_out, dw_down, dw_up, spread, pairs, got_pairs, far_k, far_v, projected, joint, peer_joint,
    got_s, s_qkv, s_up, peer_qkv, peer_up, *rest,
):
    bufs, (send, recv, local) = rest[:-3], rest[-3:]
    net = Net(send, recv)
    c, z, chip = net.c, net.z, net.chip
    loads = [pltpu.make_async_copy(src, dst, local.at[i]) for i, (src, dst) in enumerate(
        ((dw_down_in, dw_down), (dw_up_in, dw_up), (dw_out_in, dw_out), (h_q, q), (h_kv, kv), (h_att, att_grad),
         (h_first, first), (h_w_qkv, w_qkv), (h_x, x), (h_joint, joint_in)))]
    for load in loads:
        load.start()
    value[...] = value_in[...]
    net.enter()
    bufs = list(bufs)
    take3 = lambda: [bufs.pop(0) for _ in range(3)]

    def put_into(ref):
        def put(at, cols, total):
            ref[at, cols] = total

        return put

    clock, tasks = [0], []

    def advance(until):
        while clock[0] < until:
            for t, steps in tasks:
                if (clock[0] - t) % 2 == 0 and 0 <= (clock[0] - t) // 2 < len(steps):
                    steps[(clock[0] - t) // 2]()
            clock[0] += 1

    loads[0].wait()
    tasks.append((0, scatter_steps(net, dw_down, 128, 0, 512, [], *take3(), put_into(o_down))))
    tasks.append((1, scatter_steps(net, dw_down, 128, 512, 512, [], *take3(), put_into(o_down))))
    tasks.append((2, scatter_steps(net, dw_up, 64, 0, 1024, [loads[1]], *take3(), put_into(s_up))))
    tasks.append((3, scatter_steps(net, dw_up, 64, 1024, 1024, [], *take3(), put_into(s_up))))
    advance(2)
    loads[2].wait()
    swaps = []
    for h in range(8):
        theirs = dw_out.at[pl.ds(h * 64 + (1 - c) * 32, 32)]
        swaps.append(net.copy(theirs, spread.at[pl.ds((8 * c + h) * 32, 32)], net.core))
        spread[pl.ds(pl.multiple_of((8 * c + h) * 32, 32), 32), :] = dw_out[pl.ds(pl.multiple_of(h * 64 + c * 32, 32), 32), :]
    tasks.append((4, scatter_steps(net, spread, 32, 0, 1024, [], *take3(), put_into(o_out))))

    length = jnp.sum(jnp.sum(rows[pl.ds(chip * 2, 2), 5:7, :], axis=0), keepdims=True).astype(jnp.int32)
    second = jnp.broadcast_to(small[7:8, :], (PROMPT, 128)) > 0.5
    weight = small[7:8, :]
    pair_sends = []

    def back_pair(pair):
        k_at, v_at = pl.ds(128 * pair, 128), pl.ds(HC + 128 * pair, 128)
        prompts = [(kv[p * PROMPT : (p + 1) * PROMPT, k_at], kv[p * PROMPT : (p + 1) * PROMPT, v_at]) for p in range(2)]
        chosen = [jnp.where(second, b.astype(F32), a.astype(F32)).astype(BF) for a, b in zip(*prompts)]

        def both_heads(row, size, keys, values, masks, place):
            dq, dks, dvs = [], None, None
            for head in range(2):
                stat = lse[2 * pair + head, :, row : row + size]
                d, k_parts, v_parts = attend_back(
                    q[row : row + size, k_at], att_grad[row : row + size, k_at], keys, values, masks, stat, head
                )
                dq.append(d)
                dks = k_parts if dks is None else [a + b for a, b in zip(dks, k_parts)]
                dvs = v_parts if dvs is None else [a + b for a, b in zip(dvs, v_parts)]
            dq = jnp.concatenate(dq, axis=0).T
            projected[row : row + size, k_at] = turn(dq, rotary[pl.ds(place, size), :], -1.0).astype(BF)
            return dks, dvs

        near_k, near_v = None, None
        for i in range(2):
            near = 256 * i + 256
            masks = [None, seen(0, 256 * i, (near, 256), length)]
            near_keys = kv[2 * PROMPT : 2 * PROMPT + near, k_at], kv[2 * PROMPT : 2 * PROMPT + near, v_at]
            dks, dvs = both_heads(
                256 + 256 * i, 256, [chosen[0], near_keys[0]], [chosen[1], near_keys[1]], masks, PROMPT + 256 * i
            )
            if i == 0:
                far_k[...], far_v[...] = dks[0], dvs[0]
                near_k, near_v = dks[1], dvs[1]
            else:
                far_k[...] = far_k[...] + dks[0]
                far_v[...] = far_v[...] + dvs[0]
                near_k = [near_k + dks[1][:256], dks[1][256:]]
                near_v = [near_v + dvs[1][:256], dvs[1][256:]]
        for i in range(2):
            at = slice(256 + 256 * i, 512 + 256 * i)
            table = rotary[PROMPT + 256 * i : PROMPT + 256 * i + 256, :]
            projected[at, HC + 128 * pair : HC + 128 * pair + 128] = turn(near_k[i], table, -1.0).astype(BF)
            projected[at, 2 * HC + 128 * pair : 2 * HC + 128 * pair + 128] = near_v[i].astype(BF)
        for p in range(2):
            place = pl.multiple_of(z * 2 * PSH, 128)
            dks, dvs = both_heads(
                128 * p, 128, [prompts[p][0]], [prompts[p][1]], [seen(0, z * 2 * PSH, (PROMPT, 128))], place
            )
            share = weight if p == 1 else 1.0 - weight
            at = slice(p * PROMPT, p * PROMPT + PROMPT)
            pairs[pair, at, :128] = (dks[0] + share * far_k[...]).astype(BF)
            pairs[pair, at, 128:] = (dvs[0] + share * far_v[...]).astype(BF)
        for j in (1, 2, 3):
            for p in range(2):
                there = pl.ds(p * PROMPT + (z + j) % RANKS * 2 * PSH, 2 * PSH)
                pair_sends.append(
                    net.copy(pairs.at[pair, there], got_pairs.at[j - 1, pair, pl.ds(p * 2 * PSH, 2 * PSH)], net.line[j - 1])
                )

    for load in loads[3:6]:
        load.wait()
    back_pair(0)
    advance(3)
    back_pair(1)
    advance(4)
    for made in swaps:
        made.wait_recv()
    back_pair(2)
    advance(5)
    back_pair(3)
    advance(6)
    for made in pair_sends:
        made.wait_recv()
    table = rotary[pl.ds(pl.multiple_of(z * 2 * PSH, 128), 128), :]
    for pair in range(4):
        for p in range(2):
            at = slice(p * 128, p * 128 + 128)
            total = pairs[pair, pl.ds(pl.multiple_of(p * PROMPT + z * 2 * PSH, 128), 128), :].astype(F32)
            for j in range(3):
                total = total + got_pairs[j, pair, at, :].astype(F32)
            projected[at, HC + 128 * pair : HC + 128 * pair + 128] = turn(total[:, :128], table, -1.0).astype(BF)
            projected[at, 2 * HC + 128 * pair : 2 * HC + 128 * pair + 128] = total[:, 128:].astype(BF)

    def weight_columns(col, width):
        @pl.loop(0, D // 256)
        def _(i):
            part = tn(first[:, tile_at(i, 256)], projected[:, col : col + width])
            dw_qkv[tile_at(i, 256), col : col + width] = part.astype(BF)

    for load in loads[6:]:
        load.wait()
    weight_columns(0, 768)
    tasks.append((6, scatter_steps(net, dw_qkv, 64, 0, 768, [], *take3(), put_into(s_qkv))))
    advance(7)
    weight_columns(768, 768)
    tasks.append((7, scatter_steps(net, dw_qkv, 64, 768, 768, [], *take3(), put_into(s_qkv))))
    advance(8)
    fg_sum, fg_normed = jnp.zeros((1, D), F32), jnp.zeros((1, D), F32)
    bias = jnp.zeros((1, 3 * HC), F32)

    def first_rows(i, sums):
        at = tile_at(i, 128)
        here = projected[at, :]
        grad = nt(here, w_qkv[...])
        normed = norm_rows(x[at, :])
        joint[at, :] = grad * gain[...] + joint_in[at, :]
        return (
            sums[0] + jnp.sum(grad, axis=0, keepdims=True),
            sums[1] + jnp.sum(grad * normed, axis=0, keepdims=True),
            sums[2] + jnp.sum(here.astype(F32), axis=0, keepdims=True),
        )

    fg_sum, fg_normed, bias = lax.fori_loop(0, ROWS // 128, first_rows, (fg_sum, fg_normed, bias))
    ranges = ((0, PSH, lambda o: o * PSH), (PSH, PSH, lambda o: 2 * PSH + o * PSH), (2 * PSH, HALF, lambda o: 4 * PSH + o * HALF))
    joints = [
        net.copy(joint.at[pl.ds(there(1 - c), size)], peer_joint.at[pl.ds(at, size)], net.core) for at, size, there in ranges
    ]
    for i in range(8):
        cols = slice(128 * i, 128 * i + 128)
        value[i : i + 1, :] = value[i : i + 1, :] + fg_normed[:, cols]
        value[8 + i : 9 + i, :] = value[8 + i : 9 + i, :] + fg_sum[:, cols]
    for i in range(12):
        row = pl.ds(40 + i // 4 * 8 + c * 4 + i % 4, 1)
        value[row, :] = value[row, :] + bias[:, 128 * i : 128 * i + 128]
    sums = sum_steps(net, value, got_s)
    sums[0]()
    advance(9)
    for made in joints:
        made.wait_recv()
    for at, size, there in ranges:
        mine = pl.ds(pl.multiple_of(there(c), 64), size)
        joint_own[at : at + size, :] = joint[mine, :] + peer_joint[at : at + size, :]
    sums[1]()
    advance(10)
    sums[2]()
    ups = []

    def give(total, peer_ref):
        return net.copy(total.at[pl.ds((1 - c) * 32, 32)], peer_ref, net.core)

    advance(11)
    ups.append(give(s_up, peer_up))
    sums[3]()
    advance(12)
    sums[4]()
    advance(16)
    ups.append(give(s_qkv, peer_qkv))
    own_rows = pl.ds(pl.multiple_of(c * 32, 32), 32)
    ups[0].wait_recv()
    for i in range(16):
        for who, part in ((c, s_up[own_rows, 128 * i : 128 * i + 128]), (1 - c, peer_up[:, 128 * i : 128 * i + 128])):
            o_up[:, pl.ds(pl.multiple_of((2 * i + who) * 128, 128), 128)] = part
    ups[1].wait_recv()
    for i in range(3):
        for who, part in ((c, s_qkv[own_rows, HC * i : HC * i + HC]), (1 - c, peer_qkv[:, HC * i : HC * i + HC])):
            o_qkv[:, pl.ds(pl.multiple_of(i * D + who * HC, 128), HC)] = part
    net.leave()


def backward(*args):
    shape = jax.ShapeDtypeStruct
    bufs = []
    for rb, width, count in ((128, 512, 2), (64, 1024, 2), (32, 1024, 1), (64, 768, 2)):
        for _ in range(count):
            bufs += [pltpu.VMEM((12 * rb, width // 2), BF), pltpu.VMEM((12 * rb, width // 2), BF), pltpu.VMEM((3, rb, width), BF)]
    return pl.pallas_call(
        backward_kernel,
        out_shape=(
            shape((104, 128), F32), shape((32, 3 * D), F32), shape((32, D), F32), shape((32, FF), F32), shape((128, D), F32),
            shape((384, D), F32),
        ),
        in_specs=[VM] * 6 + [HBM] * 10,
        out_specs=(VM,) * 6,
        scratch_shapes=[
            pltpu.VMEM((ROWS, HC), BF), pltpu.VMEM((KEYS, 2 * HC), BF), pltpu.VMEM((ROWS, HC), BF), pltpu.VMEM((ROWS, D), BF),
            pltpu.VMEM((ROWS, D), BF), pltpu.VMEM((D, 3 * HC), BF), pltpu.VMEM((ROWS, D), F32),
            pltpu.VMEM((D, 3 * HC), BF), pltpu.VMEM((HC, D), BF), pltpu.VMEM((FF // 2, D), BF), pltpu.VMEM((D, FF // 2), BF),
            pltpu.VMEM((HC, D), BF), pltpu.VMEM((4, 2 * PROMPT, 256), BF), pltpu.VMEM((3, 4, 4 * PSH, 256), BF),
            pltpu.VMEM((PROMPT, 128), F32), pltpu.VMEM((PROMPT, 128), F32), pltpu.VMEM((ROWS, 3 * HC), BF),
            pltpu.VMEM((ROWS, D), F32), pltpu.VMEM((384, D), F32), pltpu.VMEM((7, 104, 128), F32),
            pltpu.VMEM((64, 3 * HC), F32), pltpu.VMEM((64, FF // 2), F32), pltpu.VMEM((32, 3 * HC), F32), pltpu.VMEM((32, FF // 2), F32),
        ] + bufs
        + [pltpu.SemaphoreType.DMA((140,)), pltpu.SemaphoreType.DMA((140,)), pltpu.SemaphoreType.DMA((10,))],
        compiler_params=pltpu.CompilerParams(collective_id=1, has_side_effects=True, vmem_limit_bytes=63 << 20),
    )(*args)


def fast_body(
    tokens, valid, prompt_of, teacher, cotangent,
    ln1_gain, ln1_bias, ln2_gain, ln2_bias, qkv_weight, qkv_bias, out_weight, out_bias,
    up_weight, up_bias, down_weight, down_bias,
):
    c = lax.axis_index("core")
    z = lax.axis_index("chip")
    chips = lax.axis_size("chip")
    nh = HC // HD
    rd = down_weight.shape[0]
    device = lax.axis_index(ALL)
    pad = lambda v: jnp.pad(v.astype(F32), (0, 128 - v.shape[0]))[None]
    live_own = (valid > 0).astype(F32)
    small = jnp.concatenate(
        [
            jnp.concatenate([ln1_gain, ln1_bias, ln2_gain, ln2_bias]).astype(F32)[None],
            pad(jnp.concatenate([out_bias, down_bias])),
            pad(qkv_bias),
            pad(up_bias),
            live_own.reshape(3, 128),
            jnp.broadcast_to(prompt_of.astype(F32)[:, None], (1, 128)),
        ]
    )
    rows, w_qkv, x_own, first_own, q, kv, lse, dw_out, dw_down, dw_up, att_grad, joint, output, out_grad, value = forward(
        tokens,
        small,
        qkv_weight,
        out_weight,
        up_weight,
        down_weight,
        teacher,
        cotangent,
    )
    gain1 = rows[:, 0, :32].reshape(-1)
    count_all = jnp.sum(rows[:, 4:7])
    value, s_qkv, s_out, s_up, s_down, joint = backward(
        rows, small, value, gain1[None], jnp.asarray(rotary_table(PROMPT + CONT)), lse, q, kv, att_grad, first_own, x_own,
        w_qkv, joint, dw_out, dw_down, dw_up,
    )
    own_normed, own_rstd = normalize(tokens.astype(F32))
    input_grad = out_grad + own_rstd * (
        joint
        - jnp.mean(joint, axis=-1, keepdims=True)
        - own_normed * jnp.mean(joint * own_normed, axis=-1, keepdims=True)
    )
    pick = lambda part, own: lax.dynamic_index_in_dim(part.reshape(-1, own), device, axis=0, keepdims=False)
    five = lax.dynamic_index_in_dim(value[:40].reshape(5, 32, 32), device, axis=1, keepdims=False)
    shares = [five[i] for i in range(5)] + [pick(value[40:64], 96), pick(value[64:96], 128)]
    loss_value = value[96, 0] / (count_all * D)
    return (
        output, loss_value, input_grad, shares[0], shares[1], shares[2], shares[3],
        s_qkv, shares[5], s_out, shares[4], s_up, shares[6], s_down, shares[4],
    )


def solution(mesh):
    groups, seats = mesh.shape["grp"], mesh.shape["seq"]
    fine = Mesh(mesh.devices.reshape(groups, seats // 2, 2), ALL)
    rows, row = P(ALL, None), P(ALL)
    in_specs = (rows, row, row, rows, rows) + (row,) * 4 + (rows, row) * 4
    out_specs = (rows, P(), rows) + (row,) * 4 + (rows, row) * 4
    return jax.shard_map(fast_body if (groups, seats) == (4, 8) else generic_body, mesh=fine, in_specs=in_specs, out_specs=out_specs, check_vma=False)
```

```python
import functools

import jax
import jax.numpy as jnp
import numpy as np
from jax import lax
from jax.experimental import pallas as pl
from jax.experimental.pallas import tpu as pltpu
from jax.sharding import Mesh
from jax.sharding import PartitionSpec as P

D = 1024
H = 16
HD = 64
ROT = 16
FF = 4096
PSH = 64
CONT = 512
HALF = CONT // 2
HC = H // 2 * HD
EPSILON = 1e-05
NEGATIVE = -1e30
SCALE = 0.125
BF = jnp.bfloat16
F32 = jnp.float32
ALL = ("grp", "chip", "core")
CHIPS = ("grp", "chip")


def swap_cores(x):
    return lax.ppermute(x, "core", [(0, 1), (1, 0)])


def pair_rows(own):
    both = lax.all_gather(own, "core", axis=0)
    prompts = both[:, : 2 * PSH].reshape((2, 2, PSH) + own.shape[1:])
    prompts = prompts.swapaxes(0, 1).reshape((4 * PSH,) + own.shape[1:])
    return jnp.concatenate([prompts, both[:, 2 * PSH :].reshape((CONT,) + own.shape[1:])], axis=0)


def split_rows(rows):
    prompts = rows[: 4 * PSH].reshape((2, 2, PSH) + rows.shape[1:]).swapaxes(0, 1)
    prompts = prompts.reshape((2, 2 * PSH) + rows.shape[1:])
    return jnp.concatenate([prompts, rows[4 * PSH :].reshape((2, HALF) + rows.shape[1:])], axis=1)


def normalize(values):
    center = values - jnp.mean(values, axis=-1, keepdims=True)
    inverse_dev = lax.rsqrt(jnp.mean(center * center, axis=-1, keepdims=True) + EPSILON)
    return (center * inverse_dev, inverse_dev)


def rotate_heads(values, places, direction):
    halfrot = ROT // 2
    inverse = 10000.0 ** (-jnp.arange(halfrot, dtype=F32) / halfrot)
    angles = places.astype(F32)[..., None] * inverse
    cosine = jnp.cos(angles)[..., None, :]
    sine_part = direction * jnp.sin(angles)[..., None, :]
    leading = values[..., :halfrot]
    trailing = values[..., halfrot:ROT]
    return jnp.concatenate(
        [
            leading * cosine - trailing * sine_part,
            trailing * cosine + leading * sine_part,
            values[..., ROT:],
        ],
        axis=-1,
    )


def gelu_slope(values):
    return (
        0.5 * (1.0 + lax.erf(values * 0.7071067811865476))
        + values * jnp.exp(-0.5 * values * values) * 0.3989422804014327
    )


def dot(a, b, contract):
    return lax.dot_general(a, b, ((contract[:1], contract[1:]), ((), ())), preferred_element_type=F32)


def g_weights(c, qkv_weight, out_weight, up_weight, down_weight):
    r = qkv_weight.shape[0]
    mine = functools.partial(lax.dynamic_index_in_dim, index=c, keepdims=False)
    both = lambda w: lax.all_gather(w, "core", axis=0, tiled=True)
    qkv = mine(both(qkv_weight).reshape(2 * r, 3, 2, HC), axis=2).reshape(2 * r, 3 * HC)
    qkv = lax.all_gather(qkv, CHIPS, axis=0, tiled=True)
    rd = down_weight.shape[0]
    up = mine(both(up_weight).reshape(2 * r, FF // (2 * rd), 2, rd), axis=2).reshape(2 * r, FF // 2)
    up = lax.all_gather(up, CHIPS, axis=0, tiled=True)
    down = lax.all_gather(down_weight, CHIPS, axis=0, tiled=True)
    out = lax.all_gather(out_weight, ALL, axis=0, tiled=True)
    out = mine(out.reshape(2, HC, D), axis=0)
    return qkv, out, up, down


def g_small(c, rd, ln1_gain, ln1_bias, ln2_gain, ln2_bias, qkv_bias, out_bias, up_bias, down_bias):
    sizes = [v.shape[0] for v in (ln1_gain, ln1_bias, ln2_gain, ln2_bias, out_bias, down_bias, qkv_bias, up_bias)]
    packed = jnp.concatenate([ln1_gain, ln1_bias, ln2_gain, ln2_bias, out_bias, down_bias, qkv_bias, up_bias])
    rows = lax.all_gather(packed, ALL, axis=0)
    parts, at = [], 0
    for size in sizes:
        parts.append(rows[:, at : at + size].reshape(-1).astype(F32))
        at += size
    qb = lax.dynamic_index_in_dim(parts[6].reshape(3, 2, HC), c, axis=1, keepdims=False).reshape(-1)
    ub = lax.dynamic_index_in_dim(parts[7].reshape(-1, 2, rd), c, axis=1, keepdims=False).reshape(-1)
    return parts[:6] + [qb, ub]


def places_of(z, chips):
    prompt = z * 2 * PSH + jnp.arange(2 * PSH)
    return jnp.concatenate([prompt, prompt, chips * 2 * PSH + jnp.arange(CONT)])


def masks_of(z, chips, cont_valid):
    length = chips * 2 * PSH
    prompt = jnp.arange(length)[None, :] <= z * 2 * PSH + jnp.arange(2 * PSH)[:, None]
    own = jnp.arange(CONT)[None, :] <= jnp.arange(CONT)[:, None]
    own = own & (cont_valid > 0)[None, :]
    return prompt, jnp.concatenate([jnp.ones((CONT, length), bool), own], axis=1)


def g_attention(q, prompt_kv, kv, chosen, masks):
    nh = HC // HD
    chips = prompt_kv.shape[0]
    pk = prompt_kv.reshape(chips, 2, 2 * PSH, 2, nh, HD).transpose(3, 4, 1, 0, 2, 5)
    pk = pk.reshape(2, nh, 2, chips * 2 * PSH, HD)
    qh = q.reshape(-1, nh, HD).swapaxes(0, 1)
    pq = qh[:, : 4 * PSH].reshape(nh, 2, 2 * PSH, HD)
    scores = jnp.einsum("hpqd,hpkd->hpqk", pq, pk[0], preferred_element_type=F32) * SCALE
    scores = jnp.where(masks[0], scores, NEGATIVE)
    top = jnp.max(scores, axis=-1, keepdims=True)
    weights = jnp.exp(scores - top)
    total = jnp.sum(weights, axis=-1, keepdims=True)
    p_out = jnp.einsum("hpqk,hpkd->hpqd", (weights / total).astype(BF), pk[1], preferred_element_type=F32)
    p_lse = (top + jnp.log(total))[..., 0].reshape(nh, 4 * PSH)
    far = lax.dynamic_index_in_dim(pk, chosen, axis=2, keepdims=False)
    near = kv[4 * PSH :].reshape(CONT, 2, nh, HD).transpose(1, 2, 0, 3)
    ck = jnp.concatenate([far, near], axis=2)
    cq = qh[:, 4 * PSH :]
    scores = jnp.einsum("hqd,hkd->hqk", cq, ck[0], preferred_element_type=F32) * SCALE
    scores = jnp.where(masks[1], scores, NEGATIVE)
    top = jnp.max(scores, axis=-1, keepdims=True)
    weights = jnp.exp(scores - top)
    total = jnp.sum(weights, axis=-1, keepdims=True)
    c_out = jnp.einsum("hqk,hkd->hqd", (weights / total).astype(BF), ck[1], preferred_element_type=F32)
    c_lse = (top + jnp.log(total))[..., 0]
    att = jnp.concatenate([p_out.reshape(nh, 4 * PSH, HD), c_out], axis=1)
    return att.swapaxes(0, 1).reshape(-1, HC).astype(BF), jnp.concatenate([p_lse, c_lse], axis=1)


def g_attention_back(q, prompt_kv, kv, att_grad, lse, chosen, masks):
    nh = HC // HD
    chips = prompt_kv.shape[0]
    pk = prompt_kv.reshape(chips, 2, 2 * PSH, 2, nh, HD).transpose(3, 4, 1, 0, 2, 5)
    pk = pk.reshape(2, nh, 2, chips * 2 * PSH, HD)
    qh = q.reshape(-1, nh, HD).swapaxes(0, 1)
    gh = att_grad.reshape(-1, nh, HD).swapaxes(0, 1)
    pq = qh[:, : 4 * PSH].reshape(nh, 2, 2 * PSH, HD)
    pg = gh[:, : 4 * PSH].reshape(nh, 2, 2 * PSH, HD)
    ein = functools.partial(jnp.einsum, preferred_element_type=F32)

    def back(eq, ek, query, key, value, grad, mask, lse_rows):
        scores = jnp.where(mask, ein(f"{eq},{ek}->{eq[:-1]}k", query, key) * SCALE, NEGATIVE)
        probs = jnp.exp(scores - lse_rows[..., None])
        prob_grad = ein(f"{eq},{ek}->{eq[:-1]}k", grad, value)
        inner = jnp.sum(probs * prob_grad, axis=-1, keepdims=True)
        score_grad = (probs * (prob_grad - inner)).astype(BF)
        es = eq[:-1] + "k"
        dq = ein(f"{es},{ek}->{eq}", score_grad, key) * SCALE
        dk = ein(f"{es},{eq}->{ek}", score_grad, query) * SCALE
        dv = ein(f"{es},{eq}->{ek}", probs.astype(BF), grad)
        return dq, dk, dv

    dq_p, dk_p, dv_p = back("hpqd", "hpkd", pq, pk[0], pk[1], pg, masks[0], lse[:, : 4 * PSH].reshape(nh, 2, 2 * PSH))
    far = lax.dynamic_index_in_dim(pk, chosen, axis=2, keepdims=False)
    near = kv[4 * PSH :].reshape(CONT, 2, nh, HD).transpose(1, 2, 0, 3)
    ck = jnp.concatenate([far, near], axis=2)
    dq_c, dk_c, dv_c = back("hqd", "hkd", qh[:, 4 * PSH :], ck[0], ck[1], gh[:, 4 * PSH :], masks[1], lse[:, 4 * PSH :])
    length = chips * 2 * PSH
    pick = (jnp.arange(2) == chosen).astype(F32)[None, :, None, None]
    dk_p = dk_p + pick * dk_c[:, None, :length]
    dv_p = dv_p + pick * dv_c[:, None, :length]
    dq = jnp.concatenate([dq_p.reshape(nh, 4 * PSH, HD), dq_c], axis=1).swapaxes(0, 1).reshape(-1, HC)
    pair = jnp.stack([dk_p, dv_p])
    pair = pair.reshape(2, nh, 2, chips, 2 * PSH, HD).transpose(3, 2, 4, 0, 1, 5).reshape(chips * 4 * PSH, 2 * HC)
    near_grad = jnp.stack([dk_c[:, length:], dv_c[:, length:]]).transpose(2, 0, 1, 3).reshape(CONT, 2 * HC)
    return dq, pair, near_grad


def generic_body(
    tokens, valid, prompt_of, teacher, cotangent,
    ln1_gain, ln1_bias, ln2_gain, ln2_bias, qkv_weight, qkv_bias, out_weight, out_bias,
    up_weight, up_bias, down_weight, down_bias, stop=None,
):
    c = lax.axis_index("core")
    z = lax.axis_index("chip")
    chips = lax.axis_size("chip")
    nh = HC // HD
    rd = down_weight.shape[0]
    device = lax.axis_index(ALL)
    w_qkv, w_out, w_up, w_down = g_weights(c, qkv_weight, out_weight, up_weight, down_weight)
    gain1, bias1, gain2, bias2, b_out, b_down, b_qkv, b_up = g_small(
        c, rd, ln1_gain, ln1_bias, ln2_gain, ln2_bias, qkv_bias, out_bias, up_bias, down_bias
    )
    x = pair_rows(tokens).astype(F32)
    normed, rstd = normalize(x)
    first_in = (normed * gain1 + bias1).astype(BF)
    second_in = (normed * gain2 + bias2).astype(BF)
    projected = dot(first_in, w_qkv, (1, 0)) + b_qkv
    places = places_of(z, chips)
    turn = lambda v, d: rotate_heads(v.reshape(-1, nh, HD), places, d).reshape(-1, HC)
    q = turn(projected[:, :HC], 1.0).astype(BF)
    k = turn(projected[:, HC : 2 * HC], 1.0).astype(BF)
    kv = jnp.concatenate([k, projected[:, 2 * HC :].astype(BF)], axis=1)
    prompt_kv = lax.all_gather(kv[: 4 * PSH].reshape(2, 2 * PSH, 2 * HC), "chip", axis=0)
    cont_valid = lax.all_gather(valid[2 * PSH :], "core", axis=0, tiled=True)
    masks = masks_of(z, chips, cont_valid)
    chosen = prompt_of[0]
    attended, lse = g_attention(q, prompt_kv, kv, chosen, masks)
    hidden_pre = dot(second_in, w_up, (1, 0)) + b_up
    activated = jax.nn.gelu(hidden_pre, approximate=False).astype(BF)
    partial = dot(attended, w_out, (1, 0)) + dot(activated, w_down, (1, 0))
    halves = split_rows(partial)
    take = lambda a: lax.dynamic_index_in_dim(a, c, axis=0, keepdims=False)
    give = lambda a: lax.dynamic_index_in_dim(a, 1 - c, axis=0, keepdims=False)
    output = tokens.astype(F32) + take(halves) + swap_cores(give(halves)) + b_out + b_down
    live = (valid > 0).astype(F32)[:, None]
    missed = output - teacher.astype(F32)
    count_all, squared_all = lax.psum((jnp.sum(live), jnp.sum(live * missed * missed)), ALL)
    loss_value = squared_all / (count_all * D)
    out_grad = cotangent.astype(F32) + 2.0 / (count_all * D) * live * missed
    out_low = pair_rows(out_grad.astype(BF))
    if stop == "fwd":
        return output, out_grad, out_low, attended, lse, activated, q, kv, first_in, second_in
    out_bias_grad = jnp.sum(out_grad.astype(BF).astype(F32), axis=0)
    dw_out = dot(attended, out_low, (0, 0))
    dw_down = dot(activated, out_low, (0, 0))
    att_grad = dot(out_low, w_out, (1, 1)).astype(BF)
    hidden_grad = (dot(out_low, w_down, (1, 1)) * gelu_slope(hidden_pre)).astype(BF)
    dw_up = dot(second_in, hidden_grad, (0, 0))
    db_up = jnp.sum(hidden_grad.astype(F32), axis=0)
    second_grad = dot(hidden_grad, w_up, (1, 1))
    dq, pair, near = g_attention_back(q, prompt_kv, kv, att_grad, lse, chosen, masks)
    own_pair = lax.psum_scatter(pair.astype(BF), "chip", scatter_dimension=0, tiled=True).astype(F32)
    pair = jnp.concatenate([own_pair, near], axis=0)
    projected_grad = jnp.concatenate([turn(dq, -1.0), turn(pair[:, :HC], -1.0), pair[:, HC:]], axis=1).astype(BF)
    dw_qkv = dot(first_in, projected_grad, (0, 0))
    db_qkv = jnp.sum(projected_grad.astype(F32), axis=0)
    first_grad = dot(projected_grad, w_qkv, (1, 1))
    if stop == "bwd":
        return dw_out, dw_down, dw_up, dw_qkv, second_grad, first_grad, projected_grad, hidden_grad, att_grad
    joint = first_grad * gain1 + second_grad * gain2
    halves = split_rows(joint)
    joint = take(halves) + swap_cores(give(halves))
    own_normed = take(split_rows(normed))
    own_rstd = take(split_rows(rstd))
    input_grad = out_grad + own_rstd * (
        joint
        - jnp.mean(joint, axis=-1, keepdims=True)
        - own_normed * jnp.mean(joint * own_normed, axis=-1, keepdims=True)
    )
    wide = lambda v, n: jnp.zeros((v.shape[0], 2, v.shape[1]), F32).at[:, c].set(v).reshape(-1)
    small = jnp.concatenate(
        [
            jnp.sum(first_grad * normed, axis=0),
            jnp.sum(first_grad, axis=0),
            jnp.sum(second_grad * normed, axis=0),
            jnp.sum(second_grad, axis=0),
            out_bias_grad,
            wide(db_qkv.reshape(3, HC), 3),
            wide(db_up.reshape(-1, rd), 16),
        ]
    )
    small = lax.psum(small, ALL)
    shares, at = [], 0
    for size in (D, D, D, D, D, 3 * D, FF):
        own = size // lax.axis_size(ALL)
        shares.append(lax.dynamic_slice_in_dim(small, at + device * own, own))
        at += size
    rs = lambda v: lax.psum_scatter(v.astype(BF), CHIPS, scatter_dimension=0, tiled=True).astype(F32)
    r = qkv_weight.shape[0]
    s_qkv = rs(dw_qkv).reshape(2, r, 3, HC)
    s_up = rs(dw_up).reshape(2, r, FF // (2 * rd), rd)
    s_down = rs(dw_down)
    pairs = lambda own, other, axis: jnp.where(c == 0, jnp.stack([own, other], axis), jnp.stack([other, own], axis))
    s_qkv = pairs(take(s_qkv), swap_cores(give(s_qkv)), 2).reshape(r, 3 * D)
    s_up = pairs(take(s_up), swap_cores(give(s_up)), 2).reshape(r, FF)
    o = dw_out.reshape(H // 2, -1, 2, r, D)
    o_own = lax.dynamic_index_in_dim(o, c, axis=2, keepdims=False)
    o_other = swap_cores(lax.dynamic_index_in_dim(o, 1 - c, axis=2, keepdims=False))
    s_out = rs(pairs(o_own, o_other, 0).reshape(-1, D))
    return (
        output.astype(BF), loss_value, input_grad, shares[0], shares[1], shares[2], shares[3],
        s_qkv, shares[5], s_out, shares[4], s_up, shares[6], s_down, shares[4],
    )


MESH_ID = pl.DeviceIdType.MESH
RANKS = 4


class Net:
    def __init__(self, send, recv):
        self.g, self.z, self.c = (lax.axis_index(a) for a in ALL)
        self.y, self.x = self.g // 2, self.g % 2
        self.send, self.recv, self.used = send, recv, 0
        self.chip = self.g * RANKS + self.z
        self.core = {"grp": self.g, "chip": self.z, "core": 1 - self.c}
        self.right = {"grp": self.y * 2 + 1 - self.x, "chip": self.z, "core": self.c}
        self.up = {"grp": (1 - self.y) * 2 + self.x, "chip": self.z, "core": self.c}
        self.line = [{"grp": self.g, "chip": (self.z + j) % RANKS, "core": self.c} for j in (1, 2, 3)]
        self.sent = []

    def enter(self):
        barrier = pltpu.get_barrier_semaphore()
        for peer in [self.core, self.right, self.up] + self.line:
            pl.semaphore_signal(barrier, inc=1, device_id=peer, device_id_type=MESH_ID)
        pl.semaphore_wait(barrier, 6)

    def copy(self, src, dst, peer):
        i = self.used
        self.used += 1
        made = pltpu.make_async_remote_copy(
            src_ref=src, dst_ref=dst, send_sem=self.send.at[i], recv_sem=self.recv.at[i],
            device_id=peer, device_id_type=MESH_ID,
        )
        made.start()
        self.sent.append(made)
        return made

    def same(self, view, peer):
        return self.copy(view, view, peer)

    def settle(self, made):
        made.wait_recv()
        made.wait_send()
        self.sent = [m for m in self.sent if m is not made]

    def leave(self):
        for made in self.sent:
            made.wait_send()
        self.sent = []


def gather_steps(net, dst, rb, col, width, before):
    a, b, both = pl.ds(col, width // 2), pl.ds(col + width // 2, width // 2), pl.ds(col, width)
    quad = 4 * rb
    held = {}

    def line():
        for made in before:
            made.wait_recv()
        view = dst.at[pl.ds(net.chip * rb, rb), both]
        held[0] = [net.same(view, peer) for peer in net.line]

    def first():
        for made in held[0]:
            made.wait_recv()
        rows = pl.ds(net.g * quad, quad)
        held[1] = [net.same(dst.at[rows, a], net.right), net.same(dst.at[rows, b], net.up)]

    def second():
        for made in held[1]:
            made.wait_recv()
        held[2] = [net.same(dst.at[pl.ds(net.y * 2 * quad, 2 * quad), a], net.up)]
        for y in range(2):
            held[2].append(net.same(dst.at[pl.ds((y * 2 + net.x) * quad, quad), b], net.right))

    def last():
        for made in held[2]:
            made.wait_recv()

    return [line, first, second, last]


def small_steps(net, rows):
    held = {}

    def pair():
        held[0] = [net.same(rows.at[net.chip * 2 + net.c], net.core)]

    def line():
        held[0][0].wait_recv()
        held[1] = [net.same(rows.at[pl.ds(net.chip * 2, 2)], peer) for peer in net.line]

    def first():
        for made in held[1]:
            made.wait_recv()
        held[2] = [net.same(rows.at[pl.ds(net.g * 8, 8)], net.right)]

    def second():
        held[2][0].wait_recv()
        held[3] = [net.same(rows.at[pl.ds(net.y * 16, 16)], net.up)]

    def last():
        held[3][0].wait_recv()

    return [pair, line, first, second, last]


VM = pl.BlockSpec(memory_space=pltpu.VMEM)
HBM = pl.BlockSpec(memory_space=pl.ANY)
PROMPT = RANKS * 2 * PSH
KEYS = 2 * PROMPT + CONT
ROWS = 4 * PSH + CONT


def nt(a, b):
    return lax.dot_general(a, b, (((1,), (1,)), ((), ())), preferred_element_type=F32)


def nn(a, b):
    return lax.dot_general(a, b, (((1,), (0,)), ((), ())), preferred_element_type=F32)


def tn(a, b):
    return lax.dot_general(a, b, (((0,), (0,)), ((), ())), preferred_element_type=F32)


def tile_at(i, size):
    return pl.ds(pl.multiple_of(i * size, size), size)


def move_rows(dst, to, src, at, count, tile=32):
    @pl.loop(0, count // tile)
    def _(i):
        step = pl.multiple_of(i * tile, tile)
        dst[pl.ds(pl.multiple_of(to + step, tile), tile), :] = src[pl.ds(pl.multiple_of(at + step, tile), tile), :]


def spread_row(rows, field, index, owner, lane, size):
    table = rows[:, field, :].astype(BF)
    lanes = lax.broadcasted_iota(jnp.int32, (128, size), 0)
    pick = (lanes == index[lane : lane + 1, :size]).astype(F32).astype(BF)
    wide = nn(table, pick)
    owners = lax.broadcasted_iota(jnp.int32, (rows.shape[0], size), 0)
    return jnp.sum(jnp.where(owners == index[owner : owner + 1, :size], wide, 0.0), axis=0, keepdims=True)


def norm_rows(x):
    x = x.astype(F32)
    center = x - jnp.mean(x, axis=-1, keepdims=True)
    return center * lax.rsqrt(jnp.mean(center * center, axis=-1, keepdims=True) + EPSILON)


def turn(value, table, sign):
    cos, low_sin, high_sin = (table[:, 128 * i : 128 * i + 128] for i in range(3))
    out = []
    for j in range(value.shape[1] // 128):
        v = value[:, 128 * j : 128 * j + 128]
        other = pltpu.roll(v, 120, 1) * low_sin + pltpu.roll(v, 8, 1) * high_sin
        out.append(v * cos + sign * other)
    return out[0] if len(out) == 1 else jnp.concatenate(out, axis=1)


def rotary_table(length):
    half = ROT // 2
    inverse = (10000.0 ** (-np.arange(half, dtype=np.float32) / half)).astype(np.float32)
    angles = (np.arange(length, dtype=np.float32)[:, None] * inverse).astype(np.float64)
    cos, sin = np.cos(angles), np.sin(angles)
    table = np.zeros((length, 3, 2, HD), np.float32)
    table[:, 0] = 1.0
    for head in range(2):
        table[:, 0, head, :half] = cos
        table[:, 0, head, half:ROT] = cos
        table[:, 1, head, :half] = -sin
        table[:, 2, head, half:ROT] = sin
    return table.reshape(length, 384)


def index_table(rd):
    n = np.arange(2048)
    table = np.zeros((2, 16, 2048), np.int32)
    for c in range(2):
        col = np.minimum(n // HC, 2) * D + c * HC + n % HC
        table[c, 0], table[c, 1] = col // 96, col % 96
        unit = n // rd * (2 * rd) + c * rd + n % rd
        table[c, 2], table[c, 3] = unit // rd, unit % rd
        table[c, 4] = n // 32 % 32
        for i in range(4):
            table[c, 8 + i] = n % 32 + 32 * i
    return table


def seen(keys_at, queries_at, shape, length=None):
    keys = lax.broadcasted_iota(jnp.int32, shape, 0) + keys_at
    queries = lax.broadcasted_iota(jnp.int32, shape, 1) + queries_at
    mask = keys <= queries
    return mask if length is None else mask & (keys < length)


def head_lanes(rows):
    return lax.broadcasted_iota(jnp.int32, (rows, 128), 1) < HD


def attend(query, keys, values, masks, head):
    lanes = head_lanes(query.shape[0])
    own = jnp.where(lanes if head == 0 else ~lanes, query.astype(F32) * SCALE, 0.0).astype(BF)
    scores = [nt(k, own) for k in keys]
    scores = [s if m is None else jnp.where(m, s, NEGATIVE) for s, m in zip(scores, masks)]
    top = functools.reduce(jnp.maximum, [jnp.max(s, axis=0, keepdims=True) for s in scores])
    weights = [jnp.exp(s - top) for s in scores]
    total = sum(jnp.sum(w, axis=0, keepdims=True) for w in weights)
    share = 1.0 / total
    out = sum(tn(v, (w * share).astype(BF)) for v, w in zip(values, weights))
    return out[head * HD : head * HD + HD], top + jnp.log(total)


GATHER_ORDER = (
    (0, 0), (0, 1), (6, 0), (6, 0), (1, 0), (0, 2), (0, 3), (1, 1), (6, 0), (2, 0), (6, 0), (6, 0),
    (2, 1), (6, 0), (6, 0), (6, 0), (1, 2), (0, 4), (4, 0), (1, 3), (3, 0), (6, 0), (6, 0), (2, 2),
    (5, 0), (0, 5), (2, 3), (3, 1), (1, 4), (4, 1), (6, 0), (6, 0), (5, 1), (0, 6), (4, 2), (1, 5),
    (2, 4), (3, 2), (6, 0), (6, 0), (3, 3), (5, 2), (0, 7), (2, 5), (6, 0), (1, 6), (4, 3), (6, 0),
    (3, 4), (1, 7), (0, 8), (2, 6), (5, 3), (4, 4), (3, 5), (2, 7), (5, 4), (0, 9), (4, 5), (1, 8),
    (3, 6), (6, 0), (6, 0), (6, 0), (6, 0), (6, 0), (6, 0), (3, 7), (2, 8), (6, 0), (6, 0), (5, 5),
    (0, 10), (6, 0), (1, 9), (0, 11), (6, 0), (6, 0), (6, 0), (6, 0), (6, 0), (3, 8), (2, 9), (6, 0),
    (6, 0), (6, 0), (1, 10), (1, 11), (6, 0), (6, 0), (6, 0), (3, 9), (6, 0), (6, 0), (2, 10), (2, 11),
    (6, 0), (6, 0), (6, 0), (6, 0), (3, 10), (3, 11),
)


def forward_kernel(
    tokens, small, qkv, out, up, down, h_rotary, index, h_teacher, h_cotangent,
    rows, h_w_qkv, h_x, h_first, h_q, h_kv, lse, h_dw_out, h_dw_down, h_dw_up, h_att, joint, h_output, h_out_grad, value,
    rotary, teacher, cotangent, att_grad, output, out_grad, w_qkv, x_own, first_own, q, kv, dw_out, dw_down, dw_up, w_out, w_up, w_down, second_in, attended, activated, slope, peer, low, x_all, first_in, spread, swapped, crossed, send, recv, local,
):
    net = Net(send, recv)
    c, z, chip = net.c, net.z, net.chip
    loads = [
        pltpu.make_async_copy(src, dst, local.at[11 + i])
        for i, (src, dst) in enumerate(((h_rotary, rotary), (h_teacher, teacher), (h_cotangent, cotangent)))
    ]
    for load in loads:
        load.start()
    net.enter()
    for p in range(2):
        move_rows(x_all, p * PROMPT + z * 2 * PSH + c * PSH, tokens, p * PSH, PSH)
    move_rows(x_all, 2 * PROMPT + c * HALF, tokens, 2 * PSH, HALF)
    rows[chip * 2 + c] = small[...]
    pieces_at = [pl.ds(p * PROMPT + z * 2 * PSH + c * PSH, PSH) for p in range(2)]
    smalls = small_steps(net, rows)
    smalls[0]()
    mates = [net.same(x_all.at[piece], net.core) for piece in pieces_at + [pl.ds(2 * PROMPT + c * HALF, HALF)]]
    half_rows = pl.ds(pl.multiple_of(chip * 64 + c * 32, 32), 32)
    given = pl.ds(0, 32)
    for i in range(3):
        cols = slice(HC * i, HC * i + HC)
        w_qkv[half_rows, cols] = qkv[:, pl.ds(pl.multiple_of(i * D + c * HC, 128), HC)]
        swapped[given, cols] = qkv[:, pl.ds(pl.multiple_of(i * D + (1 - c) * HC, 128), HC)]
    from_core = {}
    from_core["qkv"] = net.copy(swapped.at[given, pl.ds(0, 3 * HC)], w_qkv.at[half_rows], net.core)
    given = pl.ds(32, 32)
    for i in range(16):
        cols = slice(128 * i, 128 * i + 128)
        w_up[half_rows, cols] = up[:, pl.ds(pl.multiple_of((2 * i + c) * 128, 128), 128)]
        swapped[given, cols] = up[:, pl.ds(pl.multiple_of((2 * i + 1 - c) * 128, 128), 128)]
    from_core["up"] = net.copy(swapped.at[given, pl.ds(0, FF // 2)], w_up.at[half_rows], net.core)
    w_down[pl.ds(pl.multiple_of(chip * 128, 128), 128), :] = down[...]
    spread[pl.ds(pl.multiple_of(chip * 32, 32), 32), :] = out[...]
    none = []
    tasks = [gather_steps(net, w_up, 64, 512 * i, 512, [] if i else [from_core["up"]]) for i in range(4)]
    tasks += [gather_steps(net, w_qkv, 64, 512 * i, 512, [] if i else [from_core["qkv"]]) for i in range(3)]
    tasks += [gather_steps(net, spread, 32, 0, 1024, [])]
    tasks += [gather_steps(net, w_down, 128, 256 * i, 256, []) for i in range(4)]
    pieces, done = [], set()

    def after(needs, work, *args):
        pieces.append((set(needs), work, args))

    def run_pieces(count):
        while count and pieces and pieces[0][0] <= done:
            needs, work, args = pieces.pop(0)
            work(*args)
            count -= 1

    held = {}

    def learn():
        for load in loads:
            load.wait()
        for made in mates:
            made.wait_recv()
        places = index.at[c]
        held["norm"] = [spread_row(rows, 0, places, 4, 8 + i, D) for i in range(4)]
        held["qkv"] = spread_row(rows, 2, places, 0, 1, 3 * HC)
        held["length"] = jnp.sum(jnp.sum(rows[pl.ds(chip * 2, 2), 5:7, :], axis=0), keepdims=True).astype(jnp.int32)
        held["up"] = spread_row(rows, 3, places, 2, 3, FF // 2)

    def own_norms(first_tile, count):
        gain1, bias1, gain2, bias2 = held["norm"]

        @pl.loop(first_tile, first_tile + count)
        def _(i):
            prompt = (i // 2) * PROMPT + z * 2 * PSH + (i % 2) * 64
            here = pl.ds(pl.multiple_of(jnp.where(i < 4, prompt, 2 * PROMPT + (i - 4) * 64), 64), 64)
            at = tile_at(i, 64)
            normed = norm_rows(x_all[here, :])
            x_own[at, :] = x_all[here, :]
            narrow = (normed * gain1 + bias1).astype(BF)
            first_in[here, :] = narrow
            first_own[at, :] = narrow
            second_in[at, :] = (normed * gain2 + bias2).astype(BF)

    relays = {}
    prompt_pieces = [(j, p) for j in (1, 2, 3) for p in range(2)]

    def send_tokens(k):
        j, p = prompt_pieces[k]
        held[k] = net.same(x_all.at[pieces_at[p]], net.line[j - 1])

    def relay_tokens(k):
        j, p = prompt_pieces[k]
        held[k].wait_recv()
        relays[k] = net.same(x_all.at[pl.ds(p * PROMPT + (z + RANKS - j) % RANKS * 2 * PSH + c * PSH, PSH)], net.core)

    def other_norms(k):
        j, p = prompt_pieces[k]
        relays[k].wait_recv()
        gain1, bias1 = held["norm"][:2]

        @pl.loop(0, 2)
        def _(i):
            here = pl.ds(pl.multiple_of(p * PROMPT + (z + RANKS - j) % RANKS * 2 * PSH + i * 64, 64), 64)
            first_in[here, :] = (norm_rows(x_all[here, :]) * gain1 + bias1).astype(BF)

    def hidden(j):
        cols = slice(256 * j, 256 * j + 256)
        b_up = held["up"]

        @pl.loop(0, ROWS // 128)
        def _(i):
            at = tile_at(i, 128)
            pre = nn(second_in[at, :], w_up[:, cols]) + b_up[:, cols]
            gate = 0.5 * (1.0 + lax.erf(pre * 0.7071067811865476))
            activated[at, cols] = (pre * gate).astype(BF)
            slope[at, cols] = (gate + pre * jnp.exp(-0.5 * pre * pre) * 0.3989422804014327).astype(slope.dtype)

    def key_rows(i):
        at = slice(256 * i, 256 * i + 256)
        here = first_in[at, :]
        place = (i % 2) * 256 if i < 4 else PROMPT + (i - 4) * 256
        table = rotary[place : place + 256, :]
        for j in range(4):
            cols = slice(HC + 256 * j, HC + 256 * j + 256)
            made = nn(here, w_qkv[:, cols]) + held["qkv"][:, cols]
            kv[at, 256 * j : 256 * j + 256] = (turn(made, table, 1.0) if j < 2 else made).astype(BF)

    def query_rows(first_tile, count):
        @pl.loop(first_tile, first_tile + count)
        def _(i):
            place = pl.multiple_of(jnp.where(i < 2, z * 2 * PSH, PROMPT + (i - 2) * 128), 128)
            at = tile_at(i, 128)
            here = first_own[at, :]
            table = rotary[pl.ds(place, 128), :]
            for j in range(2):
                cols = slice(256 * j, 256 * j + 256)
                q[at, cols] = turn(nn(here, w_qkv[:, cols]) + held["qkv"][:, cols], table, 1.0).astype(BF)

    second = jnp.broadcast_to(small[7:8, :], (PROMPT, 128)) > 0.5

    def attend_pair(pair, part):
        k_at, v_at = pl.ds(128 * pair, 128), pl.ds(HC + 128 * pair, 128)
        prompts = [(kv[p * PROMPT : (p + 1) * PROMPT, k_at], kv[p * PROMPT : (p + 1) * PROMPT, v_at]) for p in range(2)]

        def put(row, size, key_list, value_list, masks):
            outs = []
            for head in range(2):
                o, stat = attend(q[row : row + size, k_at], key_list, value_list, masks, head)
                outs.append(o)
                lse[2 * pair + head, :, row : row + size] = stat
            attended[row : row + size, k_at] = jnp.concatenate(outs, axis=0).T.astype(BF)

        for p in range(2) if part == 0 else ():
            put(p * 128, 128, [prompts[p][0]], [prompts[p][1]], [seen(0, z * 2 * PSH, (PROMPT, 128))])
        chosen = [jnp.where(second, b.astype(F32), a.astype(F32)).astype(BF) for a, b in zip(*prompts)]
        for i in ((), (0, 1), (2, 3))[part]:
            near = 128 * i + 128
            put(
                256 + 128 * i, 128,
                [chosen[0], kv[2 * PROMPT : 2 * PROMPT + near, k_at]],
                [chosen[1], kv[2 * PROMPT : 2 * PROMPT + near, v_at]],
                [None, seen(0, 128 * i, (near, 128), held["length"])],
            )

    after([], smalls[1])
    after([(0, 1)], smalls[2])
    after([(1, 0)], smalls[3])
    after([(2, 0)], smalls[4])
    after([(2, 0)], learn)
    for i in range(3):
        after([], own_norms, 4 * i, 4)
    for j in range(8):
        after([(3, j // 2)], hidden, j)
    for i in range(2):
        after([(3, 6)], query_rows, 3 * i, 3)
    for i in range(2):
        after([(3, 6)], key_rows, 4 + i)
    for k in range(6):
        after([(5, k)], other_norms, k)
    for i in range(4):
        after([(5, 5)], key_rows, i)
    for pair in range(4):
        for part in range(3):
            after([], attend_pair, pair, part)
    for event in GATHER_ORDER:
        step, t = event
        if step < 4:
            tasks[t][step]()
        elif step == 4:
            send_tokens(t)
        elif step == 5:
            relay_tokens(t)
        else:
            run_pieces(1)
        done.add(event)
    run_pieces(len(pieces))
    shipped = []

    def ship(src, dst):
        made = pltpu.make_async_copy(src, dst, local.at[len(shipped)])
        made.start()
        shipped.append(made)

    for src, dst in ((w_qkv, h_w_qkv), (x_own, h_x), (first_own, h_first), (q, h_q), (kv, h_kv)):
        ship(src, dst)
    length = held["length"]
    gain2 = held["norm"][2]
    places = index.at[c]
    given = pl.ds(pl.multiple_of((1 - c) * 256, 256), 256)
    swap = net.copy(spread.at[given], crossed, net.core)
    swap.wait_recv()
    for h in range(8):
        w_out[pl.ds(pl.multiple_of(h * 64 + c * 32, 32), 32), :] = spread[pl.ds(pl.multiple_of(c * 256 + h * 32, 32), 32), :]
        w_out[pl.ds(pl.multiple_of(h * 64 + (1 - c) * 32, 32), 32), :] = crossed[h * 32 : h * 32 + 32, :]

    def share(at, size):
        here = pl.ds(pl.multiple_of(at, 128), size)
        joint[here, :] = nn(attended[here, :], w_out[...]) + nn(activated[here, :], w_down[...])

    def chip_range(i, owner):
        return ((owner * PSH, PSH, 0), (2 * PSH + owner * PSH, PSH, PSH), (4 * PSH + owner * HALF, HALF, 2 * PSH))[i]

    def pass_share(i):
        at, size, to = chip_range(i, 1 - c)
        return net.copy(joint.at[pl.ds(pl.multiple_of(at, 64), size)], peer.at[pl.ds(to, size)], net.core)

    share(4 * PSH + (1 - c) * HALF, HALF)
    passed = [pass_share(2)]
    share(0, 256)
    passed += [pass_share(0), pass_share(1)]
    share(4 * PSH + c * HALF, HALF)
    for made in passed:
        net.settle(made)
    count = jnp.sum(jnp.sum(rows[:, 4:7, :], axis=0), keepdims=True)
    pull = 2.0 / (count * D)
    bias = spread_row(rows, 1, places, 4, 8, D) + spread_row(rows, 1, places, 4, 9, D)
    value[...] = jnp.zeros_like(value)
    squared, low_sum = jnp.zeros((1, D), F32), jnp.zeros((1, D), F32)
    lows = []
    for i in range(3):
        at, size, to = chip_range(i, c)

        def rows_out(k, sums, at=at, to=to, i=i):
            here = pl.ds(pl.multiple_of(at + k * 64, 64), 64)
            own = pl.ds(pl.multiple_of(to + k * 64, 64), 64)
            result = tokens[own, :].astype(F32) + joint[here, :] + peer[own, :] + bias
            missed = result - teacher[own, :].astype(F32)
            if i == 2:
                step = lax.broadcasted_iota(jnp.int32, (64, D), 0) + (c * HALF + k * 64)
                missed = jnp.where(step < length, missed, 0.0)
            output[own, :] = result.astype(BF)
            grad = cotangent[own, :].astype(F32) + pull * missed
            out_grad[own, :] = grad
            rounded = grad.astype(BF)
            low[here, :] = rounded
            return (
                sums[0] + jnp.sum(missed * missed, axis=0, keepdims=True),
                sums[1] + jnp.sum(rounded.astype(F32), axis=0, keepdims=True),
            )

        squared, low_sum = lax.fori_loop(0, size // 64, rows_out, (squared, low_sum))
        lows.append(net.same(low.at[pl.ds(pl.multiple_of(at, 64), size)], net.core))
    total = jnp.sum(squared, keepdims=True)
    value[96:97, :] = jnp.broadcast_to(total, (1, 128))

    def put_row(row, vector):
        for k in range(vector.shape[1] // 128):
            value[row + k : row + k + 1, :] = vector[:, 128 * k : 128 * k + 128]

    ship(output, h_output)
    ship(out_grad, h_out_grad)
    put_row(32, low_sum)
    for made in lows:
        made.wait_recv()

    @pl.loop(0, 8)
    def _(i):
        at = tile_at(i, 256)
        dw_down[at, :] = tn(activated[:, at], low[...]).astype(BF)

    ship(dw_down, h_dw_down)

    @pl.loop(0, 2)
    def _(i):
        at = tile_at(i, 256)
        dw_out[at, :] = tn(attended[:, at], low[...]).astype(BF)

    ship(dw_out, h_dw_out)

    @pl.loop(0, ROWS // 128)
    def _(i):
        at = tile_at(i, 128)
        att_grad[at, :] = nt(low[at, :], w_out[...]).astype(BF)

    ship(att_grad, h_att)

    for j in range(8):
        cols = slice(256 * j, 256 * j + 256)

        def hidden_rows(i, total, cols=cols):
            at = tile_at(i, 256)
            grad = (nt(low[at, :], w_down[cols, :]) * slope[at, cols].astype(F32)).astype(BF)
            activated[at, cols] = grad
            return total + jnp.sum(grad.astype(F32), axis=0, keepdims=True)

        total = lax.fori_loop(0, ROWS // 256, hidden_rows, jnp.zeros((1, 256), F32))
        for k in range(2):
            value[pl.ds(64 + 4 * j + 2 * k + c, 1), :] = total[:, 128 * k : 128 * k + 128]

    @pl.loop(0, 4)
    def _(i):
        at = tile_at(i, 256)
        for k in range(2):
            cols = slice(1024 * k, 1024 * k + 1024)
            dw_up[at, cols] = tn(second_in[:, at], activated[:, cols]).astype(BF)

    ship(dw_up, h_dw_up)

    def second_rows(i, sums):
        at = tile_at(i, 128)
        grad = nt(activated[at, :], w_up[...])
        joint[at, :] = grad * gain2
        normed = norm_rows(x_own[at, :])
        return (
            sums[0] + jnp.sum(grad * normed, axis=0, keepdims=True),
            sums[1] + jnp.sum(grad, axis=0, keepdims=True),
        )

    sums = lax.fori_loop(0, ROWS // 128, second_rows, (jnp.zeros((1, D), F32), jnp.zeros((1, D), F32)))
    put_row(16, sums[0])
    put_row(24, sums[1])
    for made in shipped:
        made.wait()
    net.leave()


def forward(tokens, small, qkv, out, up, down, teacher, cotangent):
    shape = jax.ShapeDtypeStruct
    return pl.pallas_call(
        forward_kernel,
        out_shape=(
            shape((32, 8, 128), F32), shape((D, 3 * HC), BF), shape((ROWS, D), BF), shape((ROWS, D), BF), shape((ROWS, HC), BF),
            shape((KEYS, 2 * HC), BF), shape((8, 1, ROWS), F32), shape((HC, D), BF), shape((FF // 2, D), BF), shape((D, FF // 2), BF),
            shape((ROWS, HC), BF), shape((ROWS, D), F32), shape((384, D), BF), shape((384, D), F32), shape((104, 128), F32),
        ),
        in_specs=[VM] * 6 + [HBM, VM, HBM, HBM],
        out_specs=(VM,) + (HBM,) * 5 + (VM,) + (HBM,) * 4 + (VM,) + (HBM,) * 2 + (VM,),
        scratch_shapes=[
            pltpu.VMEM((PROMPT + CONT, 384), F32), pltpu.VMEM((384, D), BF), pltpu.VMEM((384, D), BF),
            pltpu.VMEM((ROWS, HC), BF), pltpu.VMEM((384, D), BF), pltpu.VMEM((384, D), F32),
            pltpu.VMEM((D, 3 * HC), BF), pltpu.VMEM((ROWS, D), BF), pltpu.VMEM((ROWS, D), BF), pltpu.VMEM((ROWS, HC), BF),
            pltpu.VMEM((KEYS, 2 * HC), BF), pltpu.VMEM((HC, D), BF), pltpu.VMEM((FF // 2, D), BF), pltpu.VMEM((D, FF // 2), BF),
            pltpu.VMEM((HC, D), BF), pltpu.VMEM((D, FF // 2), BF), pltpu.VMEM((FF // 2, D), BF), pltpu.VMEM((ROWS, D), BF),
            pltpu.VMEM((ROWS, HC), BF), pltpu.VMEM((ROWS, FF // 2), BF), pltpu.VMEM((ROWS, FF // 2), BF), pltpu.VMEM((384, D), F32),
            pltpu.VMEM((ROWS, D), BF), pltpu.VMEM((KEYS, D), BF), pltpu.VMEM((KEYS, D), BF), pltpu.VMEM((HC, D), BF),
            pltpu.VMEM((64, FF // 2), BF), pltpu.VMEM((256, D), BF), pltpu.SemaphoreType.DMA((140,)), pltpu.SemaphoreType.DMA((140,)), pltpu.SemaphoreType.DMA((14,)),
        ],
        compiler_params=pltpu.CompilerParams(collective_id=0, has_side_effects=True, vmem_limit_bytes=63 << 20),
    )(tokens, small, qkv, out, up, down, jnp.asarray(rotary_table(PROMPT + CONT)), jnp.asarray(index_table(128)), teacher, cotangent)


def add_rows(dst, dst_rows, src, src_rows, count, cols, tile):
    @pl.loop(0, count // tile)
    def _(i):
        to = pl.ds(pl.multiple_of(dst_rows + i * tile, tile), tile)
        more = src[pl.ds(pl.multiple_of(src_rows + i * tile, tile), tile), cols].astype(F32)
        dst[to, :] = (dst[to, :].astype(F32) + more).astype(dst.dtype)


def scatter_steps(net, src, rb, col, width, before, got_a, got_b, got_z, put):
    half = width // 2
    a, b, both = pl.ds(col, half), pl.ds(col + half, half), pl.ds(col, width)
    quad = 4 * rb
    tile = min(64, rb)
    at = lambda y, x: pl.ds((y * 2 + x) * quad, quad)
    held = {}

    def first():
        for made in before:
            made.wait()
        rows = pl.ds((1 - net.y) * 2 * quad, 2 * quad)
        held[0] = [net.copy(src.at[rows, a], got_a.at[pl.ds(0, 2 * quad)], net.up)]
        for y in range(2):
            held[0].append(net.copy(src.at[at(y, 1 - net.x), b], got_b.at[pl.ds(y * quad, quad)], net.right))

    def second():
        for made in held[0]:
            made.wait_recv()
        add_rows(got_a, (1 - net.x) * quad, src, (net.y * 2 + 1 - net.x) * quad, quad, a, tile)
        add_rows(got_b, (1 - net.y) * quad, src, ((1 - net.y) * 2 + net.x) * quad, quad, b, tile)
        held[1] = [
            net.copy(got_a.at[pl.ds((1 - net.x) * quad, quad)], got_a.at[pl.ds(2 * quad, quad)], net.right),
            net.copy(got_b.at[pl.ds((1 - net.y) * quad, quad)], got_b.at[pl.ds(2 * quad, quad)], net.up),
        ]
        add_rows(got_a, net.x * quad, src, (net.y * 2 + net.x) * quad, quad, a, tile)
        add_rows(got_b, net.y * quad, src, (net.y * 2 + net.x) * quad, quad, b, tile)

    def third():
        for made in held[1]:
            made.wait_recv()
        add_rows(got_a, net.x * quad, got_a, 2 * quad, quad, slice(None), tile)
        add_rows(got_b, net.y * quad, got_b, 2 * quad, quad, slice(None), tile)
        held[2] = []
        for j in (1, 2, 3):
            there = (net.z + j) % RANKS * rb
            peer = net.line[j - 1]
            held[2].append(net.copy(got_a.at[pl.ds(net.x * quad + there, rb)], got_z.at[j - 1, :, pl.ds(0, half)], peer))
            held[2].append(net.copy(got_b.at[pl.ds(net.y * quad + there, rb)], got_z.at[j - 1, :, pl.ds(half, half)], peer))

    def last():
        for made in held[2]:
            made.wait_recv()
        for k, (got, way) in enumerate(((got_a, net.x), (got_b, net.y))):
            cols = slice(k * half, k * half + half)

            @pl.loop(0, rb // tile)
            def _(i):
                rows = pl.ds(pl.multiple_of(way * quad + net.z * rb + i * tile, tile), tile)
                value = got[rows, :].astype(F32)
                for j in range(3):
                    value = value + got_z[j, tile_at(i, tile), cols].astype(F32)
                put(tile_at(i, tile), slice(col + k * half, col + k * half + half), value)

    return [first, second, third, last]


def sum_steps(net, value, got):
    held = {}
    peers = [net.core, net.right, net.up]

    def make(i):
        def step():
            if i > 0:
                net.settle(held[i - 1])
                value[...] = value[...] + got[i - 1]
            if i < 3:
                held[i] = net.copy(value, got.at[i], peers[i])
            else:
                held[3] = [net.copy(value, got.at[3 + net.z], peer) for peer in net.line]
                got[3 + net.z] = value[...]

        return step

    def last():
        for made in held[3]:
            net.settle(made)
        value[...] = (got[3] + got[4]) + (got[5] + got[6])

    return [make(i) for i in range(4)] + [last]


def attend_back(query, grad, keys, values, masks, stat, head):
    lanes = head_lanes(query.shape[0])
    lanes = lanes if head == 0 else ~lanes
    own = jnp.where(lanes, query.astype(F32) * SCALE, 0.0).astype(BF)
    own_grad = jnp.where(lanes, grad.astype(F32), 0.0).astype(BF)
    inner, kept = 0.0, []
    for k, v, m in zip(keys, values, masks):
        scores = nt(k, own)
        probs = jnp.exp((scores if m is None else jnp.where(m, scores, NEGATIVE)) - stat)
        prob_grad = nt(v, own_grad)
        inner = inner + jnp.sum(probs * prob_grad, axis=0, keepdims=True)
        kept.append((probs, prob_grad))
    dq, dks, dvs = 0.0, [], []
    for k, (probs, prob_grad) in zip(keys, kept):
        score_grad = (probs * (prob_grad - inner)).astype(BF)
        dq = dq + tn(k, score_grad)
        dks.append(nn(score_grad, own))
        dvs.append(nn(probs.astype(BF), own_grad))
    return dq[head * HD : head * HD + HD] * SCALE, dks, dvs


def backward_kernel(
    rows, small, value_in, gain, rotary, lse, h_q, h_kv, h_att, h_first, h_x, h_w_qkv, h_joint, dw_out_in, dw_down_in, dw_up_in,
    value, o_qkv, o_out, o_up, o_down, joint_own,
    q, kv, att_grad, first, x, w_qkv, joint_in, dw_qkv, dw_out, dw_down, dw_up, spread, pairs, got_pairs, far_k, far_v, projected, joint, peer_joint,
    got_s, s_qkv, s_up, peer_qkv, peer_up, *rest,
):
    bufs, (send, recv, local) = rest[:-3], rest[-3:]
    net = Net(send, recv)
    c, z, chip = net.c, net.z, net.chip
    loads = [pltpu.make_async_copy(src, dst, local.at[i]) for i, (src, dst) in enumerate(
        ((dw_down_in, dw_down), (dw_up_in, dw_up), (dw_out_in, dw_out), (h_q, q), (h_kv, kv), (h_att, att_grad),
         (h_first, first), (h_w_qkv, w_qkv), (h_x, x), (h_joint, joint_in)))]
    for load in loads:
        load.start()
    value[...] = value_in[...]
    net.enter()
    bufs = list(bufs)
    take3 = lambda: [bufs.pop(0) for _ in range(3)]

    def put_into(ref):
        def put(at, cols, total):
            ref[at, cols] = total

        return put

    clock, tasks = [0], []

    def advance(until):
        while clock[0] < until:
            for t, steps in tasks:
                if (clock[0] - t) % 2 == 0 and 0 <= (clock[0] - t) // 2 < len(steps):
                    steps[(clock[0] - t) // 2]()
            clock[0] += 1

    loads[0].wait()
    tasks.append((0, scatter_steps(net, dw_down, 128, 0, 512, [], *take3(), put_into(o_down))))
    tasks.append((1, scatter_steps(net, dw_down, 128, 512, 512, [], *take3(), put_into(o_down))))
    tasks.append((2, scatter_steps(net, dw_up, 64, 0, 1024, [loads[1]], *take3(), put_into(s_up))))
    tasks.append((3, scatter_steps(net, dw_up, 64, 1024, 1024, [], *take3(), put_into(s_up))))
    advance(2)
    loads[2].wait()
    swaps = []
    for h in range(8):
        theirs = dw_out.at[pl.ds(h * 64 + (1 - c) * 32, 32)]
        swaps.append(net.copy(theirs, spread.at[pl.ds((8 * c + h) * 32, 32)], net.core))
        spread[pl.ds(pl.multiple_of((8 * c + h) * 32, 32), 32), :] = dw_out[pl.ds(pl.multiple_of(h * 64 + c * 32, 32), 32), :]
    tasks.append((4, scatter_steps(net, spread, 32, 0, 1024, [], *take3(), put_into(o_out))))

    length = jnp.sum(jnp.sum(rows[pl.ds(chip * 2, 2), 5:7, :], axis=0), keepdims=True).astype(jnp.int32)
    second = jnp.broadcast_to(small[7:8, :], (PROMPT, 128)) > 0.5
    weight = small[7:8, :]
    pair_sends = []

    def back_pair(pair):
        k_at, v_at = pl.ds(128 * pair, 128), pl.ds(HC + 128 * pair, 128)
        prompts = [(kv[p * PROMPT : (p + 1) * PROMPT, k_at], kv[p * PROMPT : (p + 1) * PROMPT, v_at]) for p in range(2)]
        chosen = [jnp.where(second, b.astype(F32), a.astype(F32)).astype(BF) for a, b in zip(*prompts)]

        def both_heads(row, size, keys, values, masks, place):
            dq, dks, dvs = [], None, None
            for head in range(2):
                stat = lse[2 * pair + head, :, row : row + size]
                d, k_parts, v_parts = attend_back(
                    q[row : row + size, k_at], att_grad[row : row + size, k_at], keys, values, masks, stat, head
                )
                dq.append(d)
                dks = k_parts if dks is None else [a + b for a, b in zip(dks, k_parts)]
                dvs = v_parts if dvs is None else [a + b for a, b in zip(dvs, v_parts)]
            dq = jnp.concatenate(dq, axis=0).T
            projected[row : row + size, k_at] = turn(dq, rotary[pl.ds(place, size), :], -1.0).astype(BF)
            return dks, dvs

        near_k, near_v = None, None
        for i in range(2):
            near = 256 * i + 256
            masks = [None, seen(0, 256 * i, (near, 256), length)]
            near_keys = kv[2 * PROMPT : 2 * PROMPT + near, k_at], kv[2 * PROMPT : 2 * PROMPT + near, v_at]
            dks, dvs = both_heads(
                256 + 256 * i, 256, [chosen[0], near_keys[0]], [chosen[1], near_keys[1]], masks, PROMPT + 256 * i
            )
            if i == 0:
                far_k[...], far_v[...] = dks[0], dvs[0]
                near_k, near_v = dks[1], dvs[1]
            else:
                far_k[...] = far_k[...] + dks[0]
                far_v[...] = far_v[...] + dvs[0]
                near_k = [near_k + dks[1][:256], dks[1][256:]]
                near_v = [near_v + dvs[1][:256], dvs[1][256:]]
        for i in range(2):
            at = slice(256 + 256 * i, 512 + 256 * i)
            table = rotary[PROMPT + 256 * i : PROMPT + 256 * i + 256, :]
            projected[at, HC + 128 * pair : HC + 128 * pair + 128] = turn(near_k[i], table, -1.0).astype(BF)
            projected[at, 2 * HC + 128 * pair : 2 * HC + 128 * pair + 128] = near_v[i].astype(BF)
        for p in range(2):
            place = pl.multiple_of(z * 2 * PSH, 128)
            dks, dvs = both_heads(
                128 * p, 128, [prompts[p][0]], [prompts[p][1]], [seen(0, z * 2 * PSH, (PROMPT, 128))], place
            )
            share = weight if p == 1 else 1.0 - weight
            at = slice(p * PROMPT, p * PROMPT + PROMPT)
            pairs[pair, at, :128] = (dks[0] + share * far_k[...]).astype(BF)
            pairs[pair, at, 128:] = (dvs[0] + share * far_v[...]).astype(BF)
        for j in (1, 2, 3):
            for p in range(2):
                there = pl.ds(p * PROMPT + (z + j) % RANKS * 2 * PSH, 2 * PSH)
                pair_sends.append(
                    net.copy(pairs.at[pair, there], got_pairs.at[j - 1, pair, pl.ds(p * 2 * PSH, 2 * PSH)], net.line[j - 1])
                )

    for load in loads[3:6]:
        load.wait()
    back_pair(0)
    advance(3)
    back_pair(1)
    advance(4)
    for made in swaps:
        made.wait_recv()
    back_pair(2)
    advance(5)
    back_pair(3)
    advance(6)
    for made in pair_sends:
        made.wait_recv()
    table = rotary[pl.ds(pl.multiple_of(z * 2 * PSH, 128), 128), :]
    for pair in range(4):
        for p in range(2):
            at = slice(p * 128, p * 128 + 128)
            total = pairs[pair, pl.ds(pl.multiple_of(p * PROMPT + z * 2 * PSH, 128), 128), :].astype(F32)
            for j in range(3):
                total = total + got_pairs[j, pair, at, :].astype(F32)
            projected[at, HC + 128 * pair : HC + 128 * pair + 128] = turn(total[:, :128], table, -1.0).astype(BF)
            projected[at, 2 * HC + 128 * pair : 2 * HC + 128 * pair + 128] = total[:, 128:].astype(BF)

    def weight_columns(col, width):
        @pl.loop(0, D // 256)
        def _(i):
            part = tn(first[:, tile_at(i, 256)], projected[:, col : col + width])
            dw_qkv[tile_at(i, 256), col : col + width] = part.astype(BF)

    for load in loads[6:]:
        load.wait()
    weight_columns(0, 768)
    tasks.append((6, scatter_steps(net, dw_qkv, 64, 0, 768, [], *take3(), put_into(s_qkv))))
    advance(7)
    weight_columns(768, 768)
    tasks.append((7, scatter_steps(net, dw_qkv, 64, 768, 768, [], *take3(), put_into(s_qkv))))
    advance(8)
    fg_sum, fg_normed = jnp.zeros((1, D), F32), jnp.zeros((1, D), F32)
    bias = jnp.zeros((1, 3 * HC), F32)

    def first_rows(i, sums):
        at = tile_at(i, 128)
        here = projected[at, :]
        grad = nt(here, w_qkv[...])
        normed = norm_rows(x[at, :])
        joint[at, :] = grad * gain[...] + joint_in[at, :]
        return (
            sums[0] + jnp.sum(grad, axis=0, keepdims=True),
            sums[1] + jnp.sum(grad * normed, axis=0, keepdims=True),
            sums[2] + jnp.sum(here.astype(F32), axis=0, keepdims=True),
        )

    fg_sum, fg_normed, bias = lax.fori_loop(0, ROWS // 128, first_rows, (fg_sum, fg_normed, bias))
    ranges = ((0, PSH, lambda o: o * PSH), (PSH, PSH, lambda o: 2 * PSH + o * PSH), (2 * PSH, HALF, lambda o: 4 * PSH + o * HALF))
    joints = [
        net.copy(joint.at[pl.ds(there(1 - c), size)], peer_joint.at[pl.ds(at, size)], net.core) for at, size, there in ranges
    ]
    for i in range(8):
        cols = slice(128 * i, 128 * i + 128)
        value[i : i + 1, :] = value[i : i + 1, :] + fg_normed[:, cols]
        value[8 + i : 9 + i, :] = value[8 + i : 9 + i, :] + fg_sum[:, cols]
    for i in range(12):
        row = pl.ds(40 + i // 4 * 8 + c * 4 + i % 4, 1)
        value[row, :] = value[row, :] + bias[:, 128 * i : 128 * i + 128]
    sums = sum_steps(net, value, got_s)
    sums[0]()
    advance(9)
    for made in joints:
        made.wait_recv()
    for at, size, there in ranges:
        mine = pl.ds(pl.multiple_of(there(c), 64), size)
        joint_own[at : at + size, :] = joint[mine, :] + peer_joint[at : at + size, :]
    sums[1]()
    advance(10)
    sums[2]()
    ups = []

    def give(total, peer_ref):
        return net.copy(total.at[pl.ds((1 - c) * 32, 32)], peer_ref, net.core)

    advance(11)
    ups.append(give(s_up, peer_up))
    sums[3]()
    advance(12)
    sums[4]()
    advance(16)
    ups.append(give(s_qkv, peer_qkv))
    own_rows = pl.ds(pl.multiple_of(c * 32, 32), 32)
    ups[0].wait_recv()
    for i in range(16):
        for who, part in ((c, s_up[own_rows, 128 * i : 128 * i + 128]), (1 - c, peer_up[:, 128 * i : 128 * i + 128])):
            o_up[:, pl.ds(pl.multiple_of((2 * i + who) * 128, 128), 128)] = part
    ups[1].wait_recv()
    for i in range(3):
        for who, part in ((c, s_qkv[own_rows, HC * i : HC * i + HC]), (1 - c, peer_qkv[:, HC * i : HC * i + HC])):
            o_qkv[:, pl.ds(pl.multiple_of(i * D + who * HC, 128), HC)] = part
    net.leave()


def backward(*args):
    shape = jax.ShapeDtypeStruct
    bufs = []
    for rb, width, count in ((128, 512, 2), (64, 1024, 2), (32, 1024, 1), (64, 768, 2)):
        for _ in range(count):
            bufs += [pltpu.VMEM((12 * rb, width // 2), BF), pltpu.VMEM((12 * rb, width // 2), BF), pltpu.VMEM((3, rb, width), BF)]
    return pl.pallas_call(
        backward_kernel,
        out_shape=(
            shape((104, 128), F32), shape((32, 3 * D), F32), shape((32, D), F32), shape((32, FF), F32), shape((128, D), F32),
            shape((384, D), F32),
        ),
        in_specs=[VM] * 6 + [HBM] * 10,
        out_specs=(VM,) * 6,
        scratch_shapes=[
            pltpu.VMEM((ROWS, HC), BF), pltpu.VMEM((KEYS, 2 * HC), BF), pltpu.VMEM((ROWS, HC), BF), pltpu.VMEM((ROWS, D), BF),
            pltpu.VMEM((ROWS, D), BF), pltpu.VMEM((D, 3 * HC), BF), pltpu.VMEM((ROWS, D), F32),
            pltpu.VMEM((D, 3 * HC), BF), pltpu.VMEM((HC, D), BF), pltpu.VMEM((FF // 2, D), BF), pltpu.VMEM((D, FF // 2), BF),
            pltpu.VMEM((HC, D), BF), pltpu.VMEM((4, 2 * PROMPT, 256), BF), pltpu.VMEM((3, 4, 4 * PSH, 256), BF),
            pltpu.VMEM((PROMPT, 128), F32), pltpu.VMEM((PROMPT, 128), F32), pltpu.VMEM((ROWS, 3 * HC), BF),
            pltpu.VMEM((ROWS, D), F32), pltpu.VMEM((384, D), F32), pltpu.VMEM((7, 104, 128), F32),
            pltpu.VMEM((64, 3 * HC), F32), pltpu.VMEM((64, FF // 2), F32), pltpu.VMEM((32, 3 * HC), F32), pltpu.VMEM((32, FF // 2), F32),
        ] + bufs
        + [pltpu.SemaphoreType.DMA((140,)), pltpu.SemaphoreType.DMA((140,)), pltpu.SemaphoreType.DMA((10,))],
        compiler_params=pltpu.CompilerParams(collective_id=1, has_side_effects=True, vmem_limit_bytes=63 << 20),
    )(*args)


def fast_body(
    tokens, valid, prompt_of, teacher, cotangent,
    ln1_gain, ln1_bias, ln2_gain, ln2_bias, qkv_weight, qkv_bias, out_weight, out_bias,
    up_weight, up_bias, down_weight, down_bias,
):
    c = lax.axis_index("core")
    z = lax.axis_index("chip")
    chips = lax.axis_size("chip")
    nh = HC // HD
    rd = down_weight.shape[0]
    device = lax.axis_index(ALL)
    pad = lambda v: jnp.pad(v.astype(F32), (0, 128 - v.shape[0]))[None]
    live_own = (valid > 0).astype(F32)
    small = jnp.concatenate(
        [
            jnp.concatenate([ln1_gain, ln1_bias, ln2_gain, ln2_bias]).astype(F32)[None],
            pad(jnp.concatenate([out_bias, down_bias])),
            pad(qkv_bias),
            pad(up_bias),
            live_own.reshape(3, 128),
            jnp.broadcast_to(prompt_of.astype(F32)[:, None], (1, 128)),
        ]
    )
    rows, w_qkv, x_own, first_own, q, kv, lse, dw_out, dw_down, dw_up, att_grad, joint, output, out_grad, value = forward(
        tokens,
        small,
        qkv_weight,
        out_weight,
        up_weight,
        down_weight,
        teacher,
        cotangent,
    )
    gain1 = rows[:, 0, :32].reshape(-1)
    count_all = jnp.sum(rows[:, 4:7])
    value, s_qkv, s_out, s_up, s_down, joint = backward(
        rows, small, value, gain1[None], jnp.asarray(rotary_table(PROMPT + CONT)), lse, q, kv, att_grad, first_own, x_own,
        w_qkv, joint, dw_out, dw_down, dw_up,
    )
    own_normed, own_rstd = normalize(tokens.astype(F32))
    input_grad = out_grad + own_rstd * (
        joint
        - jnp.mean(joint, axis=-1, keepdims=True)
        - own_normed * jnp.mean(joint * own_normed, axis=-1, keepdims=True)
    )
    pick = lambda part, own: lax.dynamic_index_in_dim(part.reshape(-1, own), device, axis=0, keepdims=False)
    five = lax.dynamic_index_in_dim(value[:40].reshape(5, 32, 32), device, axis=1, keepdims=False)
    shares = [five[i] for i in range(5)] + [pick(value[40:64], 96), pick(value[64:96], 128)]
    loss_value = value[96, 0] / (count_all * D)
    return (
        output, loss_value, input_grad, shares[0], shares[1], shares[2], shares[3],
        s_qkv, shares[5], s_out, shares[4], s_up, shares[6], s_down, shares[4],
    )


def solution(mesh):
    groups, seats = mesh.shape["grp"], mesh.shape["seq"]
    fine = Mesh(mesh.devices.reshape(groups, seats // 2, 2), ALL)
    rows, row = P(ALL, None), P(ALL)
    in_specs = (rows, row, row, rows, rows) + (row,) * 4 + (rows, row) * 4
    out_specs = (rows, P(), rows) + (row,) * 4 + (rows, row) * 4
    return jax.shard_map(fast_body if (groups, seats) == (4, 8) else generic_body, mesh=fine, in_specs=in_specs, out_specs=out_specs, check_vma=False)
```
